32 devices in a mesh: groups: 2 (over y), lon: 8 (over z, x), dom: 2 (over core).
Axes of the slice: x: 2, y: 2, z: 4, core: 2. Of those that a mesh axis runs over, the one named last changes fastest.
Arguments:
- ensemble_state: float32 [32, 4, 256, 256], P(('groups', 'dom'), None, 'lon'), parts along dimension 0, may hold values from -6 to 6
- proposal_noise: bfloat16 [2, 32, 4, 256, 256], P(None, ('groups', 'dom'), None, 'lon'), parts along dimension 1, may hold values from -1.1953125 to 1.1953125
- courant: float32 [2, 512, 256], P(None, ('groups', 'lon')), parts along dimension 1, may hold values from -0.4 to 0.4
- diffusion: float32 [4], replicated, may hold values from 0.02 to 0.1
- mixing: float32 [4, 4], replicated, may hold values from -3 to 3
- prior_weight: float32 [32], P(('groups', 'dom')), parts along dimension 0, may hold values from -2 to 0
- obs_cell: int32 [4096], P(('groups', 'lon')), parts along dimension 0, may hold values from 0 to 65535, as said below
- obs_value: float32 [4096], P(('groups', 'lon')), parts along dimension 0, may hold values from -6 to 6
- source: int32 [32], P('groups'), parts along dimension 0, may hold values from 0 to 15, as said below
Outputs:
- new_state: float32 [32, 4, 256, 256], P(('groups', 'dom'), None, 'lon'), parts along dimension 0
- log_weight: float32 [32], P(('groups', 'dom')), parts along dimension 0
The draws below stay inside these ranges and needn't reach their ends.
There are 2 independent parts, one for each index of `groups`. The reference program is written for one: setup_inputs(seed, part) draws one part's arguments, and reference() takes and returns one part's arrays. A program takes and returns all parts, laid end to end along the dimension named above; an argument that names none is the same for every part. Nothing has to cross between parts.
Inputs may be any that keep to these rules, and one draw needn't show every extreme that they name: `obs_cell`: entries j * 256 to (j + 1) * 256 - 1 name distinct cells of longitude strip j, that is cells with longitude from j * 32 to (j + 1) * 32 - 1. `source`: the list is nondecreasing.
All inputs are finite; a program needn't handle non-finite values.
Results may differ from the reference program's by a relative error of at most 0.0003.
Values sent between devices are 32-bit elements; how exact they have to be, the bound alone decides.
No kernel may reach another device: no remote copies, remote signals or barrier semaphores. Data moves between devices by JAX's collectives and lax.ppermute only.
A program may use at most 64 MiB of HBM per device.

```python
import math
import jax
import jax.numpy as jnp

FIELDS = 4
STEPS = 2
STRIP = 32
NLAT = 256
OBS_DEV = 256
PART = 16
NLON = 256
NOBS = 2048


def draw_obs_cell(key, part):
    key = jax.random.fold_in(key, 11)
    block_count = NOBS // OBS_DEV
    strip_cells = STRIP * NLAT
    block_keys = jax.random.split(key, block_count)
    chosen = jax.vmap(lambda block_key: jax.random.permutation(block_key, strip_cells)[:OBS_DEV])(block_keys)
    block_start = (jnp.arange(block_count, dtype=jnp.int32) * strip_cells)[:, None]
    return (chosen.astype(jnp.int32) + block_start).reshape(-1)


def draw_obs_value(key, part):
    key = jax.random.fold_in(key, 23)
    value_key, scale_key = jax.random.split(key, 2)
    spread = jnp.exp(jax.random.uniform(scale_key, (NOBS,), jnp.float32, math.log(0.5), math.log(2.0)))
    basic = jnp.clip(jax.random.normal(value_key, (NOBS,), jnp.float32), -3.0, 3.0)
    return (basic * spread).astype(jnp.float32)


def draw_source(key, part):
    key = jax.random.fold_in(key, 37)
    subkeys = jax.random.split(key, 2)
    drawn_sources = jax.random.randint(subkeys[1], (PART,), 0, PART, dtype=jnp.int32)
    ordered = jnp.sort(drawn_sources).astype(jnp.int32)
    ordered = ordered.at[0].set(0)
    ordered = ordered.at[PART - 1].set(PART - 1)
    return ordered.astype(jnp.int32)


def shard_levels(own_key, shape, cuts, smallest, largest):
    loudness = 1.0
    for dim, shards_of in cuts:
        draws = jax.random.uniform(jax.random.fold_in(jax.random.fold_in(own_key, 6), dim), (shards_of,), jnp.float32, smallest / len(cuts), largest / len(cuts))
        loudness = loudness * jnp.repeat(jnp.exp(draws), shape[dim] // shards_of).reshape((-1,) + (1,) * (len(shape) - 1 - dim))
    return loudness


def normal_values(own_key, shape, scale, bound, shards=(), kind=jnp.bfloat16):
    drawn = scale * jax.random.normal(own_key, shape, jnp.float32)
    if shards:
        drawn = drawn * shard_levels(own_key, shape, shards, -0.22, 0.18)
    return jnp.clip(drawn, -bound, bound).astype(kind)


def setup_inputs(seed: int = 0, part: int = 0) -> dict:
    splits = jax.random.split(jax.random.key(seed), 10)
    part_keys = jax.random.split(jax.random.fold_in(splits[9], part), 10)
    ensemble_state = normal_values(part_keys[0], (PART, FIELDS, NLON, NLAT), 1.0, 6.0, ((0, 2), (2, 8)), jnp.float32)
    proposal_noise = normal_values(part_keys[1], (STEPS, PART, FIELDS, NLON, NLAT), 0.2, 1.1953125, ((1, 2), (3, 8)))
    courant = jnp.clip(jax.random.uniform(part_keys[2], (2, NLON, NLAT), jnp.float32, -0.4, 0.4) * shard_levels(part_keys[2], (2, NLON, NLAT), ((1, 8),), -0.4, 0.0), -0.4, 0.4)
    diffusion = jnp.clip(jnp.exp(jax.random.uniform(splits[3], (FIELDS,), jnp.float32, math.log(0.02), math.log(0.1))), 0.02, 0.1)
    mixing = normal_values(splits[4], (FIELDS, FIELDS), 0.2, 3.0, (), jnp.float32)
    prior_weight = jnp.clip(-2.0 + 2.0 * jax.random.uniform(part_keys[5], (PART,), jnp.float32) ** shard_levels(part_keys[5], (PART,), ((0, 2),), -0.2, 0.2), -2.0, 0.0)
    obs_cell = draw_obs_cell(jax.random.fold_in(jax.random.fold_in(splits[9], part), 71), part)
    obs_value = draw_obs_value(jax.random.fold_in(jax.random.fold_in(splits[9], part), 71), part)
    source = draw_source(jax.random.fold_in(jax.random.fold_in(splits[9], part), 71), part)
    return dict(ensemble_state=ensemble_state, proposal_noise=proposal_noise, courant=courant, diffusion=diffusion, mixing=mixing, prior_weight=prior_weight, obs_cell=obs_cell, obs_value=obs_value, source=source)


noise_var = 0.04


def advance(current, courant, diffusion, mixing):
    eastward = jnp.roll(current, -1, axis=2)
    westward = jnp.roll(current, 1, axis=2)
    northward = jnp.concatenate([current[..., 1:], current[..., -1:]], axis=3)
    southward = jnp.concatenate([current[..., :1], current[..., :-1]], axis=3)
    zonal_courant = courant[0][None, None]
    merid_courant = courant[1][None, None]
    diffusion_rate = diffusion[None, :, None, None]
    mixing_term = sum(mixing[:, other][None, :, None, None] * current[:, other:other + 1] for other in range(current.shape[1]))
    result = current - 0.5 * zonal_courant * (eastward - westward) - 0.5 * merid_courant * (northward - southward)
    result = result + (0.5 * zonal_courant * zonal_courant + diffusion_rate) * (eastward - 2.0 * current + westward)
    result = result + (0.5 * merid_courant * merid_courant + diffusion_rate) * (northward - 2.0 * current + southward)
    return result + mixing_term


def reference(ensemble_state, proposal_noise, courant, diffusion, mixing, prior_weight, obs_cell, obs_value, source):
    particles = ensemble_state.shape[0]
    precision = 1.0 + 2.0 * (obs_cell // NLAT).astype(jnp.float32) / NLON
    nudge_gain = 0.25 * precision
    current = ensemble_state
    proposal = jnp.zeros((particles,), jnp.float32)
    for step_index in range(STEPS):
        moved = advance(current, courant, diffusion, mixing)
        plane = moved[:, 0].reshape(particles, NLON * NLAT)
        observed_model = plane[:, obs_cell]
        push_value = nudge_gain[None] * (obs_value[None] - observed_model)
        noise_now = proposal_noise[step_index].astype(jnp.float32)
        noise_cells = noise_now[:, 0].reshape(particles, NLON * NLAT)[:, obs_cell]
        proposal = proposal + jnp.sum(push_value * push_value + 2.0 * push_value * noise_cells, axis=1)
        plane = plane.at[:, obs_cell].add(push_value)
        moved = moved.at[:, 0].set(plane.reshape(particles, NLON, NLAT))
        current = moved + noise_now
    observed_model = current[:, 0].reshape(particles, NLON * NLAT)[:, obs_cell]
    difference = obs_value[None] - observed_model
    misfit = jnp.sum(precision[None] * difference * difference, axis=1)
    log_weight = prior_weight - (0.5 * misfit + proposal / (2.0 * noise_var)) / (256.0 * OBS_DEV)
    new_state = current[source]
    return new_state, log_weight
```

```python
import functools

import jax
import jax.numpy as jnp
from jax import lax
from jax.experimental import pallas as pl
from jax.experimental.pallas import tpu as pltpu
from jax.sharding import PartitionSpec as P

noise_var = 0.04
VMEM = pl.BlockSpec(memory_space=pltpu.VMEM)
SMEM = pl.BlockSpec(memory_space=pltpu.SMEM)
ANY = pl.BlockSpec(memory_space=pl.ANY)
BF16 = jnp.bfloat16
F32 = jnp.float32


def north(v):
    return pltpu.roll(v, v.shape[1] - 1, 1)


def south(v):
    return pltpu.roll(v, 1, 1)


def coefficients(zonal, merid, rate, self_mix):
    lat = lax.broadcasted_iota(jnp.int32, zonal.shape, 1)
    zonal_half, zonal_rate = 0.5 * zonal, 0.5 * zonal * zonal + rate
    merid_half, merid_rate = 0.5 * merid, 0.5 * merid * merid + rate
    east, west = zonal_rate - zonal_half, zonal_rate + zonal_half
    to_north, to_south = merid_rate - merid_half, merid_rate + merid_half
    centre = 1.0 + self_mix - 2.0 * zonal_rate - 2.0 * merid_rate
    last, first = lat == zonal.shape[1] - 1, lat == 0
    centre = centre + jnp.where(last, to_north, 0.0) + jnp.where(first, to_south, 0.0)
    to_north = jnp.where(last, 0.0, to_north)
    to_south = jnp.where(first, 0.0, to_south)
    return centre, east, west, to_north, to_south


def mixed(mixing, field, values):
    total = None
    for other, value in enumerate(values):
        if other != field:
            term = mixing[field, other] * value
            total = term if total is None else total + term
    return total


def pick_rows(kinds, particles, fields, strip, rows, columns):
    out = lax.broadcasted_iota(jnp.int32, (rows, columns), 0)
    col = lax.broadcasted_iota(jnp.int32, (rows, columns), 1)
    want = jnp.full((rows, columns), -1, jnp.int32)
    for place, (field, x) in enumerate(kinds):
        inside = (out >= place * particles) & (out < (place + 1) * particles)
        target = (out - place * particles) * (fields * strip) + field * strip + x
        want = jnp.where(inside, target, want)
    return (col == want).astype(BF16)


def gather_rows(ref, first, stride, count):
    sub = lax.broadcasted_iota(jnp.int32, (count, ref.shape[1]), 0)
    out = None
    for p in range(count):
        row = jnp.broadcast_to(ref[pl.ds(first + p * stride, 1), :], sub.shape)
        out = row if out is None else jnp.where(sub == p, row, out)
    return out


def prepare(sizes, state, noise, courant, diffusion, mixing, cell, value,
            send_east, send_west, maps, noise_rows):
    particles, fields, strip, lats, strips = sizes
    x0 = lax.axis_index("lon") * strip
    shift = lats.bit_length() - 1
    local_cell = cell[...] - x0 * lats
    obs_lon = lax.shift_right_arithmetic(local_cell, shift)
    obs_lat = local_cell & (lats - 1)
    count = cell.shape[1]
    here = lax.broadcasted_iota(jnp.int32, (strip, count), 0) == obs_lon
    val = value[...]
    high = val.astype(BF16)
    rest = val - high.astype(F32)
    mid = rest.astype(BF16)
    low = (rest - mid.astype(F32)).astype(BF16)
    zero = jnp.zeros((strip, count), F32)
    parts = [jnp.where(here, 1.0, zero)]
    parts += [jnp.where(here, p.astype(F32), zero) for p in (high, mid, low)]
    left = jnp.concatenate(parts, 0).astype(BF16)
    right = (lax.broadcasted_iota(jnp.int32, (lats, count), 0) == obs_lat).astype(F32).astype(BF16)
    dense = lax.dot_general(left, right, (((1,), (1,)), ((), ())), preferred_element_type=F32)
    seen = dense[:strip]
    lon = (lax.broadcasted_iota(jnp.int32, (strip, lats), 0) + x0).astype(F32)
    precision = 1.0 + 2.0 * lon / (strip * strips)
    gain = seen * (0.25 * precision)
    weight = seen * precision
    target = dense[strip:2 * strip] + (dense[2 * strip:3 * strip] + dense[3 * strip:])
    maps[0] = gain
    maps[1] = weight
    maps[2] = target

    kinds = [(f, x) for x in (0, strip - 1) for f in range(fields)]
    pick = pick_rows(kinds, particles, fields, strip, len(kinds) * particles, noise.shape[1])
    rows = jnp.dot(pick, noise[0], preferred_element_type=F32)
    noise_rows[0] = rows[:particles]
    noise_rows[1] = rows[fields * particles:(fields + 1) * particles]

    def edge(x, inner, out, base):
        here = [gather_rows(state, f * strip + x, fields * strip, particles) for f in range(fields)]
        beside = [gather_rows(state, f * strip + inner, fields * strip, particles) for f in range(fields)]
        for f in range(fields):
            centre, east, west, to_north, to_south = coefficients(
                courant[0, x:x + 1], courant[1, x:x + 1], diffusion[f], mixing[f, f])
            known, missing = (east, west) if inner > x else (west, east)
            moved = (centre * here[f] + known * beside[f] + to_north * north(here[f])
                     + to_south * south(here[f]) + mixed(mixing, f, here))
            if f == 0:
                g = gain[x:x + 1]
                moved = moved + g * (target[x:x + 1] - moved)
                missing = (1.0 - g) * missing
            moved = moved + rows[base + f * particles:base + (f + 1) * particles]
            out[f * particles:(f + 1) * particles] = here[f]
            out[(fields + f) * particles:(fields + f + 1) * particles] = moved
            out[2 * fields * particles + f:2 * fields * particles + f + 1] = missing
        out[2 * fields * particles + fields:] = jnp.zeros((8 - fields, lats), F32)

    edge(strip - 1, strip - 2, send_east, fields * particles)
    edge(0, 1, send_west, 0)


def bulk(sizes, state, noise, courant, diffusion, mixing, maps,
         out, partial, noise_rows, coefs, middle):
    particles, fields, strip, lats, strips = sizes
    lon = lax.broadcasted_iota(jnp.int32, (strip, lats), 0)
    for f in range(fields):
        centre, east, west, to_north, to_south = coefficients(
            courant[0], courant[1], diffusion[f], mixing[f, f])
        coefs[f, 0] = centre
        coefs[f, 1] = jnp.where(lon == strip - 1, 0.0, east)
        coefs[f, 2] = jnp.where(lon == 0, 0.0, west)
        coefs[f, 3] = to_north
        coefs[f, 4] = to_south
    kinds = [(0, x) for x in (0, 1, strip - 2, strip - 1)]
    pick = pick_rows(kinds, particles, fields, strip, len(kinds) * particles, noise.shape[1])
    noise_rows[...] = jnp.dot(pick, noise[1], preferred_element_type=F32)

    def rows_of(p, f):
        return pl.ds(pl.multiple_of(p * (fields * strip) + f * strip, strip), strip)

    def moved(values, f):
        v = values[f]
        return (coefs[f, 0] * v + coefs[f, 1] * pltpu.roll(v, strip - 1, 0) + coefs[f, 2] * pltpu.roll(v, 1, 0)
                + coefs[f, 3] * north(v) + coefs[f, 4] * south(v) + mixed(mixing, f, values))

    def body(p, carry):
        values = [state[rows_of(p, f), :] for f in range(fields)]
        total = None
        for f in range(fields):
            new = moved(values, f)
            add = noise[0, rows_of(p, f), :].astype(F32)
            if f == 0:
                push = maps[0] * (maps[2] - new)
                new = new + push
                total = jnp.where((lon > 0) & (lon < strip - 1), push * (push + 2.0 * add), 0.0)
            middle[f] = new + add
        values = [middle[f] for f in range(fields)]
        for f in range(fields):
            new = moved(values, f)
            add = noise[1, rows_of(p, f), :].astype(F32)
            if f == 0:
                push = maps[0] * (maps[2] - new)
                new = new + push + add
                miss = maps[2] - new
                term = ((0.5 / noise_var) * (push * (push + 2.0 * add)) + (0.5 * maps[1]) * (miss * miss))
                total = (0.5 / noise_var) * total + jnp.where((lon > 1) & (lon < strip - 2), term, 0.0)
            else:
                new = new + add
            out[rows_of(p, f), :] = new
        total = jnp.sum(total, axis=0, keepdims=True)
        partial[pl.ds(p, 1), :] = total[:, :128] + total[:, 128:]
        return carry

    lax.fori_loop(0, particles, body, 0)


def correct(sizes, own_east, own_west, from_west, from_east, courant, diffusion, mixing, maps,
            noise0, noise1, current, partial, out, weight):
    particles, fields, strip, lats, strips = sizes
    n = fields * particles

    def split(ref, start):
        return [ref[start + f * particles:start + (f + 1) * particles] for f in range(fields)]

    def wide(v):
        return v[:, :128] + v[:, 128:]

    def push_terms(push, add):
        return (0.5 / noise_var) * (push * (push + 2.0 * add))

    for block in range(n):
        spot = pl.ds(block * strip + 8, strip - 16)
        out[spot, :] = current[spot, :]
    total = partial[...]
    for x, inner, own, other, at in ((0, 1, own_west, from_west, 0), (strip - 1, strip - 2, own_east, from_east, 1)):
        own_state, own_first = split(own, 0), split(own, n)
        other_state, other_first = split(other, 0), split(other, n)
        gain, observed, seen = maps[0, x:x + 1], maps[2, x:x + 1], maps[1, x:x + 1]
        first, outside, edge_coefs, inner_out = [], [], [], []
        for f in range(fields):
            coefs = coefficients(courant[0, x:x + 1], courant[1, x:x + 1], diffusion[f], mixing[f, f])
            outer = coefs[2] if inner > x else coefs[1]
            edge_coefs.append((coefs[0], outer, coefs[3], coefs[4]))
            coefs = coefficients(courant[0, inner:inner + 1], courant[1, inner:inner + 1], diffusion[f], mixing[f, f])
            inner_out.append(coefs[2] if inner > x else coefs[1])
            row = 2 * n + f
            outside.append(other_first[f] + other[row:row + 1] * own_state[f])
            step = outer * other_state[f]
            if f == 0:
                step = (1.0 - gain) * step
                result = own_first[0] + step
                add = noise0[at]
                push = (gain / (1.0 - gain)) * (observed - (result - add))
                total = total + wide(push_terms(push, add))
            first.append(step)
        for f in range(fields):
            centre, outer, to_north, to_south = edge_coefs[f]
            step = (centre * first[f] + outer * outside[f] + to_north * north(first[f])
                    + to_south * south(first[f]) + mixed(mixing, f, first))
            beside = inner_out[f] * first[f]
            if f == 0:
                g_in = maps[0, inner:inner + 1]
                step = (1.0 - gain) * step
                beside = (1.0 - g_in) * beside
            tile = min(x, inner) // 8 * 8
            sub = lax.broadcasted_iota(jnp.int32, (8, lats), 0)
            for p in range(particles):
                spot = pl.ds(p * fields * strip + f * strip + tile, 8)
                change = jnp.where(sub == x - tile, jnp.broadcast_to(step[p:p + 1], sub.shape),
                                   jnp.where(sub == inner - tile, jnp.broadcast_to(beside[p:p + 1], sub.shape), 0.0))
                out[spot, :] = current[spot, :] + change
            if f == 0:
                for place in (x, inner):
                    result = gather_rows(out, place, fields * strip, particles)
                    g, v, s = maps[0, place:place + 1], maps[2, place:place + 1], maps[1, place:place + 1]
                    k = (0, 1, strip - 2, strip - 1).index(place) * particles
                    add = noise1[k:k + particles]
                    push = (g / (1.0 - g)) * (v - (result - add))
                    miss = v - result
                    total = total + wide(push_terms(push, add) + (0.5 * s) * (miss * miss))
    weight[...] = total


def assemble(sizes, source, current, received, out, sems):
    particles = sizes[0]
    dom = lax.axis_index("dom")

    def copy(j, ref, at):
        return pltpu.make_async_copy(ref.at[at], out.at[j], sems.at[j])

    for j in range(particles):
        wanted = source[dom * particles + j]
        mine = wanted // particles == dom
        at = wanted % particles

        @pl.when(mine)
        def _():
            copy(j, current, at).start()

        @pl.when(jnp.logical_not(mine))
        def _():
            copy(j, received, at).start()

    for j in range(particles):
        copy(j, current, 0).wait()


def local(ensemble_state, proposal_noise, courant, diffusion, mixing, prior_weight, obs_cell, obs_value, source):
    particles, fields, strip, lats = ensemble_state.shape
    strips = lax.axis_size("lon")
    sizes = (particles, fields, strip, lats, strips)
    rows = particles * fields * strip
    state = ensemble_state.reshape(rows, lats)
    noise = proposal_noise.reshape(2, rows, lats)
    packet = jax.ShapeDtypeStruct((2 * particles * fields + 8, lats), F32)
    shape = jax.ShapeDtypeStruct

    send_east, send_west, maps, noise0 = pl.pallas_call(
        functools.partial(prepare, sizes),
        out_shape=(packet, packet, shape((3, strip, lats), F32), shape((2, particles, lats), F32)),
        in_specs=[VMEM, VMEM, VMEM, SMEM, SMEM, VMEM, VMEM],
        out_specs=(VMEM,) * 4,
        cost_estimate=pl.CostEstimate(flops=1000000, bytes_accessed=2000000, transcendentals=0),
    )(state, noise, courant, diffusion, mixing, obs_cell[None], obs_value[None])

    eastward = [(i, (i + 1) % strips) for i in range(strips)]
    westward = [(i, (i - 1) % strips) for i in range(strips)]
    from_west = lax.ppermute(send_east, "lon", eastward)
    from_east = lax.ppermute(send_west, "lon", westward)

    current, partial, noise1 = pl.pallas_call(
        functools.partial(bulk, sizes),
        out_shape=(shape((rows, lats), F32), shape((particles, 128), F32), shape((4 * particles, lats), F32)),
        in_specs=[VMEM, VMEM, VMEM, SMEM, SMEM, VMEM],
        out_specs=(VMEM,) * 3,
        scratch_shapes=[pltpu.VMEM((fields, 5, strip, lats), F32), pltpu.VMEM((fields, strip, lats), F32)],
        compiler_params=pltpu.CompilerParams(vmem_limit_bytes=32 * 1024 * 1024),
        cost_estimate=pl.CostEstimate(flops=30000000, bytes_accessed=4000000, transcendentals=0),
    )(state, noise, courant, diffusion, mixing, maps)

    current, weight = pl.pallas_call(
        functools.partial(correct, sizes),
        out_shape=(shape((rows, lats), F32), shape((particles, 128), F32)),
        in_specs=[VMEM] * 5 + [SMEM, SMEM] + [VMEM] * 5,
        out_specs=(VMEM,) * 2,
        cost_estimate=pl.CostEstimate(flops=1000000, bytes_accessed=1000000, transcendentals=0),
    )(send_east, send_west, from_west, from_east, courant, diffusion, mixing, maps, noise0, noise1, current, partial)

    current = current.reshape(particles, fields, strip, lats)
    received = lax.ppermute(current, "dom", [(0, 1), (1, 0)])
    bit = 1
    while bit < strips:
        weight = weight + lax.ppermute(weight, "lon", [(i, i ^ bit) for i in range(strips)])
        bit *= 2

    new_state = pl.pallas_call(
        functools.partial(assemble, sizes),
        out_shape=shape((particles, fields, strip, lats), F32),
        in_specs=[SMEM, ANY, ANY],
        out_specs=ANY,
        scratch_shapes=[pltpu.SemaphoreType.DMA((particles,))],
        cost_estimate=pl.CostEstimate(flops=0, bytes_accessed=2000000, transcendentals=0),
    )(source, current, received)

    log_weight = prior_weight - jnp.sum(weight, axis=1) / (256.0 * obs_cell.shape[0])
    return new_state, log_weight


def solution(mesh):
    placed = (
        P(("groups", "dom"), None, "lon", None),
        P(None, ("groups", "dom"), None, "lon", None),
        P(None, ("groups", "lon"), None),
        P(),
        P(),
        P(("groups", "dom")),
        P(("groups", "lon")),
        P(("groups", "lon")),
        P("groups"),
    )
    return jax.shard_map(
        local,
        mesh=mesh,
        in_specs=placed,
        out_specs=(P(("groups", "dom"), None, "lon", None), P(("groups", "dom"))),
        check_vma=False,
    )
```

```python
import functools

import jax
import jax.numpy as jnp
from jax import lax
from jax.experimental import pallas as pl
from jax.experimental.pallas import tpu as pltpu
from jax.sharding import PartitionSpec as P

noise_var = 0.04
VMEM = pl.BlockSpec(memory_space=pltpu.VMEM)
SMEM = pl.BlockSpec(memory_space=pltpu.SMEM)
ANY = pl.BlockSpec(memory_space=pl.ANY)
LIMIT = pltpu.CompilerParams(vmem_limit_bytes=16 * 1024 * 1024)
BF16 = jnp.bfloat16
F32 = jnp.float32


def north(v):
    return pltpu.roll(v, v.shape[1] - 1, 1)


def south(v):
    return pltpu.roll(v, 1, 1)


def coefficients(zonal, merid, rate, self_mix):
    lat = lax.broadcasted_iota(jnp.int32, zonal.shape, 1)
    zonal_half, zonal_rate = 0.5 * zonal, 0.5 * zonal * zonal + rate
    merid_half, merid_rate = 0.5 * merid, 0.5 * merid * merid + rate
    east, west = zonal_rate - zonal_half, zonal_rate + zonal_half
    to_north, to_south = merid_rate - merid_half, merid_rate + merid_half
    centre = 1.0 + self_mix - 2.0 * zonal_rate - 2.0 * merid_rate
    last, first = lat == zonal.shape[1] - 1, lat == 0
    centre = centre + jnp.where(last, to_north, 0.0) + jnp.where(first, to_south, 0.0)
    to_north = jnp.where(last, 0.0, to_north)
    to_south = jnp.where(first, 0.0, to_south)
    return centre, east, west, to_north, to_south


def mixed(mixing, field, values):
    total = None
    for other, value in enumerate(values):
        if other != field:
            term = mixing[field, other] * value
            total = term if total is None else total + term
    return total


def pick_rows(kinds, particles, fields, strip, rows, columns):
    out = lax.broadcasted_iota(jnp.int32, (rows, columns), 0)
    col = lax.broadcasted_iota(jnp.int32, (rows, columns), 1)
    want = jnp.full((rows, columns), -1, jnp.int32)
    for place, (field, x) in enumerate(kinds):
        inside = (out >= place * particles) & (out < (place + 1) * particles)
        target = (out - place * particles) * (fields * strip) + field * strip + x
        want = jnp.where(inside, target, want)
    return (col == want).astype(BF16)


def gather_rows(ref, first, stride, count):
    sub = lax.broadcasted_iota(jnp.int32, (count, ref.shape[1]), 0)
    out = None
    for p in range(count):
        row = jnp.broadcast_to(ref[pl.ds(first + p * stride, 1), :], sub.shape)
        out = row if out is None else jnp.where(sub == p, row, out)
    return out


def prepare(sizes, state, noise, courant, diffusion, mixing, cell, value,
            send_east, send_west, maps, noise_rows):
    particles, fields, strip, lats, strips = sizes
    x0 = lax.axis_index("lon") * strip
    shift = lats.bit_length() - 1
    local_cell = cell[...] - x0 * lats
    obs_lon = lax.shift_right_arithmetic(local_cell, shift)
    obs_lat = local_cell & (lats - 1)
    count = cell.shape[1]
    here = lax.broadcasted_iota(jnp.int32, (strip, count), 0) == obs_lon
    val = value[...]
    high = val.astype(BF16)
    rest = val - high.astype(F32)
    mid = rest.astype(BF16)
    low = (rest - mid.astype(F32)).astype(BF16)
    zero = jnp.zeros((strip, count), F32)
    parts = [jnp.where(here, 1.0, zero)]
    parts += [jnp.where(here, p.astype(F32), zero) for p in (high, mid, low)]
    left = jnp.concatenate(parts, 0).astype(BF16)
    right = (lax.broadcasted_iota(jnp.int32, (lats, count), 0) == obs_lat).astype(F32).astype(BF16)
    dense = lax.dot_general(left, right, (((1,), (1,)), ((), ())), preferred_element_type=F32)
    seen = dense[:strip]
    lon = (lax.broadcasted_iota(jnp.int32, (strip, lats), 0) + x0).astype(F32)
    precision = 1.0 + 2.0 * lon / (strip * strips)
    gain = seen * (0.25 * precision)
    weight = seen * precision
    target = dense[strip:2 * strip] + (dense[2 * strip:3 * strip] + dense[3 * strip:])
    maps[0] = gain
    maps[1] = weight
    maps[2] = target

    kinds = [(f, x) for x in (0, strip - 1) for f in range(fields)]
    pick = pick_rows(kinds, particles, fields, strip, len(kinds) * particles, noise.shape[1])
    rows = jnp.dot(pick, noise[0], preferred_element_type=F32)
    noise_rows[0] = rows[:particles]
    noise_rows[1] = rows[fields * particles:(fields + 1) * particles]

    def edge(x, inner, out, base):
        here = [gather_rows(state, f * strip + x, fields * strip, particles) for f in range(fields)]
        beside = [gather_rows(state, f * strip + inner, fields * strip, particles) for f in range(fields)]
        for f in range(fields):
            centre, east, west, to_north, to_south = coefficients(
                courant[0, x:x + 1], courant[1, x:x + 1], diffusion[f], mixing[f, f])
            known, missing = (east, west) if inner > x else (west, east)
            moved = (centre * here[f] + known * beside[f] + to_north * north(here[f])
                     + to_south * south(here[f]) + mixed(mixing, f, here))
            if f == 0:
                g = gain[x:x + 1]
                moved = moved + g * (target[x:x + 1] - moved)
                missing = (1.0 - g) * missing
            moved = moved + rows[base + f * particles:base + (f + 1) * particles]
            out[f * particles:(f + 1) * particles] = here[f]
            out[(fields + f) * particles:(fields + f + 1) * particles] = moved
            out[2 * fields * particles + f:2 * fields * particles + f + 1] = missing
        out[2 * fields * particles + fields:] = jnp.zeros((8 - fields, lats), F32)

    edge(strip - 1, strip - 2, send_east, fields * particles)
    edge(0, 1, send_west, 0)


def bulk(sizes, state, noise, courant, diffusion, mixing, maps,
         out, partial, noise_rows, coefs, middle):
    particles, fields, strip, lats, strips = sizes
    lon = lax.broadcasted_iota(jnp.int32, (strip, lats), 0)
    for f in range(fields):
        centre, east, west, to_north, to_south = coefficients(
            courant[0], courant[1], diffusion[f], mixing[f, f])
        coefs[f, 0] = centre
        coefs[f, 1] = jnp.where(lon == strip - 1, 0.0, east)
        coefs[f, 2] = jnp.where(lon == 0, 0.0, west)
        coefs[f, 3] = to_north
        coefs[f, 4] = to_south
    kinds = [(0, x) for x in (0, 1, strip - 2, strip - 1)]
    pick = pick_rows(kinds, particles, fields, strip, len(kinds) * particles, noise.shape[1])
    noise_rows[...] = jnp.dot(pick, noise[1], preferred_element_type=F32)

    def rows_of(p, f):
        return pl.ds(pl.multiple_of(p * (fields * strip) + f * strip, strip), strip)

    def moved(values, f):
        v = values[f]
        return (coefs[f, 0] * v + coefs[f, 1] * pltpu.roll(v, strip - 1, 0) + coefs[f, 2] * pltpu.roll(v, 1, 0)
                + coefs[f, 3] * north(v) + coefs[f, 4] * south(v) + mixed(mixing, f, values))

    def body(p, carry):
        values = [state[rows_of(p, f), :] for f in range(fields)]
        total = None
        for f in range(fields):
            new = moved(values, f)
            add = noise[0, rows_of(p, f), :].astype(F32)
            if f == 0:
                push = maps[0] * (maps[2] - new)
                new = new + push
                total = jnp.where((lon > 0) & (lon < strip - 1), push * (push + 2.0 * add), 0.0)
            middle[f] = new + add
        values = [middle[f] for f in range(fields)]
        for f in range(fields):
            new = moved(values, f)
            add = noise[1, rows_of(p, f), :].astype(F32)
            if f == 0:
                push = maps[0] * (maps[2] - new)
                new = new + push + add
                miss = maps[2] - new
                term = ((0.5 / noise_var) * (push * (push + 2.0 * add)) + (0.5 * maps[1]) * (miss * miss))
                total = (0.5 / noise_var) * total + jnp.where((lon > 1) & (lon < strip - 2), term, 0.0)
            else:
                new = new + add
            out[rows_of(p, f), :] = new
        total = jnp.sum(total, axis=0, keepdims=True)
        partial[pl.ds(p, 1), :] = total[:, :128] + total[:, 128:]
        return carry

    lax.fori_loop(0, particles, body, 0)


def correct(sizes, own_east, own_west, from_west, from_east, courant, diffusion, mixing, maps,
            noise0, noise1, current, partial, out, weight):
    particles, fields, strip, lats, strips = sizes
    n = fields * particles

    def split(ref, start):
        return [ref[start + f * particles:start + (f + 1) * particles] for f in range(fields)]

    def wide(v):
        return v[:, :128] + v[:, 128:]

    def push_terms(push, add):
        return (0.5 / noise_var) * (push * (push + 2.0 * add))

    for block in range(n):
        spot = pl.ds(block * strip + 8, strip - 16)
        out[spot, :] = current[spot, :]
    total = partial[...]
    for x, inner, own, other, at in ((0, 1, own_west, from_west, 0), (strip - 1, strip - 2, own_east, from_east, 1)):
        own_state, own_first = split(own, 0), split(own, n)
        other_state, other_first = split(other, 0), split(other, n)
        gain, observed, seen = maps[0, x:x + 1], maps[2, x:x + 1], maps[1, x:x + 1]
        first, outside, edge_coefs, inner_out = [], [], [], []
        for f in range(fields):
            coefs = coefficients(courant[0, x:x + 1], courant[1, x:x + 1], diffusion[f], mixing[f, f])
            outer = coefs[2] if inner > x else coefs[1]
            edge_coefs.append((coefs[0], outer, coefs[3], coefs[4]))
            coefs = coefficients(courant[0, inner:inner + 1], courant[1, inner:inner + 1], diffusion[f], mixing[f, f])
            inner_out.append(coefs[2] if inner > x else coefs[1])
            row = 2 * n + f
            outside.append(other_first[f] + other[row:row + 1] * own_state[f])
            step = outer * other_state[f]
            if f == 0:
                step = (1.0 - gain) * step
                result = own_first[0] + step
                add = noise0[at]
                push = (gain / (1.0 - gain)) * (observed - (result - add))
                total = total + wide(push_terms(push, add))
            first.append(step)
        for f in range(fields):
            centre, outer, to_north, to_south = edge_coefs[f]
            step = (centre * first[f] + outer * outside[f] + to_north * north(first[f])
                    + to_south * south(first[f]) + mixed(mixing, f, first))
            beside = inner_out[f] * first[f]
            if f == 0:
                g_in = maps[0, inner:inner + 1]
                step = (1.0 - gain) * step
                beside = (1.0 - g_in) * beside
            tile = min(x, inner) // 8 * 8
            sub = lax.broadcasted_iota(jnp.int32, (8, lats), 0)
            for p in range(particles):
                spot = pl.ds(p * fields * strip + f * strip + tile, 8)
                change = jnp.where(sub == x - tile, jnp.broadcast_to(step[p:p + 1], sub.shape),
                                   jnp.where(sub == inner - tile, jnp.broadcast_to(beside[p:p + 1], sub.shape), 0.0))
                out[spot, :] = current[spot, :] + change
            if f == 0:
                for place in (x, inner):
                    result = gather_rows(out, place, fields * strip, particles)
                    g, v, s = maps[0, place:place + 1], maps[2, place:place + 1], maps[1, place:place + 1]
                    k = (0, 1, strip - 2, strip - 1).index(place) * particles
                    add = noise1[k:k + particles]
                    push = (g / (1.0 - g)) * (v - (result - add))
                    miss = v - result
                    total = total + wide(push_terms(push, add) + (0.5 * s) * (miss * miss))
    weight[...] = total


def assemble(sizes, source, current, received, out, sems):
    particles = sizes[0]
    dom = lax.axis_index("dom")

    def copy(j, ref, at):
        return pltpu.make_async_copy(ref.at[at], out.at[j], sems.at[j])

    for j in range(particles):
        wanted = source[dom * particles + j]
        mine = wanted // particles == dom
        at = wanted % particles

        @pl.when(mine)
        def _():
            copy(j, current, at).start()

        @pl.when(jnp.logical_not(mine))
        def _():
            copy(j, received, at).start()

    for j in range(particles):
        copy(j, current, 0).wait()


def local(ensemble_state, proposal_noise, courant, diffusion, mixing, prior_weight, obs_cell, obs_value, source):
    particles, fields, strip, lats = ensemble_state.shape
    strips = lax.axis_size("lon")
    sizes = (particles, fields, strip, lats, strips)
    rows = particles * fields * strip
    state = ensemble_state.reshape(rows, lats)
    noise = proposal_noise.reshape(2, rows, lats)
    packet = jax.ShapeDtypeStruct((2 * particles * fields + 8, lats), F32)
    shape = jax.ShapeDtypeStruct

    send_east, send_west, maps, noise0 = pl.pallas_call(
        functools.partial(prepare, sizes),
        out_shape=(packet, packet, shape((3, strip, lats), F32), shape((2, particles, lats), F32)),
        in_specs=[VMEM, VMEM, VMEM, SMEM, SMEM, VMEM, VMEM],
        out_specs=(VMEM,) * 4,
        compiler_params=LIMIT,
        cost_estimate=pl.CostEstimate(flops=1000000, bytes_accessed=2000000, transcendentals=0),
    )(state, noise, courant, diffusion, mixing, obs_cell[None], obs_value[None])

    eastward = [(i, (i + 1) % strips) for i in range(strips)]
    westward = [(i, (i - 1) % strips) for i in range(strips)]
    from_west = lax.ppermute(send_east, "lon", eastward)
    from_east = lax.ppermute(send_west, "lon", westward)

    current, partial, noise1 = pl.pallas_call(
        functools.partial(bulk, sizes),
        out_shape=(shape((rows, lats), F32), shape((particles, 128), F32), shape((4 * particles, lats), F32)),
        in_specs=[VMEM, VMEM, VMEM, SMEM, SMEM, VMEM],
        out_specs=(VMEM,) * 3,
        scratch_shapes=[pltpu.VMEM((fields, 5, strip, lats), F32), pltpu.VMEM((fields, strip, lats), F32)],
        compiler_params=LIMIT,
        cost_estimate=pl.CostEstimate(flops=30000000, bytes_accessed=4000000, transcendentals=0),
    )(state, noise, courant, diffusion, mixing, maps)

    current, weight = pl.pallas_call(
        functools.partial(correct, sizes),
        out_shape=(shape((rows, lats), F32), shape((particles, 128), F32)),
        in_specs=[VMEM] * 5 + [SMEM, SMEM] + [VMEM] * 5,
        out_specs=(VMEM,) * 2,
        compiler_params=LIMIT,
        cost_estimate=pl.CostEstimate(flops=1000000, bytes_accessed=1000000, transcendentals=0),
    )(send_east, send_west, from_west, from_east, courant, diffusion, mixing, maps, noise0, noise1, current, partial)

    current = current.reshape(particles, fields, strip, lats)
    received = lax.ppermute(current, "dom", [(0, 1), (1, 0)])
    done = 1
    while done < strips:
        radix = min(8, strips // done)
        others = [lax.ppermute(weight, "lon", [(i, i ^ (done * step)) for i in range(strips)])
                  for step in range(1, radix)]
        weight = sum(others, weight)
        done *= radix

    new_state = pl.pallas_call(
        functools.partial(assemble, sizes),
        out_shape=shape((particles, fields, strip, lats), F32),
        in_specs=[SMEM, VMEM, VMEM],
        out_specs=ANY,
        scratch_shapes=[pltpu.SemaphoreType.DMA((particles,))],
        compiler_params=LIMIT,
        cost_estimate=pl.CostEstimate(flops=0, bytes_accessed=2000000, transcendentals=0),
    )(source, current, received)

    log_weight = prior_weight - jnp.sum(weight, axis=1) / (256.0 * obs_cell.shape[0])
    return new_state, log_weight


def solution(mesh):
    placed = (
        P(("groups", "dom"), None, "lon", None),
        P(None, ("groups", "dom"), None, "lon", None),
        P(None, ("groups", "lon"), None),
        P(),
        P(),
        P(("groups", "dom")),
        P(("groups", "lon")),
        P(("groups", "lon")),
        P("groups"),
    )
    return jax.shard_map(
        local,
        mesh=mesh,
        in_specs=placed,
        out_specs=(P(("groups", "dom"), None, "lon", None), P(("groups", "dom"))),
        check_vma=False,
    )
```

```python
import functools

import jax
import jax.numpy as jnp
from jax import lax
from jax.experimental import pallas as pl
from jax.experimental.pallas import tpu as pltpu
from jax.sharding import PartitionSpec as P

noise_var = 0.04
VMEM = pl.BlockSpec(memory_space=pltpu.VMEM)
SMEM = pl.BlockSpec(memory_space=pltpu.SMEM)
ANY = pl.BlockSpec(memory_space=pl.ANY)
HBM = pl.BlockSpec(memory_space=pltpu.HBM)
LIMIT = pltpu.CompilerParams(vmem_limit_bytes=16 * 1024 * 1024)
BF16 = jnp.bfloat16
F32 = jnp.float32


def north(v):
    return pltpu.roll(v, v.shape[1] - 1, 1)


def south(v):
    return pltpu.roll(v, 1, 1)


def coefficients(zonal, merid, rate, self_mix):
    lat = lax.broadcasted_iota(jnp.int32, zonal.shape, 1)
    zonal_half, zonal_rate = 0.5 * zonal, 0.5 * zonal * zonal + rate
    merid_half, merid_rate = 0.5 * merid, 0.5 * merid * merid + rate
    east, west = zonal_rate - zonal_half, zonal_rate + zonal_half
    to_north, to_south = merid_rate - merid_half, merid_rate + merid_half
    centre = 1.0 + self_mix - 2.0 * zonal_rate - 2.0 * merid_rate
    last, first = lat == zonal.shape[1] - 1, lat == 0
    centre = centre + jnp.where(last, to_north, 0.0) + jnp.where(first, to_south, 0.0)
    to_north = jnp.where(last, 0.0, to_north)
    to_south = jnp.where(first, 0.0, to_south)
    return centre, east, west, to_north, to_south


def mixed(mixing, field, values):
    total = None
    for other, value in enumerate(values):
        if other != field:
            term = mixing[field, other] * value
            total = term if total is None else total + term
    return total


def pick_rows(kinds, particles, fields, strip, rows, columns):
    out = lax.broadcasted_iota(jnp.int32, (rows, columns), 0)
    col = lax.broadcasted_iota(jnp.int32, (rows, columns), 1)
    want = jnp.full((rows, columns), -1, jnp.int32)
    for place, (field, x) in enumerate(kinds):
        inside = (out >= place * particles) & (out < (place + 1) * particles)
        target = (out - place * particles) * (fields * strip) + field * strip + x
        want = jnp.where(inside, target, want)
    return (col == want).astype(BF16)


def gather_rows(ref, first, stride, count):
    return stack_rows([ref[pl.ds(first + p * stride, 1), :] for p in range(count)])


def stack_rows(rows):
    sub = lax.broadcasted_iota(jnp.int32, (len(rows), rows[0].shape[1]), 0)
    out = None
    for p, row in enumerate(rows):
        row = jnp.broadcast_to(row, sub.shape)
        out = row if out is None else jnp.where(sub == p, row, out)
    return out


def prepare(sizes, state_hbm, noise_hbm, courant_hbm, diffusion_hbm, mixing_hbm, cell_hbm, value_hbm,
            send_east, send_west, maps, noise_rows,
            low, high, noise, courant, diffusion, mixing, cell, value, sems):
    particles, fields, strip, lats, strips = sizes
    copies = [pltpu.make_async_copy(source, target, sems.at[k]) for k, (source, target) in enumerate((
        (cell_hbm, cell), (value_hbm, value), (noise_hbm.at[0], noise), (state_hbm.at[:, :8], low),
        (state_hbm.at[:, strip - 8:], high), (courant_hbm, courant), (diffusion_hbm, diffusion),
        (mixing_hbm, mixing)))]
    for copy in copies:
        copy.start()
    copies[0].wait()
    copies[1].wait()
    x0 = lax.axis_index("lon") * strip
    shift = lats.bit_length() - 1
    local_cell = cell[...] - x0 * lats
    obs_lon = lax.shift_right_arithmetic(local_cell, shift)
    obs_lat = local_cell & (lats - 1)
    count = cell.shape[1]
    here = lax.broadcasted_iota(jnp.int32, (strip, count), 0) == obs_lon
    val = value[...]
    val_high = val.astype(BF16)
    rest = val - val_high.astype(F32)
    val_mid = rest.astype(BF16)
    val_low = (rest - val_mid.astype(F32)).astype(BF16)
    zero = jnp.zeros((strip, count), F32)
    parts = [jnp.where(here, 1.0, zero)]
    parts += [jnp.where(here, p.astype(F32), zero) for p in (val_high, val_mid, val_low)]
    left = jnp.concatenate(parts, 0).astype(BF16)
    right = (lax.broadcasted_iota(jnp.int32, (lats, count), 0) == obs_lat).astype(F32).astype(BF16)
    dense = lax.dot_general(left, right, (((1,), (1,)), ((), ())), preferred_element_type=F32)
    seen = dense[:strip]
    lon = (lax.broadcasted_iota(jnp.int32, (strip, lats), 0) + x0).astype(F32)
    precision = 1.0 + 2.0 * lon / (strip * strips)
    gain = seen * (0.25 * precision)
    weight = seen * precision
    target = dense[strip:2 * strip] + (dense[2 * strip:3 * strip] + dense[3 * strip:])
    maps[0] = gain
    maps[1] = weight
    maps[2] = target

    kinds = [(f, x) for x in (0, strip - 1) for f in range(fields)]
    pick = pick_rows(kinds, particles, fields, strip, len(kinds) * particles, noise.shape[0])
    copies[2].wait()
    rows = jnp.dot(pick, noise[...], preferred_element_type=F32)
    noise_rows[0] = rows[:particles]
    noise_rows[1] = rows[fields * particles:(fields + 1) * particles]

    for copy in copies[3:]:
        copy.wait()

    def edge(x, inner, out, base):
        tile, first = (low, 0) if x < 8 else (high, strip - 8)

        def rows_at(f, place):
            return stack_rows([tile[p * fields + f, place:place + 1] for p in range(particles)])

        here = [rows_at(f, x - first) for f in range(fields)]
        beside = [rows_at(f, inner - first) for f in range(fields)]
        for f in range(fields):
            centre, east, west, to_north, to_south = coefficients(
                courant[0, x:x + 1], courant[1, x:x + 1], diffusion[f], mixing[f, f])
            known, missing = (east, west) if inner > x else (west, east)
            moved = (centre * here[f] + known * beside[f] + to_north * north(here[f])
                     + to_south * south(here[f]) + mixed(mixing, f, here))
            if f == 0:
                g = gain[x:x + 1]
                moved = moved + g * (target[x:x + 1] - moved)
                missing = (1.0 - g) * missing
            moved = moved + rows[base + f * particles:base + (f + 1) * particles]
            out[f * particles:(f + 1) * particles] = here[f]
            out[(fields + f) * particles:(fields + f + 1) * particles] = moved
            out[2 * fields * particles + f:2 * fields * particles + f + 1] = missing
        out[2 * fields * particles + fields:] = jnp.zeros((8 - fields, lats), F32)

    edge(strip - 1, strip - 2, send_east, fields * particles)
    edge(0, 1, send_west, 0)


def bulk(sizes, state, noise, courant, diffusion, mixing, maps,
         out, partial, noise_rows, coefs, middle):
    particles, fields, strip, lats, strips = sizes
    lon = lax.broadcasted_iota(jnp.int32, (strip, lats), 0)
    for f in range(fields):
        centre, east, west, to_north, to_south = coefficients(
            courant[0], courant[1], diffusion[f], mixing[f, f])
        coefs[f, 0] = centre
        coefs[f, 1] = jnp.where(lon == strip - 1, 0.0, east)
        coefs[f, 2] = jnp.where(lon == 0, 0.0, west)
        coefs[f, 3] = to_north
        coefs[f, 4] = to_south
    kinds = [(0, x) for x in (0, 1, strip - 2, strip - 1)]
    pick = pick_rows(kinds, particles, fields, strip, len(kinds) * particles, noise.shape[1])
    noise_rows[...] = jnp.dot(pick, noise[1], preferred_element_type=F32)

    def rows_of(p, f):
        return pl.ds(pl.multiple_of(p * (fields * strip) + f * strip, strip), strip)

    def moved(values, f):
        v = values[f]
        return (coefs[f, 0] * v + coefs[f, 1] * pltpu.roll(v, strip - 1, 0) + coefs[f, 2] * pltpu.roll(v, 1, 0)
                + coefs[f, 3] * north(v) + coefs[f, 4] * south(v) + mixed(mixing, f, values))

    def body(p, carry):
        values = [state[rows_of(p, f), :] for f in range(fields)]
        total = None
        for f in range(fields):
            new = moved(values, f)
            add = noise[0, rows_of(p, f), :].astype(F32)
            if f == 0:
                push = maps[0] * (maps[2] - new)
                new = new + push
                total = jnp.where((lon > 0) & (lon < strip - 1), push * (push + 2.0 * add), 0.0)
            middle[f] = new + add
        values = [middle[f] for f in range(fields)]
        for f in range(fields):
            new = moved(values, f)
            add = noise[1, rows_of(p, f), :].astype(F32)
            if f == 0:
                push = maps[0] * (maps[2] - new)
                new = new + push + add
                miss = maps[2] - new
                term = ((0.5 / noise_var) * (push * (push + 2.0 * add)) + (0.5 * maps[1]) * (miss * miss))
                total = (0.5 / noise_var) * total + jnp.where((lon > 1) & (lon < strip - 2), term, 0.0)
            else:
                new = new + add
            out[rows_of(p, f), :] = new
        total = jnp.sum(total, axis=0, keepdims=True)
        partial[pl.ds(p, 1), :] = total[:, :128] + total[:, 128:]
        return carry

    lax.fori_loop(0, particles, body, 0)


def correct(sizes, own_east, own_west, from_west, from_east, courant, diffusion, mixing, maps,
            noise0, noise1, current, partial, out, weight):
    particles, fields, strip, lats, strips = sizes
    n = fields * particles

    def split(ref, start):
        return [ref[start + f * particles:start + (f + 1) * particles] for f in range(fields)]

    def wide(v):
        return v[:, :128] + v[:, 128:]

    def push_terms(push, add):
        return (0.5 / noise_var) * (push * (push + 2.0 * add))

    for block in range(n):
        spot = pl.ds(block * strip + 8, strip - 16)
        out[spot, :] = current[spot, :]
    total = partial[...]
    for x, inner, own, other, at in ((0, 1, own_west, from_west, 0), (strip - 1, strip - 2, own_east, from_east, 1)):
        own_state, own_first = split(own, 0), split(own, n)
        other_state, other_first = split(other, 0), split(other, n)
        gain, observed, seen = maps[0, x:x + 1], maps[2, x:x + 1], maps[1, x:x + 1]
        first, outside, edge_coefs, inner_out = [], [], [], []
        for f in range(fields):
            coefs = coefficients(courant[0, x:x + 1], courant[1, x:x + 1], diffusion[f], mixing[f, f])
            outer = coefs[2] if inner > x else coefs[1]
            edge_coefs.append((coefs[0], outer, coefs[3], coefs[4]))
            coefs = coefficients(courant[0, inner:inner + 1], courant[1, inner:inner + 1], diffusion[f], mixing[f, f])
            inner_out.append(coefs[2] if inner > x else coefs[1])
            row = 2 * n + f
            outside.append(other_first[f] + other[row:row + 1] * own_state[f])
            step = outer * other_state[f]
            if f == 0:
                step = (1.0 - gain) * step
                result = own_first[0] + step
                add = noise0[at]
                push = (gain / (1.0 - gain)) * (observed - (result - add))
                total = total + wide(push_terms(push, add))
            first.append(step)
        for f in range(fields):
            centre, outer, to_north, to_south = edge_coefs[f]
            step = (centre * first[f] + outer * outside[f] + to_north * north(first[f])
                    + to_south * south(first[f]) + mixed(mixing, f, first))
            beside = inner_out[f] * first[f]
            if f == 0:
                g_in = maps[0, inner:inner + 1]
                step = (1.0 - gain) * step
                beside = (1.0 - g_in) * beside
            tile = min(x, inner) // 8 * 8
            sub = lax.broadcasted_iota(jnp.int32, (8, lats), 0)
            for p in range(particles):
                spot = pl.ds(p * fields * strip + f * strip + tile, 8)
                change = jnp.where(sub == x - tile, jnp.broadcast_to(step[p:p + 1], sub.shape),
                                   jnp.where(sub == inner - tile, jnp.broadcast_to(beside[p:p + 1], sub.shape), 0.0))
                out[spot, :] = current[spot, :] + change
            if f == 0:
                for place in (x, inner):
                    result = gather_rows(out, place, fields * strip, particles)
                    g, v, s = maps[0, place:place + 1], maps[2, place:place + 1], maps[1, place:place + 1]
                    k = (0, 1, strip - 2, strip - 1).index(place) * particles
                    add = noise1[k:k + particles]
                    push = (g / (1.0 - g)) * (v - (result - add))
                    miss = v - result
                    total = total + wide(push_terms(push, add) + (0.5 * s) * (miss * miss))
    weight[...] = total


def assemble(sizes, source, current, received, out, sems):
    particles = sizes[0]
    dom = lax.axis_index("dom")

    def copy(j, ref, at):
        return pltpu.make_async_copy(ref.at[at], out.at[j], sems.at[j])

    for j in range(particles):
        wanted = source[dom * particles + j]
        mine = wanted // particles == dom
        at = wanted % particles

        @pl.when(mine)
        def _():
            copy(j, current, at).start()

        @pl.when(jnp.logical_not(mine))
        def _():
            copy(j, received, at).start()

    for j in range(particles):
        copy(j, current, 0).wait()


def local(ensemble_state, proposal_noise, courant, diffusion, mixing, prior_weight, obs_cell, obs_value, source):
    particles, fields, strip, lats = ensemble_state.shape
    strips = lax.axis_size("lon")
    sizes = (particles, fields, strip, lats, strips)
    rows = particles * fields * strip
    state = ensemble_state.reshape(rows, lats)
    noise = proposal_noise.reshape(2, rows, lats)
    packet = jax.ShapeDtypeStruct((2 * particles * fields + 8, lats), F32)
    shape = jax.ShapeDtypeStruct

    send_east, send_west, maps, noise0 = pl.pallas_call(
        functools.partial(prepare, sizes),
        out_shape=(packet, packet, shape((3, strip, lats), F32), shape((2, particles, lats), F32)),
        in_specs=[HBM] * 7,
        out_specs=(VMEM,) * 4,
        scratch_shapes=[
            pltpu.VMEM((particles * fields, 8, lats), F32),
            pltpu.VMEM((particles * fields, 8, lats), F32),
            pltpu.VMEM((rows, lats), BF16),
            pltpu.VMEM(courant.shape, F32),
            pltpu.SMEM(diffusion.shape, F32),
            pltpu.SMEM(mixing.shape, F32),
            pltpu.VMEM((1,) + obs_cell.shape, jnp.int32),
            pltpu.VMEM((1,) + obs_value.shape, F32),
            pltpu.SemaphoreType.DMA((8,)),
        ],
        compiler_params=LIMIT,
        cost_estimate=pl.CostEstimate(flops=1000000, bytes_accessed=2000000, transcendentals=0),
    )(state.reshape(particles * fields, strip, lats), noise, courant, diffusion, mixing, obs_cell[None], obs_value[None])

    eastward = [(i, (i + 1) % strips) for i in range(strips)]
    westward = [(i, (i - 1) % strips) for i in range(strips)]
    from_west = lax.ppermute(send_east, "lon", eastward)
    from_east = lax.ppermute(send_west, "lon", westward)

    current, partial, noise1 = pl.pallas_call(
        functools.partial(bulk, sizes),
        out_shape=(shape((rows, lats), F32), shape((particles, 128), F32), shape((4 * particles, lats), F32)),
        in_specs=[VMEM, VMEM, VMEM, SMEM, SMEM, VMEM],
        out_specs=(VMEM,) * 3,
        scratch_shapes=[pltpu.VMEM((fields, 5, strip, lats), F32), pltpu.VMEM((fields, strip, lats), F32)],
        compiler_params=LIMIT,
        cost_estimate=pl.CostEstimate(flops=30000000, bytes_accessed=4000000, transcendentals=0),
    )(state, noise, courant, diffusion, mixing, maps)

    current, weight = pl.pallas_call(
        functools.partial(correct, sizes),
        out_shape=(shape((rows, lats), F32), shape((particles, 128), F32)),
        in_specs=[VMEM] * 5 + [SMEM, SMEM] + [VMEM] * 5,
        out_specs=(VMEM,) * 2,
        compiler_params=LIMIT,
        cost_estimate=pl.CostEstimate(flops=1000000, bytes_accessed=1000000, transcendentals=0),
    )(send_east, send_west, from_west, from_east, courant, diffusion, mixing, maps, noise0, noise1, current, partial)

    current = current.reshape(particles, fields, strip, lats)
    received = lax.ppermute(current, "dom", [(0, 1), (1, 0)])
    weights = lax.all_to_all(jnp.broadcast_to(weight[None], (strips, particles, 128)), "lon", 0, 0)

    new_state = pl.pallas_call(
        functools.partial(assemble, sizes),
        out_shape=shape((particles, fields, strip, lats), F32),
        in_specs=[SMEM, VMEM, VMEM],
        out_specs=ANY,
        scratch_shapes=[pltpu.SemaphoreType.DMA((particles,))],
        compiler_params=LIMIT,
        cost_estimate=pl.CostEstimate(flops=0, bytes_accessed=2000000, transcendentals=0),
    )(source, current, received)

    log_weight = prior_weight - jnp.sum(weights, axis=(0, 2)) / (256.0 * obs_cell.shape[0])
    return new_state, log_weight


def solution(mesh):
    placed = (
        P(("groups", "dom"), None, "lon", None),
        P(None, ("groups", "dom"), None, "lon", None),
        P(None, ("groups", "lon"), None),
        P(),
        P(),
        P(("groups", "dom")),
        P(("groups", "lon")),
        P(("groups", "lon")),
        P("groups"),
    )
    return jax.shard_map(
        local,
        mesh=mesh,
        in_specs=placed,
        out_specs=(P(("groups", "dom"), None, "lon", None), P(("groups", "dom"))),
        check_vma=False,
    )
```

```python
import functools

import jax
import jax.numpy as jnp
from jax import lax
from jax.experimental import pallas as pl
from jax.experimental.pallas import tpu as pltpu
from jax.sharding import PartitionSpec as P

noise_var = 0.04
VMEM = pl.BlockSpec(memory_space=pltpu.VMEM)
SMEM = pl.BlockSpec(memory_space=pltpu.SMEM)
HBM = pl.BlockSpec(memory_space=pltpu.HBM)
LIMIT = pltpu.CompilerParams(vmem_limit_bytes=16 * 1024 * 1024)
BF16 = jnp.bfloat16
F32 = jnp.float32


def north(v):
    return pltpu.roll(v, v.shape[1] - 1, 1)


def south(v):
    return pltpu.roll(v, 1, 1)


def coefficients(zonal, merid, rate, self_mix):
    lat = lax.broadcasted_iota(jnp.int32, zonal.shape, 1)
    zonal_half, zonal_rate = 0.5 * zonal, 0.5 * zonal * zonal + rate
    merid_half, merid_rate = 0.5 * merid, 0.5 * merid * merid + rate
    east, west = zonal_rate - zonal_half, zonal_rate + zonal_half
    to_north, to_south = merid_rate - merid_half, merid_rate + merid_half
    centre = 1.0 + self_mix - 2.0 * zonal_rate - 2.0 * merid_rate
    last, first = lat == zonal.shape[1] - 1, lat == 0
    centre = centre + jnp.where(last, to_north, 0.0) + jnp.where(first, to_south, 0.0)
    to_north = jnp.where(last, 0.0, to_north)
    to_south = jnp.where(first, 0.0, to_south)
    return centre, east, west, to_north, to_south


def mixed(mixing, field, values):
    total = None
    for other, value in enumerate(values):
        if other != field:
            term = mixing[field, other] * value
            total = term if total is None else total + term
    return total


def pick_rows(kinds, particles, fields, strip, columns):
    rows = len(kinds) * particles
    out = lax.broadcasted_iota(jnp.int32, (rows, columns), 0)
    col = lax.broadcasted_iota(jnp.int32, (rows, columns), 1)
    want = jnp.full((rows, columns), -1, jnp.int32)
    for place, (field, x) in enumerate(kinds):
        inside = (out >= place * particles) & (out < (place + 1) * particles)
        target = (out - place * particles) * (fields * strip) + field * strip + x
        want = jnp.where(inside, target, want)
    return (col == want).astype(BF16)


def stack_rows(rows):
    sub = lax.broadcasted_iota(jnp.int32, (len(rows), rows[0].shape[1]), 0)
    out = None
    for p, row in enumerate(rows):
        row = jnp.broadcast_to(row, sub.shape)
        out = row if out is None else jnp.where(sub == p, row, out)
    return out


def observation_maps(sizes, cell, value):
    particles, fields, strip, lats, strips = sizes
    x0 = lax.axis_index("lon") * strip
    shift = lats.bit_length() - 1
    local_cell = cell - x0 * lats
    obs_lon = lax.shift_right_arithmetic(local_cell, shift)
    obs_lat = local_cell & (lats - 1)
    count = cell.shape[1]
    here = lax.broadcasted_iota(jnp.int32, (strip, count), 0) == obs_lon
    high = value.astype(BF16)
    rest = value - high.astype(F32)
    mid = rest.astype(BF16)
    low = (rest - mid.astype(F32)).astype(BF16)
    zero = jnp.zeros((strip, count), F32)
    parts = [jnp.where(here, 1.0, zero)]
    parts += [jnp.where(here, p.astype(F32), zero) for p in (high, mid, low)]
    left = jnp.concatenate(parts, 0).astype(BF16)
    right = (lax.broadcasted_iota(jnp.int32, (lats, count), 0) == obs_lat).astype(F32).astype(BF16)
    dense = lax.dot_general(left, right, (((1,), (1,)), ((), ())), preferred_element_type=F32)
    seen = dense[:strip]
    lon = (lax.broadcasted_iota(jnp.int32, (strip, lats), 0) + x0).astype(F32)
    precision = 1.0 + 2.0 * lon / (strip * strips)
    target = dense[strip:2 * strip] + (dense[2 * strip:3 * strip] + dense[3 * strip:])
    return seen * (0.25 * precision), seen * precision, target


def prepare(sizes, state_hbm, noise_hbm, courant_hbm, diffusion_hbm, mixing_hbm, cell_hbm, value_hbm,
            send_east, send_west,
            low, high, noise, courant, diffusion, mixing, cell, value, sems):
    particles, fields, strip, lats, strips = sizes
    copies = [pltpu.make_async_copy(source, target, sems.at[k]) for k, (source, target) in enumerate((
        (cell_hbm, cell), (value_hbm, value), (noise_hbm.at[0], noise), (state_hbm.at[:, :8], low),
        (state_hbm.at[:, strip - 8:], high), (courant_hbm, courant), (diffusion_hbm, diffusion),
        (mixing_hbm, mixing)))]
    for copy in copies:
        copy.start()
    copies[0].wait()
    copies[1].wait()
    gain, _, target = observation_maps(sizes, cell[...], value[...])

    kinds = [(f, x) for x in (0, strip - 1) for f in range(fields)]
    pick = pick_rows(kinds, particles, fields, strip, noise.shape[0])
    copies[2].wait()
    rows = jnp.dot(pick, noise[...], preferred_element_type=F32)
    for copy in copies[3:]:
        copy.wait()

    def edge(x, inner, out, base):
        tile, first = (low, 0) if x < 8 else (high, strip - 8)

        def rows_at(f, place):
            return stack_rows([tile[p * fields + f, place:place + 1] for p in range(particles)])

        here = [rows_at(f, x - first) for f in range(fields)]
        beside = [rows_at(f, inner - first) for f in range(fields)]
        for f in range(fields):
            centre, east, west, to_north, to_south = coefficients(
                courant[0, x:x + 1], courant[1, x:x + 1], diffusion[f], mixing[f, f])
            known, missing = (east, west) if inner > x else (west, east)
            moved = (centre * here[f] + known * beside[f] + to_north * north(here[f])
                     + to_south * south(here[f]) + mixed(mixing, f, here))
            if f == 0:
                g = gain[x:x + 1]
                moved = moved + g * (target[x:x + 1] - moved)
                missing = (1.0 - g) * missing
            moved = moved + rows[base + f * particles:base + (f + 1) * particles]
            out[f * particles:(f + 1) * particles] = here[f]
            out[(fields + f) * particles:(fields + f + 1) * particles] = moved
            out[2 * fields * particles + f:2 * fields * particles + f + 1] = missing
        out[2 * fields * particles + fields:] = jnp.zeros((8 - fields, lats), F32)

    edge(strip - 1, strip - 2, send_east, fields * particles)
    edge(0, 1, send_west, 0)


def bulk(sizes, state, noise, courant, diffusion, mixing, cell, value,
         out, partial, noise_rows, first_rows, edge_coefs, edge_maps, coefs, maps, middle):
    particles, fields, strip, lats, strips = sizes
    maps[0], maps[1], maps[2] = observation_maps(sizes, cell[...], value[...])
    places = (0, 1, strip - 2, strip - 1)
    for k, x in enumerate(places):
        for m in range(3):
            edge_maps[m * 4 + k:m * 4 + k + 1] = maps[m, x:x + 1]
    lon = lax.broadcasted_iota(jnp.int32, (strip, lats), 0)
    for f in range(fields):
        centre, east, west, to_north, to_south = coefficients(
            courant[0], courant[1], diffusion[f], mixing[f, f])
        coefs[f, 0] = centre
        coefs[f, 1] = jnp.where(lon == strip - 1, 0.0, east)
        coefs[f, 2] = jnp.where(lon == 0, 0.0, west)
        coefs[f, 3] = to_north
        coefs[f, 4] = to_south
        for side, (x, inner, outward) in enumerate(((0, 1, west), (strip - 1, strip - 2, east))):
            row = (side * fields + f) * 5
            for k, (values, at) in enumerate(((centre, x), (outward, x), (to_north, x), (to_south, x), (outward, inner))):
                edge_coefs[row + k:row + k + 1] = values[at:at + 1]
    kinds = [(0, x) for x in places]
    pick = pick_rows(kinds, particles, fields, strip, noise.shape[1])
    noise_rows[:4 * particles] = jnp.dot(pick, noise[1], preferred_element_type=F32)
    noise_rows[4 * particles:] = jnp.dot(pick, noise[0], preferred_element_type=F32)

    def rows_of(p, f):
        return pl.ds(pl.multiple_of(p * (fields * strip) + f * strip, strip), strip)

    def moved(values, f):
        v = values[f]
        return (coefs[f, 0] * v + coefs[f, 1] * pltpu.roll(v, strip - 1, 0) + coefs[f, 2] * pltpu.roll(v, 1, 0)
                + coefs[f, 3] * north(v) + coefs[f, 4] * south(v) + mixed(mixing, f, values))

    def body(p, carry):
        values = [state[rows_of(p, f), :] for f in range(fields)]
        total = None
        for f in range(fields):
            new = moved(values, f)
            add = noise[0, rows_of(p, f), :].astype(F32)
            if f == 0:
                push = maps[0] * (maps[2] - new)
                new = new + push
                total = jnp.where((lon > 0) & (lon < strip - 1), push * (push + 2.0 * add), 0.0)
            middle[f] = new + add
        values = [middle[f] for f in range(fields)]
        for f in range(fields):
            new = moved(values, f)
            add = noise[1, rows_of(p, f), :].astype(F32)
            if f == 0:
                push = maps[0] * (maps[2] - new)
                new = new + push + add
                miss = maps[2] - new
                term = ((0.5 / noise_var) * (push * (push + 2.0 * add)) + (0.5 * maps[1]) * (miss * miss))
                total = (0.5 / noise_var) * total + jnp.where((lon > 1) & (lon < strip - 2), term, 0.0)
            else:
                new = new + add
            out[rows_of(p, f), :] = new
        total = jnp.sum(total, axis=0, keepdims=True)
        partial[pl.ds(p, 1), :] = total[:, :128] + total[:, 128:]
        return carry

    lax.fori_loop(0, particles, body, 0)
    for k, x in enumerate(places):
        first_rows[k * particles:(k + 1) * particles] = stack_rows(
            [out[p * fields * strip + x:p * fields * strip + x + 1] for p in range(particles)])


def correct(sizes, own_east, own_west, from_west, from_east, mixing, edge_coefs, edge_maps, noise_rows, first_rows,
            partial, weight, changes):
    particles, fields, strip, lats, strips = sizes
    n = fields * particles

    def split(ref, start):
        return [ref[start + f * particles:start + (f + 1) * particles] for f in range(fields)]

    def wide(v):
        return v[:, :128] + v[:, 128:]

    def push_terms(push, add):
        return (0.5 / noise_var) * (push * (push + 2.0 * add))

    total = partial[...]
    for side, (k_edge, k_in, own, other) in enumerate(((0, 1, own_west, from_west), (3, 2, own_east, from_east))):
        own_state, other_state, other_first = split(own, 0), split(other, 0), split(other, n)

        def maps_at(k):
            return [edge_maps[m * 4 + k:m * 4 + k + 1] for m in range(3)]

        gain, seen, observed = maps_at(k_edge)
        coefs = [[edge_coefs[(side * fields + f) * 5 + k:(side * fields + f) * 5 + k + 1] for k in range(5)]
                 for f in range(fields)]
        first, outside = [], []
        for f in range(fields):
            row = 2 * n + f
            outside.append(other_first[f] + other[row:row + 1] * own_state[f])
            step = coefs[f][1] * other_state[f]
            if f == 0:
                step = (1.0 - gain) * step
                result = own[n:n + particles] + step
                add = noise_rows[(4 + k_edge) * particles:(5 + k_edge) * particles]
                push = (gain / (1.0 - gain)) * (observed - (result - add))
                total = total + wide(push_terms(push, add))
            first.append(step)
        for f in range(fields):
            centre, outward, to_north, to_south, outward_in = coefs[f]
            step = (centre * first[f] + outward * outside[f] + to_north * north(first[f])
                    + to_south * south(first[f]) + mixed(mixing, f, first))
            beside = outward_in * first[f]
            if f == 0:
                step = (1.0 - gain) * step
                beside = (1.0 - maps_at(k_in)[0]) * beside
                for k, change in ((k_edge, step), (k_in, beside)):
                    g, s, v = maps_at(k)
                    result = first_rows[k * particles:(k + 1) * particles] + change
                    add = noise_rows[k * particles:(k + 1) * particles]
                    push = (g / (1.0 - g)) * (v - (result - add))
                    miss = v - result
                    total = total + wide(push_terms(push, add) + (0.5 * s) * (miss * miss))
            changes[k_edge, f * particles:(f + 1) * particles] = step
            changes[k_in, f * particles:(f + 1) * particles] = beside
    total = jnp.broadcast_to(jnp.sum(total, axis=1, keepdims=True), total.shape)
    diagonal = lax.broadcasted_iota(jnp.int32, total.shape, 0) == lax.broadcasted_iota(jnp.int32, total.shape, 1)
    weight[...] = jnp.sum(jnp.where(diagonal, total, 0.0), axis=0, keepdims=True)


def apply_changes(sizes, current, changes, out):
    particles, fields, strip, lats, strips = sizes
    sub = lax.broadcasted_iota(jnp.int32, (8, lats), 0)
    for p in range(particles):
        for f in range(fields):
            start = (p * fields + f) * strip
            row = f * particles + p
            rows = [jnp.broadcast_to(changes[k, row:row + 1], sub.shape) for k in range(4)]
            out[start:start + 8] = current[start:start + 8] + jnp.where(
                sub == 0, rows[0], jnp.where(sub == 1, rows[1], 0.0))
            out[start + 8:start + strip - 8] = current[start + 8:start + strip - 8]
            out[start + strip - 8:start + strip] = current[start + strip - 8:start + strip] + jnp.where(
                sub == 7, rows[3], jnp.where(sub == 6, rows[2], 0.0))


def assemble(sizes, source, current, received, out, sems):
    particles = sizes[0]
    dom = lax.axis_index("dom")

    def copy(j, ref, at):
        return pltpu.make_async_copy(ref.at[at], out.at[j], sems.at[j])

    for j in range(particles):
        wanted = source[dom * particles + j]
        mine = wanted // particles == dom
        at = wanted % particles

        @pl.when(mine)
        def _():
            copy(j, current, at).start()

        @pl.when(jnp.logical_not(mine))
        def _():
            copy(j, received, at).start()

    for j in range(particles):
        copy(j, current, 0).wait()


def local(ensemble_state, proposal_noise, courant, diffusion, mixing, prior_weight, obs_cell, obs_value, source):
    particles, fields, strip, lats = ensemble_state.shape
    strips = lax.axis_size("lon")
    sizes = (particles, fields, strip, lats, strips)
    rows = particles * fields * strip
    state = ensemble_state.reshape(rows, lats)
    noise = proposal_noise.reshape(2, rows, lats)
    packet = jax.ShapeDtypeStruct((2 * particles * fields + 8, lats), F32)
    cell, value = obs_cell[None], obs_value[None]

    def shape(*dims):
        return jax.ShapeDtypeStruct(dims, F32)

    send_east, send_west = pl.pallas_call(
        functools.partial(prepare, sizes),
        out_shape=(packet, packet),
        in_specs=[HBM] * 7,
        out_specs=(VMEM,) * 2,
        scratch_shapes=[
            pltpu.VMEM((particles * fields, 8, lats), F32),
            pltpu.VMEM((particles * fields, 8, lats), F32),
            pltpu.VMEM((rows, lats), BF16),
            pltpu.VMEM(courant.shape, F32),
            pltpu.SMEM(diffusion.shape, F32),
            pltpu.SMEM(mixing.shape, F32),
            pltpu.VMEM(cell.shape, jnp.int32),
            pltpu.VMEM(value.shape, F32),
            pltpu.SemaphoreType.DMA((8,)),
        ],
        compiler_params=pltpu.CompilerParams(vmem_limit_bytes=60 * 1024 * 1024),
        cost_estimate=pl.CostEstimate(flops=1000000, bytes_accessed=2000000, transcendentals=0),
    )(state.reshape(particles * fields, strip, lats), noise, courant, diffusion, mixing, cell, value)

    eastward = [(i, (i + 1) % strips) for i in range(strips)]
    westward = [(i, (i - 1) % strips) for i in range(strips)]
    from_west = lax.ppermute(send_east, "lon", eastward)
    from_east = lax.ppermute(send_west, "lon", westward)

    current, partial, noise_rows, first_rows, edge_coefs, edge_maps = pl.pallas_call(
        functools.partial(bulk, sizes),
        out_shape=(shape(rows, lats), shape(particles, 128), shape(8 * particles, lats), shape(4 * particles, lats),
                   shape(2 * fields * 5, lats), shape(12, lats)),
        in_specs=[VMEM, VMEM, VMEM, SMEM, SMEM, VMEM, VMEM],
        out_specs=(VMEM,) * 6,
        scratch_shapes=[pltpu.VMEM((fields, 5, strip, lats), F32), pltpu.VMEM((3, strip, lats), F32),
                        pltpu.VMEM((fields, strip, lats), F32)],
        compiler_params=LIMIT,
        cost_estimate=pl.CostEstimate(flops=30000000, bytes_accessed=4000000, transcendentals=0),
    )(state, noise, courant, diffusion, mixing, cell, value)

    weight, changes = pl.pallas_call(
        functools.partial(correct, sizes),
        out_shape=(shape(1, 128), shape(4, particles * fields, lats)),
        in_specs=[VMEM] * 4 + [SMEM] + [VMEM] * 5,
        out_specs=(VMEM,) * 2,
        compiler_params=LIMIT,
        cost_estimate=pl.CostEstimate(flops=1000000, bytes_accessed=1000000, transcendentals=0),
    )(send_east, send_west, from_west, from_east, mixing, edge_coefs, edge_maps, noise_rows, first_rows, partial)

    current = pl.pallas_call(
        functools.partial(apply_changes, sizes),
        out_shape=shape(rows, lats),
        in_specs=[VMEM] * 2,
        out_specs=VMEM,
        compiler_params=LIMIT,
        cost_estimate=pl.CostEstimate(flops=1000000, bytes_accessed=2000000, transcendentals=0),
    )(current, changes).reshape(particles, fields, strip, lats)

    received = lax.ppermute(current, "dom", [(0, 1), (1, 0)])
    bit = 1
    while bit < strips:
        if 2 * bit >= strips:
            weight, received = lax.optimization_barrier((weight, received))
        weight = weight + lax.ppermute(weight, "lon", [(i, i ^ bit) for i in range(strips)])
        bit *= 2

    new_state = pl.pallas_call(
        functools.partial(assemble, sizes),
        out_shape=shape(particles, fields, strip, lats),
        in_specs=[SMEM, VMEM, VMEM],
        out_specs=HBM,
        scratch_shapes=[pltpu.SemaphoreType.DMA((particles,))],
        compiler_params=LIMIT,
        cost_estimate=pl.CostEstimate(flops=0, bytes_accessed=2000000, transcendentals=0),
    )(source, current, received)

    log_weight = prior_weight - weight[0, :particles] / (256.0 * obs_cell.shape[0])
    return new_state, log_weight


def solution(mesh):
    placed = (
        P(("groups", "dom"), None, "lon", None),
        P(None, ("groups", "dom"), None, "lon", None),
        P(None, ("groups", "lon"), None),
        P(),
        P(),
        P(("groups", "dom")),
        P(("groups", "lon")),
        P(("groups", "lon")),
        P("groups"),
    )
    return jax.shard_map(
        local,
        mesh=mesh,
        in_specs=placed,
        out_specs=(P(("groups", "dom"), None, "lon", None), P(("groups", "dom"))),
        check_vma=False,
    )
```

```python
import functools

import jax
import jax.numpy as jnp
from jax import lax
from jax.experimental import pallas as pl
from jax.experimental.pallas import tpu as pltpu
from jax.sharding import PartitionSpec as P

noise_var = 0.04
VMEM = pl.BlockSpec(memory_space=pltpu.VMEM)
SMEM = pl.BlockSpec(memory_space=pltpu.SMEM)
HBM = pl.BlockSpec(memory_space=pltpu.HBM)
LIMIT = pltpu.CompilerParams(vmem_limit_bytes=16 * 1024 * 1024)
BF16 = jnp.bfloat16
F32 = jnp.float32


def north(v):
    return pltpu.roll(v, v.shape[1] - 1, 1)


def south(v):
    return pltpu.roll(v, 1, 1)


def coefficients(zonal, merid, rate, self_mix):
    lat = lax.broadcasted_iota(jnp.int32, zonal.shape, 1)
    zonal_half, zonal_rate = 0.5 * zonal, 0.5 * zonal * zonal + rate
    merid_half, merid_rate = 0.5 * merid, 0.5 * merid * merid + rate
    east, west = zonal_rate - zonal_half, zonal_rate + zonal_half
    to_north, to_south = merid_rate - merid_half, merid_rate + merid_half
    centre = 1.0 + self_mix - 2.0 * zonal_rate - 2.0 * merid_rate
    last, first = lat == zonal.shape[1] - 1, lat == 0
    centre = centre + jnp.where(last, to_north, 0.0) + jnp.where(first, to_south, 0.0)
    to_north = jnp.where(last, 0.0, to_north)
    to_south = jnp.where(first, 0.0, to_south)
    return centre, east, west, to_north, to_south


def mixed(mixing, field, values):
    total = None
    for other, value in enumerate(values):
        if other != field:
            term = mixing[field, other] * value
            total = term if total is None else total + term
    return total


def pick_rows(kinds, particles, fields, strip, columns):
    rows = len(kinds) * particles
    out = lax.broadcasted_iota(jnp.int32, (rows, columns), 0)
    col = lax.broadcasted_iota(jnp.int32, (rows, columns), 1)
    want = jnp.full((rows, columns), -1, jnp.int32)
    for place, (field, x) in enumerate(kinds):
        inside = (out >= place * particles) & (out < (place + 1) * particles)
        target = (out - place * particles) * (fields * strip) + field * strip + x
        want = jnp.where(inside, target, want)
    return (col == want).astype(BF16)


def stack_rows(rows):
    sub = lax.broadcasted_iota(jnp.int32, (len(rows), rows[0].shape[1]), 0)
    out = None
    for p, row in enumerate(rows):
        row = jnp.broadcast_to(row, sub.shape)
        out = row if out is None else jnp.where(sub == p, row, out)
    return out


def observation_maps(sizes, cell, value):
    particles, fields, strip, lats, strips = sizes
    x0 = lax.axis_index("lon") * strip
    shift = lats.bit_length() - 1
    local_cell = cell - x0 * lats
    obs_lon = lax.shift_right_arithmetic(local_cell, shift)
    obs_lat = local_cell & (lats - 1)
    count = cell.shape[1]
    here = lax.broadcasted_iota(jnp.int32, (strip, count), 0) == obs_lon
    high = value.astype(BF16)
    rest = value - high.astype(F32)
    mid = rest.astype(BF16)
    low = (rest - mid.astype(F32)).astype(BF16)
    zero = jnp.zeros((strip, count), F32)
    parts = [jnp.where(here, 1.0, zero)]
    parts += [jnp.where(here, p.astype(F32), zero) for p in (high, mid, low)]
    left = jnp.concatenate(parts, 0).astype(BF16)
    right = (lax.broadcasted_iota(jnp.int32, (lats, count), 0) == obs_lat).astype(F32).astype(BF16)
    dense = lax.dot_general(left, right, (((1,), (1,)), ((), ())), preferred_element_type=F32)
    seen = dense[:strip]
    lon = (lax.broadcasted_iota(jnp.int32, (strip, lats), 0) + x0).astype(F32)
    precision = 1.0 + 2.0 * lon / (strip * strips)
    target = dense[strip:2 * strip] + (dense[2 * strip:3 * strip] + dense[3 * strip:])
    return seen * (0.25 * precision), seen * precision, target


def prepare(sizes, state_hbm, noise_hbm, courant_hbm, diffusion_hbm, mixing_hbm, cell_hbm, value_hbm,
            send_east, send_west,
            low, high, noise, courant, diffusion, mixing, cell, value, sems):
    particles, fields, strip, lats, strips = sizes
    copies = [pltpu.make_async_copy(source, target, sems.at[k]) for k, (source, target) in enumerate((
        (cell_hbm, cell), (value_hbm, value), (noise_hbm.at[0], noise), (state_hbm.at[:, :8], low),
        (state_hbm.at[:, strip - 8:], high), (courant_hbm, courant), (diffusion_hbm, diffusion),
        (mixing_hbm, mixing)))]
    for copy in copies:
        copy.start()
    copies[0].wait()
    copies[1].wait()
    gain, _, target = observation_maps(sizes, cell[...], value[...])

    kinds = [(f, x) for x in (0, strip - 1) for f in range(fields)]
    pick = pick_rows(kinds, particles, fields, strip, noise.shape[0])
    copies[2].wait()
    rows = jnp.dot(pick, noise[...], preferred_element_type=F32)
    for copy in copies[3:]:
        copy.wait()

    def edge(x, inner, out, base):
        tile, first = (low, 0) if x < 8 else (high, strip - 8)

        def rows_at(f, place):
            return stack_rows([tile[p * fields + f, place:place + 1] for p in range(particles)])

        here = [rows_at(f, x - first) for f in range(fields)]
        beside = [rows_at(f, inner - first) for f in range(fields)]
        for f in range(fields):
            centre, east, west, to_north, to_south = coefficients(
                courant[0, x:x + 1], courant[1, x:x + 1], diffusion[f], mixing[f, f])
            known, missing = (east, west) if inner > x else (west, east)
            moved = (centre * here[f] + known * beside[f] + to_north * north(here[f])
                     + to_south * south(here[f]) + mixed(mixing, f, here))
            if f == 0:
                g = gain[x:x + 1]
                moved = moved + g * (target[x:x + 1] - moved)
                missing = (1.0 - g) * missing
            moved = moved + rows[base + f * particles:base + (f + 1) * particles]
            out[f * particles:(f + 1) * particles] = here[f]
            out[(fields + f) * particles:(fields + f + 1) * particles] = moved
            out[2 * fields * particles + f:2 * fields * particles + f + 1] = missing
        out[2 * fields * particles + fields:] = jnp.zeros((8 - fields, lats), F32)

    edge(strip - 1, strip - 2, send_east, fields * particles)
    edge(0, 1, send_west, 0)


def bulk(sizes, state, noise, courant, diffusion, mixing, cell, value,
         out, partial, noise_rows, first_rows, edge_coefs, edge_maps, coefs, maps, middle):
    particles, fields, strip, lats, strips = sizes
    maps[0], maps[1], maps[2] = observation_maps(sizes, cell[...], value[...])
    places = (0, 1, strip - 2, strip - 1)
    for k, x in enumerate(places):
        for m in range(3):
            edge_maps[m * 4 + k:m * 4 + k + 1] = maps[m, x:x + 1]
    lon = lax.broadcasted_iota(jnp.int32, (strip, lats), 0)
    for f in range(fields):
        centre, east, west, to_north, to_south = coefficients(
            courant[0], courant[1], diffusion[f], mixing[f, f])
        coefs[f, 0] = centre
        coefs[f, 1] = jnp.where(lon == strip - 1, 0.0, east)
        coefs[f, 2] = jnp.where(lon == 0, 0.0, west)
        coefs[f, 3] = to_north
        coefs[f, 4] = to_south
        for side, (x, inner, outward) in enumerate(((0, 1, west), (strip - 1, strip - 2, east))):
            row = (side * fields + f) * 5
            for k, (values, at) in enumerate(((centre, x), (outward, x), (to_north, x), (to_south, x), (outward, inner))):
                edge_coefs[row + k:row + k + 1] = values[at:at + 1]
    kinds = [(0, x) for x in places]
    pick = pick_rows(kinds, particles, fields, strip, noise.shape[1])
    noise_rows[:4 * particles] = jnp.dot(pick, noise[1], preferred_element_type=F32)
    noise_rows[4 * particles:] = jnp.dot(pick, noise[0], preferred_element_type=F32)

    def rows_of(p, f):
        return pl.ds(pl.multiple_of(p * (fields * strip) + f * strip, strip), strip)

    def moved(values, f):
        v = values[f]
        return (coefs[f, 0] * v + coefs[f, 1] * pltpu.roll(v, strip - 1, 0) + coefs[f, 2] * pltpu.roll(v, 1, 0)
                + coefs[f, 3] * north(v) + coefs[f, 4] * south(v) + mixed(mixing, f, values))

    def body(p, carry):
        values = [state[rows_of(p, f), :] for f in range(fields)]
        total = None
        for f in range(fields):
            new = moved(values, f)
            add = noise[0, rows_of(p, f), :].astype(F32)
            if f == 0:
                push = maps[0] * (maps[2] - new)
                new = new + push
                total = jnp.where((lon > 0) & (lon < strip - 1), push * (push + 2.0 * add), 0.0)
            middle[f] = new + add
        values = [middle[f] for f in range(fields)]
        for f in range(fields):
            new = moved(values, f)
            add = noise[1, rows_of(p, f), :].astype(F32)
            if f == 0:
                push = maps[0] * (maps[2] - new)
                new = new + push + add
                miss = maps[2] - new
                term = ((0.5 / noise_var) * (push * (push + 2.0 * add)) + (0.5 * maps[1]) * (miss * miss))
                total = (0.5 / noise_var) * total + jnp.where((lon > 1) & (lon < strip - 2), term, 0.0)
            else:
                new = new + add
            out[rows_of(p, f), :] = new
        total = jnp.sum(total, axis=0, keepdims=True)
        partial[pl.ds(p, 1), :] = total[:, :128] + total[:, 128:]
        return carry

    lax.fori_loop(0, particles, body, 0)
    for k, x in enumerate(places):
        first_rows[k * particles:(k + 1) * particles] = stack_rows(
            [out[p * fields * strip + x:p * fields * strip + x + 1] for p in range(particles)])


def correct(sizes, own_east, own_west, from_west, from_east, mixing, edge_coefs, edge_maps, noise_rows, first_rows,
            partial, weights, changes):
    particles, fields, strip, lats, strips = sizes
    n = fields * particles

    def split(ref, start):
        return [ref[start + f * particles:start + (f + 1) * particles] for f in range(fields)]

    def wide(v):
        return v[:, :128] + v[:, 128:]

    def push_terms(push, add):
        return (0.5 / noise_var) * (push * (push + 2.0 * add))

    total = partial[...]
    for side, (k_edge, k_in, own, other) in enumerate(((0, 1, own_west, from_west), (3, 2, own_east, from_east))):
        own_state, other_state, other_first = split(own, 0), split(other, 0), split(other, n)

        def maps_at(k):
            return [edge_maps[m * 4 + k:m * 4 + k + 1] for m in range(3)]

        gain, seen, observed = maps_at(k_edge)
        coefs = [[edge_coefs[(side * fields + f) * 5 + k:(side * fields + f) * 5 + k + 1] for k in range(5)]
                 for f in range(fields)]
        first, outside = [], []
        for f in range(fields):
            row = 2 * n + f
            outside.append(other_first[f] + other[row:row + 1] * own_state[f])
            step = coefs[f][1] * other_state[f]
            if f == 0:
                step = (1.0 - gain) * step
                result = own[n:n + particles] + step
                add = noise_rows[(4 + k_edge) * particles:(5 + k_edge) * particles]
                push = (gain / (1.0 - gain)) * (observed - (result - add))
                total = total + wide(push_terms(push, add))
            first.append(step)
        for f in range(fields):
            centre, outward, to_north, to_south, outward_in = coefs[f]
            step = (centre * first[f] + outward * outside[f] + to_north * north(first[f])
                    + to_south * south(first[f]) + mixed(mixing, f, first))
            beside = outward_in * first[f]
            if f == 0:
                step = (1.0 - gain) * step
                beside = (1.0 - maps_at(k_in)[0]) * beside
                for k, change in ((k_edge, step), (k_in, beside)):
                    g, s, v = maps_at(k)
                    result = first_rows[k * particles:(k + 1) * particles] + change
                    add = noise_rows[k * particles:(k + 1) * particles]
                    push = (g / (1.0 - g)) * (v - (result - add))
                    miss = v - result
                    total = total + wide(push_terms(push, add) + (0.5 * s) * (miss * miss))
            changes[k_edge, f * particles:(f + 1) * particles] = step
            changes[k_in, f * particles:(f + 1) * particles] = beside
    total = jnp.broadcast_to(jnp.sum(total, axis=1, keepdims=True), total.shape)
    diagonal = lax.broadcasted_iota(jnp.int32, total.shape, 0) == lax.broadcasted_iota(jnp.int32, total.shape, 1)
    total = jnp.sum(jnp.where(diagonal, total, 0.0), axis=0, keepdims=True)
    for k in range(strips):
        weights[k] = total


def apply_changes(sizes, current, changes, out):
    particles, fields, strip, lats, strips = sizes
    sub = lax.broadcasted_iota(jnp.int32, (8, lats), 0)
    for p in range(particles):
        for f in range(fields):
            start = (p * fields + f) * strip
            row = f * particles + p
            rows = [jnp.broadcast_to(changes[k, row:row + 1], sub.shape) for k in range(4)]
            out[start:start + 8] = current[start:start + 8] + jnp.where(
                sub == 0, rows[0], jnp.where(sub == 1, rows[1], 0.0))
            out[start + 8:start + strip - 8] = current[start + 8:start + strip - 8]
            out[start + strip - 8:start + strip] = current[start + strip - 8:start + strip] + jnp.where(
                sub == 7, rows[3], jnp.where(sub == 6, rows[2], 0.0))


def assemble(sizes, scale, source, current, received, weights, prior, out, log_weight, held, sems):
    particles, strips = sizes[0], sizes[4]
    dom = lax.axis_index("dom")

    def copy(j, ref, at):
        return pltpu.make_async_copy(ref.at[at], out.at[j], sems.at[j])

    for j in range(particles):
        wanted = source[dom * particles + j]
        mine = wanted // particles == dom
        at = wanted % particles

        @pl.when(mine)
        def _():
            copy(j, current, at).start()

        @pl.when(jnp.logical_not(mine))
        def _():
            copy(j, received, at).start()

    total = weights[0]
    for k in range(1, strips):
        total = total + weights[k]
    held[...] = prior[...] - scale * total[:, :particles]
    last = pltpu.make_async_copy(held, log_weight, sems.at[particles])
    last.start()
    for j in range(particles):
        copy(j, current, 0).wait()
    last.wait()


def local(ensemble_state, proposal_noise, courant, diffusion, mixing, prior_weight, obs_cell, obs_value, source):
    particles, fields, strip, lats = ensemble_state.shape
    strips = lax.axis_size("lon")
    sizes = (particles, fields, strip, lats, strips)
    rows = particles * fields * strip
    state = ensemble_state.reshape(rows, lats)
    noise = proposal_noise.reshape(2, rows, lats)
    packet = jax.ShapeDtypeStruct((2 * particles * fields + 8, lats), F32)
    cell, value = obs_cell[None], obs_value[None]

    def shape(*dims):
        return jax.ShapeDtypeStruct(dims, F32)

    send_east, send_west = pl.pallas_call(
        functools.partial(prepare, sizes),
        out_shape=(packet, packet),
        in_specs=[HBM] * 7,
        out_specs=(VMEM,) * 2,
        scratch_shapes=[
            pltpu.VMEM((particles * fields, 8, lats), F32),
            pltpu.VMEM((particles * fields, 8, lats), F32),
            pltpu.VMEM((rows, lats), BF16),
            pltpu.VMEM(courant.shape, F32),
            pltpu.SMEM(diffusion.shape, F32),
            pltpu.SMEM(mixing.shape, F32),
            pltpu.VMEM(cell.shape, jnp.int32),
            pltpu.VMEM(value.shape, F32),
            pltpu.SemaphoreType.DMA((8,)),
        ],
        compiler_params=pltpu.CompilerParams(vmem_limit_bytes=60 * 1024 * 1024),
        cost_estimate=pl.CostEstimate(flops=1000000, bytes_accessed=2000000, transcendentals=0),
    )(state.reshape(particles * fields, strip, lats), noise, courant, diffusion, mixing, cell, value)

    eastward = [(i, (i + 1) % strips) for i in range(strips)]
    westward = [(i, (i - 1) % strips) for i in range(strips)]
    from_west = lax.ppermute(send_east, "lon", eastward)
    from_east = lax.ppermute(send_west, "lon", westward)

    current, partial, noise_rows, first_rows, edge_coefs, edge_maps = pl.pallas_call(
        functools.partial(bulk, sizes),
        out_shape=(shape(rows, lats), shape(particles, 128), shape(8 * particles, lats), shape(4 * particles, lats),
                   shape(2 * fields * 5, lats), shape(12, lats)),
        in_specs=[VMEM, VMEM, VMEM, SMEM, SMEM, VMEM, VMEM],
        out_specs=(VMEM,) * 6,
        scratch_shapes=[pltpu.VMEM((fields, 5, strip, lats), F32), pltpu.VMEM((3, strip, lats), F32),
                        pltpu.VMEM((fields, strip, lats), F32)],
        compiler_params=LIMIT,
        cost_estimate=pl.CostEstimate(flops=30000000, bytes_accessed=4000000, transcendentals=0),
    )(state, noise, courant, diffusion, mixing, cell, value)

    weights, changes = pl.pallas_call(
        functools.partial(correct, sizes),
        out_shape=(shape(strips, 1, 128), shape(4, particles * fields, lats)),
        in_specs=[VMEM] * 4 + [SMEM] + [VMEM] * 5,
        out_specs=(VMEM,) * 2,
        compiler_params=LIMIT,
        cost_estimate=pl.CostEstimate(flops=1000000, bytes_accessed=1000000, transcendentals=0),
    )(send_east, send_west, from_west, from_east, mixing, edge_coefs, edge_maps, noise_rows, first_rows, partial)

    current = pl.pallas_call(
        functools.partial(apply_changes, sizes),
        out_shape=shape(rows, lats),
        in_specs=[VMEM] * 2,
        out_specs=VMEM,
        compiler_params=LIMIT,
        cost_estimate=pl.CostEstimate(flops=1000000, bytes_accessed=2000000, transcendentals=0),
    )(current, changes).reshape(particles, fields, strip, lats)

    received = lax.ppermute(current, "dom", [(0, 1), (1, 0)])
    weights = lax.all_to_all(weights, "lon", 0, 0)

    new_state, log_weight = pl.pallas_call(
        functools.partial(assemble, sizes, 1.0 / (256.0 * obs_cell.shape[0])),
        out_shape=(shape(particles, fields, strip, lats), shape(1, particles)),
        in_specs=[SMEM, VMEM, VMEM, VMEM, VMEM],
        out_specs=(HBM, HBM),
        scratch_shapes=[pltpu.VMEM((1, particles), F32), pltpu.SemaphoreType.DMA((particles + 1,))],
        compiler_params=LIMIT,
        cost_estimate=pl.CostEstimate(flops=0, bytes_accessed=2000000, transcendentals=0),
    )(source, current, received, weights, prior_weight[None])
    return new_state, log_weight[0]


def solution(mesh):
    placed = (
        P(("groups", "dom"), None, "lon", None),
        P(None, ("groups", "dom"), None, "lon", None),
        P(None, ("groups", "lon"), None),
        P(),
        P(),
        P(("groups", "dom")),
        P(("groups", "lon")),
        P(("groups", "lon")),
        P("groups"),
    )
    return jax.shard_map(
        local,
        mesh=mesh,
        in_specs=placed,
        out_specs=(P(("groups", "dom"), None, "lon", None), P(("groups", "dom"))),
        check_vma=False,
    )
```

```python
import functools

import jax
import jax.numpy as jnp
from jax import lax
from jax.experimental import pallas as pl
from jax.experimental.pallas import tpu as pltpu
from jax.sharding import PartitionSpec as P

noise_var = 0.04
VMEM = pl.BlockSpec(memory_space=pltpu.VMEM)
SMEM = pl.BlockSpec(memory_space=pltpu.SMEM)
HBM = pl.BlockSpec(memory_space=pltpu.HBM)
LIMIT = pltpu.CompilerParams(vmem_limit_bytes=16 * 1024 * 1024)
BF16 = jnp.bfloat16
F32 = jnp.float32


def north(v):
    return pltpu.roll(v, v.shape[1] - 1, 1)


def south(v):
    return pltpu.roll(v, 1, 1)


def coefficients(zonal, merid, rate, self_mix):
    lat = lax.broadcasted_iota(jnp.int32, zonal.shape, 1)
    zonal_half, zonal_rate = 0.5 * zonal, 0.5 * zonal * zonal + rate
    merid_half, merid_rate = 0.5 * merid, 0.5 * merid * merid + rate
    east, west = zonal_rate - zonal_half, zonal_rate + zonal_half
    to_north, to_south = merid_rate - merid_half, merid_rate + merid_half
    centre = 1.0 + self_mix - 2.0 * zonal_rate - 2.0 * merid_rate
    last, first = lat == zonal.shape[1] - 1, lat == 0
    centre = centre + jnp.where(last, to_north, 0.0) + jnp.where(first, to_south, 0.0)
    to_north = jnp.where(last, 0.0, to_north)
    to_south = jnp.where(first, 0.0, to_south)
    return centre, east, west, to_north, to_south


def mixed(mixing, field, values):
    total = None
    for other, value in enumerate(values):
        if other != field:
            term = mixing[field, other] * value
            total = term if total is None else total + term
    return total


def pick_rows(kinds, particles, fields, strip, columns):
    rows = len(kinds) * particles
    out = lax.broadcasted_iota(jnp.int32, (rows, columns), 0)
    col = lax.broadcasted_iota(jnp.int32, (rows, columns), 1)
    want = jnp.full((rows, columns), -1, jnp.int32)
    for place, (field, x) in enumerate(kinds):
        inside = (out >= place * particles) & (out < (place + 1) * particles)
        target = (out - place * particles) * (fields * strip) + field * strip + x
        want = jnp.where(inside, target, want)
    return (col == want).astype(BF16)


def stack_rows(rows):
    sub = lax.broadcasted_iota(jnp.int32, (len(rows), rows[0].shape[1]), 0)
    out = None
    for p, row in enumerate(rows):
        row = jnp.broadcast_to(row, sub.shape)
        out = row if out is None else jnp.where(sub == p, row, out)
    return out


def in_row(column):
    total = jnp.broadcast_to(jnp.sum(column, axis=1, keepdims=True), column.shape)
    diagonal = lax.broadcasted_iota(jnp.int32, total.shape, 0) == lax.broadcasted_iota(jnp.int32, total.shape, 1)
    return jnp.sum(jnp.where(diagonal, total, 0.0), axis=0, keepdims=True)


def wide(v):
    return v[:, :128] + v[:, 128:]


def observation_maps(sizes, cell, value):
    particles, fields, strip, lats, strips = sizes
    x0 = lax.axis_index("lon") * strip
    shift = lats.bit_length() - 1
    local_cell = cell - x0 * lats
    obs_lon = lax.shift_right_arithmetic(local_cell, shift)
    obs_lat = local_cell & (lats - 1)
    count = cell.shape[1]
    here = lax.broadcasted_iota(jnp.int32, (strip, count), 0) == obs_lon
    high = value.astype(BF16)
    rest = value - high.astype(F32)
    mid = rest.astype(BF16)
    low = (rest - mid.astype(F32)).astype(BF16)
    zero = jnp.zeros((strip, count), F32)
    parts = [jnp.where(here, 1.0, zero)]
    parts += [jnp.where(here, p.astype(F32), zero) for p in (high, mid, low)]
    left = jnp.concatenate(parts, 0).astype(BF16)
    right = (lax.broadcasted_iota(jnp.int32, (lats, count), 0) == obs_lat).astype(F32).astype(BF16)
    dense = lax.dot_general(left, right, (((1,), (1,)), ((), ())), preferred_element_type=F32)
    lon = (lax.broadcasted_iota(jnp.int32, (strip, lats), 0) + x0).astype(F32)
    precision = 1.0 + 2.0 * lon / (strip * strips)
    target = dense[strip:2 * strip] + (dense[2 * strip:3 * strip] + dense[3 * strip:])
    return dense[:strip] * (0.25 * precision), target


def prepare(sizes, state_hbm, noise_hbm, courant_hbm, diffusion_hbm, mixing_hbm, cell_hbm, value_hbm,
            send_east, send_west,
            low, high, noise0, noise1, courant, diffusion, mixing, cell, value, sems):
    particles, fields, strip, lats, strips = sizes
    n = fields * particles
    copies = [pltpu.make_async_copy(source, target, sems.at[k]) for k, (source, target) in enumerate((
        (cell_hbm, cell), (value_hbm, value), (courant_hbm, courant), (diffusion_hbm, diffusion),
        (mixing_hbm, mixing), (noise_hbm.at[0], noise0), (noise_hbm.at[1, :, 0], noise1),
        (state_hbm.at[:, :, :8], low), (state_hbm.at[:, :, strip - 8:], high)))]
    for copy in copies:
        copy.start()
    copies[0].wait()
    copies[1].wait()
    gain, target = observation_maps(sizes, cell[...], value[...])
    kinds = []
    for x, step in ((strip - 1, -1), (0, 1)):
        kinds += [(f, x) for f in range(fields)] + [(f, x + step) for f in range(fields)] + [(0, x + 2 * step)]
    pick0 = pick_rows(kinds, particles, fields, strip, n * strip)
    pick1 = pick_rows([(0, x) for x in (strip - 1, strip - 2, 0, 1)], particles, 1, strip, particles * strip)
    for copy in copies[2:5]:
        copy.wait()

    sides = []
    for first, inward, outward in ((strip - 8, 2, 1), (0, 1, 2)):
        tile = [coefficients(courant[0, first:first + 8], courant[1, first:first + 8], diffusion[f], mixing[f, f])
                for f in range(fields)]
        sides.append([[c[0], c[inward], c[outward], c[3], c[4]] for c in tile])
    copies[5].wait()
    rows0 = jnp.dot(pick0, noise0[...].reshape(n * strip, lats), preferred_element_type=F32)
    copies[6].wait()
    rows1 = jnp.dot(pick1, noise1[...].reshape(particles * strip, lats), preferred_element_type=F32)
    copies[7].wait()
    copies[8].wait()

    def edge(side, out):
        tile, x, first, step = ((high, strip - 1, strip - 8, -1), (low, 0, 0, 1))[side]
        base0, base1 = side * (2 * fields + 1) * particles, side * 2 * particles

        def coefs_at(f, k):
            at = x + k * step - first
            return [c[at:at + 1] for c in sides[side][f]]

        def maps_at(k):
            at = x + k * step
            return gain[at:at + 1], target[at:at + 1]

        def state_at(f, k):
            at = x + k * step - first
            return stack_rows([tile[p, f, at:at + 1] for p in range(particles)])

        def moved(f, k, here, inner, outer):
            centre, inward, outward, to_north, to_south = coefs_at(f, k)
            v = here[f]
            total = centre * v + inward * inner + to_north * north(v) + to_south * south(v) + mixed(mixing, f, here)
            return total if outer is None else total + outward * outer

        def noisy0(k, f):
            at = base0 + (k * fields + f) * particles
            return rows0[at:at + particles]

        def noisy1(k):
            at = base1 + k * particles
            return rows1[at:at + particles]

        def nudged(value, k):
            g, v = maps_at(k)
            push = g * (v - value)
            return value + push, push

        state = [[state_at(f, k) for f in range(fields)] for k in range(3)]
        third = state_at(0, 3)
        result = [[], []]
        pushes = []
        for k in range(2):
            for f in range(fields):
                new = moved(f, k, state[k], state[k + 1][f], state[k - 1][f] if k else None)
                if f == 0:
                    new, push = nudged(new, k)
                    pushes.append(push)
                result[k].append(new + noisy0(k, f))
        new, _ = nudged(moved(0, 2, state[2], third, state[1][0]), 2)
        inside = new + noisy0(2, 0)

        g0, _ = maps_at(0)
        g1, _ = maps_at(1)
        slope = [-(1.0 / noise_var) * g0 * (pushes[0] + noisy0(0, 0))]
        bend = [(0.5 / noise_var) * g0 * g0]
        for k, g in enumerate((g0, g1)):
            new = moved(0, k, result[k], result[1][0] if k == 0 else inside, result[0][0] if k else None)
            new, push = nudged(new, k)
            miss = maps_at(k)[1] - (new + noisy1(k))
            weight = 4.0 * g
            slope.append(-(1.0 / noise_var) * g * (push + noisy1(k)) - weight * (1.0 - g) * miss)
            bend.append((0.5 / noise_var) * g * g + 0.5 * weight * (1.0 - g) * (1.0 - g))
        outward = coefs_at(0, 0)[2]
        onward = coefs_at(0, 1)[2] * (1.0 - g0) * outward

        for f in range(fields):
            out[f * particles:(f + 1) * particles] = state[0][f]
            out[n + f * particles:n + (f + 1) * particles] = result[0][f]
        out[2 * n:2 * n + particles] = outward * slope[0] + onward * slope[2]
        out[2 * n + particles:2 * n + 2 * particles] = slope[1]
        inner = x + step
        last = (outward * outward * bend[0] + onward * onward * bend[2], bend[1],
                courant[0, x:x + 1], courant[1, x:x + 1], g0, courant[0, inner:inner + 1], g1,
                jnp.zeros((1, lats), F32))
        out[2 * n + 2 * particles:] = stack_rows(last)

    edge(0, send_east)
    edge(1, send_west)


def zero_halo(sizes, courant, diffusion, mixing, coefs):
    particles, fields, strip, lats, strips = sizes
    lon = lax.broadcasted_iota(jnp.int32, (strip, lats), 0)
    for f in range(fields):
        centre, east, west, to_north, to_south = coefficients(
            courant[0], courant[1], diffusion[f], mixing[f, f])
        coefs[f, 0] = centre
        coefs[f, 1] = jnp.where(lon == strip - 1, 0.0, east)
        coefs[f, 2] = jnp.where(lon == 0, 0.0, west)
        coefs[f, 3] = to_north
        coefs[f, 4] = to_south

    def moved(values, f):
        v = values[f]
        return (coefs[f, 0] * v + coefs[f, 1] * pltpu.roll(v, strip - 1, 0) + coefs[f, 2] * pltpu.roll(v, 1, 0)
                + coefs[f, 3] * north(v) + coefs[f, 4] * south(v) + mixed(mixing, f, values))

    return moved


def observed_bulk(sizes, state, noise, courant, diffusion, mixing, cell, value, middle, out, weight,
                  coefs, maps, partial):
    particles, fields, strip, lats, strips = sizes
    maps[0], maps[1] = observation_maps(sizes, cell[...], value[...])
    moved = zero_halo(sizes, courant, diffusion, mixing, coefs)

    def body(p, carry):
        values = [state[p, f] for f in range(fields)]
        total = None
        for f in range(fields):
            new = moved(values, f)
            add = noise[0, p, f].astype(F32)
            if f == 0:
                push = maps[0] * (maps[1] - new)
                new = new + push
                total = push * (push + 2.0 * add)
            middle[p, f] = new + add
        values = [middle[p, f] for f in range(fields)]
        new = moved(values, 0)
        add = noise[1, p, 0].astype(F32)
        push = maps[0] * (maps[1] - new)
        new = new + push + add
        miss = maps[1] - new
        total = (0.5 / noise_var) * (total + push * (push + 2.0 * add)) + (2.0 * maps[0]) * (miss * miss)
        out[p] = new
        partial[pl.ds(p, 1), :] = wide(jnp.sum(total, axis=0, keepdims=True))
        return carry

    lax.fori_loop(0, particles, body, 0)
    weight[...] = in_row(partial[...])


def other_bulk(sizes, middle, observed, noise, courant, diffusion, mixing, out, coefs):
    particles, fields, strip, lats, strips = sizes
    moved = zero_halo(sizes, courant, diffusion, mixing, coefs)

    def body(p, carry):
        values = [middle[p, f] for f in range(fields)]
        out[p, 0] = observed[p]
        for f in range(1, fields):
            out[p, f] = moved(values, f) + noise[1, p, f].astype(F32)
        return carry

    lax.fori_loop(0, particles, body, 0)


def correct(sizes, own_east, own_west, from_west, from_east, diffusion, mixing, bulk_weight, bulk_beside,
            weight, changes):
    particles, fields, strip, lats, strips = sizes
    n = fields * particles

    def field_rows(ref, start, f):
        return ref[start + f * particles:start + (f + 1) * particles]

    packets = (own_east, from_east, own_west, from_west)
    last = 2 * n + 2 * particles
    zonal = stack_rows([ref[last + 2:last + 3] for ref in packets] + [ref[last + 5:last + 6] for ref in packets])
    merid = stack_rows([ref[last + 3:last + 4] for ref in packets] * 2)
    tile = [coefficients(zonal, merid, diffusion[f], mixing[f, f]) for f in range(fields)]
    total = jnp.zeros((particles, lats), F32)
    for k, owner in enumerate(packets):
        other_k = k ^ 1
        other = packets[other_k]
        outward_at = (1, 2, 2, 1)[k]
        outward_other = (1, 2, 2, 1)[other_k]
        gain = owner[last + 4:last + 5]
        gain_other = other[last + 4:last + 5]
        first = []
        for f in range(fields):
            step = tile[f][outward_at][k:k + 1] * field_rows(other, 0, f)
            first.append((1.0 - gain) * step if f == 0 else step)
        mine = k in (0, 2)
        for f in range(fields if mine else 1):
            centre, to_north, to_south = [tile[f][c][k:k + 1] for c in (0, 3, 4)]
            outward = tile[f][outward_at][k:k + 1]
            reach = tile[f][outward_other][other_k:other_k + 1]
            if f == 0:
                reach = (1.0 - gain_other) * reach
            outside = field_rows(other, n, f) + reach * field_rows(owner, 0, f)
            step = (centre * first[f] + outward * outside + to_north * north(first[f])
                    + to_south * south(first[f]) + mixed(mixing, f, first))
            if f == 0:
                seen = field_rows(other, 0, 0)
                slope, slope_step = owner[2 * n:2 * n + particles], owner[2 * n + particles:last]
                bend, bend_step = owner[last:last + 1], owner[last + 1:last + 2]
                total = total + seen * (slope + bend * seen) + step * (slope_step + bend_step * step)
            if mine:
                beside = tile[f][outward_at][4 + k:5 + k] * first[f]
                if f == 0:
                    step = (1.0 - gain) * step
                    beside = (1.0 - owner[last + 6:last + 7]) * beside
                edge, inner = (3, 2) if k == 0 else (0, 1)
                changes[edge, f * particles:(f + 1) * particles] = step
                changes[inner, f * particles:(f + 1) * particles] = beside
    weight[...] = in_row(wide(total)) + (bulk_weight[...] + bulk_beside[...])


def apply_changes(sizes, current, changes, out):
    particles, fields, strip, lats, strips = sizes
    sub = lax.broadcasted_iota(jnp.int32, (8, lats), 0)
    for p in range(particles):
        for f in range(fields):
            row = f * particles + p
            rows = [jnp.broadcast_to(changes[k, row:row + 1], sub.shape) for k in range(4)]
            out[p, f, :8] = current[p, f, :8] + jnp.where(sub == 0, rows[0], jnp.where(sub == 1, rows[1], 0.0))
            out[p, f, 8:strip - 8] = current[p, f, 8:strip - 8]
            out[p, f, strip - 8:] = current[p, f, strip - 8:] + jnp.where(
                sub == 7, rows[3], jnp.where(sub == 6, rows[2], 0.0))


def assemble(sizes, source, current, received, out, sems):
    particles = sizes[0]
    dom = lax.axis_index("dom")

    def copy(j, ref, at):
        return pltpu.make_async_copy(ref.at[at], out.at[j], sems.at[j])

    for j in range(particles):
        wanted = source[dom * particles + j]
        mine = wanted // particles == dom
        at = wanted % particles

        @pl.when(mine)
        def _():
            copy(j, current, at).start()

        @pl.when(jnp.logical_not(mine))
        def _():
            copy(j, received, at).start()

    for j in range(particles):
        copy(j, current, 0).wait()


def local(ensemble_state, proposal_noise, courant, diffusion, mixing, prior_weight, obs_cell, obs_value, source):
    particles, fields, strip, lats = ensemble_state.shape
    strips = lax.axis_size("lon")
    sizes = (particles, fields, strip, lats, strips)
    packet = jax.ShapeDtypeStruct((2 * particles * fields + 2 * particles + 8, lats), F32)
    cell, value = obs_cell[None], obs_value[None]

    def shape(*dims):
        return jax.ShapeDtypeStruct(dims, F32)

    send_east, send_west = pl.pallas_call(
        functools.partial(prepare, sizes),
        out_shape=(packet, packet),
        in_specs=[HBM] * 7,
        out_specs=(VMEM,) * 2,
        scratch_shapes=[
            pltpu.VMEM((particles, fields, 8, lats), F32),
            pltpu.VMEM((particles, fields, 8, lats), F32),
            pltpu.VMEM((particles, fields, strip, lats), BF16),
            pltpu.VMEM((particles, strip, lats), BF16),
            pltpu.VMEM(courant.shape, F32),
            pltpu.SMEM(diffusion.shape, F32),
            pltpu.SMEM(mixing.shape, F32),
            pltpu.VMEM(cell.shape, jnp.int32),
            pltpu.VMEM(value.shape, F32),
            pltpu.SemaphoreType.DMA((9,)),
        ],
        compiler_params=pltpu.CompilerParams(vmem_limit_bytes=60 * 1024 * 1024),
        cost_estimate=pl.CostEstimate(flops=1000000, bytes_accessed=2000000, transcendentals=0),
    )(ensemble_state, proposal_noise, courant, diffusion, mixing, cell, value)

    eastward = [(i, (i + 1) % strips) for i in range(strips)]
    westward = [(i, (i - 1) % strips) for i in range(strips)]
    from_west = lax.ppermute(send_east, "lon", eastward)
    from_east = lax.ppermute(send_west, "lon", westward)

    whole = (particles, fields, strip, lats)
    middle, observed, bulk_weight = pl.pallas_call(
        functools.partial(observed_bulk, sizes),
        out_shape=(shape(*whole), shape(particles, strip, lats), shape(1, 128)),
        in_specs=[VMEM, VMEM, VMEM, SMEM, SMEM, VMEM, VMEM],
        out_specs=(VMEM,) * 3,
        scratch_shapes=[pltpu.VMEM((fields, 5, strip, lats), F32), pltpu.VMEM((2, strip, lats), F32),
                        pltpu.VMEM((particles, 128), F32)],
        compiler_params=LIMIT,
        cost_estimate=pl.CostEstimate(flops=20000000, bytes_accessed=4000000, transcendentals=0),
    )(ensemble_state, proposal_noise, courant, diffusion, mixing, cell, value)
    beside = lax.ppermute(bulk_weight, "lon", [(i, i ^ 1) for i in range(strips)])

    current = pl.pallas_call(
        functools.partial(other_bulk, sizes),
        out_shape=shape(*whole),
        in_specs=[VMEM] * 4 + [SMEM] * 2,
        out_specs=VMEM,
        scratch_shapes=[pltpu.VMEM((fields, 5, strip, lats), F32)],
        compiler_params=LIMIT,
        cost_estimate=pl.CostEstimate(flops=10000000, bytes_accessed=4000000, transcendentals=0),
    )(middle, observed, proposal_noise, courant, diffusion, mixing)

    from_west, from_east, beside = lax.optimization_barrier((from_west, from_east, beside))
    weight, changes = pl.pallas_call(
        functools.partial(correct, sizes),
        out_shape=(shape(1, 128), shape(4, particles * fields, lats)),
        in_specs=[VMEM] * 4 + [SMEM] * 2 + [VMEM] * 2,
        out_specs=(VMEM,) * 2,
        compiler_params=LIMIT,
        cost_estimate=pl.CostEstimate(flops=1000000, bytes_accessed=1000000, transcendentals=0),
    )(send_east, send_west, from_west, from_east, diffusion, mixing, bulk_weight, beside)

    current = pl.pallas_call(
        functools.partial(apply_changes, sizes),
        out_shape=shape(*whole),
        in_specs=[VMEM] * 2,
        out_specs=VMEM,
        compiler_params=LIMIT,
        cost_estimate=pl.CostEstimate(flops=1000000, bytes_accessed=2000000, transcendentals=0),
    )(current, changes)

    received = lax.ppermute(current, "dom", [(0, 1), (1, 0)])
    bit = 2
    while bit < strips:
        if 2 * bit >= strips:
            weight, received = lax.optimization_barrier((weight, received))
        weight = weight + lax.ppermute(weight, "lon", [(i, i ^ bit) for i in range(strips)])
        bit *= 2

    new_state = pl.pallas_call(
        functools.partial(assemble, sizes),
        out_shape=shape(*whole),
        in_specs=[SMEM, VMEM, VMEM],
        out_specs=HBM,
        scratch_shapes=[pltpu.SemaphoreType.DMA((particles,))],
        compiler_params=LIMIT,
        cost_estimate=pl.CostEstimate(flops=0, bytes_accessed=2000000, transcendentals=0),
    )(source, current, received)

    log_weight = prior_weight - weight[0, :particles] / (256.0 * obs_cell.shape[0])
    return new_state, log_weight


def solution(mesh):
    placed = (
        P(("groups", "dom"), None, "lon", None),
        P(None, ("groups", "dom"), None, "lon", None),
        P(None, ("groups", "lon"), None),
        P(),
        P(),
        P(("groups", "dom")),
        P(("groups", "lon")),
        P(("groups", "lon")),
        P("groups"),
    )
    return jax.shard_map(
        local,
        mesh=mesh,
        in_specs=placed,
        out_specs=(P(("groups", "dom"), None, "lon", None), P(("groups", "dom"))),
        check_vma=False,
    )
```

```python
import functools

import jax
import jax.numpy as jnp
from jax import lax
from jax.experimental import pallas as pl
from jax.experimental.pallas import tpu as pltpu
from jax.sharding import PartitionSpec as P

noise_var = 0.04
VMEM = pl.BlockSpec(memory_space=pltpu.VMEM)
SMEM = pl.BlockSpec(memory_space=pltpu.SMEM)
HBM = pl.BlockSpec(memory_space=pltpu.HBM)
LIMIT = pltpu.CompilerParams(vmem_limit_bytes=16 * 1024 * 1024)
FREE = pl.CostEstimate(flops=0, bytes_accessed=0, transcendentals=0)
BF16 = jnp.bfloat16
F32 = jnp.float32


def north(v):
    return pltpu.roll(v, v.shape[1] - 1, 1)


def south(v):
    return pltpu.roll(v, 1, 1)


def coefficients(zonal, merid, rate, self_mix):
    lat = lax.broadcasted_iota(jnp.int32, zonal.shape, 1)
    zonal_half, zonal_rate = 0.5 * zonal, 0.5 * zonal * zonal + rate
    merid_half, merid_rate = 0.5 * merid, 0.5 * merid * merid + rate
    east, west = zonal_rate - zonal_half, zonal_rate + zonal_half
    to_north, to_south = merid_rate - merid_half, merid_rate + merid_half
    centre = 1.0 + self_mix - 2.0 * zonal_rate - 2.0 * merid_rate
    last, first = lat == zonal.shape[1] - 1, lat == 0
    centre = centre + jnp.where(last, to_north, 0.0) + jnp.where(first, to_south, 0.0)
    to_north = jnp.where(last, 0.0, to_north)
    to_south = jnp.where(first, 0.0, to_south)
    return centre, east, west, to_north, to_south


def mixed(mixing, field, values):
    total = None
    for other, value in enumerate(values):
        if other != field:
            term = mixing[field, other] * value
            total = term if total is None else total + term
    return total


def pick_rows(kinds, particles, fields, strip, columns):
    rows = len(kinds) * particles
    out = lax.broadcasted_iota(jnp.int32, (rows, columns), 0)
    col = lax.broadcasted_iota(jnp.int32, (rows, columns), 1)
    want = jnp.full((rows, columns), -1, jnp.int32)
    for place, (field, x) in enumerate(kinds):
        inside = (out >= place * particles) & (out < (place + 1) * particles)
        target = (out - place * particles) * (fields * strip) + field * strip + x
        want = jnp.where(inside, target, want)
    return (col == want).astype(BF16)


def stack_rows(rows):
    sub = lax.broadcasted_iota(jnp.int32, (len(rows), rows[0].shape[1]), 0)
    out = None
    for p, row in enumerate(rows):
        row = jnp.broadcast_to(row, sub.shape)
        out = row if out is None else jnp.where(sub == p, row, out)
    return out


def in_row(column):
    total = jnp.broadcast_to(jnp.sum(column, axis=1, keepdims=True), column.shape)
    diagonal = lax.broadcasted_iota(jnp.int32, total.shape, 0) == lax.broadcasted_iota(jnp.int32, total.shape, 1)
    return jnp.sum(jnp.where(diagonal, total, 0.0), axis=0, keepdims=True)


def wide(v):
    return v[:, :128] + v[:, 128:]


def observation_maps(sizes, cell, value):
    particles, fields, strip, lats, strips = sizes
    x0 = lax.axis_index("lon") * strip
    shift = lats.bit_length() - 1
    local_cell = cell - x0 * lats
    obs_lon = lax.shift_right_arithmetic(local_cell, shift)
    obs_lat = local_cell & (lats - 1)
    count = cell.shape[1]
    here = lax.broadcasted_iota(jnp.int32, (strip, count), 0) == obs_lon
    high = value.astype(BF16)
    rest = value - high.astype(F32)
    mid = rest.astype(BF16)
    low = (rest - mid.astype(F32)).astype(BF16)
    zero = jnp.zeros((strip, count), F32)
    parts = [jnp.where(here, 1.0, zero)]
    parts += [jnp.where(here, p.astype(F32), zero) for p in (high, mid, low)]
    left = jnp.concatenate(parts, 0).astype(BF16)
    right = (lax.broadcasted_iota(jnp.int32, (lats, count), 0) == obs_lat).astype(F32).astype(BF16)
    dense = lax.dot_general(left, right, (((1,), (1,)), ((), ())), preferred_element_type=F32)
    lon = (lax.broadcasted_iota(jnp.int32, (strip, lats), 0) + x0).astype(F32)
    precision = 1.0 + 2.0 * lon / (strip * strips)
    target = dense[strip:2 * strip] + (dense[2 * strip:3 * strip] + dense[3 * strip:])
    return dense[:strip] * (0.25 * precision), target


def prepare(sizes, state_hbm, noise_hbm, courant_hbm, diffusion_hbm, mixing_hbm, cell_hbm, value_hbm,
            send_east, send_west,
            low, high, noise0, noise1, courant, diffusion, mixing, cell, value, sems):
    particles, fields, strip, lats, strips = sizes
    n = fields * particles
    copies = [pltpu.make_async_copy(source, target, sems.at[k]) for k, (source, target) in enumerate((
        (cell_hbm, cell), (value_hbm, value), (courant_hbm, courant), (diffusion_hbm, diffusion),
        (mixing_hbm, mixing), (state_hbm.at[:, :, :8], low), (state_hbm.at[:, :, strip - 8:], high),
        (noise_hbm.at[0], noise0), (noise_hbm.at[1, :, 0], noise1)))]
    for copy in copies:
        copy.start()
    copies[0].wait()
    copies[1].wait()
    gain, target = observation_maps(sizes, cell[...], value[...])
    kinds = []
    for x, step in ((strip - 1, -1), (0, 1)):
        kinds += [(f, x) for f in range(fields)] + [(f, x + step) for f in range(fields)] + [(0, x + 2 * step)]
    pick0 = pick_rows(kinds, particles, fields, strip, n * strip)
    pick1 = pick_rows([(0, x) for x in (strip - 1, strip - 2, 0, 1)], particles, 1, strip, particles * strip)
    for copy in copies[2:5]:
        copy.wait()

    sides = []
    for first, inward, outward in ((strip - 8, 2, 1), (0, 1, 2)):
        tile = [coefficients(courant[0, first:first + 8], courant[1, first:first + 8], diffusion[f], mixing[f, f])
                for f in range(fields)]
        sides.append([[c[0], c[inward], c[outward], c[3], c[4]] for c in tile])
    def coefs_at(side, f, k):
        at = places[side][0] + k * places[side][2] - places[side][1]
        return [c[at:at + 1] for c in sides[side][f]]

    def maps_at(side, k):
        at = places[side][0] + k * places[side][2]
        return gain[at:at + 1], target[at:at + 1]

    def moved(side, f, k, here, inner, outer):
        centre, inward, outward, to_north, to_south = coefs_at(side, f, k)
        v = here[f]
        total = centre * v + inward * inner + to_north * north(v) + to_south * south(v) + mixed(mixing, f, here)
        return total if outer is None else total + outward * outer

    def nudged(side, value, k):
        g, v = maps_at(side, k)
        push = g * (v - value)
        return value + push, push

    def first_step(side, tile, out):
        def state_at(f, k):
            at = places[side][0] + k * places[side][2] - places[side][1]
            return stack_rows([tile[p, f, at:at + 1] for p in range(particles)])

        state = [[state_at(f, k) for f in range(fields)] for k in range(3)]
        third = state_at(0, 3)
        for f in range(fields):
            out[f * particles:(f + 1) * particles] = state[0][f]
        result, pushes = [[], []], []
        for k in range(2):
            for f in range(fields):
                new = moved(side, f, k, state[k], state[k + 1][f], state[k - 1][f] if k else None)
                if f == 0:
                    new, push = nudged(side, new, k)
                    pushes.append(push)
                result[k].append(new)
        inside, _ = nudged(side, moved(side, 0, 2, state[2], third, state[1][0]), 2)
        return result, pushes, inside

    places = ((strip - 1, strip - 8, -1), (0, 0, 1))
    copies[5].wait()
    copies[6].wait()
    started = [first_step(0, high, send_east), first_step(1, low, send_west)]
    copies[7].wait()
    copies[8].wait()
    rows0 = jnp.dot(pick0, noise0[...].reshape(n * strip, lats), preferred_element_type=F32)
    rows1 = jnp.dot(pick1, noise1[...].reshape(particles * strip, lats), preferred_element_type=F32)

    def edge(side, out):
        x, _, step = places[side]
        base0, base1 = side * (2 * fields + 1) * particles, side * 2 * particles
        result, pushes, inside = started[side]

        def noisy0(k, f):
            at = base0 + (k * fields + f) * particles
            return rows0[at:at + particles]

        def noisy1(k):
            at = base1 + k * particles
            return rows1[at:at + particles]

        result = [[result[k][f] + noisy0(k, f) for f in range(fields)] for k in range(2)]
        inside = inside + noisy0(2, 0)
        g0, _ = maps_at(side, 0)
        g1, _ = maps_at(side, 1)
        slope = [-(1.0 / noise_var) * g0 * (pushes[0] + noisy0(0, 0))]
        bend = [(0.5 / noise_var) * g0 * g0]
        for k, g in enumerate((g0, g1)):
            new = moved(side, 0, k, result[k], result[1][0] if k == 0 else inside, result[0][0] if k else None)
            new, push = nudged(side, new, k)
            miss = maps_at(side, k)[1] - (new + noisy1(k))
            weight = 4.0 * g
            slope.append(-(1.0 / noise_var) * g * (push + noisy1(k)) - weight * (1.0 - g) * miss)
            bend.append((0.5 / noise_var) * g * g + 0.5 * weight * (1.0 - g) * (1.0 - g))
        outward = coefs_at(side, 0, 0)[2]
        onward = coefs_at(side, 0, 1)[2] * (1.0 - g0) * outward
        for f in range(fields):
            out[n + f * particles:n + (f + 1) * particles] = result[0][f]
        out[2 * n:2 * n + particles] = outward * slope[0] + onward * slope[2]
        out[2 * n + particles:2 * n + 2 * particles] = slope[1]
        inner = x + step
        last = (outward * outward * bend[0] + onward * onward * bend[2], bend[1],
                courant[0, x:x + 1], courant[1, x:x + 1], g0, courant[0, inner:inner + 1], g1,
                jnp.zeros((1, lats), F32))
        out[2 * n + 2 * particles:] = stack_rows(last)

    edge(0, send_east)
    edge(1, send_west)


class Spread:
    def __init__(self, ref):
        self.ref = ref

    def __getitem__(self, at):
        return self.ref[at[0]:at[0] + 1, at[1]:at[1] + 1]


def zero_halo(sizes, courant, diffusion, mixing, mixing_scalars, coefs):
    particles, fields, strip, lats, strips = sizes
    diffusion, mixing = Spread(diffusion), Spread(mixing)
    lon = lax.broadcasted_iota(jnp.int32, (strip, lats), 0)
    for f in range(fields):
        centre, east, west, to_north, to_south = coefficients(
            courant[0], courant[1], diffusion[0, f], mixing[f, f])
        coefs[f, 0] = centre
        coefs[f, 1] = jnp.where(lon == strip - 1, 0.0, east)
        coefs[f, 2] = jnp.where(lon == 0, 0.0, west)
        coefs[f, 3] = to_north
        coefs[f, 4] = to_south

    def moved(values, f):
        v = values[f]
        return (coefs[f, 0] * v + coefs[f, 1] * pltpu.roll(v, strip - 1, 0) + coefs[f, 2] * pltpu.roll(v, 1, 0)
                + coefs[f, 3] * north(v) + coefs[f, 4] * south(v) + mixed(mixing_scalars, f, values))

    return moved


def observed_bulk(sizes, state, noise, courant, diffusion, mixing, cell, value, middle, out, weight,
                  coefs, maps, partial, mixing_scalars, sem):
    particles, fields, strip, lats, strips = sizes
    copy = pltpu.make_async_copy(mixing, mixing_scalars, sem)
    copy.start()
    maps[0], maps[1] = observation_maps(sizes, cell[...], value[...])
    moved = zero_halo(sizes, courant, diffusion, mixing, mixing_scalars, coefs)
    copy.wait()

    def one(p):
        values = [state[p, f] for f in range(fields)]
        results = []
        for f in range(fields):
            new = moved(values, f)
            add = noise[0, p, f].astype(F32)
            if f == 0:
                push = maps[0] * (maps[1] - new)
                new = new + push
                total = push * (push + 2.0 * add)
            results.append(new + add)
            middle[p, f] = new + add
        new = moved(results, 0)
        add = noise[1, p, 0].astype(F32)
        push = maps[0] * (maps[1] - new)
        new = new + push + add
        miss = maps[1] - new
        total = (0.5 / noise_var) * (total + push * (push + 2.0 * add)) + (2.0 * maps[0]) * (miss * miss)
        out[p] = new
        partial[pl.ds(p, 1), :] = wide(jnp.sum(total, axis=0, keepdims=True))

    def body(pair, carry):
        one(2 * pair)
        one(2 * pair + 1)
        return carry

    lax.fori_loop(0, particles // 2, body, 0)
    weight[...] = in_row(partial[...])


def other_bulk(sizes, middle, observed, noise, courant, diffusion, mixing, out, coefs, mixing_scalars, sem):
    particles, fields, strip, lats, strips = sizes
    copy = pltpu.make_async_copy(mixing, mixing_scalars, sem)
    copy.start()
    moved = zero_halo(sizes, courant, diffusion, mixing, mixing_scalars, coefs)
    copy.wait()

    def body(p, carry):
        values = [middle[p, f] for f in range(fields)]
        out[p, 0] = observed[p]
        for f in range(1, fields):
            out[p, f] = moved(values, f) + noise[1, p, f].astype(F32)
        return carry

    lax.fori_loop(0, particles, body, 0)


def correct(sizes, own_east, own_west, from_west, from_east, diffusion, mixing, bulk_weight, weight, changes):
    particles, fields, strip, lats, strips = sizes
    n = fields * particles
    diffusion, mixing = Spread(diffusion), Spread(mixing)

    def field_rows(ref, start, f):
        return ref[start + f * particles:start + (f + 1) * particles]

    packets = (own_east, from_east, own_west, from_west)
    last = 2 * n + 2 * particles
    zonal = stack_rows([ref[last + 2:last + 3] for ref in packets] + [ref[last + 5:last + 6] for ref in packets])
    merid = stack_rows([ref[last + 3:last + 4] for ref in packets] * 2)
    tile = [coefficients(zonal, merid, diffusion[0, f], mixing[f, f]) for f in range(fields)]
    total = jnp.zeros((particles, lats), F32)
    for k, owner in enumerate(packets):
        other_k = k ^ 1
        other = packets[other_k]
        outward_at = (1, 2, 2, 1)[k]
        outward_other = (1, 2, 2, 1)[other_k]
        gain = owner[last + 4:last + 5]
        gain_other = other[last + 4:last + 5]
        first = []
        for f in range(fields):
            step = tile[f][outward_at][k:k + 1] * field_rows(other, 0, f)
            first.append((1.0 - gain) * step if f == 0 else step)
        mine = k in (0, 2)
        for f in range(fields if mine else 1):
            centre, to_north, to_south = [tile[f][c][k:k + 1] for c in (0, 3, 4)]
            outward = tile[f][outward_at][k:k + 1]
            reach = tile[f][outward_other][other_k:other_k + 1]
            if f == 0:
                reach = (1.0 - gain_other) * reach
            outside = field_rows(other, n, f) + reach * field_rows(owner, 0, f)
            step = (centre * first[f] + outward * outside + to_north * north(first[f])
                    + to_south * south(first[f]) + mixed(mixing, f, first))
            if f == 0:
                seen = field_rows(other, 0, 0)
                slope, slope_step = owner[2 * n:2 * n + particles], owner[2 * n + particles:last]
                bend, bend_step = owner[last:last + 1], owner[last + 1:last + 2]
                total = total + seen * (slope + bend * seen) + step * (slope_step + bend_step * step)
            if mine:
                beside = tile[f][outward_at][4 + k:5 + k] * first[f]
                if f == 0:
                    step = (1.0 - gain) * step
                    beside = (1.0 - owner[last + 6:last + 7]) * beside
                edge, inner = (3, 2) if k == 0 else (0, 1)
                changes[edge, f * particles:(f + 1) * particles] = step
                changes[inner, f * particles:(f + 1) * particles] = beside
    weight[...] = in_row(wide(total)) + bulk_weight[...]


def apply_changes(sizes, current, changes, out):
    particles, fields, strip, lats, strips = sizes
    sub = lax.broadcasted_iota(jnp.int32, (8, lats), 0)
    for p in range(particles):
        for f in range(fields):
            row = f * particles + p
            rows = [jnp.broadcast_to(changes[k, row:row + 1], sub.shape) for k in range(4)]
            out[p, f, :8] = current[p, f, :8] + jnp.where(sub == 0, rows[0], jnp.where(sub == 1, rows[1], 0.0))
            out[p, f, 8:strip - 8] = current[p, f, 8:strip - 8]
            out[p, f, strip - 8:] = current[p, f, strip - 8:] + jnp.where(
                sub == 7, rows[3], jnp.where(sub == 6, rows[2], 0.0))


def assemble(sizes, source, current, received, out, sems):
    particles = sizes[0]
    dom = lax.axis_index("dom")

    def copy(j, ref, at):
        return pltpu.make_async_copy(ref.at[at], out.at[j], sems.at[j])

    for j in range(particles):
        wanted = source[dom * particles + j]
        mine = wanted // particles == dom
        at = wanted % particles

        @pl.when(mine)
        def _():
            copy(j, current, at).start()

        @pl.when(jnp.logical_not(mine))
        def _():
            copy(j, received, at).start()

    for j in range(particles):
        copy(j, current, 0).wait()


def local(ensemble_state, proposal_noise, courant, diffusion, mixing, prior_weight, obs_cell, obs_value, source):
    particles, fields, strip, lats = ensemble_state.shape
    strips = lax.axis_size("lon")
    sizes = (particles, fields, strip, lats, strips)
    packet = jax.ShapeDtypeStruct((2 * particles * fields + 2 * particles + 8, lats), F32)
    cell, value = obs_cell[None], obs_value[None]

    def shape(*dims):
        return jax.ShapeDtypeStruct(dims, F32)

    send_east, send_west = pl.pallas_call(
        functools.partial(prepare, sizes),
        out_shape=(packet, packet),
        in_specs=[HBM] * 7,
        out_specs=(VMEM,) * 2,
        scratch_shapes=[
            pltpu.VMEM((particles, fields, 8, lats), F32),
            pltpu.VMEM((particles, fields, 8, lats), F32),
            pltpu.VMEM((particles, fields, strip, lats), BF16),
            pltpu.VMEM((particles, strip, lats), BF16),
            pltpu.VMEM(courant.shape, F32),
            pltpu.SMEM(diffusion.shape, F32),
            pltpu.SMEM(mixing.shape, F32),
            pltpu.VMEM(cell.shape, jnp.int32),
            pltpu.VMEM(value.shape, F32),
            pltpu.SemaphoreType.DMA((9,)),
        ],
        compiler_params=pltpu.CompilerParams(vmem_limit_bytes=60 * 1024 * 1024),
        cost_estimate=pl.CostEstimate(flops=1000000, bytes_accessed=2000000, transcendentals=0),
    )(ensemble_state, proposal_noise, courant, diffusion, mixing, cell, value)

    eastward = [(i, (i + 1) % strips) for i in range(strips)]
    westward = [(i, (i - 1) % strips) for i in range(strips)]
    from_west = lax.ppermute(send_east, "lon", eastward)
    from_east = lax.ppermute(send_west, "lon", westward)

    whole = (particles, fields, strip, lats)
    spread = diffusion[None]
    scalars = [pltpu.SMEM(mixing.shape, F32), pltpu.SemaphoreType.DMA]
    middle, observed, bulk_weight = pl.pallas_call(
        functools.partial(observed_bulk, sizes),
        out_shape=(shape(*whole), shape(particles, strip, lats), shape(1, 128)),
        in_specs=[VMEM] * 7,
        out_specs=(VMEM,) * 3,
        scratch_shapes=[pltpu.VMEM((fields, 5, strip, lats), F32), pltpu.VMEM((2, strip, lats), F32),
                        pltpu.VMEM((particles, 128), F32)] + scalars,
        compiler_params=LIMIT,
        cost_estimate=pl.CostEstimate(flops=20000000, bytes_accessed=4000000, transcendentals=0),
    )(ensemble_state, proposal_noise, courant, spread, mixing, cell, value)
    beside = lax.ppermute(bulk_weight, "lon", [(i, i ^ 1) for i in range(strips)])

    weight, changes = pl.pallas_call(
        functools.partial(correct, sizes),
        out_shape=(shape(1, 128), shape(4, particles * fields, lats)),
        in_specs=[VMEM] * 7,
        out_specs=(VMEM,) * 2,
        compiler_params=LIMIT,
        cost_estimate=FREE,
    )(send_east, send_west, from_west, from_east, spread, mixing, bulk_weight)

    current = pl.pallas_call(
        functools.partial(other_bulk, sizes),
        out_shape=shape(*whole),
        in_specs=[VMEM] * 6,
        out_specs=VMEM,
        scratch_shapes=[pltpu.VMEM((fields, 5, strip, lats), F32)] + scalars,
        compiler_params=LIMIT,
        cost_estimate=FREE,
    )(middle, observed, proposal_noise, courant, spread, mixing)

    current = pl.pallas_call(
        functools.partial(apply_changes, sizes),
        out_shape=shape(*whole),
        in_specs=[VMEM] * 2,
        out_specs=VMEM,
        compiler_params=LIMIT,
        cost_estimate=FREE,
    )(current, changes)

    current, beside = lax.optimization_barrier((current, beside))
    weight = weight + beside
    received = lax.ppermute(current, "dom", [(0, 1), (1, 0)])
    bit = 2
    while bit < strips:
        if 2 * bit >= strips:
            weight, received = lax.optimization_barrier((weight, received))
        weight = weight + lax.ppermute(weight, "lon", [(i, i ^ bit) for i in range(strips)])
        bit *= 2

    new_state = pl.pallas_call(
        functools.partial(assemble, sizes),
        out_shape=shape(*whole),
        in_specs=[SMEM, VMEM, VMEM],
        out_specs=HBM,
        scratch_shapes=[pltpu.SemaphoreType.DMA((particles,))],
        compiler_params=LIMIT,
        cost_estimate=pl.CostEstimate(flops=0, bytes_accessed=2000000, transcendentals=0),
    )(source, current, received)

    log_weight = prior_weight - weight[0, :particles] / (256.0 * obs_cell.shape[0])
    return new_state, log_weight


def solution(mesh):
    placed = (
        P(("groups", "dom"), None, "lon", None),
        P(None, ("groups", "dom"), None, "lon", None),
        P(None, ("groups", "lon"), None),
        P(),
        P(),
        P(("groups", "dom")),
        P(("groups", "lon")),
        P(("groups", "lon")),
        P("groups"),
    )
    return jax.shard_map(
        local,
        mesh=mesh,
        in_specs=placed,
        out_specs=(P(("groups", "dom"), None, "lon", None), P(("groups", "dom"))),
        check_vma=False,
    )
```

```python
import functools

import jax
import jax.numpy as jnp
from jax import lax
from jax.experimental import pallas as pl
from jax.experimental.pallas import tpu as pltpu
from jax.sharding import PartitionSpec as P

noise_var = 0.04
VMEM = pl.BlockSpec(memory_space=pltpu.VMEM)
SMEM = pl.BlockSpec(memory_space=pltpu.SMEM)
HBM = pl.BlockSpec(memory_space=pltpu.HBM)
LIMIT = pltpu.CompilerParams(vmem_limit_bytes=16 * 1024 * 1024)
FREE = pl.CostEstimate(flops=0, bytes_accessed=0, transcendentals=0)
BF16 = jnp.bfloat16
F32 = jnp.float32


def north(v):
    return pltpu.roll(v, v.shape[1] - 1, 1)


def south(v):
    return pltpu.roll(v, 1, 1)


def coefficients(zonal, merid, rate, self_mix):
    lat = lax.broadcasted_iota(jnp.int32, zonal.shape, 1)
    zonal_half, zonal_rate = 0.5 * zonal, 0.5 * zonal * zonal + rate
    merid_half, merid_rate = 0.5 * merid, 0.5 * merid * merid + rate
    east, west = zonal_rate - zonal_half, zonal_rate + zonal_half
    to_north, to_south = merid_rate - merid_half, merid_rate + merid_half
    centre = 1.0 + self_mix - 2.0 * zonal_rate - 2.0 * merid_rate
    last, first = lat == zonal.shape[1] - 1, lat == 0
    centre = centre + jnp.where(last, to_north, 0.0) + jnp.where(first, to_south, 0.0)
    to_north = jnp.where(last, 0.0, to_north)
    to_south = jnp.where(first, 0.0, to_south)
    return centre, east, west, to_north, to_south


def mixed(mixing, field, values):
    total = None
    for other, value in enumerate(values):
        if other != field:
            term = mixing[field, other] * value
            total = term if total is None else total + term
    return total


def pick_rows(kinds, particles, fields, strip):
    shape = (particles, particles * fields * strip)
    place = lax.broadcasted_iota(jnp.int32, shape, 1) - lax.broadcasted_iota(jnp.int32, shape, 0) * (fields * strip)
    blocks = [jnp.where(place == f * strip + x, 1.0, 0.0) for f, x in kinds]
    return jnp.concatenate(blocks, 0).astype(BF16)


def stack_rows(rows):
    sub = lax.broadcasted_iota(jnp.int32, (len(rows), rows[0].shape[1]), 0)
    out = None
    for p, row in enumerate(rows):
        row = jnp.broadcast_to(row, sub.shape)
        out = row if out is None else jnp.where(sub == p, row, out)
    return out


def in_row(column):
    total = jnp.broadcast_to(jnp.sum(column, axis=1, keepdims=True), column.shape)
    diagonal = lax.broadcasted_iota(jnp.int32, total.shape, 0) == lax.broadcasted_iota(jnp.int32, total.shape, 1)
    return jnp.sum(jnp.where(diagonal, total, 0.0), axis=0, keepdims=True)


def wide(v):
    return v[:, :128] + v[:, 128:]


def observation_maps(sizes, cell, value):
    particles, fields, strip, lats, strips = sizes
    x0 = lax.axis_index("lon") * strip
    shift = lats.bit_length() - 1
    local_cell = cell - x0 * lats
    obs_lon = lax.shift_right_arithmetic(local_cell, shift)
    obs_lat = local_cell & (lats - 1)
    count = cell.shape[1]
    here = lax.broadcasted_iota(jnp.int32, (strip, count), 0) == obs_lon
    high = value.astype(BF16)
    rest = value - high.astype(F32)
    mid = rest.astype(BF16)
    low = (rest - mid.astype(F32)).astype(BF16)
    zero = jnp.zeros((strip, count), F32)
    parts = [jnp.where(here, 1.0, zero)]
    parts += [jnp.where(here, p.astype(F32), zero) for p in (high, mid, low)]
    left = jnp.concatenate(parts, 0).astype(BF16)
    right = (lax.broadcasted_iota(jnp.int32, (lats, count), 0) == obs_lat).astype(F32).astype(BF16)
    dense = lax.dot_general(left, right, (((1,), (1,)), ((), ())), preferred_element_type=F32)
    lon = (lax.broadcasted_iota(jnp.int32, (strip, lats), 0) + x0).astype(F32)
    precision = 1.0 + 2.0 * lon / (strip * strips)
    target = dense[strip:2 * strip] + (dense[2 * strip:3 * strip] + dense[3 * strip:])
    return dense[:strip] * (0.25 * precision), target


def prepare(sizes, state_hbm, noise_hbm, courant_hbm, diffusion_hbm, mixing_hbm, cell_hbm, value_hbm,
            send_east, send_west,
            low, high, noise0, noise1, courant, diffusion, mixing, cell, value, sems):
    particles, fields, strip, lats, strips = sizes
    n = fields * particles
    copies = [pltpu.make_async_copy(source, target, sems.at[k]) for k, (source, target) in enumerate((
        (cell_hbm, cell), (value_hbm, value), (courant_hbm, courant), (diffusion_hbm, diffusion),
        (mixing_hbm, mixing), (state_hbm.at[:, :, :8], low), (state_hbm.at[:, :, strip - 8:], high),
        (noise_hbm.at[0], noise0), (noise_hbm.at[1, :, 0], noise1)))]
    for copy in copies:
        copy.start()
    copies[0].wait()
    copies[1].wait()
    gain, target = observation_maps(sizes, cell[...], value[...])
    kinds = []
    for x, step in ((strip - 1, -1), (0, 1)):
        kinds += [(f, x) for f in range(fields)] + [(f, x + step) for f in range(fields)] + [(0, x + 2 * step)]
    pick0 = pick_rows(kinds, particles, fields, strip)
    pick1 = pick_rows([(0, x) for x in (strip - 1, strip - 2, 0, 1)], particles, 1, strip)
    for copy in copies[2:5]:
        copy.wait()

    sides = []
    for first, inward, outward in ((strip - 8, 2, 1), (0, 1, 2)):
        tile = [coefficients(courant[0, first:first + 8], courant[1, first:first + 8], diffusion[f], mixing[f, f])
                for f in range(fields)]
        sides.append([[c[0], c[inward], c[outward], c[3], c[4]] for c in tile])
    def coefs_at(side, f, k):
        at = places[side][0] + k * places[side][2] - places[side][1]
        return [c[at:at + 1] for c in sides[side][f]]

    def maps_at(side, k):
        at = places[side][0] + k * places[side][2]
        return gain[at:at + 1], target[at:at + 1]

    def moved(side, f, k, here, inner, outer):
        centre, inward, outward, to_north, to_south = coefs_at(side, f, k)
        v = here[f]
        total = centre * v + inward * inner + to_north * north(v) + to_south * south(v) + mixed(mixing, f, here)
        return total if outer is None else total + outward * outer

    def nudged(side, value, k):
        g, v = maps_at(side, k)
        push = g * (v - value)
        return value + push, push

    def first_step(side, tile, out):
        def state_at(f, k):
            at = places[side][0] + k * places[side][2] - places[side][1]
            return stack_rows([tile[p, f, at:at + 1] for p in range(particles)])

        state = [[state_at(f, k) for f in range(fields)] for k in range(3)]
        third = state_at(0, 3)
        for f in range(fields):
            out[f * particles:(f + 1) * particles] = state[0][f]
        result, pushes = [[], []], []
        for k in range(2):
            for f in range(fields):
                new = moved(side, f, k, state[k], state[k + 1][f], state[k - 1][f] if k else None)
                if f == 0:
                    new, push = nudged(side, new, k)
                    pushes.append(push)
                result[k].append(new)
        inside, _ = nudged(side, moved(side, 0, 2, state[2], third, state[1][0]), 2)
        return result, pushes, inside

    places = ((strip - 1, strip - 8, -1), (0, 0, 1))
    copies[5].wait()
    copies[6].wait()
    started = [first_step(0, high, send_east), first_step(1, low, send_west)]
    copies[7].wait()
    copies[8].wait()
    rows0 = jnp.dot(pick0, noise0[...].reshape(n * strip, lats), preferred_element_type=F32)
    rows1 = jnp.dot(pick1, noise1[...].reshape(particles * strip, lats), preferred_element_type=F32)

    def edge(side, out):
        x, _, step = places[side]
        base0, base1 = side * (2 * fields + 1) * particles, side * 2 * particles
        result, pushes, inside = started[side]

        def noisy0(k, f):
            at = base0 + (k * fields + f) * particles
            return rows0[at:at + particles]

        def noisy1(k):
            at = base1 + k * particles
            return rows1[at:at + particles]

        result = [[result[k][f] + noisy0(k, f) for f in range(fields)] for k in range(2)]
        inside = inside + noisy0(2, 0)
        g0, _ = maps_at(side, 0)
        g1, _ = maps_at(side, 1)
        slope = [-(1.0 / noise_var) * g0 * (pushes[0] + noisy0(0, 0))]
        bend = [(0.5 / noise_var) * g0 * g0]
        for k, g in enumerate((g0, g1)):
            new = moved(side, 0, k, result[k], result[1][0] if k == 0 else inside, result[0][0] if k else None)
            new, push = nudged(side, new, k)
            miss = maps_at(side, k)[1] - (new + noisy1(k))
            weight = 4.0 * g
            slope.append(-(1.0 / noise_var) * g * (push + noisy1(k)) - weight * (1.0 - g) * miss)
            bend.append((0.5 / noise_var) * g * g + 0.5 * weight * (1.0 - g) * (1.0 - g))
        outward = coefs_at(side, 0, 0)[2]
        onward = coefs_at(side, 0, 1)[2] * (1.0 - g0) * outward
        for f in range(fields):
            out[n + f * particles:n + (f + 1) * particles] = result[0][f]
        out[2 * n:2 * n + particles] = outward * slope[0] + onward * slope[2]
        out[2 * n + particles:2 * n + 2 * particles] = slope[1]
        inner = x + step
        last = (outward * outward * bend[0] + onward * onward * bend[2], bend[1],
                courant[0, x:x + 1], courant[1, x:x + 1], g0, courant[0, inner:inner + 1], g1,
                jnp.zeros((1, lats), F32))
        out[2 * n + 2 * particles:] = stack_rows(last)

    edge(0, send_east)
    edge(1, send_west)


class Spread:
    def __init__(self, ref):
        self.ref = ref

    def __getitem__(self, at):
        return self.ref[at[0]:at[0] + 1, at[1]:at[1] + 1]


def zero_halo(sizes, courant, diffusion, mixing, mixing_scalars, coefs):
    particles, fields, strip, lats, strips = sizes
    diffusion, mixing = Spread(diffusion), Spread(mixing)
    lon = lax.broadcasted_iota(jnp.int32, (strip, lats), 0)
    for f in range(fields):
        centre, east, west, to_north, to_south = coefficients(
            courant[0], courant[1], diffusion[0, f], mixing[f, f])
        coefs[f, 0] = centre
        coefs[f, 1] = jnp.where(lon == strip - 1, 0.0, east)
        coefs[f, 2] = jnp.where(lon == 0, 0.0, west)
        coefs[f, 3] = to_north
        coefs[f, 4] = to_south

    def moved(values, f):
        v = values[f]
        return (coefs[f, 0] * v + coefs[f, 1] * pltpu.roll(v, strip - 1, 0) + coefs[f, 2] * pltpu.roll(v, 1, 0)
                + coefs[f, 3] * north(v) + coefs[f, 4] * south(v) + mixed(mixing_scalars, f, values))

    return moved


def observed_bulk(sizes, state, noise, courant, diffusion, mixing, cell, value, middle, out, weight,
                  coefs, maps, partial, mixing_scalars, sem):
    particles, fields, strip, lats, strips = sizes
    copy = pltpu.make_async_copy(mixing, mixing_scalars, sem)
    copy.start()
    maps[0], maps[1] = observation_maps(sizes, cell[...], value[...])
    moved = zero_halo(sizes, courant, diffusion, mixing, mixing_scalars, coefs)
    copy.wait()

    def one(p):
        values = [state[p, f] for f in range(fields)]
        results = []
        for f in range(fields):
            new = moved(values, f)
            add = noise[0, p, f].astype(F32)
            if f == 0:
                push = maps[0] * (maps[1] - new)
                new = new + push
                total = push * (push + 2.0 * add)
            results.append(new + add)
            middle[p, f] = new + add
        new = moved(results, 0)
        add = noise[1, p, 0].astype(F32)
        push = maps[0] * (maps[1] - new)
        new = new + push + add
        miss = maps[1] - new
        total = (0.5 / noise_var) * (total + push * (push + 2.0 * add)) + (2.0 * maps[0]) * (miss * miss)
        out[p] = new
        partial[pl.ds(p, 1), :] = wide(jnp.sum(total, axis=0, keepdims=True))

    def body(pair, carry):
        one(2 * pair)
        one(2 * pair + 1)
        return carry

    lax.fori_loop(0, particles // 2, body, 0)
    weight[...] = in_row(partial[...])


def other_bulk(sizes, middle, observed, noise, courant, diffusion, mixing, out, coefs, mixing_scalars, sem):
    particles, fields, strip, lats, strips = sizes
    copy = pltpu.make_async_copy(mixing, mixing_scalars, sem)
    copy.start()
    moved = zero_halo(sizes, courant, diffusion, mixing, mixing_scalars, coefs)
    copy.wait()

    def body(p, carry):
        values = [middle[p, f] for f in range(fields)]
        out[p, 0] = observed[p]
        for f in range(1, fields):
            out[p, f] = moved(values, f) + noise[1, p, f].astype(F32)
        return carry

    lax.fori_loop(0, particles, body, 0)


def correct(sizes, own_east, own_west, from_west, from_east, diffusion, mixing, bulk_weight, weight, changes):
    particles, fields, strip, lats, strips = sizes
    n = fields * particles
    diffusion, mixing = Spread(diffusion), Spread(mixing)

    def field_rows(ref, start, f):
        return ref[start + f * particles:start + (f + 1) * particles]

    packets = (own_east, from_east, own_west, from_west)
    last = 2 * n + 2 * particles
    zonal = stack_rows([ref[last + 2:last + 3] for ref in packets] + [ref[last + 5:last + 6] for ref in packets])
    merid = stack_rows([ref[last + 3:last + 4] for ref in packets] * 2)
    tile = [coefficients(zonal, merid, diffusion[0, f], mixing[f, f]) for f in range(fields)]
    total = jnp.zeros((particles, lats), F32)
    for k, owner in enumerate(packets):
        other_k = k ^ 1
        other = packets[other_k]
        outward_at = (1, 2, 2, 1)[k]
        outward_other = (1, 2, 2, 1)[other_k]
        gain = owner[last + 4:last + 5]
        gain_other = other[last + 4:last + 5]
        first = []
        for f in range(fields):
            step = tile[f][outward_at][k:k + 1] * field_rows(other, 0, f)
            first.append((1.0 - gain) * step if f == 0 else step)
        mine = k in (0, 2)
        for f in range(fields if mine else 1):
            centre, to_north, to_south = [tile[f][c][k:k + 1] for c in (0, 3, 4)]
            outward = tile[f][outward_at][k:k + 1]
            reach = tile[f][outward_other][other_k:other_k + 1]
            if f == 0:
                reach = (1.0 - gain_other) * reach
            outside = field_rows(other, n, f) + reach * field_rows(owner, 0, f)
            step = (centre * first[f] + outward * outside + to_north * north(first[f])
                    + to_south * south(first[f]) + mixed(mixing, f, first))
            if f == 0:
                seen = field_rows(other, 0, 0)
                slope, slope_step = owner[2 * n:2 * n + particles], owner[2 * n + particles:last]
                bend, bend_step = owner[last:last + 1], owner[last + 1:last + 2]
                total = total + seen * (slope + bend * seen) + step * (slope_step + bend_step * step)
            if mine:
                beside = tile[f][outward_at][4 + k:5 + k] * first[f]
                if f == 0:
                    step = (1.0 - gain) * step
                    beside = (1.0 - owner[last + 6:last + 7]) * beside
                edge, inner = (3, 2) if k == 0 else (0, 1)
                changes[edge, f * particles:(f + 1) * particles] = step
                changes[inner, f * particles:(f + 1) * particles] = beside
    weight[...] = in_row(wide(total)) + bulk_weight[...]


def apply_changes(sizes, current, changes, out):
    particles, fields, strip, lats, strips = sizes
    sub = lax.broadcasted_iota(jnp.int32, (8, lats), 0)
    for p in range(particles):
        for f in range(fields):
            row = f * particles + p
            rows = [jnp.broadcast_to(changes[k, row:row + 1], sub.shape) for k in range(4)]
            out[p, f, :8] = current[p, f, :8] + jnp.where(sub == 0, rows[0], jnp.where(sub == 1, rows[1], 0.0))
            out[p, f, 8:strip - 8] = current[p, f, 8:strip - 8]
            out[p, f, strip - 8:] = current[p, f, strip - 8:] + jnp.where(
                sub == 7, rows[3], jnp.where(sub == 6, rows[2], 0.0))


def assemble(sizes, source, current, received, out, sems):
    particles = sizes[0]
    dom = lax.axis_index("dom")

    def copy(j, ref, at):
        return pltpu.make_async_copy(ref.at[at], out.at[j], sems.at[j])

    for j in range(particles):
        wanted = source[dom * particles + j]
        mine = wanted // particles == dom
        at = wanted % particles

        @pl.when(mine)
        def _():
            copy(j, current, at).start()

        @pl.when(jnp.logical_not(mine))
        def _():
            copy(j, received, at).start()

    for j in range(particles):
        copy(j, current, 0).wait()


def local(ensemble_state, proposal_noise, courant, diffusion, mixing, prior_weight, obs_cell, obs_value, source):
    particles, fields, strip, lats = ensemble_state.shape
    strips = lax.axis_size("lon")
    sizes = (particles, fields, strip, lats, strips)
    packet = jax.ShapeDtypeStruct((2 * particles * fields + 2 * particles + 8, lats), F32)
    cell, value = obs_cell[None], obs_value[None]

    def shape(*dims):
        return jax.ShapeDtypeStruct(dims, F32)

    send_east, send_west = pl.pallas_call(
        functools.partial(prepare, sizes),
        out_shape=(packet, packet),
        in_specs=[HBM] * 7,
        out_specs=(VMEM,) * 2,
        scratch_shapes=[
            pltpu.VMEM((particles, fields, 8, lats), F32),
            pltpu.VMEM((particles, fields, 8, lats), F32),
            pltpu.VMEM((particles, fields, strip, lats), BF16),
            pltpu.VMEM((particles, strip, lats), BF16),
            pltpu.VMEM(courant.shape, F32),
            pltpu.SMEM(diffusion.shape, F32),
            pltpu.SMEM(mixing.shape, F32),
            pltpu.VMEM(cell.shape, jnp.int32),
            pltpu.VMEM(value.shape, F32),
            pltpu.SemaphoreType.DMA((9,)),
        ],
        compiler_params=pltpu.CompilerParams(vmem_limit_bytes=60 * 1024 * 1024),
        cost_estimate=pl.CostEstimate(flops=1000000, bytes_accessed=2000000, transcendentals=0),
    )(ensemble_state, proposal_noise, courant, diffusion, mixing, cell, value)

    eastward = [(i, (i + 1) % strips) for i in range(strips)]
    westward = [(i, (i - 1) % strips) for i in range(strips)]
    from_west = lax.ppermute(send_east, "lon", eastward)
    from_east = lax.ppermute(send_west, "lon", westward)

    whole = (particles, fields, strip, lats)
    spread = diffusion[None]
    scalars = [pltpu.SMEM(mixing.shape, F32), pltpu.SemaphoreType.DMA]
    middle, observed, bulk_weight = pl.pallas_call(
        functools.partial(observed_bulk, sizes),
        out_shape=(shape(*whole), shape(particles, strip, lats), shape(1, 128)),
        in_specs=[VMEM] * 7,
        out_specs=(VMEM,) * 3,
        scratch_shapes=[pltpu.VMEM((fields, 5, strip, lats), F32), pltpu.VMEM((2, strip, lats), F32),
                        pltpu.VMEM((particles, 128), F32)] + scalars,
        compiler_params=LIMIT,
        cost_estimate=pl.CostEstimate(flops=20000000, bytes_accessed=4000000, transcendentals=0),
    )(ensemble_state, proposal_noise, courant, spread, mixing, cell, value)
    beside = lax.ppermute(bulk_weight, "lon", [(i, i ^ 1) for i in range(strips)])

    weight, changes = pl.pallas_call(
        functools.partial(correct, sizes),
        out_shape=(shape(1, 128), shape(4, particles * fields, lats)),
        in_specs=[VMEM] * 7,
        out_specs=(VMEM,) * 2,
        compiler_params=LIMIT,
        cost_estimate=FREE,
    )(send_east, send_west, from_west, from_east, spread, mixing, bulk_weight)

    current = pl.pallas_call(
        functools.partial(other_bulk, sizes),
        out_shape=shape(*whole),
        in_specs=[VMEM] * 6,
        out_specs=VMEM,
        scratch_shapes=[pltpu.VMEM((fields, 5, strip, lats), F32)] + scalars,
        compiler_params=LIMIT,
        cost_estimate=FREE,
    )(middle, observed, proposal_noise, courant, spread, mixing)

    current = pl.pallas_call(
        functools.partial(apply_changes, sizes),
        out_shape=shape(*whole),
        in_specs=[VMEM] * 2,
        out_specs=VMEM,
        compiler_params=LIMIT,
        cost_estimate=FREE,
    )(current, changes)

    current, beside = lax.optimization_barrier((current, beside))
    weight = weight + beside
    received = lax.ppermute(current, "dom", [(0, 1), (1, 0)])
    bit = 2
    while bit < strips:
        if 2 * bit >= strips:
            weight, received = lax.optimization_barrier((weight, received))
        weight = weight + lax.ppermute(weight, "lon", [(i, i ^ bit) for i in range(strips)])
        bit *= 2

    new_state = pl.pallas_call(
        functools.partial(assemble, sizes),
        out_shape=shape(*whole),
        in_specs=[SMEM, VMEM, VMEM],
        out_specs=HBM,
        scratch_shapes=[pltpu.SemaphoreType.DMA((particles,))],
        compiler_params=LIMIT,
        cost_estimate=pl.CostEstimate(flops=0, bytes_accessed=2000000, transcendentals=0),
    )(source, current, received)

    log_weight = prior_weight - weight[0, :particles] / (256.0 * obs_cell.shape[0])
    return new_state, log_weight


def solution(mesh):
    placed = (
        P(("groups", "dom"), None, "lon", None),
        P(None, ("groups", "dom"), None, "lon", None),
        P(None, ("groups", "lon"), None),
        P(),
        P(),
        P(("groups", "dom")),
        P(("groups", "lon")),
        P(("groups", "lon")),
        P("groups"),
    )
    return jax.shard_map(
        local,
        mesh=mesh,
        in_specs=placed,
        out_specs=(P(("groups", "dom"), None, "lon", None), P(("groups", "dom"))),
        check_vma=False,
    )
```

```python
import functools

import jax
import jax.numpy as jnp
from jax import lax
from jax.experimental import pallas as pl
from jax.experimental.pallas import tpu as pltpu
from jax.sharding import PartitionSpec as P

noise_var = 0.04
VMEM = pl.BlockSpec(memory_space=pltpu.VMEM)
SMEM = pl.BlockSpec(memory_space=pltpu.SMEM)
HBM = pl.BlockSpec(memory_space=pltpu.HBM)
LIMIT = pltpu.CompilerParams(vmem_limit_bytes=16 * 1024 * 1024)
FREE = pl.CostEstimate(flops=0, bytes_accessed=0, transcendentals=0)
BF16 = jnp.bfloat16
F32 = jnp.float32


def north(v):
    return pltpu.roll(v, v.shape[1] - 1, 1)


def south(v):
    return pltpu.roll(v, 1, 1)


def coefficients(zonal, merid, rate, self_mix):
    lat = lax.broadcasted_iota(jnp.int32, zonal.shape, 1)
    zonal_half, zonal_rate = 0.5 * zonal, 0.5 * zonal * zonal + rate
    merid_half, merid_rate = 0.5 * merid, 0.5 * merid * merid + rate
    east, west = zonal_rate - zonal_half, zonal_rate + zonal_half
    to_north, to_south = merid_rate - merid_half, merid_rate + merid_half
    centre = 1.0 + self_mix - 2.0 * zonal_rate - 2.0 * merid_rate
    last, first = lat == zonal.shape[1] - 1, lat == 0
    centre = centre + jnp.where(last, to_north, 0.0) + jnp.where(first, to_south, 0.0)
    to_north = jnp.where(last, 0.0, to_north)
    to_south = jnp.where(first, 0.0, to_south)
    return centre, east, west, to_north, to_south


def mixed(mixing, field, values):
    total = None
    for other, value in enumerate(values):
        if other != field:
            term = mixing[field, other] * value
            total = term if total is None else total + term
    return total


def pick_rows(kinds, particles, fields, strip):
    shape = (particles, particles * fields * strip)
    place = lax.broadcasted_iota(jnp.int32, shape, 1) - lax.broadcasted_iota(jnp.int32, shape, 0) * (fields * strip)
    blocks = [jnp.where(place == f * strip + x, 1.0, 0.0) for f, x in kinds]
    return jnp.concatenate(blocks, 0).astype(BF16)


def stack_rows(rows):
    sub = lax.broadcasted_iota(jnp.int32, (len(rows), rows[0].shape[1]), 0)
    out = None
    for p, row in enumerate(rows):
        row = jnp.broadcast_to(row, sub.shape)
        out = row if out is None else jnp.where(sub == p, row, out)
    return out


def in_row(column):
    total = jnp.broadcast_to(jnp.sum(column, axis=1, keepdims=True), column.shape)
    diagonal = lax.broadcasted_iota(jnp.int32, total.shape, 0) == lax.broadcasted_iota(jnp.int32, total.shape, 1)
    return jnp.sum(jnp.where(diagonal, total, 0.0), axis=0, keepdims=True)


def wide(v):
    return v[:, :128] + v[:, 128:]


def observation_maps(sizes, cell, value):
    particles, fields, strip, lats, strips = sizes
    x0 = lax.axis_index("lon") * strip
    shift = lats.bit_length() - 1
    local_cell = cell - x0 * lats
    obs_lon = lax.shift_right_arithmetic(local_cell, shift)
    obs_lat = local_cell & (lats - 1)
    count = cell.shape[1]
    here = lax.broadcasted_iota(jnp.int32, (strip, count), 0) == obs_lon
    high = value.astype(BF16)
    rest = value - high.astype(F32)
    mid = rest.astype(BF16)
    low = (rest - mid.astype(F32)).astype(BF16)
    zero = jnp.zeros((strip, count), F32)
    parts = [jnp.where(here, 1.0, zero)]
    parts += [jnp.where(here, p.astype(F32), zero) for p in (high, mid, low)]
    left = jnp.concatenate(parts, 0).astype(BF16)
    right = (lax.broadcasted_iota(jnp.int32, (lats, count), 0) == obs_lat).astype(F32).astype(BF16)
    dense = lax.dot_general(left, right, (((1,), (1,)), ((), ())), preferred_element_type=F32)
    lon = (lax.broadcasted_iota(jnp.int32, (strip, lats), 0) + x0).astype(F32)
    precision = 1.0 + 2.0 * lon / (strip * strips)
    target = dense[strip:2 * strip] + (dense[2 * strip:3 * strip] + dense[3 * strip:])
    return dense[:strip] * (0.25 * precision), target


class Spread:
    def __init__(self, ref):
        self.ref = ref

    def __getitem__(self, at):
        return self.ref[at[0]:at[0] + 1, at[1]:at[1] + 1]


def prepare(sizes, state_hbm, noise_hbm, courant_hbm, diffusion_hbm, mixing_hbm, cell_hbm, value_hbm,
            send_east, send_west, state, noise, maps,
            courant, diffusion, mixing, cell, value, sems):
    particles, fields, strip, lats, strips = sizes
    n = fields * particles
    copies = [pltpu.make_async_copy(source, target, sems.at[k]) for k, (source, target) in enumerate((
        (cell_hbm, cell), (value_hbm, value), (courant_hbm, courant), (diffusion_hbm, diffusion),
        (mixing_hbm, mixing), (state_hbm.at[:, :, :8], state.at[:, :, :8]),
        (state_hbm.at[:, :, strip - 8:], state.at[:, :, strip - 8:]), (noise_hbm.at[0], noise.at[0]),
        (noise_hbm.at[1, :, 0], noise.at[1, :, 0]), (state_hbm.at[:, :, 8:strip - 8], state.at[:, :, 8:strip - 8]),
        (noise_hbm.at[1, :, 1:], noise.at[1, :, 1:])))]
    for copy in copies:
        copy.start()
    copies[0].wait()
    copies[1].wait()
    gain, target = observation_maps(sizes, cell[...], value[...])
    maps[0], maps[1] = gain, target
    diffusion, mixing = Spread(diffusion), Spread(mixing)
    kinds = []
    for x, step in ((strip - 1, -1), (0, 1)):
        kinds += [(f, x) for f in range(fields)] + [(f, x + step) for f in range(fields)] + [(0, x + 2 * step)]
    pick0 = pick_rows(kinds, particles, fields, strip)
    pick1 = pick_rows([(0, x) for x in (strip - 1, strip - 2, 0, 1)], particles, 1, strip)
    for copy in copies[2:5]:
        copy.wait()

    sides = []
    for first, inward, outward in ((strip - 8, 2, 1), (0, 1, 2)):
        tile = [coefficients(courant[0, first:first + 8], courant[1, first:first + 8], diffusion[0, f], mixing[f, f])
                for f in range(fields)]
        sides.append([[c[0], c[inward], c[outward], c[3], c[4]] for c in tile])
    def coefs_at(side, f, k):
        at = places[side][0] + k * places[side][2] - places[side][1]
        return [c[at:at + 1] for c in sides[side][f]]

    def maps_at(side, k):
        at = places[side][0] + k * places[side][2]
        return gain[at:at + 1], target[at:at + 1]

    def moved(side, f, k, here, inner, outer):
        centre, inward, outward, to_north, to_south = coefs_at(side, f, k)
        v = here[f]
        total = centre * v + inward * inner + to_north * north(v) + to_south * south(v) + mixed(mixing, f, here)
        return total if outer is None else total + outward * outer

    def nudged(side, value, k):
        g, v = maps_at(side, k)
        push = g * (v - value)
        return value + push, push

    def first_step(side, out):
        def state_at(f, k):
            at = places[side][0] + k * places[side][2]
            return stack_rows([state[p, f, at:at + 1] for p in range(particles)])

        near = [[state_at(f, k) for f in range(fields)] for k in range(3)]
        third = state_at(0, 3)
        for f in range(fields):
            out[f * particles:(f + 1) * particles] = near[0][f]
        result, pushes = [[], []], []
        for k in range(2):
            for f in range(fields):
                new = moved(side, f, k, near[k], near[k + 1][f], near[k - 1][f] if k else None)
                if f == 0:
                    new, push = nudged(side, new, k)
                    pushes.append(push)
                result[k].append(new)
        inside, _ = nudged(side, moved(side, 0, 2, near[2], third, near[1][0]), 2)
        return result, pushes, inside

    places = ((strip - 1, strip - 8, -1), (0, 0, 1))
    copies[5].wait()
    copies[6].wait()
    started = [first_step(0, send_east), first_step(1, send_west)]
    copies[7].wait()
    copies[8].wait()
    rows0 = jnp.dot(pick0, noise[0].reshape(n * strip, lats), preferred_element_type=F32)
    rows1 = jnp.dot(pick1, noise[1, :, 0].reshape(particles * strip, lats), preferred_element_type=F32)

    def edge(side, out):
        x, _, step = places[side]
        base0, base1 = side * (2 * fields + 1) * particles, side * 2 * particles
        result, pushes, inside = started[side]

        def noisy0(k, f):
            at = base0 + (k * fields + f) * particles
            return rows0[at:at + particles]

        def noisy1(k):
            at = base1 + k * particles
            return rows1[at:at + particles]

        result = [[result[k][f] + noisy0(k, f) for f in range(fields)] for k in range(2)]
        inside = inside + noisy0(2, 0)
        g0, _ = maps_at(side, 0)
        g1, _ = maps_at(side, 1)
        slope = [-(1.0 / noise_var) * g0 * (pushes[0] + noisy0(0, 0))]
        bend = [(0.5 / noise_var) * g0 * g0]
        for k, g in enumerate((g0, g1)):
            new = moved(side, 0, k, result[k], result[1][0] if k == 0 else inside, result[0][0] if k else None)
            new, push = nudged(side, new, k)
            miss = maps_at(side, k)[1] - (new + noisy1(k))
            weight = 4.0 * g
            slope.append(-(1.0 / noise_var) * g * (push + noisy1(k)) - weight * (1.0 - g) * miss)
            bend.append((0.5 / noise_var) * g * g + 0.5 * weight * (1.0 - g) * (1.0 - g))
        outward = coefs_at(side, 0, 0)[2]
        onward = coefs_at(side, 0, 1)[2] * (1.0 - g0) * outward
        for f in range(fields):
            out[n + f * particles:n + (f + 1) * particles] = result[0][f]
        out[2 * n:2 * n + particles] = outward * slope[0] + onward * slope[2]
        out[2 * n + particles:2 * n + 2 * particles] = slope[1]
        inner = x + step
        last = (outward * outward * bend[0] + onward * onward * bend[2], bend[1],
                courant[0, x:x + 1], courant[1, x:x + 1], g0, courant[0, inner:inner + 1], g1,
                jnp.zeros((1, lats), F32))
        out[2 * n + 2 * particles:] = stack_rows(last)

    edge(0, send_east)
    edge(1, send_west)
    copies[9].wait()
    copies[10].wait()


def zero_halo(sizes, courant, diffusion, mixing, mixing_scalars, coefs):
    particles, fields, strip, lats, strips = sizes
    diffusion, mixing = Spread(diffusion), Spread(mixing)
    lon = lax.broadcasted_iota(jnp.int32, (strip, lats), 0)
    for f in range(fields):
        centre, east, west, to_north, to_south = coefficients(
            courant[0], courant[1], diffusion[0, f], mixing[f, f])
        coefs[f, 0] = centre
        coefs[f, 1] = jnp.where(lon == strip - 1, 0.0, east)
        coefs[f, 2] = jnp.where(lon == 0, 0.0, west)
        coefs[f, 3] = to_north
        coefs[f, 4] = to_south

    def moved(values, f):
        v = values[f]
        return (coefs[f, 0] * v + coefs[f, 1] * pltpu.roll(v, strip - 1, 0) + coefs[f, 2] * pltpu.roll(v, 1, 0)
                + coefs[f, 3] * north(v) + coefs[f, 4] * south(v) + mixed(mixing_scalars, f, values))

    return moved


def observed_bulk(sizes, state, noise, maps, courant, diffusion, mixing, middle, out, weight,
                  coefs, partial, mixing_scalars, sem):
    particles, fields, strip, lats, strips = sizes
    copy = pltpu.make_async_copy(mixing, mixing_scalars, sem)
    copy.start()
    moved = zero_halo(sizes, courant, diffusion, mixing, mixing_scalars, coefs)
    copy.wait()

    def one(p):
        values = [state[p, f] for f in range(fields)]
        results = []
        for f in range(fields):
            new = moved(values, f)
            add = noise[0, p, f].astype(F32)
            if f == 0:
                push = maps[0] * (maps[1] - new)
                new = new + push
                total = push * (push + 2.0 * add)
            results.append(new + add)
            middle[p, f] = new + add
        new = moved(results, 0)
        add = noise[1, p, 0].astype(F32)
        push = maps[0] * (maps[1] - new)
        new = new + push + add
        miss = maps[1] - new
        total = (0.5 / noise_var) * (total + push * (push + 2.0 * add)) + (2.0 * maps[0]) * (miss * miss)
        out[p] = new
        partial[pl.ds(p, 1), :] = wide(jnp.sum(total, axis=0, keepdims=True))

    def body(pair, carry):
        one(2 * pair)
        one(2 * pair + 1)
        return carry

    lax.fori_loop(0, particles // 2, body, 0)
    weight[...] = in_row(partial[...])


def other_bulk(sizes, middle, observed, noise, courant, diffusion, mixing, out, coefs, mixing_scalars, sem):
    particles, fields, strip, lats, strips = sizes
    copy = pltpu.make_async_copy(mixing, mixing_scalars, sem)
    copy.start()
    moved = zero_halo(sizes, courant, diffusion, mixing, mixing_scalars, coefs)
    copy.wait()

    def body(p, carry):
        values = [middle[p, f] for f in range(fields)]
        out[p, 0] = observed[p]
        for f in range(1, fields):
            out[p, f] = moved(values, f) + noise[1, p, f].astype(F32)
        return carry

    lax.fori_loop(0, particles, body, 0)


def correct(sizes, own_east, own_west, from_west, from_east, diffusion, mixing, bulk_weight, weight, changes):
    particles, fields, strip, lats, strips = sizes
    n = fields * particles
    diffusion, mixing = Spread(diffusion), Spread(mixing)

    def field_rows(ref, start, f):
        return ref[start + f * particles:start + (f + 1) * particles]

    packets = (own_east, from_east, own_west, from_west)
    last = 2 * n + 2 * particles
    zonal = stack_rows([ref[last + 2:last + 3] for ref in packets] + [ref[last + 5:last + 6] for ref in packets])
    merid = stack_rows([ref[last + 3:last + 4] for ref in packets] * 2)
    tile = [coefficients(zonal, merid, diffusion[0, f], mixing[f, f]) for f in range(fields)]
    total = jnp.zeros((particles, lats), F32)
    for k, owner in enumerate(packets):
        other_k = k ^ 1
        other = packets[other_k]
        outward_at = (1, 2, 2, 1)[k]
        outward_other = (1, 2, 2, 1)[other_k]
        gain = owner[last + 4:last + 5]
        gain_other = other[last + 4:last + 5]
        first = []
        for f in range(fields):
            step = tile[f][outward_at][k:k + 1] * field_rows(other, 0, f)
            first.append((1.0 - gain) * step if f == 0 else step)
        mine = k in (0, 2)
        for f in range(fields if mine else 1):
            centre, to_north, to_south = [tile[f][c][k:k + 1] for c in (0, 3, 4)]
            outward = tile[f][outward_at][k:k + 1]
            reach = tile[f][outward_other][other_k:other_k + 1]
            if f == 0:
                reach = (1.0 - gain_other) * reach
            outside = field_rows(other, n, f) + reach * field_rows(owner, 0, f)
            step = (centre * first[f] + outward * outside + to_north * north(first[f])
                    + to_south * south(first[f]) + mixed(mixing, f, first))
            if f == 0:
                seen = field_rows(other, 0, 0)
                slope, slope_step = owner[2 * n:2 * n + particles], owner[2 * n + particles:last]
                bend, bend_step = owner[last:last + 1], owner[last + 1:last + 2]
                total = total + seen * (slope + bend * seen) + step * (slope_step + bend_step * step)
            if mine:
                beside = tile[f][outward_at][4 + k:5 + k] * first[f]
                if f == 0:
                    step = (1.0 - gain) * step
                    beside = (1.0 - owner[last + 6:last + 7]) * beside
                edge, inner = (3, 2) if k == 0 else (0, 1)
                changes[edge, f * particles:(f + 1) * particles] = step
                changes[inner, f * particles:(f + 1) * particles] = beside
    weight[...] = in_row(wide(total)) + bulk_weight[...]


def apply_changes(sizes, current, changes, out):
    particles, fields, strip, lats, strips = sizes
    sub = lax.broadcasted_iota(jnp.int32, (8, lats), 0)
    for p in range(particles):
        for f in range(fields):
            row = f * particles + p
            rows = [jnp.broadcast_to(changes[k, row:row + 1], sub.shape) for k in range(4)]
            out[p, f, :8] = current[p, f, :8] + jnp.where(sub == 0, rows[0], jnp.where(sub == 1, rows[1], 0.0))
            out[p, f, 8:strip - 8] = current[p, f, 8:strip - 8]
            out[p, f, strip - 8:] = current[p, f, strip - 8:] + jnp.where(
                sub == 7, rows[3], jnp.where(sub == 6, rows[2], 0.0))


def assemble(sizes, source, current, received, out, sems):
    particles = sizes[0]
    dom = lax.axis_index("dom")

    def copy(j, ref, at):
        return pltpu.make_async_copy(ref.at[at], out.at[j], sems.at[j])

    for j in range(particles):
        wanted = source[dom * particles + j]
        mine = wanted // particles == dom
        at = wanted % particles

        @pl.when(mine)
        def _():
            copy(j, current, at).start()

        @pl.when(jnp.logical_not(mine))
        def _():
            copy(j, received, at).start()

    for j in range(particles):
        copy(j, current, 0).wait()


def local(ensemble_state, proposal_noise, courant, diffusion, mixing, prior_weight, obs_cell, obs_value, source):
    particles, fields, strip, lats = ensemble_state.shape
    strips = lax.axis_size("lon")
    sizes = (particles, fields, strip, lats, strips)
    packet = jax.ShapeDtypeStruct((2 * particles * fields + 2 * particles + 8, lats), F32)
    cell, value = obs_cell[None], obs_value[None]

    def shape(*dims):
        return jax.ShapeDtypeStruct(dims, F32)

    whole = (particles, fields, strip, lats)
    spread = diffusion[None]

    def in_hbm(array):
        return pltpu.with_memory_space_constraint(array, pltpu.HBM)

    arrays = (ensemble_state, proposal_noise, courant, spread, mixing, cell, value)
    send_east, send_west, state, noise, maps = pl.pallas_call(
        functools.partial(prepare, sizes),
        out_shape=(packet, packet, shape(*whole), jax.ShapeDtypeStruct((2,) + whole, BF16), shape(2, strip, lats)),
        in_specs=[HBM] * 7,
        out_specs=(VMEM,) * 5,
        scratch_shapes=[pltpu.VMEM(array.shape, array.dtype) for array in arrays[2:]]
        + [pltpu.SemaphoreType.DMA((11,))],
        compiler_params=LIMIT,
        cost_estimate=pl.CostEstimate(flops=1000000, bytes_accessed=2000000, transcendentals=0),
    )(*[in_hbm(array) for array in arrays])

    eastward = [(i, (i + 1) % strips) for i in range(strips)]
    westward = [(i, (i - 1) % strips) for i in range(strips)]
    from_west = lax.ppermute(send_east, "lon", eastward)
    from_east = lax.ppermute(send_west, "lon", westward)

    scalars = [pltpu.SMEM(mixing.shape, F32), pltpu.SemaphoreType.DMA]
    middle, observed, bulk_weight = pl.pallas_call(
        functools.partial(observed_bulk, sizes),
        out_shape=(shape(*whole), shape(particles, strip, lats), shape(1, 128)),
        in_specs=[VMEM] * 6,
        out_specs=(VMEM,) * 3,
        scratch_shapes=[pltpu.VMEM((fields, 5, strip, lats), F32), pltpu.VMEM((particles, 128), F32)] + scalars,
        compiler_params=LIMIT,
        cost_estimate=pl.CostEstimate(flops=20000000, bytes_accessed=4000000, transcendentals=0),
    )(state, noise, maps, courant, spread, mixing)
    beside = lax.ppermute(bulk_weight, "lon", [(i, i ^ 1) for i in range(strips)])

    weight, changes = pl.pallas_call(
        functools.partial(correct, sizes),
        out_shape=(shape(1, 128), shape(4, particles * fields, lats)),
        in_specs=[VMEM] * 7,
        out_specs=(VMEM,) * 2,
        compiler_params=LIMIT,
        cost_estimate=FREE,
    )(send_east, send_west, from_west, from_east, spread, mixing, bulk_weight)

    current = pl.pallas_call(
        functools.partial(other_bulk, sizes),
        out_shape=shape(*whole),
        in_specs=[VMEM] * 6,
        out_specs=VMEM,
        scratch_shapes=[pltpu.VMEM((fields, 5, strip, lats), F32)] + scalars,
        compiler_params=LIMIT,
        cost_estimate=FREE,
    )(middle, observed, noise, courant, spread, mixing)

    current = pl.pallas_call(
        functools.partial(apply_changes, sizes),
        out_shape=shape(*whole),
        in_specs=[VMEM] * 2,
        out_specs=VMEM,
        compiler_params=LIMIT,
        cost_estimate=FREE,
    )(current, changes)

    current, beside = lax.optimization_barrier((current, beside))
    weight = weight + beside
    received = lax.ppermute(current, "dom", [(0, 1), (1, 0)])
    bit = 2
    while bit < strips:
        if 2 * bit >= strips:
            weight, received = lax.optimization_barrier((weight, received))
        weight = weight + lax.ppermute(weight, "lon", [(i, i ^ bit) for i in range(strips)])
        bit *= 2

    new_state = pl.pallas_call(
        functools.partial(assemble, sizes),
        out_shape=shape(*whole),
        in_specs=[SMEM, VMEM, VMEM],
        out_specs=HBM,
        scratch_shapes=[pltpu.SemaphoreType.DMA((particles,))],
        compiler_params=LIMIT,
        cost_estimate=pl.CostEstimate(flops=0, bytes_accessed=2000000, transcendentals=0),
    )(source, current, received)

    log_weight = prior_weight - weight[0, :particles] / (256.0 * obs_cell.shape[0])
    return new_state, log_weight


def solution(mesh):
    placed = (
        P(("groups", "dom"), None, "lon", None),
        P(None, ("groups", "dom"), None, "lon", None),
        P(None, ("groups", "lon"), None),
        P(),
        P(),
        P(("groups", "dom")),
        P(("groups", "lon")),
        P(("groups", "lon")),
        P("groups"),
    )
    return jax.shard_map(
        local,
        mesh=mesh,
        in_specs=placed,
        out_specs=(P(("groups", "dom"), None, "lon", None), P(("groups", "dom"))),
        check_vma=False,
    )
```

```python
import functools

import jax
import jax.numpy as jnp
from jax import lax
from jax.experimental import pallas as pl
from jax.experimental.pallas import tpu as pltpu
from jax.sharding import PartitionSpec as P

noise_var = 0.04
VMEM = pl.BlockSpec(memory_space=pltpu.VMEM)
SMEM = pl.BlockSpec(memory_space=pltpu.SMEM)
HBM = pl.BlockSpec(memory_space=pltpu.HBM)
LIMIT = pltpu.CompilerParams(vmem_limit_bytes=16 * 1024 * 1024)
FREE = pl.CostEstimate(flops=0, bytes_accessed=0, transcendentals=0)
BF16 = jnp.bfloat16
F32 = jnp.float32


def north(v):
    return pltpu.roll(v, v.shape[1] - 1, 1)


def south(v):
    return pltpu.roll(v, 1, 1)


def coefficients(zonal, merid, rate, self_mix):
    lat = lax.broadcasted_iota(jnp.int32, zonal.shape, 1)
    zonal_half, zonal_rate = 0.5 * zonal, 0.5 * zonal * zonal + rate
    merid_half, merid_rate = 0.5 * merid, 0.5 * merid * merid + rate
    east, west = zonal_rate - zonal_half, zonal_rate + zonal_half
    to_north, to_south = merid_rate - merid_half, merid_rate + merid_half
    centre = 1.0 + self_mix - 2.0 * zonal_rate - 2.0 * merid_rate
    last, first = lat == zonal.shape[1] - 1, lat == 0
    centre = centre + jnp.where(last, to_north, 0.0) + jnp.where(first, to_south, 0.0)
    to_north = jnp.where(last, 0.0, to_north)
    to_south = jnp.where(first, 0.0, to_south)
    return centre, east, west, to_north, to_south


def mixed(mixing, field, values):
    total = None
    for other, value in enumerate(values):
        if other != field:
            term = mixing[field, other] * value
            total = term if total is None else total + term
    return total


def pick_rows(kinds, particles, fields, strip):
    shape = (particles, particles * fields * strip)
    place = lax.broadcasted_iota(jnp.int32, shape, 1) - lax.broadcasted_iota(jnp.int32, shape, 0) * (fields * strip)
    blocks = [jnp.where(place == f * strip + x, 1.0, 0.0) for f, x in kinds]
    return jnp.concatenate(blocks, 0).astype(BF16)


def stack_rows(rows):
    sub = lax.broadcasted_iota(jnp.int32, (len(rows), rows[0].shape[1]), 0)
    out = None
    for p, row in enumerate(rows):
        row = jnp.broadcast_to(row, sub.shape)
        out = row if out is None else jnp.where(sub == p, row, out)
    return out


def in_row(column):
    total = jnp.broadcast_to(jnp.sum(column, axis=1, keepdims=True), column.shape)
    diagonal = lax.broadcasted_iota(jnp.int32, total.shape, 0) == lax.broadcasted_iota(jnp.int32, total.shape, 1)
    return jnp.sum(jnp.where(diagonal, total, 0.0), axis=0, keepdims=True)


def wide(v):
    return v[:, :128] + v[:, 128:]


def observation_maps(sizes, cell, value):
    particles, fields, strip, lats, strips = sizes
    x0 = lax.axis_index("lon") * strip
    shift = lats.bit_length() - 1
    local_cell = cell - x0 * lats
    obs_lon = lax.shift_right_arithmetic(local_cell, shift)
    obs_lat = local_cell & (lats - 1)
    count = cell.shape[1]
    here = lax.broadcasted_iota(jnp.int32, (strip, count), 0) == obs_lon
    high = value.astype(BF16)
    rest = value - high.astype(F32)
    mid = rest.astype(BF16)
    low = (rest - mid.astype(F32)).astype(BF16)
    zero = jnp.zeros((strip, count), F32)
    parts = [jnp.where(here, 1.0, zero)]
    parts += [jnp.where(here, p.astype(F32), zero) for p in (high, mid, low)]
    left = jnp.concatenate(parts, 0).astype(BF16)
    right = (lax.broadcasted_iota(jnp.int32, (lats, count), 0) == obs_lat).astype(F32).astype(BF16)
    dense = lax.dot_general(left, right, (((1,), (1,)), ((), ())), preferred_element_type=F32)
    lon = (lax.broadcasted_iota(jnp.int32, (strip, lats), 0) + x0).astype(F32)
    precision = 1.0 + 2.0 * lon / (strip * strips)
    target = dense[strip:2 * strip] + (dense[2 * strip:3 * strip] + dense[3 * strip:])
    return dense[:strip] * (0.25 * precision), target


class Rows:
    def __init__(self, ref, first, columns):
        self.ref, self.first, self.columns = ref, first, columns

    def __getitem__(self, at):
        row = self.first + at[0] * self.columns + at[1]
        return self.ref[row:row + 1]


def scalars_in(ref, fields):
    return Rows(ref, fields * fields, fields), Rows(ref, 0, fields)


def prepare(sizes, state_hbm, noise_hbm, courant_hbm, diffusion_hbm, mixing_hbm, cell_hbm, value_hbm,
            send_east, send_west, state, noise, maps, courant, scalars,
            diffusion, mixing, cell, value, sems):
    particles, fields, strip, lats, strips = sizes
    n = fields * particles
    copies = [pltpu.make_async_copy(source, target, sems.at[k]) for k, (source, target) in enumerate((
        (cell_hbm, cell), (value_hbm, value), (courant_hbm, courant), (diffusion_hbm, diffusion),
        (mixing_hbm, mixing), (state_hbm.at[:, :, :8], state.at[:, :, :8]),
        (state_hbm.at[:, :, strip - 8:], state.at[:, :, strip - 8:]), (noise_hbm.at[0], noise.at[0]),
        (noise_hbm.at[1, :, 0], noise.at[1, :, 0]), (state_hbm.at[:, :, 8:strip - 8], state.at[:, :, 8:strip - 8]),
        (noise_hbm.at[1, :, 1:], noise.at[1, :, 1:])))]
    for copy in copies:
        copy.start()
    copies[0].wait()
    copies[1].wait()
    gain, target = observation_maps(sizes, cell[...], value[...])
    maps[0], maps[1] = gain, target
    kinds = []
    for x, step in ((strip - 1, -1), (0, 1)):
        kinds += [(f, x) for f in range(fields)] + [(f, x + step) for f in range(fields)] + [(0, x + 2 * step)]
    pick0 = pick_rows(kinds, particles, fields, strip)
    pick1 = pick_rows([(0, x) for x in (strip - 1, strip - 2, 0, 1)], particles, 1, strip)
    for copy in copies[2:5]:
        copy.wait()
    for f in range(fields):
        for g in range(fields):
            scalars[f * fields + g:f * fields + g + 1] = jnp.broadcast_to(mixing[f:f + 1, g:g + 1], (1, lats))
        at = fields * fields + f
        scalars[at:at + 1] = jnp.broadcast_to(diffusion[:, f:f + 1], (1, lats))
    diffusion, mixing = scalars_in(scalars, fields)

    sides = []
    for first, inward, outward in ((strip - 8, 2, 1), (0, 1, 2)):
        tile = [coefficients(courant[0, first:first + 8], courant[1, first:first + 8], diffusion[0, f], mixing[f, f])
                for f in range(fields)]
        sides.append([[c[0], c[inward], c[outward], c[3], c[4]] for c in tile])
    def coefs_at(side, f, k):
        at = places[side][0] + k * places[side][2] - places[side][1]
        return [c[at:at + 1] for c in sides[side][f]]

    def maps_at(side, k):
        at = places[side][0] + k * places[side][2]
        return gain[at:at + 1], target[at:at + 1]

    def moved(side, f, k, here, inner, outer):
        centre, inward, outward, to_north, to_south = coefs_at(side, f, k)
        v = here[f]
        total = centre * v + inward * inner + to_north * north(v) + to_south * south(v) + mixed(mixing, f, here)
        return total if outer is None else total + outward * outer

    def nudged(side, value, k):
        g, v = maps_at(side, k)
        push = g * (v - value)
        return value + push, push

    def first_step(side, out):
        def state_at(f, k):
            at = places[side][0] + k * places[side][2]
            return stack_rows([state[p, f, at:at + 1] for p in range(particles)])

        near = [[state_at(f, k) for f in range(fields)] for k in range(3)]
        third = state_at(0, 3)
        for f in range(fields):
            out[f * particles:(f + 1) * particles] = near[0][f]
        result, pushes = [[], []], []
        for k in range(2):
            for f in range(fields):
                new = moved(side, f, k, near[k], near[k + 1][f], near[k - 1][f] if k else None)
                if f == 0:
                    new, push = nudged(side, new, k)
                    pushes.append(push)
                result[k].append(new)
        inside, _ = nudged(side, moved(side, 0, 2, near[2], third, near[1][0]), 2)
        return result, pushes, inside

    places = ((strip - 1, strip - 8, -1), (0, 0, 1))
    copies[5].wait()
    copies[6].wait()
    started = [first_step(0, send_east), first_step(1, send_west)]
    copies[7].wait()
    copies[8].wait()
    rows0 = jnp.dot(pick0, noise[0].reshape(n * strip, lats), preferred_element_type=F32)
    rows1 = jnp.dot(pick1, noise[1, :, 0].reshape(particles * strip, lats), preferred_element_type=F32)

    def edge(side, out):
        x, _, step = places[side]
        base0, base1 = side * (2 * fields + 1) * particles, side * 2 * particles
        result, pushes, inside = started[side]

        def noisy0(k, f):
            at = base0 + (k * fields + f) * particles
            return rows0[at:at + particles]

        def noisy1(k):
            at = base1 + k * particles
            return rows1[at:at + particles]

        result = [[result[k][f] + noisy0(k, f) for f in range(fields)] for k in range(2)]
        inside = inside + noisy0(2, 0)
        g0, _ = maps_at(side, 0)
        g1, _ = maps_at(side, 1)
        slope = [-(1.0 / noise_var) * g0 * (pushes[0] + noisy0(0, 0))]
        bend = [(0.5 / noise_var) * g0 * g0]
        for k, g in enumerate((g0, g1)):
            new = moved(side, 0, k, result[k], result[1][0] if k == 0 else inside, result[0][0] if k else None)
            new, push = nudged(side, new, k)
            miss = maps_at(side, k)[1] - (new + noisy1(k))
            weight = 4.0 * g
            slope.append(-(1.0 / noise_var) * g * (push + noisy1(k)) - weight * (1.0 - g) * miss)
            bend.append((0.5 / noise_var) * g * g + 0.5 * weight * (1.0 - g) * (1.0 - g))
        outward = coefs_at(side, 0, 0)[2]
        onward = coefs_at(side, 0, 1)[2] * (1.0 - g0) * outward
        for f in range(fields):
            out[n + f * particles:n + (f + 1) * particles] = result[0][f]
        out[2 * n:2 * n + particles] = outward * slope[0] + onward * slope[2]
        out[2 * n + particles:2 * n + 2 * particles] = slope[1]
        inner = x + step
        last = (outward * outward * bend[0] + onward * onward * bend[2], bend[1],
                courant[0, x:x + 1], courant[1, x:x + 1], g0, courant[0, inner:inner + 1], g1,
                jnp.zeros((1, lats), F32))
        out[2 * n + 2 * particles:] = stack_rows(last)

    edge(0, send_east)
    edge(1, send_west)
    copies[9].wait()
    copies[10].wait()


def zero_halo_coefs(sizes, courant, scalars, coefs):
    particles, fields, strip, lats, strips = sizes
    diffusion, mixing = scalars_in(scalars, fields)
    lon = lax.broadcasted_iota(jnp.int32, (strip, lats), 0)
    for f in range(fields):
        centre, east, west, to_north, to_south = coefficients(
            courant[0], courant[1], diffusion[0, f], mixing[f, f])
        coefs[f, 0] = centre
        coefs[f, 1] = jnp.where(lon == strip - 1, 0.0, east)
        coefs[f, 2] = jnp.where(lon == 0, 0.0, west)
        coefs[f, 3] = to_north
        coefs[f, 4] = to_south


def zero_halo_step(sizes, scalars, coefs):
    particles, fields, strip, lats, strips = sizes
    _, mixing = scalars_in(scalars, fields)

    def moved(values, f):
        v = values[f]
        return (coefs[f, 0] * v + coefs[f, 1] * pltpu.roll(v, strip - 1, 0) + coefs[f, 2] * pltpu.roll(v, 1, 0)
                + coefs[f, 3] * north(v) + coefs[f, 4] * south(v) + mixed(mixing, f, values))

    return moved


def observed_bulk(sizes, state, noise, maps, courant, scalars, middle, out, weight, coefs, partial):
    particles, fields, strip, lats, strips = sizes
    zero_halo_coefs(sizes, courant, scalars, coefs)
    moved = zero_halo_step(sizes, scalars, coefs)

    def one(p):
        values = [state[p, f] for f in range(fields)]
        results = []
        for f in range(fields):
            new = moved(values, f)
            add = noise[0, p, f].astype(F32)
            if f == 0:
                push = maps[0] * (maps[1] - new)
                new = new + push
                total = push * (push + 2.0 * add)
            results.append(new + add)
            middle[p, f] = new + add
        new = moved(results, 0)
        add = noise[1, p, 0].astype(F32)
        push = maps[0] * (maps[1] - new)
        new = new + push + add
        miss = maps[1] - new
        total = (0.5 / noise_var) * (total + push * (push + 2.0 * add)) + (2.0 * maps[0]) * (miss * miss)
        out[p] = new
        partial[pl.ds(p, 1), :] = wide(jnp.sum(total, axis=0, keepdims=True))

    def body(pair, carry):
        one(2 * pair)
        one(2 * pair + 1)
        return carry

    lax.fori_loop(0, particles // 2, body, 0)
    weight[...] = in_row(partial[...])


def other_bulk(sizes, middle, observed, noise, scalars, coefs, out):
    particles, fields, strip, lats, strips = sizes
    moved = zero_halo_step(sizes, scalars, coefs)

    def body(p, carry):
        values = [middle[p, f] for f in range(fields)]
        out[p, 0] = observed[p]
        for f in range(1, fields):
            out[p, f] = moved(values, f) + noise[1, p, f].astype(F32)
        return carry

    lax.fori_loop(0, particles, body, 0)


def correct(sizes, own_east, own_west, from_west, from_east, scalars, bulk_weight, weight, changes):
    particles, fields, strip, lats, strips = sizes
    n = fields * particles
    diffusion, mixing = scalars_in(scalars, fields)

    def field_rows(ref, start, f):
        return ref[start + f * particles:start + (f + 1) * particles]

    packets = (own_east, from_east, own_west, from_west)
    last = 2 * n + 2 * particles
    zonal = stack_rows([ref[last + 2:last + 3] for ref in packets] + [ref[last + 5:last + 6] for ref in packets])
    merid = stack_rows([ref[last + 3:last + 4] for ref in packets] * 2)
    tile = [coefficients(zonal, merid, diffusion[0, f], mixing[f, f]) for f in range(fields)]
    total = jnp.zeros((particles, lats), F32)
    for k, owner in enumerate(packets):
        other_k = k ^ 1
        other = packets[other_k]
        outward_at = (1, 2, 2, 1)[k]
        outward_other = (1, 2, 2, 1)[other_k]
        gain = owner[last + 4:last + 5]
        gain_other = other[last + 4:last + 5]
        first = []
        for f in range(fields):
            step = tile[f][outward_at][k:k + 1] * field_rows(other, 0, f)
            first.append((1.0 - gain) * step if f == 0 else step)
        mine = k in (0, 2)
        for f in range(fields if mine else 1):
            centre, to_north, to_south = [tile[f][c][k:k + 1] for c in (0, 3, 4)]
            outward = tile[f][outward_at][k:k + 1]
            reach = tile[f][outward_other][other_k:other_k + 1]
            if f == 0:
                reach = (1.0 - gain_other) * reach
            outside = field_rows(other, n, f) + reach * field_rows(owner, 0, f)
            step = (centre * first[f] + outward * outside + to_north * north(first[f])
                    + to_south * south(first[f]) + mixed(mixing, f, first))
            if f == 0:
                seen = field_rows(other, 0, 0)
                slope, slope_step = owner[2 * n:2 * n + particles], owner[2 * n + particles:last]
                bend, bend_step = owner[last:last + 1], owner[last + 1:last + 2]
                total = total + seen * (slope + bend * seen) + step * (slope_step + bend_step * step)
            if mine:
                beside = tile[f][outward_at][4 + k:5 + k] * first[f]
                if f == 0:
                    step = (1.0 - gain) * step
                    beside = (1.0 - owner[last + 6:last + 7]) * beside
                edge, inner = (3, 2) if k == 0 else (0, 1)
                changes[edge, f * particles:(f + 1) * particles] = step
                changes[inner, f * particles:(f + 1) * particles] = beside
    weight[...] = in_row(wide(total)) + bulk_weight[...]


def apply_changes(sizes, current, changes, out):
    particles, fields, strip, lats, strips = sizes
    sub = lax.broadcasted_iota(jnp.int32, (8, lats), 0)
    for p in range(particles):
        for f in range(fields):
            row = f * particles + p
            rows = [jnp.broadcast_to(changes[k, row:row + 1], sub.shape) for k in range(4)]
            out[p, f, :8] = current[p, f, :8] + jnp.where(sub == 0, rows[0], jnp.where(sub == 1, rows[1], 0.0))
            out[p, f, 8:strip - 8] = current[p, f, 8:strip - 8]
            out[p, f, strip - 8:] = current[p, f, strip - 8:] + jnp.where(
                sub == 7, rows[3], jnp.where(sub == 6, rows[2], 0.0))


def assemble(sizes, source, current, received, out, sems):
    particles = sizes[0]
    dom = lax.axis_index("dom")

    def copy(j, ref, at):
        return pltpu.make_async_copy(ref.at[at], out.at[j], sems.at[j])

    for j in range(particles):
        wanted = source[dom * particles + j]
        mine = wanted // particles == dom
        at = wanted % particles

        @pl.when(mine)
        def _():
            copy(j, current, at).start()

        @pl.when(jnp.logical_not(mine))
        def _():
            copy(j, received, at).start()

    for j in range(particles):
        copy(j, current, 0).wait()


def local(ensemble_state, proposal_noise, courant, diffusion, mixing, prior_weight, obs_cell, obs_value, source):
    particles, fields, strip, lats = ensemble_state.shape
    strips = lax.axis_size("lon")
    sizes = (particles, fields, strip, lats, strips)
    packet = jax.ShapeDtypeStruct((2 * particles * fields + 2 * particles + 8, lats), F32)
    cell, value = obs_cell[None], obs_value[None]

    def shape(*dims):
        return jax.ShapeDtypeStruct(dims, F32)

    whole = (particles, fields, strip, lats)

    def in_hbm(array):
        return pltpu.with_memory_space_constraint(array, pltpu.HBM)

    arrays = (ensemble_state, proposal_noise, courant, diffusion[None], mixing, cell, value)
    send_east, send_west, state, noise, maps, courant, scalars = pl.pallas_call(
        functools.partial(prepare, sizes),
        out_shape=(packet, packet, shape(*whole), jax.ShapeDtypeStruct((2,) + whole, BF16), shape(2, strip, lats),
                   shape(*courant.shape), shape(fields * (fields + 2), lats)),
        in_specs=[HBM] * 7,
        out_specs=(VMEM,) * 7,
        scratch_shapes=[pltpu.VMEM(array.shape, array.dtype) for array in arrays[3:]]
        + [pltpu.SemaphoreType.DMA((11,))],
        compiler_params=LIMIT,
        cost_estimate=pl.CostEstimate(flops=1000000, bytes_accessed=2000000, transcendentals=0),
    )(*[in_hbm(array) for array in arrays])

    eastward = [(i, (i + 1) % strips) for i in range(strips)]
    westward = [(i, (i - 1) % strips) for i in range(strips)]
    from_west = lax.ppermute(send_east, "lon", eastward)
    from_east = lax.ppermute(send_west, "lon", westward)

    middle, observed, bulk_weight, coefs = pl.pallas_call(
        functools.partial(observed_bulk, sizes),
        out_shape=(shape(*whole), shape(particles, strip, lats), shape(1, 128), shape(fields, 5, strip, lats)),
        in_specs=[VMEM] * 5,
        out_specs=(VMEM,) * 4,
        scratch_shapes=[pltpu.VMEM((particles, 128), F32)],
        compiler_params=LIMIT,
        cost_estimate=pl.CostEstimate(flops=20000000, bytes_accessed=4000000, transcendentals=0),
    )(state, noise, maps, courant, scalars)
    beside = lax.ppermute(bulk_weight, "lon", [(i, i ^ 1) for i in range(strips)])

    weight, changes = pl.pallas_call(
        functools.partial(correct, sizes),
        out_shape=(shape(1, 128), shape(4, particles * fields, lats)),
        in_specs=[VMEM] * 6,
        out_specs=(VMEM,) * 2,
        compiler_params=LIMIT,
        cost_estimate=FREE,
    )(send_east, send_west, from_west, from_east, scalars, bulk_weight)

    current = pl.pallas_call(
        functools.partial(other_bulk, sizes),
        out_shape=shape(*whole),
        in_specs=[VMEM] * 5,
        out_specs=VMEM,
        compiler_params=LIMIT,
        cost_estimate=FREE,
    )(middle, observed, noise, scalars, coefs)

    current = pl.pallas_call(
        functools.partial(apply_changes, sizes),
        out_shape=shape(*whole),
        in_specs=[VMEM] * 2,
        out_specs=VMEM,
        compiler_params=LIMIT,
        cost_estimate=FREE,
    )(current, changes)

    current, beside = lax.optimization_barrier((current, beside))
    weight = weight + beside
    received = lax.ppermute(current, "dom", [(0, 1), (1, 0)])
    bit = 2
    while bit < strips:
        if 2 * bit >= strips:
            weight, received = lax.optimization_barrier((weight, received))
        weight = weight + lax.ppermute(weight, "lon", [(i, i ^ bit) for i in range(strips)])
        bit *= 2

    new_state = pl.pallas_call(
        functools.partial(assemble, sizes),
        out_shape=shape(*whole),
        in_specs=[SMEM, VMEM, VMEM],
        out_specs=HBM,
        scratch_shapes=[pltpu.SemaphoreType.DMA((particles,))],
        compiler_params=LIMIT,
        cost_estimate=pl.CostEstimate(flops=0, bytes_accessed=2000000, transcendentals=0),
    )(source, current, received)

    log_weight = prior_weight - weight[0, :particles] / (256.0 * obs_cell.shape[0])
    return new_state, log_weight


def solution(mesh):
    placed = (
        P(("groups", "dom"), None, "lon", None),
        P(None, ("groups", "dom"), None, "lon", None),
        P(None, ("groups", "lon"), None),
        P(),
        P(),
        P(("groups", "dom")),
        P(("groups", "lon")),
        P(("groups", "lon")),
        P("groups"),
    )
    return jax.shard_map(
        local,
        mesh=mesh,
        in_specs=placed,
        out_specs=(P(("groups", "dom"), None, "lon", None), P(("groups", "dom"))),
        check_vma=False,
    )
```

```python
import functools

import jax
import jax.numpy as jnp
from jax import lax
from jax.experimental import pallas as pl
from jax.experimental.pallas import tpu as pltpu
from jax.sharding import PartitionSpec as P

noise_var = 0.04
VMEM = pl.BlockSpec(memory_space=pltpu.VMEM)
SMEM = pl.BlockSpec(memory_space=pltpu.SMEM)
HBM = pl.BlockSpec(memory_space=pltpu.HBM)
LIMIT = pltpu.CompilerParams(vmem_limit_bytes=16 * 1024 * 1024)
FREE = pl.CostEstimate(flops=0, bytes_accessed=0, transcendentals=0)
BF16 = jnp.bfloat16
F32 = jnp.float32


def north(v):
    return pltpu.roll(v, v.shape[1] - 1, 1)


def south(v):
    return pltpu.roll(v, 1, 1)


def coefficients(zonal, merid, rate, self_mix):
    lat = lax.broadcasted_iota(jnp.int32, zonal.shape, 1)
    zonal_half, zonal_rate = 0.5 * zonal, 0.5 * zonal * zonal + rate
    merid_half, merid_rate = 0.5 * merid, 0.5 * merid * merid + rate
    east, west = zonal_rate - zonal_half, zonal_rate + zonal_half
    to_north, to_south = merid_rate - merid_half, merid_rate + merid_half
    centre = 1.0 + self_mix - 2.0 * zonal_rate - 2.0 * merid_rate
    last, first = lat == zonal.shape[1] - 1, lat == 0
    centre = centre + jnp.where(last, to_north, 0.0) + jnp.where(first, to_south, 0.0)
    to_north = jnp.where(last, 0.0, to_north)
    to_south = jnp.where(first, 0.0, to_south)
    return centre, east, west, to_north, to_south


def mixed(mixing, field, values):
    total = None
    for other, value in enumerate(values):
        if other != field:
            term = mixing[field, other] * value
            total = term if total is None else total + term
    return total


def pick_rows(kinds, particles, fields, strip):
    shape = (particles, particles * fields * strip)
    place = lax.broadcasted_iota(jnp.int32, shape, 1) - lax.broadcasted_iota(jnp.int32, shape, 0) * (fields * strip)
    blocks = [jnp.where(place == f * strip + x, 1.0, 0.0) for f, x in kinds]
    return jnp.concatenate(blocks, 0).astype(BF16)


def stack_rows(rows):
    sub = lax.broadcasted_iota(jnp.int32, (len(rows), rows[0].shape[1]), 0)
    out = None
    for p, row in enumerate(rows):
        row = jnp.broadcast_to(row, sub.shape)
        out = row if out is None else jnp.where(sub == p, row, out)
    return out


def in_row(column):
    total = jnp.broadcast_to(jnp.sum(column, axis=1, keepdims=True), column.shape)
    diagonal = lax.broadcasted_iota(jnp.int32, total.shape, 0) == lax.broadcasted_iota(jnp.int32, total.shape, 1)
    return jnp.sum(jnp.where(diagonal, total, 0.0), axis=0, keepdims=True)


def wide(v):
    return v[:, :128] + v[:, 128:]


def observation_maps(sizes, cell, value):
    particles, fields, strip, lats, strips = sizes
    x0 = lax.axis_index("lon") * strip
    shift = lats.bit_length() - 1
    local_cell = cell - x0 * lats
    obs_lon = lax.shift_right_arithmetic(local_cell, shift)
    obs_lat = local_cell & (lats - 1)
    count = cell.shape[1]
    here = lax.broadcasted_iota(jnp.int32, (strip, count), 0) == obs_lon
    high = value.astype(BF16)
    rest = value - high.astype(F32)
    mid = rest.astype(BF16)
    low = (rest - mid.astype(F32)).astype(BF16)
    zero = jnp.zeros((strip, count), F32)
    parts = [jnp.where(here, 1.0, zero)]
    parts += [jnp.where(here, p.astype(F32), zero) for p in (high, mid, low)]
    left = jnp.concatenate(parts, 0).astype(BF16)
    right = (lax.broadcasted_iota(jnp.int32, (lats, count), 0) == obs_lat).astype(F32).astype(BF16)
    dense = lax.dot_general(left, right, (((1,), (1,)), ((), ())), preferred_element_type=F32)
    lon = (lax.broadcasted_iota(jnp.int32, (strip, lats), 0) + x0).astype(F32)
    precision = 1.0 + 2.0 * lon / (strip * strips)
    target = dense[strip:2 * strip] + (dense[2 * strip:3 * strip] + dense[3 * strip:])
    return dense[:strip] * (0.25 * precision), target


class Rows:
    def __init__(self, ref, first, columns):
        self.ref, self.first, self.columns = ref, first, columns

    def __getitem__(self, at):
        row = self.first + at[0] * self.columns + at[1]
        return self.ref[row:row + 1]


def scalars_in(ref, fields):
    return Rows(ref, fields * fields, fields), Rows(ref, 0, fields)


def prepare(sizes, state_hbm, noise_hbm, courant_hbm, diffusion_hbm, mixing_hbm, cell_hbm, value_hbm,
            send_east, send_west, state, noise, maps, courant, scalars,
            diffusion, mixing, cell, value, sems):
    particles, fields, strip, lats, strips = sizes
    n = fields * particles
    copies = [pltpu.make_async_copy(source, target, sems.at[k]) for k, (source, target) in enumerate((
        (cell_hbm, cell), (value_hbm, value), (courant_hbm, courant), (diffusion_hbm, diffusion),
        (mixing_hbm, mixing), (state_hbm.at[:, :, :8], state.at[:, :, :8]),
        (state_hbm.at[:, :, strip - 8:], state.at[:, :, strip - 8:]), (noise_hbm.at[0], noise.at[0]),
        (noise_hbm.at[1, :, 0], noise.at[1, :, 0]), (state_hbm.at[:, :, 8:strip - 8], state.at[:, :, 8:strip - 8]),
        (noise_hbm.at[1, :, 1:], noise.at[1, :, 1:])))]
    for copy in copies:
        copy.start()
    copies[0].wait()
    copies[1].wait()
    gain, target = observation_maps(sizes, cell[...], value[...])
    maps[0], maps[1] = gain, target
    kinds = []
    for x, step in ((strip - 1, -1), (0, 1)):
        kinds += [(f, x) for f in range(fields)] + [(f, x + step) for f in range(fields)] + [(0, x + 2 * step)]
    pick0 = pick_rows(kinds, particles, fields, strip)
    pick1 = pick_rows([(0, x) for x in (strip - 1, strip - 2, 0, 1)], particles, 1, strip)
    for copy in copies[2:5]:
        copy.wait()
    for f in range(fields):
        for g in range(fields):
            scalars[f * fields + g:f * fields + g + 1] = jnp.broadcast_to(mixing[f:f + 1, g:g + 1], (1, lats))
        at = fields * fields + f
        scalars[at:at + 1] = jnp.broadcast_to(diffusion[:, f:f + 1], (1, lats))
    diffusion, mixing = scalars_in(scalars, fields)

    sides = []
    for first, inward, outward in ((strip - 8, 2, 1), (0, 1, 2)):
        tile = [coefficients(courant[0, first:first + 8], courant[1, first:first + 8], diffusion[0, f], mixing[f, f])
                for f in range(fields)]
        sides.append([[c[0], c[inward], c[outward], c[3], c[4]] for c in tile])
    def coefs_at(side, f, k):
        at = places[side][0] + k * places[side][2] - places[side][1]
        return [c[at:at + 1] for c in sides[side][f]]

    def maps_at(side, k):
        at = places[side][0] + k * places[side][2]
        return gain[at:at + 1], target[at:at + 1]

    def moved(side, f, k, here, inner, outer):
        centre, inward, outward, to_north, to_south = coefs_at(side, f, k)
        v = here[f]
        total = centre * v + inward * inner + to_north * north(v) + to_south * south(v) + mixed(mixing, f, here)
        return total if outer is None else total + outward * outer

    def nudged(side, value, k):
        g, v = maps_at(side, k)
        push = g * (v - value)
        return value + push, push

    def first_step(side, out):
        def state_at(f, k):
            at = places[side][0] + k * places[side][2]
            return stack_rows([state[p, f, at:at + 1] for p in range(particles)])

        near = [[state_at(f, k) for f in range(fields)] for k in range(3)]
        third = state_at(0, 3)
        for f in range(fields):
            out[f * particles:(f + 1) * particles] = near[0][f]
        result, pushes = [[], []], []
        for k in range(2):
            for f in range(fields):
                new = moved(side, f, k, near[k], near[k + 1][f], near[k - 1][f] if k else None)
                if f == 0:
                    new, push = nudged(side, new, k)
                    pushes.append(push)
                result[k].append(new)
        inside, _ = nudged(side, moved(side, 0, 2, near[2], third, near[1][0]), 2)
        return result, pushes, inside

    places = ((strip - 1, strip - 8, -1), (0, 0, 1))
    copies[5].wait()
    copies[6].wait()
    started = [first_step(0, send_east), first_step(1, send_west)]
    copies[7].wait()
    copies[8].wait()
    rows0 = jnp.dot(pick0, noise[0].reshape(n * strip, lats), preferred_element_type=F32)
    rows1 = jnp.dot(pick1, noise[1, :, 0].reshape(particles * strip, lats), preferred_element_type=F32)

    def edge(side, out):
        x, _, step = places[side]
        base0, base1 = side * (2 * fields + 1) * particles, side * 2 * particles
        result, pushes, inside = started[side]

        def noisy0(k, f):
            at = base0 + (k * fields + f) * particles
            return rows0[at:at + particles]

        def noisy1(k):
            at = base1 + k * particles
            return rows1[at:at + particles]

        result = [[result[k][f] + noisy0(k, f) for f in range(fields)] for k in range(2)]
        inside = inside + noisy0(2, 0)
        g0, _ = maps_at(side, 0)
        g1, _ = maps_at(side, 1)
        slope = [-(1.0 / noise_var) * g0 * (pushes[0] + noisy0(0, 0))]
        bend = [(0.5 / noise_var) * g0 * g0]
        for k, g in enumerate((g0, g1)):
            new = moved(side, 0, k, result[k], result[1][0] if k == 0 else inside, result[0][0] if k else None)
            new, push = nudged(side, new, k)
            miss = maps_at(side, k)[1] - (new + noisy1(k))
            weight = 4.0 * g
            slope.append(-(1.0 / noise_var) * g * (push + noisy1(k)) - weight * (1.0 - g) * miss)
            bend.append((0.5 / noise_var) * g * g + 0.5 * weight * (1.0 - g) * (1.0 - g))
        outward = coefs_at(side, 0, 0)[2]
        onward = coefs_at(side, 0, 1)[2] * (1.0 - g0) * outward
        for f in range(fields):
            out[n + f * particles:n + (f + 1) * particles] = result[0][f]
        out[2 * n:2 * n + particles] = outward * slope[0] + onward * slope[2]
        out[2 * n + particles:2 * n + 2 * particles] = slope[1]
        inner = x + step
        last = (outward * outward * bend[0] + onward * onward * bend[2], bend[1],
                courant[0, x:x + 1], courant[1, x:x + 1], g0, courant[0, inner:inner + 1], g1,
                jnp.zeros((1, lats), F32))
        out[2 * n + 2 * particles:] = stack_rows(last)

    edge(0, send_east)
    edge(1, send_west)
    copies[9].wait()
    copies[10].wait()


def zero_halo_coefs(sizes, courant, scalars, coefs):
    particles, fields, strip, lats, strips = sizes
    diffusion, mixing = scalars_in(scalars, fields)
    lon = lax.broadcasted_iota(jnp.int32, (strip, lats), 0)
    for f in range(fields):
        centre, east, west, to_north, to_south = coefficients(
            courant[0], courant[1], diffusion[0, f], mixing[f, f])
        coefs[f, 0] = centre
        coefs[f, 1] = jnp.where(lon == strip - 1, 0.0, east)
        coefs[f, 2] = jnp.where(lon == 0, 0.0, west)
        coefs[f, 3] = to_north
        coefs[f, 4] = to_south


def zero_halo_step(sizes, scalars, coefs):
    particles, fields, strip, lats, strips = sizes
    _, mixing = scalars_in(scalars, fields)

    def moved(values, f):
        v = values[f]
        return (coefs[f, 0] * v + coefs[f, 1] * pltpu.roll(v, strip - 1, 0) + coefs[f, 2] * pltpu.roll(v, 1, 0)
                + coefs[f, 3] * north(v) + coefs[f, 4] * south(v) + mixed(mixing, f, values))

    return moved


def observed_bulk(sizes, parity, state, noise, maps, courant, scalars, middle, out, weight, coefs, partial):
    particles, fields, strip, lats, strips = sizes

    def one(p):
        moved = zero_halo_step(sizes, scalars, coefs)
        values = [state[p, f] for f in range(fields)]
        results = []
        for f in range(fields):
            new = moved(values, f)
            add = noise[0, p, f].astype(F32)
            if f == 0:
                push = maps[0] * (maps[1] - new)
                new = new + push
                total = push * (push + 2.0 * add)
            results.append(new + add)
            middle[p, f] = new + add
        new = moved(results, 0)
        add = noise[1, p, 0].astype(F32)
        push = maps[0] * (maps[1] - new)
        new = new + push + add
        miss = maps[1] - new
        total = (0.5 / noise_var) * (total + push * (push + 2.0 * add)) + (2.0 * maps[0]) * (miss * miss)
        out[p] = new
        partial[pl.ds(p, 1), :] = wide(jnp.sum(total, axis=0, keepdims=True))

    def body(pair, carry):
        one(2 * pair)
        one(2 * pair + 1)
        return carry

    here = lax.axis_index("lon") % 2 == parity

    @pl.when(here)
    def _():
        zero_halo_coefs(sizes, courant, scalars, coefs)
        lax.fori_loop(0, particles // 2, body, 0)
        weight[...] = in_row(partial[...])

    @pl.when(jnp.logical_not(here))
    def _():
        weight[...] = jnp.zeros_like(weight)


def other_bulk(sizes, even_middle, even_observed, even_coefs, odd_middle, odd_observed, odd_coefs,
               noise, scalars, out):
    particles, fields, strip, lats, strips = sizes

    def run(middle, observed, coefs):
        moved = zero_halo_step(sizes, scalars, coefs)

        def body(p, carry):
            values = [middle[p, f] for f in range(fields)]
            out[p, 0] = observed[p]
            for f in range(1, fields):
                out[p, f] = moved(values, f) + noise[1, p, f].astype(F32)
            return carry

        lax.fori_loop(0, particles, body, 0)

    even = lax.axis_index("lon") % 2 == 0

    @pl.when(even)
    def _():
        run(even_middle, even_observed, even_coefs)

    @pl.when(jnp.logical_not(even))
    def _():
        run(odd_middle, odd_observed, odd_coefs)


def correct(sizes, own_east, own_west, from_west, from_east, scalars, even_weight, odd_weight,
            weight, changes):
    particles, fields, strip, lats, strips = sizes
    n = fields * particles
    diffusion, mixing = scalars_in(scalars, fields)

    def field_rows(ref, start, f):
        return ref[start + f * particles:start + (f + 1) * particles]

    packets = (own_east, from_east, own_west, from_west)
    last = 2 * n + 2 * particles
    zonal = stack_rows([ref[last + 2:last + 3] for ref in packets] + [ref[last + 5:last + 6] for ref in packets])
    merid = stack_rows([ref[last + 3:last + 4] for ref in packets] * 2)
    tile = [coefficients(zonal, merid, diffusion[0, f], mixing[f, f]) for f in range(fields)]
    total = jnp.zeros((particles, lats), F32)
    for k, owner in enumerate(packets):
        other_k = k ^ 1
        other = packets[other_k]
        outward_at = (1, 2, 2, 1)[k]
        outward_other = (1, 2, 2, 1)[other_k]
        gain = owner[last + 4:last + 5]
        gain_other = other[last + 4:last + 5]
        first = []
        for f in range(fields):
            step = tile[f][outward_at][k:k + 1] * field_rows(other, 0, f)
            first.append((1.0 - gain) * step if f == 0 else step)
        mine = k in (0, 2)
        for f in range(fields if mine else 1):
            centre, to_north, to_south = [tile[f][c][k:k + 1] for c in (0, 3, 4)]
            outward = tile[f][outward_at][k:k + 1]
            reach = tile[f][outward_other][other_k:other_k + 1]
            if f == 0:
                reach = (1.0 - gain_other) * reach
            outside = field_rows(other, n, f) + reach * field_rows(owner, 0, f)
            step = (centre * first[f] + outward * outside + to_north * north(first[f])
                    + to_south * south(first[f]) + mixed(mixing, f, first))
            if f == 0:
                seen = field_rows(other, 0, 0)
                slope, slope_step = owner[2 * n:2 * n + particles], owner[2 * n + particles:last]
                bend, bend_step = owner[last:last + 1], owner[last + 1:last + 2]
                total = total + seen * (slope + bend * seen) + step * (slope_step + bend_step * step)
            if mine:
                beside = tile[f][outward_at][4 + k:5 + k] * first[f]
                if f == 0:
                    step = (1.0 - gain) * step
                    beside = (1.0 - owner[last + 6:last + 7]) * beside
                edge, inner = (3, 2) if k == 0 else (0, 1)
                changes[edge, f * particles:(f + 1) * particles] = step
                changes[inner, f * particles:(f + 1) * particles] = beside
    weight[...] = in_row(wide(total)) + (even_weight[...] + odd_weight[...])


def apply_changes(sizes, current, changes, out):
    particles, fields, strip, lats, strips = sizes
    sub = lax.broadcasted_iota(jnp.int32, (8, lats), 0)
    for p in range(particles):
        for f in range(fields):
            row = f * particles + p
            rows = [jnp.broadcast_to(changes[k, row:row + 1], sub.shape) for k in range(4)]
            out[p, f, :8] = current[p, f, :8] + jnp.where(sub == 0, rows[0], jnp.where(sub == 1, rows[1], 0.0))
            out[p, f, 8:strip - 8] = current[p, f, 8:strip - 8]
            out[p, f, strip - 8:] = current[p, f, strip - 8:] + jnp.where(
                sub == 7, rows[3], jnp.where(sub == 6, rows[2], 0.0))


def assemble(sizes, source, current, received, out, sems):
    particles = sizes[0]
    dom = lax.axis_index("dom")

    def copy(j, ref, at):
        return pltpu.make_async_copy(ref.at[at], out.at[j], sems.at[j])

    for j in range(particles):
        wanted = source[dom * particles + j]
        mine = wanted // particles == dom
        at = wanted % particles

        @pl.when(mine)
        def _():
            copy(j, current, at).start()

        @pl.when(jnp.logical_not(mine))
        def _():
            copy(j, received, at).start()

    for j in range(particles):
        copy(j, current, 0).wait()


def local(ensemble_state, proposal_noise, courant, diffusion, mixing, prior_weight, obs_cell, obs_value, source):
    particles, fields, strip, lats = ensemble_state.shape
    strips = lax.axis_size("lon")
    sizes = (particles, fields, strip, lats, strips)
    packet = jax.ShapeDtypeStruct((2 * particles * fields + 2 * particles + 8, lats), F32)
    cell, value = obs_cell[None], obs_value[None]

    def shape(*dims):
        return jax.ShapeDtypeStruct(dims, F32)

    whole = (particles, fields, strip, lats)

    def in_hbm(array):
        return pltpu.with_memory_space_constraint(array, pltpu.HBM)

    arrays = (ensemble_state, proposal_noise, courant, diffusion[None], mixing, cell, value)
    send_east, send_west, state, noise, maps, courant, scalars = pl.pallas_call(
        functools.partial(prepare, sizes),
        out_shape=(packet, packet, shape(*whole), jax.ShapeDtypeStruct((2,) + whole, BF16), shape(2, strip, lats),
                   shape(*courant.shape), shape(fields * (fields + 2), lats)),
        in_specs=[HBM] * 7,
        out_specs=(VMEM,) * 7,
        scratch_shapes=[pltpu.VMEM(array.shape, array.dtype) for array in arrays[3:]]
        + [pltpu.SemaphoreType.DMA((11,))],
        compiler_params=LIMIT,
        cost_estimate=pl.CostEstimate(flops=1000000, bytes_accessed=2000000, transcendentals=0),
    )(*[in_hbm(array) for array in arrays])

    eastward = [(i, (i + 1) % strips) for i in range(strips)]
    westward = [(i, (i - 1) % strips) for i in range(strips)]
    from_west = lax.ppermute(send_east, "lon", eastward)
    from_east = lax.ppermute(send_west, "lon", westward)

    def bulk_of(parity, cost):
        return pl.pallas_call(
            functools.partial(observed_bulk, sizes, parity),
            out_shape=(shape(*whole), shape(particles, strip, lats), shape(1, 128), shape(fields, 5, strip, lats)),
            in_specs=[VMEM] * 5,
            out_specs=(VMEM,) * 4,
            scratch_shapes=[pltpu.VMEM((particles, 128), F32)],
            compiler_params=LIMIT,
            cost_estimate=cost,
        )(state, noise, maps, courant, scalars)

    odd_middle, odd_observed, odd_weight, odd_coefs = bulk_of(
        1, pl.CostEstimate(flops=20000000, bytes_accessed=4000000, transcendentals=0))
    to_even = lax.ppermute(odd_weight, "lon", [(i + 1, i) for i in range(0, strips, 2)])
    even_middle, even_observed, even_weight, even_coefs = bulk_of(0, FREE)

    current = pl.pallas_call(
        functools.partial(other_bulk, sizes),
        out_shape=shape(*whole),
        in_specs=[VMEM] * 8,
        out_specs=VMEM,
        compiler_params=LIMIT,
        cost_estimate=FREE,
    )(even_middle, even_observed, even_coefs, odd_middle, odd_observed, odd_coefs, noise, scalars)

    current, from_west, from_east = lax.optimization_barrier((current, from_west, from_east))
    weight, changes = pl.pallas_call(
        functools.partial(correct, sizes),
        out_shape=(shape(1, 128), shape(4, particles * fields, lats)),
        in_specs=[VMEM] * 7,
        out_specs=(VMEM,) * 2,
        compiler_params=LIMIT,
        cost_estimate=FREE,
    )(send_east, send_west, from_west, from_east, scalars, even_weight, odd_weight)
    even_weight, changes = lax.optimization_barrier((even_weight, changes))
    to_odd = lax.ppermute(even_weight, "lon", [(i, i + 1) for i in range(0, strips, 2)])

    current = pl.pallas_call(
        functools.partial(apply_changes, sizes),
        out_shape=shape(*whole),
        in_specs=[VMEM] * 2,
        out_specs=VMEM,
        compiler_params=LIMIT,
        cost_estimate=FREE,
    )(current, changes)

    current, to_even, to_odd = lax.optimization_barrier((current, to_even, to_odd))
    weight = weight + (to_even + to_odd)
    received = lax.ppermute(current, "dom", [(0, 1), (1, 0)])
    bit = 2
    while bit < strips:
        if 2 * bit >= strips:
            weight, received = lax.optimization_barrier((weight, received))
        weight = weight + lax.ppermute(weight, "lon", [(i, i ^ bit) for i in range(strips)])
        bit *= 2

    new_state = pl.pallas_call(
        functools.partial(assemble, sizes),
        out_shape=shape(*whole),
        in_specs=[SMEM, VMEM, VMEM],
        out_specs=HBM,
        scratch_shapes=[pltpu.SemaphoreType.DMA((particles,))],
        compiler_params=LIMIT,
        cost_estimate=pl.CostEstimate(flops=0, bytes_accessed=2000000, transcendentals=0),
    )(source, current, received)

    log_weight = prior_weight - weight[0, :particles] / (256.0 * obs_cell.shape[0])
    return new_state, log_weight


def solution(mesh):
    placed = (
        P(("groups", "dom"), None, "lon", None),
        P(None, ("groups", "dom"), None, "lon", None),
        P(None, ("groups", "lon"), None),
        P(),
        P(),
        P(("groups", "dom")),
        P(("groups", "lon")),
        P(("groups", "lon")),
        P("groups"),
    )
    return jax.shard_map(
        local,
        mesh=mesh,
        in_specs=placed,
        out_specs=(P(("groups", "dom"), None, "lon", None), P(("groups", "dom"))),
        check_vma=False,
    )
```

```python
import functools

import jax
import jax.numpy as jnp
from jax import lax
from jax.experimental import pallas as pl
from jax.experimental.pallas import tpu as pltpu
from jax.sharding import PartitionSpec as P

noise_var = 0.04
VMEM = pl.BlockSpec(memory_space=pltpu.VMEM)
SMEM = pl.BlockSpec(memory_space=pltpu.SMEM)
HBM = pl.BlockSpec(memory_space=pltpu.HBM)
LIMIT = pltpu.CompilerParams(vmem_limit_bytes=16 * 1024 * 1024)
FREE = pl.CostEstimate(flops=0, bytes_accessed=0, transcendentals=0)
BF16 = jnp.bfloat16
F32 = jnp.float32


def north(v):
    return pltpu.roll(v, v.shape[1] - 1, 1)


def south(v):
    return pltpu.roll(v, 1, 1)


def coefficients(zonal, merid, rate, self_mix):
    lat = lax.broadcasted_iota(jnp.int32, zonal.shape, 1)
    zonal_half, zonal_rate = 0.5 * zonal, 0.5 * zonal * zonal + rate
    merid_half, merid_rate = 0.5 * merid, 0.5 * merid * merid + rate
    east, west = zonal_rate - zonal_half, zonal_rate + zonal_half
    to_north, to_south = merid_rate - merid_half, merid_rate + merid_half
    centre = 1.0 + self_mix - 2.0 * zonal_rate - 2.0 * merid_rate
    last, first = lat == zonal.shape[1] - 1, lat == 0
    centre = centre + jnp.where(last, to_north, 0.0) + jnp.where(first, to_south, 0.0)
    to_north = jnp.where(last, 0.0, to_north)
    to_south = jnp.where(first, 0.0, to_south)
    return centre, east, west, to_north, to_south


def mixed(mixing, field, values):
    total = None
    for other, value in enumerate(values):
        if other != field:
            term = mixing[field, other] * value
            total = term if total is None else total + term
    return total


def pick_rows(kinds, particles, fields, strip):
    shape = (particles, particles * fields * strip)
    place = lax.broadcasted_iota(jnp.int32, shape, 1) - lax.broadcasted_iota(jnp.int32, shape, 0) * (fields * strip)
    blocks = [jnp.where(place == f * strip + x, 1.0, 0.0) for f, x in kinds]
    return jnp.concatenate(blocks, 0).astype(BF16)


def stack_rows(rows):
    sub = lax.broadcasted_iota(jnp.int32, (len(rows), rows[0].shape[1]), 0)
    out = None
    for p, row in enumerate(rows):
        row = jnp.broadcast_to(row, sub.shape)
        out = row if out is None else jnp.where(sub == p, row, out)
    return out


def in_row(column):
    total = jnp.broadcast_to(jnp.sum(column, axis=1, keepdims=True), column.shape)
    diagonal = lax.broadcasted_iota(jnp.int32, total.shape, 0) == lax.broadcasted_iota(jnp.int32, total.shape, 1)
    return jnp.sum(jnp.where(diagonal, total, 0.0), axis=0, keepdims=True)


def wide(v):
    return v[:, :128] + v[:, 128:]


def observation_maps(sizes, cell, value):
    particles, fields, strip, lats, strips = sizes
    x0 = lax.axis_index("lon") * strip
    shift = lats.bit_length() - 1
    local_cell = cell - x0 * lats
    obs_lon = lax.shift_right_arithmetic(local_cell, shift)
    obs_lat = local_cell & (lats - 1)
    count = cell.shape[1]
    here = lax.broadcasted_iota(jnp.int32, (strip, count), 0) == obs_lon
    high = value.astype(BF16)
    rest = value - high.astype(F32)
    mid = rest.astype(BF16)
    low = (rest - mid.astype(F32)).astype(BF16)
    zero = jnp.zeros((strip, count), F32)
    parts = [jnp.where(here, 1.0, zero)]
    parts += [jnp.where(here, p.astype(F32), zero) for p in (high, mid, low)]
    left = jnp.concatenate(parts, 0).astype(BF16)
    right = (lax.broadcasted_iota(jnp.int32, (lats, count), 0) == obs_lat).astype(F32).astype(BF16)
    dense = lax.dot_general(left, right, (((1,), (1,)), ((), ())), preferred_element_type=F32)
    lon = (lax.broadcasted_iota(jnp.int32, (strip, lats), 0) + x0).astype(F32)
    precision = 1.0 + 2.0 * lon / (strip * strips)
    target = dense[strip:2 * strip] + (dense[2 * strip:3 * strip] + dense[3 * strip:])
    return dense[:strip] * (0.25 * precision), target


class Rows:
    def __init__(self, ref, first, columns):
        self.ref, self.first, self.columns = ref, first, columns

    def __getitem__(self, at):
        row = self.first + at[0] * self.columns + at[1]
        return self.ref[row:row + 1]


def scalars_in(ref, fields):
    return Rows(ref, fields * fields, fields), Rows(ref, 0, fields)


def prepare(sizes, state_hbm, noise_hbm, courant_hbm, diffusion_hbm, mixing_hbm, cell_hbm, value_hbm,
            send_east, send_west, state, noise, maps, courant, scalars,
            diffusion, mixing, cell, value, sems):
    particles, fields, strip, lats, strips = sizes
    n = fields * particles
    copies = [pltpu.make_async_copy(source, target, sems.at[k]) for k, (source, target) in enumerate((
        (cell_hbm, cell), (value_hbm, value), (courant_hbm, courant), (diffusion_hbm, diffusion),
        (mixing_hbm, mixing), (state_hbm.at[:, :, :8], state.at[:, :, :8]),
        (state_hbm.at[:, :, strip - 8:], state.at[:, :, strip - 8:]), (noise_hbm.at[0], noise.at[0]),
        (noise_hbm.at[1, :, 0], noise.at[1, :, 0]), (state_hbm.at[:, :, 8:strip - 8], state.at[:, :, 8:strip - 8]),
        (noise_hbm.at[1, :, 1:], noise.at[1, :, 1:])))]
    for copy in copies:
        copy.start()
    copies[0].wait()
    copies[1].wait()
    gain, target = observation_maps(sizes, cell[...], value[...])
    maps[0], maps[1] = gain, target
    kinds = []
    for x, step in ((strip - 1, -1), (0, 1)):
        kinds += [(f, x) for f in range(fields)] + [(f, x + step) for f in range(fields)] + [(0, x + 2 * step)]
    pick0 = pick_rows(kinds, particles, fields, strip)
    pick1 = pick_rows([(0, x) for x in (strip - 1, strip - 2, 0, 1)], particles, 1, strip)
    for copy in copies[2:5]:
        copy.wait()
    for f in range(fields):
        for g in range(fields):
            scalars[f * fields + g:f * fields + g + 1] = jnp.broadcast_to(mixing[f:f + 1, g:g + 1], (1, lats))
        at = fields * fields + f
        scalars[at:at + 1] = jnp.broadcast_to(diffusion[:, f:f + 1], (1, lats))
    diffusion, mixing = scalars_in(scalars, fields)

    sides = []
    for first, inward, outward in ((strip - 8, 2, 1), (0, 1, 2)):
        tile = [coefficients(courant[0, first:first + 8], courant[1, first:first + 8], diffusion[0, f], mixing[f, f])
                for f in range(fields)]
        sides.append([[c[0], c[inward], c[outward], c[3], c[4]] for c in tile])
    def coefs_at(side, f, k):
        at = places[side][0] + k * places[side][2] - places[side][1]
        return [c[at:at + 1] for c in sides[side][f]]

    def maps_at(side, k):
        at = places[side][0] + k * places[side][2]
        return gain[at:at + 1], target[at:at + 1]

    def moved(side, f, k, here, inner, outer):
        centre, inward, outward, to_north, to_south = coefs_at(side, f, k)
        v = here[f]
        total = centre * v + inward * inner + to_north * north(v) + to_south * south(v) + mixed(mixing, f, here)
        return total if outer is None else total + outward * outer

    def nudged(side, value, k):
        g, v = maps_at(side, k)
        push = g * (v - value)
        return value + push, push

    def first_step(side, out):
        def state_at(f, k):
            at = places[side][0] + k * places[side][2]
            return stack_rows([state[p, f, at:at + 1] for p in range(particles)])

        near = [[state_at(f, k) for f in range(fields)] for k in range(3)]
        third = state_at(0, 3)
        for f in range(fields):
            out[f * particles:(f + 1) * particles] = near[0][f]
        result, pushes = [[], []], []
        for k in range(2):
            for f in range(fields):
                new = moved(side, f, k, near[k], near[k + 1][f], near[k - 1][f] if k else None)
                if f == 0:
                    new, push = nudged(side, new, k)
                    pushes.append(push)
                result[k].append(new)
        inside, _ = nudged(side, moved(side, 0, 2, near[2], third, near[1][0]), 2)
        return result, pushes, inside

    places = ((strip - 1, strip - 8, -1), (0, 0, 1))
    copies[5].wait()
    copies[6].wait()
    started = [first_step(0, send_east), first_step(1, send_west)]
    copies[7].wait()
    copies[8].wait()
    rows0 = jnp.dot(pick0, noise[0].reshape(n * strip, lats), preferred_element_type=F32)
    rows1 = jnp.dot(pick1, noise[1, :, 0].reshape(particles * strip, lats), preferred_element_type=F32)

    def edge(side, out):
        x, _, step = places[side]
        base0, base1 = side * (2 * fields + 1) * particles, side * 2 * particles
        result, pushes, inside = started[side]

        def noisy0(k, f):
            at = base0 + (k * fields + f) * particles
            return rows0[at:at + particles]

        def noisy1(k):
            at = base1 + k * particles
            return rows1[at:at + particles]

        result = [[result[k][f] + noisy0(k, f) for f in range(fields)] for k in range(2)]
        inside = inside + noisy0(2, 0)
        g0, _ = maps_at(side, 0)
        g1, _ = maps_at(side, 1)
        slope = [-(1.0 / noise_var) * g0 * (pushes[0] + noisy0(0, 0))]
        bend = [(0.5 / noise_var) * g0 * g0]
        for k, g in enumerate((g0, g1)):
            new = moved(side, 0, k, result[k], result[1][0] if k == 0 else inside, result[0][0] if k else None)
            new, push = nudged(side, new, k)
            miss = maps_at(side, k)[1] - (new + noisy1(k))
            weight = 4.0 * g
            slope.append(-(1.0 / noise_var) * g * (push + noisy1(k)) - weight * (1.0 - g) * miss)
            bend.append((0.5 / noise_var) * g * g + 0.5 * weight * (1.0 - g) * (1.0 - g))
        outward = coefs_at(side, 0, 0)[2]
        onward = coefs_at(side, 0, 1)[2] * (1.0 - g0) * outward
        for f in range(fields):
            out[n + f * particles:n + (f + 1) * particles] = result[0][f]
        out[2 * n:2 * n + particles] = outward * slope[0] + onward * slope[2]
        out[2 * n + particles:2 * n + 2 * particles] = slope[1]
        inner = x + step
        last = (outward * outward * bend[0] + onward * onward * bend[2], bend[1],
                courant[0, x:x + 1], courant[1, x:x + 1], g0, courant[0, inner:inner + 1], g1,
                jnp.zeros((1, lats), F32))
        out[2 * n + 2 * particles:] = stack_rows(last)

    edge(0, send_east)
    edge(1, send_west)
    copies[9].wait()
    copies[10].wait()


def zero_halo_coefs(sizes, courant, scalars, coefs):
    particles, fields, strip, lats, strips = sizes
    diffusion, mixing = scalars_in(scalars, fields)
    lon = lax.broadcasted_iota(jnp.int32, (strip, lats), 0)
    for f in range(fields):
        centre, east, west, to_north, to_south = coefficients(
            courant[0], courant[1], diffusion[0, f], mixing[f, f])
        coefs[f, 0] = centre
        coefs[f, 1] = jnp.where(lon == strip - 1, 0.0, east)
        coefs[f, 2] = jnp.where(lon == 0, 0.0, west)
        coefs[f, 3] = to_north
        coefs[f, 4] = to_south


def zero_halo_step(sizes, scalars, coefs):
    particles, fields, strip, lats, strips = sizes
    _, mixing = scalars_in(scalars, fields)

    def moved(values, f):
        v = values[f]
        return (coefs[f, 0] * v + coefs[f, 1] * pltpu.roll(v, strip - 1, 0) + coefs[f, 2] * pltpu.roll(v, 1, 0)
                + coefs[f, 3] * north(v) + coefs[f, 4] * south(v) + mixed(mixing, f, values))

    return moved


def observed_bulk(sizes, state, noise, maps, courant, scalars, middle, out, weight, coefs, partial):
    particles, fields, strip, lats, strips = sizes
    zero_halo_coefs(sizes, courant, scalars, coefs)
    moved = zero_halo_step(sizes, scalars, coefs)

    def one(p):
        values = [state[p, f] for f in range(fields)]
        results = []
        for f in range(fields):
            new = moved(values, f)
            add = noise[0, p, f].astype(F32)
            if f == 0:
                push = maps[0] * (maps[1] - new)
                new = new + push
                total = push * (push + 2.0 * add)
            results.append(new + add)
            middle[p, f] = new + add
        new = moved(results, 0)
        add = noise[1, p, 0].astype(F32)
        push = maps[0] * (maps[1] - new)
        new = new + push + add
        miss = maps[1] - new
        total = (0.5 / noise_var) * (total + push * (push + 2.0 * add)) + (2.0 * maps[0]) * (miss * miss)
        out[p] = new
        partial[pl.ds(p, 1), :] = wide(jnp.sum(total, axis=0, keepdims=True))

    def body(pair, carry):
        one(2 * pair)
        one(2 * pair + 1)
        return carry

    lax.fori_loop(0, particles // 2, body, 0)
    weight[...] = in_row(partial[...])


def other_bulk(sizes, middle, observed, noise, scalars, coefs, out):
    particles, fields, strip, lats, strips = sizes
    moved = zero_halo_step(sizes, scalars, coefs)

    def body(p, carry):
        values = [middle[p, f] for f in range(fields)]
        out[p, 0] = observed[p]
        for f in range(1, fields):
            out[p, f] = moved(values, f) + noise[1, p, f].astype(F32)
        return carry

    lax.fori_loop(0, particles, body, 0)


def correct(sizes, own_east, own_west, from_west, from_east, scalars, bulk_weight, weight, changes):
    particles, fields, strip, lats, strips = sizes
    n = fields * particles
    diffusion, mixing = scalars_in(scalars, fields)

    def field_rows(ref, start, f):
        return ref[start + f * particles:start + (f + 1) * particles]

    packets = (own_east, from_east, own_west, from_west)
    last = 2 * n + 2 * particles
    zonal = stack_rows([ref[last + 2:last + 3] for ref in packets] + [ref[last + 5:last + 6] for ref in packets])
    merid = stack_rows([ref[last + 3:last + 4] for ref in packets] * 2)
    tile = [coefficients(zonal, merid, diffusion[0, f], mixing[f, f]) for f in range(fields)]
    total = jnp.zeros((particles, lats), F32)
    for k, owner in enumerate(packets):
        other_k = k ^ 1
        other = packets[other_k]
        outward_at = (1, 2, 2, 1)[k]
        outward_other = (1, 2, 2, 1)[other_k]
        gain = owner[last + 4:last + 5]
        gain_other = other[last + 4:last + 5]
        first = []
        for f in range(fields):
            step = tile[f][outward_at][k:k + 1] * field_rows(other, 0, f)
            first.append((1.0 - gain) * step if f == 0 else step)
        mine = k in (0, 2)
        for f in range(fields if mine else 1):
            centre, to_north, to_south = [tile[f][c][k:k + 1] for c in (0, 3, 4)]
            outward = tile[f][outward_at][k:k + 1]
            reach = tile[f][outward_other][other_k:other_k + 1]
            if f == 0:
                reach = (1.0 - gain_other) * reach
            outside = field_rows(other, n, f) + reach * field_rows(owner, 0, f)
            step = (centre * first[f] + outward * outside + to_north * north(first[f])
                    + to_south * south(first[f]) + mixed(mixing, f, first))
            if f == 0:
                seen = field_rows(other, 0, 0)
                slope, slope_step = owner[2 * n:2 * n + particles], owner[2 * n + particles:last]
                bend, bend_step = owner[last:last + 1], owner[last + 1:last + 2]
                total = total + seen * (slope + bend * seen) + step * (slope_step + bend_step * step)
            if mine:
                beside = tile[f][outward_at][4 + k:5 + k] * first[f]
                if f == 0:
                    step = (1.0 - gain) * step
                    beside = (1.0 - owner[last + 6:last + 7]) * beside
                edge, inner = (3, 2) if k == 0 else (0, 1)
                changes[edge, f * particles:(f + 1) * particles] = step
                changes[inner, f * particles:(f + 1) * particles] = beside
    weight[...] = in_row(wide(total)) + bulk_weight[...]


def apply_changes(sizes, current, changes, out):
    particles, fields, strip, lats, strips = sizes
    sub = lax.broadcasted_iota(jnp.int32, (8, lats), 0)
    for p in range(particles):
        for f in range(fields):
            row = f * particles + p
            rows = [jnp.broadcast_to(changes[k, row:row + 1], sub.shape) for k in range(4)]
            out[p, f, :8] = current[p, f, :8] + jnp.where(sub == 0, rows[0], jnp.where(sub == 1, rows[1], 0.0))
            out[p, f, 8:strip - 8] = current[p, f, 8:strip - 8]
            out[p, f, strip - 8:] = current[p, f, strip - 8:] + jnp.where(
                sub == 7, rows[3], jnp.where(sub == 6, rows[2], 0.0))


def assemble(sizes, source, current, received, out, sems):
    particles = sizes[0]
    dom = lax.axis_index("dom")

    def copy(j, ref, at):
        return pltpu.make_async_copy(ref.at[at], out.at[j], sems.at[j])

    for j in range(particles):
        wanted = source[dom * particles + j]
        mine = wanted // particles == dom
        at = wanted % particles

        @pl.when(mine)
        def _():
            copy(j, current, at).start()

        @pl.when(jnp.logical_not(mine))
        def _():
            copy(j, received, at).start()

    for j in range(particles):
        copy(j, current, 0).wait()


def local(ensemble_state, proposal_noise, courant, diffusion, mixing, prior_weight, obs_cell, obs_value, source):
    particles, fields, strip, lats = ensemble_state.shape
    strips = lax.axis_size("lon")
    sizes = (particles, fields, strip, lats, strips)
    packet = jax.ShapeDtypeStruct((2 * particles * fields + 2 * particles + 8, lats), F32)
    cell, value = obs_cell[None], obs_value[None]

    def shape(*dims):
        return jax.ShapeDtypeStruct(dims, F32)

    whole = (particles, fields, strip, lats)

    def in_hbm(array):
        return pltpu.with_memory_space_constraint(array, pltpu.HBM)

    arrays = (ensemble_state, proposal_noise, courant, diffusion[None], mixing, cell, value)
    send_east, send_west, state, noise, maps, courant, scalars = pl.pallas_call(
        functools.partial(prepare, sizes),
        out_shape=(packet, packet, shape(*whole), jax.ShapeDtypeStruct((2,) + whole, BF16), shape(2, strip, lats),
                   shape(*courant.shape), shape(fields * (fields + 2), lats)),
        in_specs=[HBM] * 7,
        out_specs=(VMEM,) * 7,
        scratch_shapes=[pltpu.VMEM(array.shape, array.dtype) for array in arrays[3:]]
        + [pltpu.SemaphoreType.DMA((11,))],
        compiler_params=LIMIT,
        cost_estimate=pl.CostEstimate(flops=1000000, bytes_accessed=2000000, transcendentals=0),
    )(*[in_hbm(array) for array in arrays])

    eastward = [(i, (i + 1) % strips) for i in range(strips)]
    westward = [(i, (i - 1) % strips) for i in range(strips)]
    from_west = lax.ppermute(send_east, "lon", eastward)

    middle, observed, bulk_weight, coefs = pl.pallas_call(
        functools.partial(observed_bulk, sizes),
        out_shape=(shape(*whole), shape(particles, strip, lats), shape(1, 128), shape(fields, 5, strip, lats)),
        in_specs=[VMEM] * 5,
        out_specs=(VMEM,) * 4,
        scratch_shapes=[pltpu.VMEM((particles, 128), F32)],
        compiler_params=LIMIT,
        cost_estimate=pl.CostEstimate(flops=20000000, bytes_accessed=4000000, transcendentals=0),
    )(state, noise, maps, courant, scalars)
    send_west, bulk_weight = lax.optimization_barrier((send_west, bulk_weight))
    from_east = lax.ppermute(send_west, "lon", westward)
    beside = lax.ppermute(bulk_weight, "lon", [(i, i ^ 1) for i in range(strips)])

    weight, changes = pl.pallas_call(
        functools.partial(correct, sizes),
        out_shape=(shape(1, 128), shape(4, particles * fields, lats)),
        in_specs=[VMEM] * 6,
        out_specs=(VMEM,) * 2,
        compiler_params=LIMIT,
        cost_estimate=FREE,
    )(send_east, send_west, from_west, from_east, scalars, bulk_weight)

    middle, from_west = lax.optimization_barrier((middle, from_west))
    current = pl.pallas_call(
        functools.partial(other_bulk, sizes),
        out_shape=shape(*whole),
        in_specs=[VMEM] * 5,
        out_specs=VMEM,
        compiler_params=LIMIT,
        cost_estimate=pl.CostEstimate(flops=10000000, bytes_accessed=4000000, transcendentals=0),
    )(middle, observed, noise, scalars, coefs)

    current = pl.pallas_call(
        functools.partial(apply_changes, sizes),
        out_shape=shape(*whole),
        in_specs=[VMEM] * 2,
        out_specs=VMEM,
        compiler_params=LIMIT,
        cost_estimate=FREE,
    )(current, changes)

    current, beside = lax.optimization_barrier((current, beside))
    weight = weight + beside
    received = lax.ppermute(current, "dom", [(0, 1), (1, 0)])
    bit = 2
    while bit < strips:
        if 2 * bit >= strips:
            weight, received = lax.optimization_barrier((weight, received))
        weight = weight + lax.ppermute(weight, "lon", [(i, i ^ bit) for i in range(strips)])
        bit *= 2

    new_state = pl.pallas_call(
        functools.partial(assemble, sizes),
        out_shape=shape(*whole),
        in_specs=[SMEM, VMEM, VMEM],
        out_specs=HBM,
        scratch_shapes=[pltpu.SemaphoreType.DMA((particles,))],
        compiler_params=LIMIT,
        cost_estimate=pl.CostEstimate(flops=0, bytes_accessed=2000000, transcendentals=0),
    )(source, current, received)

    log_weight = prior_weight - weight[0, :particles] / (256.0 * obs_cell.shape[0])
    return new_state, log_weight


def solution(mesh):
    placed = (
        P(("groups", "dom"), None, "lon", None),
        P(None, ("groups", "dom"), None, "lon", None),
        P(None, ("groups", "lon"), None),
        P(),
        P(),
        P(("groups", "dom")),
        P(("groups", "lon")),
        P(("groups", "lon")),
        P("groups"),
    )
    return jax.shard_map(
        local,
        mesh=mesh,
        in_specs=placed,
        out_specs=(P(("groups", "dom"), None, "lon", None), P(("groups", "dom"))),
        check_vma=False,
    )
```

```python
import functools

import jax
import jax.numpy as jnp
from jax import lax
from jax.experimental import pallas as pl
from jax.experimental.pallas import tpu as pltpu
from jax.sharding import PartitionSpec as P

noise_var = 0.04
VMEM = pl.BlockSpec(memory_space=pltpu.VMEM)
SMEM = pl.BlockSpec(memory_space=pltpu.SMEM)
HBM = pl.BlockSpec(memory_space=pltpu.HBM)
LIMIT = pltpu.CompilerParams(vmem_limit_bytes=16 * 1024 * 1024)
FREE = pl.CostEstimate(flops=0, bytes_accessed=0, transcendentals=0)
BF16 = jnp.bfloat16
F32 = jnp.float32


def north(v):
    return pltpu.roll(v, v.shape[1] - 1, 1)


def south(v):
    return pltpu.roll(v, 1, 1)


def coefficients(zonal, merid, rate, self_mix):
    lat = lax.broadcasted_iota(jnp.int32, zonal.shape, 1)
    zonal_half, zonal_rate = 0.5 * zonal, 0.5 * zonal * zonal + rate
    merid_half, merid_rate = 0.5 * merid, 0.5 * merid * merid + rate
    east, west = zonal_rate - zonal_half, zonal_rate + zonal_half
    to_north, to_south = merid_rate - merid_half, merid_rate + merid_half
    centre = 1.0 + self_mix - 2.0 * zonal_rate - 2.0 * merid_rate
    last, first = lat == zonal.shape[1] - 1, lat == 0
    centre = centre + jnp.where(last, to_north, 0.0) + jnp.where(first, to_south, 0.0)
    to_north = jnp.where(last, 0.0, to_north)
    to_south = jnp.where(first, 0.0, to_south)
    return centre, east, west, to_north, to_south


def mixed(mixing, field, values):
    total = None
    for other, value in enumerate(values):
        if other != field:
            term = mixing[field, other] * value
            total = term if total is None else total + term
    return total


def pick_rows(kinds, particles, fields, strip):
    shape = (particles, particles * fields * strip)
    place = lax.broadcasted_iota(jnp.int32, shape, 1) - lax.broadcasted_iota(jnp.int32, shape, 0) * (fields * strip)
    blocks = [jnp.where(place == f * strip + x, 1.0, 0.0) for f, x in kinds]
    return jnp.concatenate(blocks, 0).astype(BF16)


def stack_rows(rows):
    sub = lax.broadcasted_iota(jnp.int32, (len(rows), rows[0].shape[1]), 0)
    out = None
    for p, row in enumerate(rows):
        row = jnp.broadcast_to(row, sub.shape)
        out = row if out is None else jnp.where(sub == p, row, out)
    return out


def in_row(column):
    total = jnp.broadcast_to(jnp.sum(column, axis=1, keepdims=True), column.shape)
    diagonal = lax.broadcasted_iota(jnp.int32, total.shape, 0) == lax.broadcasted_iota(jnp.int32, total.shape, 1)
    return jnp.sum(jnp.where(diagonal, total, 0.0), axis=0, keepdims=True)


def wide(v):
    return v[:, :128] + v[:, 128:]


def observation_maps(sizes, cell, value):
    particles, fields, strip, lats, strips = sizes
    x0 = lax.axis_index("lon") * strip
    shift = lats.bit_length() - 1
    local_cell = cell - x0 * lats
    obs_lon = lax.shift_right_arithmetic(local_cell, shift)
    obs_lat = local_cell & (lats - 1)
    count = cell.shape[1]
    here = lax.broadcasted_iota(jnp.int32, (strip, count), 0) == obs_lon
    high = value.astype(BF16)
    rest = value - high.astype(F32)
    mid = rest.astype(BF16)
    low = (rest - mid.astype(F32)).astype(BF16)
    zero = jnp.zeros((strip, count), F32)
    parts = [jnp.where(here, 1.0, zero)]
    parts += [jnp.where(here, p.astype(F32), zero) for p in (high, mid, low)]
    left = jnp.concatenate(parts, 0).astype(BF16)
    right = (lax.broadcasted_iota(jnp.int32, (lats, count), 0) == obs_lat).astype(F32).astype(BF16)
    dense = lax.dot_general(left, right, (((1,), (1,)), ((), ())), preferred_element_type=F32)
    lon = (lax.broadcasted_iota(jnp.int32, (strip, lats), 0) + x0).astype(F32)
    precision = 1.0 + 2.0 * lon / (strip * strips)
    target = dense[strip:2 * strip] + (dense[2 * strip:3 * strip] + dense[3 * strip:])
    return dense[:strip] * (0.25 * precision), target


class Rows:
    def __init__(self, ref, first, columns):
        self.ref, self.first, self.columns = ref, first, columns

    def __getitem__(self, at):
        row = self.first + at[0] * self.columns + at[1]
        return self.ref[row:row + 1]


def scalars_in(ref, fields):
    return Rows(ref, fields * fields, fields), Rows(ref, 0, fields)


def prepare(sizes, state_hbm, noise_hbm, courant_hbm, diffusion_hbm, mixing_hbm, cell_hbm, value_hbm,
            send_east, send_west, state, noise, maps, courant, scalars,
            diffusion, mixing, cell, value, sems):
    particles, fields, strip, lats, strips = sizes
    n = fields * particles
    copies = [pltpu.make_async_copy(source, target, sems.at[k]) for k, (source, target) in enumerate((
        (cell_hbm, cell), (value_hbm, value), (courant_hbm, courant), (diffusion_hbm, diffusion),
        (mixing_hbm, mixing), (state_hbm.at[:, :, :8], state.at[:, :, :8]),
        (state_hbm.at[:, :, strip - 8:], state.at[:, :, strip - 8:]), (noise_hbm.at[0], noise.at[0]),
        (noise_hbm.at[1, :, 0], noise.at[1, :, 0]), (state_hbm.at[:, :, 8:strip - 8], state.at[:, :, 8:strip - 8]),
        (noise_hbm.at[1, :, 1:], noise.at[1, :, 1:])))]
    for copy in copies:
        copy.start()
    copies[0].wait()
    copies[1].wait()
    gain, target = observation_maps(sizes, cell[...], value[...])
    maps[0], maps[1] = gain, target
    kinds = []
    for x, step in ((strip - 1, -1), (0, 1)):
        kinds += [(f, x) for f in range(fields)] + [(f, x + step) for f in range(fields)] + [(0, x + 2 * step)]
    pick0 = pick_rows(kinds, particles, fields, strip)
    pick1 = pick_rows([(0, x) for x in (strip - 1, strip - 2, 0, 1)], particles, 1, strip)
    for copy in copies[2:5]:
        copy.wait()
    for f in range(fields):
        for g in range(fields):
            scalars[f * fields + g:f * fields + g + 1] = jnp.broadcast_to(mixing[f:f + 1, g:g + 1], (1, lats))
        at = fields * fields + f
        scalars[at:at + 1] = jnp.broadcast_to(diffusion[:, f:f + 1], (1, lats))
    diffusion, mixing = scalars_in(scalars, fields)

    sides = []
    for first, inward, outward in ((strip - 8, 2, 1), (0, 1, 2)):
        tile = [coefficients(courant[0, first:first + 8], courant[1, first:first + 8], diffusion[0, f], mixing[f, f])
                for f in range(fields)]
        sides.append([[c[0], c[inward], c[outward], c[3], c[4]] for c in tile])
    def coefs_at(side, f, k):
        at = places[side][0] + k * places[side][2] - places[side][1]
        return [c[at:at + 1] for c in sides[side][f]]

    def maps_at(side, k):
        at = places[side][0] + k * places[side][2]
        return gain[at:at + 1], target[at:at + 1]

    def moved(side, f, k, here, inner, outer):
        centre, inward, outward, to_north, to_south = coefs_at(side, f, k)
        v = here[f]
        total = centre * v + inward * inner + to_north * north(v) + to_south * south(v) + mixed(mixing, f, here)
        return total if outer is None else total + outward * outer

    def nudged(side, value, k):
        g, v = maps_at(side, k)
        push = g * (v - value)
        return value + push, push

    def first_step(side, out):
        def state_at(f, k):
            at = places[side][0] + k * places[side][2]
            return stack_rows([state[p, f, at:at + 1] for p in range(particles)])

        near = [[state_at(f, k) for f in range(fields)] for k in range(3)]
        third = state_at(0, 3)
        for f in range(fields):
            out[f * particles:(f + 1) * particles] = near[0][f]
        result, pushes = [[], []], []
        for k in range(2):
            for f in range(fields):
                new = moved(side, f, k, near[k], near[k + 1][f], near[k - 1][f] if k else None)
                if f == 0:
                    new, push = nudged(side, new, k)
                    pushes.append(push)
                result[k].append(new)
        inside, _ = nudged(side, moved(side, 0, 2, near[2], third, near[1][0]), 2)
        return result, pushes, inside

    places = ((strip - 1, strip - 8, -1), (0, 0, 1))
    copies[5].wait()
    copies[6].wait()
    started = [first_step(0, send_east), first_step(1, send_west)]
    copies[7].wait()
    copies[8].wait()
    rows0 = jnp.dot(pick0, noise[0].reshape(n * strip, lats), preferred_element_type=F32)
    rows1 = jnp.dot(pick1, noise[1, :, 0].reshape(particles * strip, lats), preferred_element_type=F32)

    def edge(side, out):
        x, _, step = places[side]
        base0, base1 = side * (2 * fields + 1) * particles, side * 2 * particles
        result, pushes, inside = started[side]

        def noisy0(k, f):
            at = base0 + (k * fields + f) * particles
            return rows0[at:at + particles]

        def noisy1(k):
            at = base1 + k * particles
            return rows1[at:at + particles]

        result = [[result[k][f] + noisy0(k, f) for f in range(fields)] for k in range(2)]
        inside = inside + noisy0(2, 0)
        g0, _ = maps_at(side, 0)
        g1, _ = maps_at(side, 1)
        slope = [-(1.0 / noise_var) * g0 * (pushes[0] + noisy0(0, 0))]
        bend = [(0.5 / noise_var) * g0 * g0]
        for k, g in enumerate((g0, g1)):
            new = moved(side, 0, k, result[k], result[1][0] if k == 0 else inside, result[0][0] if k else None)
            new, push = nudged(side, new, k)
            miss = maps_at(side, k)[1] - (new + noisy1(k))
            weight = 4.0 * g
            slope.append(-(1.0 / noise_var) * g * (push + noisy1(k)) - weight * (1.0 - g) * miss)
            bend.append((0.5 / noise_var) * g * g + 0.5 * weight * (1.0 - g) * (1.0 - g))
        outward = coefs_at(side, 0, 0)[2]
        onward = coefs_at(side, 0, 1)[2] * (1.0 - g0) * outward
        for f in range(fields):
            out[n + f * particles:n + (f + 1) * particles] = result[0][f]
        out[2 * n:2 * n + particles] = outward * slope[0] + onward * slope[2]
        out[2 * n + particles:2 * n + 2 * particles] = slope[1]
        inner = x + step
        last = (outward * outward * bend[0] + onward * onward * bend[2], bend[1],
                courant[0, x:x + 1], courant[1, x:x + 1], g0, courant[0, inner:inner + 1], g1,
                jnp.zeros((1, lats), F32))
        out[2 * n + 2 * particles:] = stack_rows(last)

    edge(0, send_east)
    edge(1, send_west)
    copies[9].wait()
    copies[10].wait()


def zero_halo_coefs(sizes, courant, scalars, coefs):
    particles, fields, strip, lats, strips = sizes
    diffusion, mixing = scalars_in(scalars, fields)
    lon = lax.broadcasted_iota(jnp.int32, (strip, lats), 0)
    for f in range(fields):
        centre, east, west, to_north, to_south = coefficients(
            courant[0], courant[1], diffusion[0, f], mixing[f, f])
        coefs[f, 0] = centre
        coefs[f, 1] = jnp.where(lon == strip - 1, 0.0, east)
        coefs[f, 2] = jnp.where(lon == 0, 0.0, west)
        coefs[f, 3] = to_north
        coefs[f, 4] = to_south


def zero_halo_step(sizes, scalars, coefs):
    particles, fields, strip, lats, strips = sizes
    _, mixing = scalars_in(scalars, fields)

    def moved(values, f):
        v = values[f]
        return (coefs[f, 0] * v + coefs[f, 1] * pltpu.roll(v, strip - 1, 0) + coefs[f, 2] * pltpu.roll(v, 1, 0)
                + coefs[f, 3] * north(v) + coefs[f, 4] * south(v) + mixed(mixing, f, values))

    return moved


def observed_bulk(sizes, parity, state, noise, maps, courant, scalars, earlier, middle, out, weight, coefs, partial):
    particles, fields, strip, lats, strips = sizes

    def one(p):
        moved = zero_halo_step(sizes, scalars, coefs)
        values = [state[p, f] for f in range(fields)]
        results = []
        for f in range(fields):
            new = moved(values, f)
            add = noise[0, p, f].astype(F32)
            if f == 0:
                push = maps[0] * (maps[1] - new)
                new = new + push
                total = push * (push + 2.0 * add)
            results.append(new + add)
            middle[p, f] = new + add
        new = moved(results, 0)
        add = noise[1, p, 0].astype(F32)
        push = maps[0] * (maps[1] - new)
        new = new + push + add
        miss = maps[1] - new
        total = (0.5 / noise_var) * (total + push * (push + 2.0 * add)) + (2.0 * maps[0]) * (miss * miss)
        out[p] = new
        partial[pl.ds(p, 1), :] = wide(jnp.sum(total, axis=0, keepdims=True))

    def body(pair, carry):
        one(2 * pair)
        one(2 * pair + 1)
        return carry

    here = lax.axis_index("lon") % 2 == parity

    @pl.when(here)
    def _():
        zero_halo_coefs(sizes, courant, scalars, coefs)
        lax.fori_loop(0, particles // 2, body, 0)
        weight[...] = in_row(partial[...])

    @pl.when(jnp.logical_not(here))
    def _():
        weight[...] = earlier[:1, :128]


def other_bulk(sizes, even_middle, even_observed, even_coefs, odd_middle, odd_observed, odd_coefs,
               noise, scalars, out):
    particles, fields, strip, lats, strips = sizes

    def run(middle, observed, coefs):
        moved = zero_halo_step(sizes, scalars, coefs)

        def body(p, carry):
            values = [middle[p, f] for f in range(fields)]
            out[p, 0] = observed[p]
            for f in range(1, fields):
                out[p, f] = moved(values, f) + noise[1, p, f].astype(F32)
            return carry

        lax.fori_loop(0, particles, body, 0)

    even = lax.axis_index("lon") % 2 == 0

    @pl.when(even)
    def _():
        run(even_middle, even_observed, even_coefs)

    @pl.when(jnp.logical_not(even))
    def _():
        run(odd_middle, odd_observed, odd_coefs)


def correct(sizes, own_east, own_west, from_west, from_east, scalars, bulk_weight, weight, changes):
    particles, fields, strip, lats, strips = sizes
    n = fields * particles
    diffusion, mixing = scalars_in(scalars, fields)

    def field_rows(ref, start, f):
        return ref[start + f * particles:start + (f + 1) * particles]

    packets = (own_east, from_east, own_west, from_west)
    last = 2 * n + 2 * particles
    zonal = stack_rows([ref[last + 2:last + 3] for ref in packets] + [ref[last + 5:last + 6] for ref in packets])
    merid = stack_rows([ref[last + 3:last + 4] for ref in packets] * 2)
    tile = [coefficients(zonal, merid, diffusion[0, f], mixing[f, f]) for f in range(fields)]
    total = jnp.zeros((particles, lats), F32)
    for k, owner in enumerate(packets):
        other_k = k ^ 1
        other = packets[other_k]
        outward_at = (1, 2, 2, 1)[k]
        outward_other = (1, 2, 2, 1)[other_k]
        gain = owner[last + 4:last + 5]
        gain_other = other[last + 4:last + 5]
        first = []
        for f in range(fields):
            step = tile[f][outward_at][k:k + 1] * field_rows(other, 0, f)
            first.append((1.0 - gain) * step if f == 0 else step)
        mine = k in (0, 2)
        for f in range(fields if mine else 1):
            centre, to_north, to_south = [tile[f][c][k:k + 1] for c in (0, 3, 4)]
            outward = tile[f][outward_at][k:k + 1]
            reach = tile[f][outward_other][other_k:other_k + 1]
            if f == 0:
                reach = (1.0 - gain_other) * reach
            outside = field_rows(other, n, f) + reach * field_rows(owner, 0, f)
            step = (centre * first[f] + outward * outside + to_north * north(first[f])
                    + to_south * south(first[f]) + mixed(mixing, f, first))
            if f == 0:
                seen = field_rows(other, 0, 0)
                slope, slope_step = owner[2 * n:2 * n + particles], owner[2 * n + particles:last]
                bend, bend_step = owner[last:last + 1], owner[last + 1:last + 2]
                total = total + seen * (slope + bend * seen) + step * (slope_step + bend_step * step)
            if mine:
                beside = tile[f][outward_at][4 + k:5 + k] * first[f]
                if f == 0:
                    step = (1.0 - gain) * step
                    beside = (1.0 - owner[last + 6:last + 7]) * beside
                edge, inner = (3, 2) if k == 0 else (0, 1)
                changes[edge, f * particles:(f + 1) * particles] = step
                changes[inner, f * particles:(f + 1) * particles] = beside
    weight[...] = in_row(wide(total)) + bulk_weight[...]


def apply_changes(sizes, current, changes, out):
    particles, fields, strip, lats, strips = sizes
    sub = lax.broadcasted_iota(jnp.int32, (8, lats), 0)
    for p in range(particles):
        for f in range(fields):
            row = f * particles + p
            rows = [jnp.broadcast_to(changes[k, row:row + 1], sub.shape) for k in range(4)]
            out[p, f, :8] = current[p, f, :8] + jnp.where(sub == 0, rows[0], jnp.where(sub == 1, rows[1], 0.0))
            out[p, f, 8:strip - 8] = current[p, f, 8:strip - 8]
            out[p, f, strip - 8:] = current[p, f, strip - 8:] + jnp.where(
                sub == 7, rows[3], jnp.where(sub == 6, rows[2], 0.0))


def assemble(sizes, source, current, received, out, sems):
    particles = sizes[0]
    dom = lax.axis_index("dom")

    def copy(j, ref, at):
        return pltpu.make_async_copy(ref.at[at], out.at[j], sems.at[j])

    for j in range(particles):
        wanted = source[dom * particles + j]
        mine = wanted // particles == dom
        at = wanted % particles

        @pl.when(mine)
        def _():
            copy(j, current, at).start()

        @pl.when(jnp.logical_not(mine))
        def _():
            copy(j, received, at).start()

    for j in range(particles):
        copy(j, current, 0).wait()


def local(ensemble_state, proposal_noise, courant, diffusion, mixing, prior_weight, obs_cell, obs_value, source):
    particles, fields, strip, lats = ensemble_state.shape
    strips = lax.axis_size("lon")
    sizes = (particles, fields, strip, lats, strips)
    packet = jax.ShapeDtypeStruct((2 * particles * fields + 2 * particles + 8, lats), F32)
    cell, value = obs_cell[None], obs_value[None]

    def shape(*dims):
        return jax.ShapeDtypeStruct(dims, F32)

    whole = (particles, fields, strip, lats)

    def in_hbm(array):
        return pltpu.with_memory_space_constraint(array, pltpu.HBM)

    arrays = (ensemble_state, proposal_noise, courant, diffusion[None], mixing, cell, value)
    send_east, send_west, state, noise, maps, courant, scalars = pl.pallas_call(
        functools.partial(prepare, sizes),
        out_shape=(packet, packet, shape(*whole), jax.ShapeDtypeStruct((2,) + whole, BF16), shape(2, strip, lats),
                   shape(*courant.shape), shape(fields * (fields + 2), lats)),
        in_specs=[HBM] * 7,
        out_specs=(VMEM,) * 7,
        scratch_shapes=[pltpu.VMEM(array.shape, array.dtype) for array in arrays[3:]]
        + [pltpu.SemaphoreType.DMA((11,))],
        compiler_params=LIMIT,
        cost_estimate=pl.CostEstimate(flops=1000000, bytes_accessed=2000000, transcendentals=0),
    )(*[in_hbm(array) for array in arrays])

    def bulk_of(parity, earlier):
        return pl.pallas_call(
            functools.partial(observed_bulk, sizes, parity),
            out_shape=(shape(*whole), shape(particles, strip, lats), shape(1, 128), shape(fields, 5, strip, lats)),
            in_specs=[VMEM] * 6,
            out_specs=(VMEM,) * 4,
            scratch_shapes=[pltpu.VMEM((particles, 128), F32)],
            compiler_params=LIMIT,
            cost_estimate=pl.CostEstimate(flops=20000000, bytes_accessed=4000000, transcendentals=0),
        )(state, noise, maps, courant, scalars, earlier)

    even_middle, even_observed, bulk_weight, even_coefs = bulk_of(0, scalars)
    send_east, send_west, bulk_weight = lax.optimization_barrier((send_east, send_west, bulk_weight))
    eastward = [(i, (i + 1) % strips) for i in range(strips)]
    westward = [(i, (i - 1) % strips) for i in range(strips)]
    from_west = lax.ppermute(send_east, "lon", eastward)
    from_east = lax.ppermute(send_west, "lon", westward)
    odd_middle, odd_observed, bulk_weight, odd_coefs = bulk_of(1, bulk_weight)
    beside = lax.ppermute(bulk_weight, "lon", [(i, i ^ 1) for i in range(strips)])

    current = pl.pallas_call(
        functools.partial(other_bulk, sizes),
        out_shape=shape(*whole),
        in_specs=[VMEM] * 8,
        out_specs=VMEM,
        compiler_params=LIMIT,
        cost_estimate=FREE,
    )(even_middle, even_observed, even_coefs, odd_middle, odd_observed, odd_coefs, noise, scalars)

    weight, changes = pl.pallas_call(
        functools.partial(correct, sizes),
        out_shape=(shape(1, 128), shape(4, particles * fields, lats)),
        in_specs=[VMEM] * 6,
        out_specs=(VMEM,) * 2,
        compiler_params=LIMIT,
        cost_estimate=FREE,
    )(send_east, send_west, from_west, from_east, scalars, bulk_weight)

    current = pl.pallas_call(
        functools.partial(apply_changes, sizes),
        out_shape=shape(*whole),
        in_specs=[VMEM] * 2,
        out_specs=VMEM,
        compiler_params=LIMIT,
        cost_estimate=FREE,
    )(current, changes)

    current, beside = lax.optimization_barrier((current, beside))
    weight = weight + beside
    received = lax.ppermute(current, "dom", [(0, 1), (1, 0)])
    bit = 2
    while bit < strips:
        if 2 * bit >= strips:
            weight, received = lax.optimization_barrier((weight, received))
        weight = weight + lax.ppermute(weight, "lon", [(i, i ^ bit) for i in range(strips)])
        bit *= 2

    new_state = pl.pallas_call(
        functools.partial(assemble, sizes),
        out_shape=shape(*whole),
        in_specs=[SMEM, VMEM, VMEM],
        out_specs=HBM,
        scratch_shapes=[pltpu.SemaphoreType.DMA((particles,))],
        compiler_params=LIMIT,
        cost_estimate=pl.CostEstimate(flops=0, bytes_accessed=2000000, transcendentals=0),
    )(source, current, received)

    log_weight = prior_weight - weight[0, :particles] / (256.0 * obs_cell.shape[0])
    return new_state, log_weight


def solution(mesh):
    placed = (
        P(("groups", "dom"), None, "lon", None),
        P(None, ("groups", "dom"), None, "lon", None),
        P(None, ("groups", "lon"), None),
        P(),
        P(),
        P(("groups", "dom")),
        P(("groups", "lon")),
        P(("groups", "lon")),
        P("groups"),
    )
    return jax.shard_map(
        local,
        mesh=mesh,
        in_specs=placed,
        out_specs=(P(("groups", "dom"), None, "lon", None), P(("groups", "dom"))),
        check_vma=False,
    )
```

```python
import functools

import jax
import jax.numpy as jnp
from jax import lax
from jax.experimental import pallas as pl
from jax.experimental.pallas import tpu as pltpu
from jax.sharding import PartitionSpec as P

noise_var = 0.04
VMEM = pl.BlockSpec(memory_space=pltpu.VMEM)
SMEM = pl.BlockSpec(memory_space=pltpu.SMEM)
HBM = pl.BlockSpec(memory_space=pltpu.HBM)
LIMIT = pltpu.CompilerParams(vmem_limit_bytes=16 * 1024 * 1024)
FREE = pl.CostEstimate(flops=0, bytes_accessed=0, transcendentals=0)
BF16 = jnp.bfloat16
F32 = jnp.float32


def north(v):
    return pltpu.roll(v, v.shape[1] - 1, 1)


def south(v):
    return pltpu.roll(v, 1, 1)


def coefficients(zonal, merid, rate, self_mix):
    lat = lax.broadcasted_iota(jnp.int32, zonal.shape, 1)
    zonal_half, zonal_rate = 0.5 * zonal, 0.5 * zonal * zonal + rate
    merid_half, merid_rate = 0.5 * merid, 0.5 * merid * merid + rate
    east, west = zonal_rate - zonal_half, zonal_rate + zonal_half
    to_north, to_south = merid_rate - merid_half, merid_rate + merid_half
    centre = 1.0 + self_mix - 2.0 * zonal_rate - 2.0 * merid_rate
    last, first = lat == zonal.shape[1] - 1, lat == 0
    centre = centre + jnp.where(last, to_north, 0.0) + jnp.where(first, to_south, 0.0)
    to_north = jnp.where(last, 0.0, to_north)
    to_south = jnp.where(first, 0.0, to_south)
    return centre, east, west, to_north, to_south


def mixed(mixing, field, values):
    total = None
    for other, value in enumerate(values):
        if other != field:
            term = mixing[field, other] * value
            total = term if total is None else total + term
    return total


def pick_rows(kinds, particles, fields, strip):
    shape = (particles, particles * fields * strip)
    place = lax.broadcasted_iota(jnp.int32, shape, 1) - lax.broadcasted_iota(jnp.int32, shape, 0) * (fields * strip)
    blocks = [jnp.where(place == f * strip + x, 1.0, 0.0) for f, x in kinds]
    return jnp.concatenate(blocks, 0).astype(BF16)


def stack_rows(rows):
    sub = lax.broadcasted_iota(jnp.int32, (len(rows), rows[0].shape[1]), 0)
    out = None
    for p, row in enumerate(rows):
        row = jnp.broadcast_to(row, sub.shape)
        out = row if out is None else jnp.where(sub == p, row, out)
    return out


def in_row(column):
    total = jnp.broadcast_to(jnp.sum(column, axis=1, keepdims=True), column.shape)
    diagonal = lax.broadcasted_iota(jnp.int32, total.shape, 0) == lax.broadcasted_iota(jnp.int32, total.shape, 1)
    return jnp.sum(jnp.where(diagonal, total, 0.0), axis=0, keepdims=True)


def wide(v):
    return v[:, :128] + v[:, 128:]


def observation_maps(sizes, cell, value):
    particles, fields, strip, lats, strips = sizes
    x0 = lax.axis_index("lon") * strip
    shift = lats.bit_length() - 1
    local_cell = cell - x0 * lats
    obs_lon = lax.shift_right_arithmetic(local_cell, shift)
    obs_lat = local_cell & (lats - 1)
    count = cell.shape[1]
    here = lax.broadcasted_iota(jnp.int32, (strip, count), 0) == obs_lon
    high = value.astype(BF16)
    rest = value - high.astype(F32)
    mid = rest.astype(BF16)
    low = (rest - mid.astype(F32)).astype(BF16)
    zero = jnp.zeros((strip, count), F32)
    parts = [jnp.where(here, 1.0, zero)]
    parts += [jnp.where(here, p.astype(F32), zero) for p in (high, mid, low)]
    left = jnp.concatenate(parts, 0).astype(BF16)
    right = (lax.broadcasted_iota(jnp.int32, (lats, count), 0) == obs_lat).astype(F32).astype(BF16)
    dense = lax.dot_general(left, right, (((1,), (1,)), ((), ())), preferred_element_type=F32)
    lon = (lax.broadcasted_iota(jnp.int32, (strip, lats), 0) + x0).astype(F32)
    precision = 1.0 + 2.0 * lon / (strip * strips)
    target = dense[strip:2 * strip] + (dense[2 * strip:3 * strip] + dense[3 * strip:])
    return dense[:strip] * (0.25 * precision), target


class Rows:
    def __init__(self, ref, first, columns):
        self.ref, self.first, self.columns = ref, first, columns

    def __getitem__(self, at):
        row = self.first + at[0] * self.columns + at[1]
        return self.ref[row:row + 1]


def scalars_in(ref, fields):
    return Rows(ref, fields * fields, fields), Rows(ref, 0, fields)


def prepare(sizes, state_hbm, noise_hbm, courant_hbm, diffusion_hbm, mixing_hbm, cell_hbm, value_hbm,
            send_east, send_west, state, noise, maps, courant, scalars,
            diffusion, mixing, cell, value, sems):
    particles, fields, strip, lats, strips = sizes
    n = fields * particles
    copies = [pltpu.make_async_copy(source, target, sems.at[k]) for k, (source, target) in enumerate((
        (cell_hbm, cell), (value_hbm, value), (courant_hbm, courant), (diffusion_hbm, diffusion),
        (mixing_hbm, mixing), (state_hbm.at[:, :, :8], state.at[:, :, :8]),
        (state_hbm.at[:, :, strip - 8:], state.at[:, :, strip - 8:]), (noise_hbm.at[0], noise.at[0]),
        (noise_hbm.at[1, :, 0], noise.at[1, :, 0]), (state_hbm.at[:, :, 8:strip - 8], state.at[:, :, 8:strip - 8]),
        (noise_hbm.at[1, :, 1:], noise.at[1, :, 1:])))]
    for copy in copies:
        copy.start()
    copies[0].wait()
    copies[1].wait()
    gain, target = observation_maps(sizes, cell[...], value[...])
    maps[0], maps[1] = gain, target
    kinds = []
    for x, step in ((strip - 1, -1), (0, 1)):
        kinds += [(f, x) for f in range(fields)] + [(f, x + step) for f in range(fields)] + [(0, x + 2 * step)]
    pick0 = pick_rows(kinds, particles, fields, strip)
    pick1 = pick_rows([(0, x) for x in (strip - 1, strip - 2, 0, 1)], particles, 1, strip)
    for copy in copies[2:5]:
        copy.wait()
    for f in range(fields):
        for g in range(fields):
            scalars[f * fields + g:f * fields + g + 1] = jnp.broadcast_to(mixing[f:f + 1, g:g + 1], (1, lats))
        at = fields * fields + f
        scalars[at:at + 1] = jnp.broadcast_to(diffusion[:, f:f + 1], (1, lats))
    diffusion, mixing = scalars_in(scalars, fields)

    sides = []
    for first, inward, outward in ((strip - 8, 2, 1), (0, 1, 2)):
        tile = [coefficients(courant[0, first:first + 8], courant[1, first:first + 8], diffusion[0, f], mixing[f, f])
                for f in range(fields)]
        sides.append([[c[0], c[inward], c[outward], c[3], c[4]] for c in tile])
    def coefs_at(side, f, k):
        at = places[side][0] + k * places[side][2] - places[side][1]
        return [c[at:at + 1] for c in sides[side][f]]

    def maps_at(side, k):
        at = places[side][0] + k * places[side][2]
        return gain[at:at + 1], target[at:at + 1]

    def moved(side, f, k, here, inner, outer):
        centre, inward, outward, to_north, to_south = coefs_at(side, f, k)
        v = here[f]
        total = centre * v + inward * inner + to_north * north(v) + to_south * south(v) + mixed(mixing, f, here)
        return total if outer is None else total + outward * outer

    def nudged(side, value, k):
        g, v = maps_at(side, k)
        push = g * (v - value)
        return value + push, push

    def first_step(side, out):
        def state_at(f, k):
            at = places[side][0] + k * places[side][2]
            return stack_rows([state[p, f, at:at + 1] for p in range(particles)])

        near = [[state_at(f, k) for f in range(fields)] for k in range(3)]
        third = state_at(0, 3)
        for f in range(fields):
            out[f * particles:(f + 1) * particles] = near[0][f]
        result, pushes = [[], []], []
        for k in range(2):
            for f in range(fields):
                new = moved(side, f, k, near[k], near[k + 1][f], near[k - 1][f] if k else None)
                if f == 0:
                    new, push = nudged(side, new, k)
                    pushes.append(push)
                result[k].append(new)
        inside, _ = nudged(side, moved(side, 0, 2, near[2], third, near[1][0]), 2)
        return result, pushes, inside

    places = ((strip - 1, strip - 8, -1), (0, 0, 1))
    copies[5].wait()
    copies[6].wait()
    started = [first_step(0, send_east), first_step(1, send_west)]
    copies[7].wait()
    copies[8].wait()
    rows0 = jnp.dot(pick0, noise[0].reshape(n * strip, lats), preferred_element_type=F32)
    rows1 = jnp.dot(pick1, noise[1, :, 0].reshape(particles * strip, lats), preferred_element_type=F32)

    def edge(side, out):
        x, _, step = places[side]
        base0, base1 = side * (2 * fields + 1) * particles, side * 2 * particles
        result, pushes, inside = started[side]

        def noisy0(k, f):
            at = base0 + (k * fields + f) * particles
            return rows0[at:at + particles]

        def noisy1(k):
            at = base1 + k * particles
            return rows1[at:at + particles]

        result = [[result[k][f] + noisy0(k, f) for f in range(fields)] for k in range(2)]
        inside = inside + noisy0(2, 0)
        g0, _ = maps_at(side, 0)
        g1, _ = maps_at(side, 1)
        slope = [-(1.0 / noise_var) * g0 * (pushes[0] + noisy0(0, 0))]
        bend = [(0.5 / noise_var) * g0 * g0]
        for k, g in enumerate((g0, g1)):
            new = moved(side, 0, k, result[k], result[1][0] if k == 0 else inside, result[0][0] if k else None)
            new, push = nudged(side, new, k)
            miss = maps_at(side, k)[1] - (new + noisy1(k))
            weight = 4.0 * g
            slope.append(-(1.0 / noise_var) * g * (push + noisy1(k)) - weight * (1.0 - g) * miss)
            bend.append((0.5 / noise_var) * g * g + 0.5 * weight * (1.0 - g) * (1.0 - g))
        outward = coefs_at(side, 0, 0)[2]
        onward = coefs_at(side, 0, 1)[2] * (1.0 - g0) * outward
        for f in range(fields):
            out[n + f * particles:n + (f + 1) * particles] = result[0][f]
        out[2 * n:2 * n + particles] = outward * slope[0] + onward * slope[2]
        out[2 * n + particles:2 * n + 2 * particles] = slope[1]
        inner = x + step
        last = (outward * outward * bend[0] + onward * onward * bend[2], bend[1],
                courant[0, x:x + 1], courant[1, x:x + 1], g0, courant[0, inner:inner + 1], g1,
                jnp.zeros((1, lats), F32))
        out[2 * n + 2 * particles:] = stack_rows(last)

    edge(0, send_east)
    edge(1, send_west)
    copies[9].wait()
    copies[10].wait()


def zero_halo_coefs(sizes, courant, scalars, coefs):
    particles, fields, strip, lats, strips = sizes
    diffusion, mixing = scalars_in(scalars, fields)
    lon = lax.broadcasted_iota(jnp.int32, (strip, lats), 0)
    for f in range(fields):
        centre, east, west, to_north, to_south = coefficients(
            courant[0], courant[1], diffusion[0, f], mixing[f, f])
        coefs[f, 0] = centre
        coefs[f, 1] = jnp.where(lon == strip - 1, 0.0, east)
        coefs[f, 2] = jnp.where(lon == 0, 0.0, west)
        coefs[f, 3] = to_north
        coefs[f, 4] = to_south


def zero_halo_step(sizes, scalars, coefs):
    particles, fields, strip, lats, strips = sizes
    _, mixing = scalars_in(scalars, fields)

    def moved(values, f):
        v = values[f]
        return (coefs[f, 0] * v + coefs[f, 1] * pltpu.roll(v, strip - 1, 0) + coefs[f, 2] * pltpu.roll(v, 1, 0)
                + coefs[f, 3] * north(v) + coefs[f, 4] * south(v) + mixed(mixing, f, values))

    return moved


def goes_first():
    return jnp.logical_or(lax.axis_index("lon") % 2 == 0, lax.axis_index("dom") == 1)


def observed_bulk(sizes, first, state, noise, maps, courant, scalars, earlier, middle, out, weight, coefs, partial):
    particles, fields, strip, lats, strips = sizes

    def one(p):
        moved = zero_halo_step(sizes, scalars, coefs)
        values = [state[p, f] for f in range(fields)]
        results = []
        for f in range(fields):
            new = moved(values, f)
            add = noise[0, p, f].astype(F32)
            if f == 0:
                push = maps[0] * (maps[1] - new)
                new = new + push
                total = push * (push + 2.0 * add)
            results.append(new + add)
            middle[p, f] = new + add
        new = moved(results, 0)
        add = noise[1, p, 0].astype(F32)
        push = maps[0] * (maps[1] - new)
        new = new + push + add
        miss = maps[1] - new
        total = (0.5 / noise_var) * (total + push * (push + 2.0 * add)) + (2.0 * maps[0]) * (miss * miss)
        out[p] = new
        partial[pl.ds(p, 1), :] = wide(jnp.sum(total, axis=0, keepdims=True))

    def body(pair, carry):
        one(2 * pair)
        one(2 * pair + 1)
        return carry

    here = goes_first() == first

    @pl.when(here)
    def _():
        zero_halo_coefs(sizes, courant, scalars, coefs)
        lax.fori_loop(0, particles // 2, body, 0)
        weight[...] = in_row(partial[...])

    @pl.when(jnp.logical_not(here))
    def _():
        weight[...] = earlier[:1, :128]


def other_bulk(sizes, early_middle, early_observed, early_coefs, late_middle, late_observed, late_coefs,
               noise, scalars, out):
    particles, fields, strip, lats, strips = sizes

    def run(middle, observed, coefs):
        moved = zero_halo_step(sizes, scalars, coefs)

        def body(p, carry):
            values = [middle[p, f] for f in range(fields)]
            out[p, 0] = observed[p]
            for f in range(1, fields):
                out[p, f] = moved(values, f) + noise[1, p, f].astype(F32)
            return carry

        lax.fori_loop(0, particles, body, 0)

    @pl.when(goes_first())
    def _():
        run(early_middle, early_observed, early_coefs)

    @pl.when(jnp.logical_not(goes_first()))
    def _():
        run(late_middle, late_observed, late_coefs)


def correct(sizes, own_east, own_west, from_west, from_east, scalars, bulk_weight, weight, changes):
    particles, fields, strip, lats, strips = sizes
    n = fields * particles
    diffusion, mixing = scalars_in(scalars, fields)

    def field_rows(ref, start, f):
        return ref[start + f * particles:start + (f + 1) * particles]

    packets = (own_east, from_east, own_west, from_west)
    last = 2 * n + 2 * particles
    zonal = stack_rows([ref[last + 2:last + 3] for ref in packets] + [ref[last + 5:last + 6] for ref in packets])
    merid = stack_rows([ref[last + 3:last + 4] for ref in packets] * 2)
    tile = [coefficients(zonal, merid, diffusion[0, f], mixing[f, f]) for f in range(fields)]
    total = jnp.zeros((particles, lats), F32)
    for k, owner in enumerate(packets):
        other_k = k ^ 1
        other = packets[other_k]
        outward_at = (1, 2, 2, 1)[k]
        outward_other = (1, 2, 2, 1)[other_k]
        gain = owner[last + 4:last + 5]
        gain_other = other[last + 4:last + 5]
        first = []
        for f in range(fields):
            step = tile[f][outward_at][k:k + 1] * field_rows(other, 0, f)
            first.append((1.0 - gain) * step if f == 0 else step)
        mine = k in (0, 2)
        for f in range(fields if mine else 1):
            centre, to_north, to_south = [tile[f][c][k:k + 1] for c in (0, 3, 4)]
            outward = tile[f][outward_at][k:k + 1]
            reach = tile[f][outward_other][other_k:other_k + 1]
            if f == 0:
                reach = (1.0 - gain_other) * reach
            outside = field_rows(other, n, f) + reach * field_rows(owner, 0, f)
            step = (centre * first[f] + outward * outside + to_north * north(first[f])
                    + to_south * south(first[f]) + mixed(mixing, f, first))
            if f == 0:
                seen = field_rows(other, 0, 0)
                slope, slope_step = owner[2 * n:2 * n + particles], owner[2 * n + particles:last]
                bend, bend_step = owner[last:last + 1], owner[last + 1:last + 2]
                total = total + seen * (slope + bend * seen) + step * (slope_step + bend_step * step)
            if mine:
                beside = tile[f][outward_at][4 + k:5 + k] * first[f]
                if f == 0:
                    step = (1.0 - gain) * step
                    beside = (1.0 - owner[last + 6:last + 7]) * beside
                edge, inner = (3, 2) if k == 0 else (0, 1)
                changes[edge, f * particles:(f + 1) * particles] = step
                changes[inner, f * particles:(f + 1) * particles] = beside
    weight[...] = in_row(wide(total)) + bulk_weight[...]


def apply_changes(sizes, current, changes, out):
    particles, fields, strip, lats, strips = sizes
    sub = lax.broadcasted_iota(jnp.int32, (8, lats), 0)
    for p in range(particles):
        for f in range(fields):
            row = f * particles + p
            rows = [jnp.broadcast_to(changes[k, row:row + 1], sub.shape) for k in range(4)]
            out[p, f, :8] = current[p, f, :8] + jnp.where(sub == 0, rows[0], jnp.where(sub == 1, rows[1], 0.0))
            out[p, f, 8:strip - 8] = current[p, f, 8:strip - 8]
            out[p, f, strip - 8:] = current[p, f, strip - 8:] + jnp.where(
                sub == 7, rows[3], jnp.where(sub == 6, rows[2], 0.0))


def assemble(sizes, source, current, received, out, sems):
    particles = sizes[0]
    dom = lax.axis_index("dom")

    def copy(j, ref, at):
        return pltpu.make_async_copy(ref.at[at], out.at[j], sems.at[j])

    for j in range(particles):
        wanted = source[dom * particles + j]
        mine = wanted // particles == dom
        at = wanted % particles

        @pl.when(mine)
        def _():
            copy(j, current, at).start()

        @pl.when(jnp.logical_not(mine))
        def _():
            copy(j, received, at).start()

    for j in range(particles):
        copy(j, current, 0).wait()


def local(ensemble_state, proposal_noise, courant, diffusion, mixing, prior_weight, obs_cell, obs_value, source):
    particles, fields, strip, lats = ensemble_state.shape
    strips = lax.axis_size("lon")
    sizes = (particles, fields, strip, lats, strips)
    packet = jax.ShapeDtypeStruct((2 * particles * fields + 2 * particles + 8, lats), F32)
    cell, value = obs_cell[None], obs_value[None]

    def shape(*dims):
        return jax.ShapeDtypeStruct(dims, F32)

    whole = (particles, fields, strip, lats)

    def in_hbm(array):
        return pltpu.with_memory_space_constraint(array, pltpu.HBM)

    arrays = (ensemble_state, proposal_noise, courant, diffusion[None], mixing, cell, value)
    send_east, send_west, state, noise, maps, courant, scalars = pl.pallas_call(
        functools.partial(prepare, sizes),
        out_shape=(packet, packet, shape(*whole), jax.ShapeDtypeStruct((2,) + whole, BF16), shape(2, strip, lats),
                   shape(*courant.shape), shape(fields * (fields + 2), lats)),
        in_specs=[HBM] * 7,
        out_specs=(VMEM,) * 7,
        scratch_shapes=[pltpu.VMEM(array.shape, array.dtype) for array in arrays[3:]]
        + [pltpu.SemaphoreType.DMA((11,))],
        compiler_params=LIMIT,
        cost_estimate=pl.CostEstimate(flops=1000000, bytes_accessed=2000000, transcendentals=0),
    )(*[in_hbm(array) for array in arrays])

    def bulk_of(first, earlier):
        return pl.pallas_call(
            functools.partial(observed_bulk, sizes, first),
            out_shape=(shape(*whole), shape(particles, strip, lats), shape(1, 128), shape(fields, 5, strip, lats)),
            in_specs=[VMEM] * 6,
            out_specs=(VMEM,) * 4,
            scratch_shapes=[pltpu.VMEM((particles, 128), F32)],
            compiler_params=LIMIT,
            cost_estimate=pl.CostEstimate(flops=20000000, bytes_accessed=4000000, transcendentals=0),
        )(state, noise, maps, courant, scalars, earlier)

    early_middle, early_observed, bulk_weight, early_coefs = bulk_of(True, scalars)
    send_east, send_west, bulk_weight = lax.optimization_barrier((send_east, send_west, bulk_weight))
    eastward = [(i, (i + 1) % strips) for i in range(strips)]
    westward = [(i, (i - 1) % strips) for i in range(strips)]
    from_west = lax.ppermute(send_east, "lon", eastward)
    from_east = lax.ppermute(send_west, "lon", westward)
    late_middle, late_observed, bulk_weight, late_coefs = bulk_of(False, bulk_weight)
    beside = lax.ppermute(bulk_weight, "lon", [(i, i ^ 1) for i in range(strips)])

    current = pl.pallas_call(
        functools.partial(other_bulk, sizes),
        out_shape=shape(*whole),
        in_specs=[VMEM] * 8,
        out_specs=VMEM,
        compiler_params=LIMIT,
        cost_estimate=FREE,
    )(early_middle, early_observed, early_coefs, late_middle, late_observed, late_coefs, noise, scalars)

    weight, changes = pl.pallas_call(
        functools.partial(correct, sizes),
        out_shape=(shape(1, 128), shape(4, particles * fields, lats)),
        in_specs=[VMEM] * 6,
        out_specs=(VMEM,) * 2,
        compiler_params=LIMIT,
        cost_estimate=FREE,
    )(send_east, send_west, from_west, from_east, scalars, bulk_weight)

    current = pl.pallas_call(
        functools.partial(apply_changes, sizes),
        out_shape=shape(*whole),
        in_specs=[VMEM] * 2,
        out_specs=VMEM,
        compiler_params=LIMIT,
        cost_estimate=FREE,
    )(current, changes)

    current, beside = lax.optimization_barrier((current, beside))
    weight = weight + beside
    received = lax.ppermute(current, "dom", [(0, 1), (1, 0)])
    bit = 2
    while bit < strips:
        if 2 * bit >= strips:
            weight, received = lax.optimization_barrier((weight, received))
        weight = weight + lax.ppermute(weight, "lon", [(i, i ^ bit) for i in range(strips)])
        bit *= 2

    new_state = pl.pallas_call(
        functools.partial(assemble, sizes),
        out_shape=shape(*whole),
        in_specs=[SMEM, VMEM, VMEM],
        out_specs=HBM,
        scratch_shapes=[pltpu.SemaphoreType.DMA((particles,))],
        compiler_params=LIMIT,
        cost_estimate=pl.CostEstimate(flops=0, bytes_accessed=2000000, transcendentals=0),
    )(source, current, received)

    log_weight = prior_weight - weight[0, :particles] / (256.0 * obs_cell.shape[0])
    return new_state, log_weight


def solution(mesh):
    placed = (
        P(("groups", "dom"), None, "lon", None),
        P(None, ("groups", "dom"), None, "lon", None),
        P(None, ("groups", "lon"), None),
        P(),
        P(),
        P(("groups", "dom")),
        P(("groups", "lon")),
        P(("groups", "lon")),
        P("groups"),
    )
    return jax.shard_map(
        local,
        mesh=mesh,
        in_specs=placed,
        out_specs=(P(("groups", "dom"), None, "lon", None), P(("groups", "dom"))),
        check_vma=False,
    )
```

```python
import functools

import jax
import jax.numpy as jnp
from jax import lax
from jax.experimental import pallas as pl
from jax.experimental.pallas import tpu as pltpu
from jax.sharding import PartitionSpec as P

noise_var = 0.04
VMEM = pl.BlockSpec(memory_space=pltpu.VMEM)
SMEM = pl.BlockSpec(memory_space=pltpu.SMEM)
HBM = pl.BlockSpec(memory_space=pltpu.HBM)
LIMIT = pltpu.CompilerParams(vmem_limit_bytes=16 * 1024 * 1024)
FREE = pl.CostEstimate(flops=0, bytes_accessed=0, transcendentals=0)
BF16 = jnp.bfloat16
F32 = jnp.float32


def north(v):
    return pltpu.roll(v, v.shape[1] - 1, 1)


def south(v):
    return pltpu.roll(v, 1, 1)


def coefficients(zonal, merid, rate, self_mix):
    lat = lax.broadcasted_iota(jnp.int32, zonal.shape, 1)
    zonal_half, zonal_rate = 0.5 * zonal, 0.5 * zonal * zonal + rate
    merid_half, merid_rate = 0.5 * merid, 0.5 * merid * merid + rate
    east, west = zonal_rate - zonal_half, zonal_rate + zonal_half
    to_north, to_south = merid_rate - merid_half, merid_rate + merid_half
    centre = 1.0 + self_mix - 2.0 * zonal_rate - 2.0 * merid_rate
    last, first = lat == zonal.shape[1] - 1, lat == 0
    centre = centre + jnp.where(last, to_north, 0.0) + jnp.where(first, to_south, 0.0)
    to_north = jnp.where(last, 0.0, to_north)
    to_south = jnp.where(first, 0.0, to_south)
    return centre, east, west, to_north, to_south


def mixed(mixing, field, values):
    total = None
    for other, value in enumerate(values):
        if other != field:
            term = mixing[field, other] * value
            total = term if total is None else total + term
    return total


def pick_rows(kinds, particles, fields, strip):
    shape = (particles, particles * fields * strip)
    place = lax.broadcasted_iota(jnp.int32, shape, 1) - lax.broadcasted_iota(jnp.int32, shape, 0) * (fields * strip)
    blocks = [jnp.where(place == f * strip + x, 1.0, 0.0) for f, x in kinds]
    return jnp.concatenate(blocks, 0).astype(BF16)


def stack_rows(rows):
    sub = lax.broadcasted_iota(jnp.int32, (len(rows), rows[0].shape[1]), 0)
    out = None
    for p, row in enumerate(rows):
        row = jnp.broadcast_to(row, sub.shape)
        out = row if out is None else jnp.where(sub == p, row, out)
    return out


def in_row(column):
    total = jnp.broadcast_to(jnp.sum(column, axis=1, keepdims=True), column.shape)
    diagonal = lax.broadcasted_iota(jnp.int32, total.shape, 0) == lax.broadcasted_iota(jnp.int32, total.shape, 1)
    return jnp.sum(jnp.where(diagonal, total, 0.0), axis=0, keepdims=True)


def wide(v):
    return v[:, :128] + v[:, 128:]


def observation_maps(sizes, cell, value):
    particles, fields, strip, lats, strips = sizes
    x0 = lax.axis_index("lon") * strip
    shift = lats.bit_length() - 1
    local_cell = cell - x0 * lats
    obs_lon = lax.shift_right_arithmetic(local_cell, shift)
    obs_lat = local_cell & (lats - 1)
    count = cell.shape[1]
    here = lax.broadcasted_iota(jnp.int32, (strip, count), 0) == obs_lon
    high = value.astype(BF16)
    rest = value - high.astype(F32)
    mid = rest.astype(BF16)
    low = (rest - mid.astype(F32)).astype(BF16)
    zero = jnp.zeros((strip, count), F32)
    parts = [jnp.where(here, 1.0, zero)]
    parts += [jnp.where(here, p.astype(F32), zero) for p in (high, mid, low)]
    left = jnp.concatenate(parts, 0).astype(BF16)
    right = (lax.broadcasted_iota(jnp.int32, (lats, count), 0) == obs_lat).astype(F32).astype(BF16)
    dense = lax.dot_general(left, right, (((1,), (1,)), ((), ())), preferred_element_type=F32)
    lon = (lax.broadcasted_iota(jnp.int32, (strip, lats), 0) + x0).astype(F32)
    precision = 1.0 + 2.0 * lon / (strip * strips)
    target = dense[strip:2 * strip] + (dense[2 * strip:3 * strip] + dense[3 * strip:])
    return dense[:strip] * (0.25 * precision), target


class Rows:
    def __init__(self, ref, first, columns):
        self.ref, self.first, self.columns = ref, first, columns

    def __getitem__(self, at):
        row = self.first + at[0] * self.columns + at[1]
        return self.ref[row:row + 1]


def scalars_in(ref, fields):
    return Rows(ref, fields * fields, fields), Rows(ref, 0, fields)


def prepare(sizes, state_hbm, noise_hbm, courant_hbm, diffusion_hbm, mixing_hbm, cell_hbm, value_hbm,
            send_east, send_west, state, noise, maps, courant, scalars,
            diffusion, mixing, cell, value, sems):
    particles, fields, strip, lats, strips = sizes
    n = fields * particles
    copies = [pltpu.make_async_copy(source, target, sems.at[k]) for k, (source, target) in enumerate((
        (cell_hbm, cell), (value_hbm, value), (courant_hbm, courant), (diffusion_hbm, diffusion),
        (mixing_hbm, mixing), (state_hbm.at[:, :, :8], state.at[:, :, :8]),
        (state_hbm.at[:, :, strip - 8:], state.at[:, :, strip - 8:]), (noise_hbm.at[0], noise.at[0]),
        (noise_hbm.at[1, :, 0], noise.at[1, :, 0]), (state_hbm.at[:, :, 8:strip - 8], state.at[:, :, 8:strip - 8]),
        (noise_hbm.at[1, :, 1:], noise.at[1, :, 1:])))]
    for copy in copies:
        copy.start()
    copies[0].wait()
    copies[1].wait()
    gain, target = observation_maps(sizes, cell[...], value[...])
    maps[0], maps[1] = gain, target
    kinds = []
    for x, step in ((strip - 1, -1), (0, 1)):
        kinds += [(f, x) for f in range(fields)] + [(f, x + step) for f in range(fields)] + [(0, x + 2 * step)]
    pick0 = pick_rows(kinds, particles, fields, strip)
    pick1 = pick_rows([(0, x) for x in (strip - 1, strip - 2, 0, 1)], particles, 1, strip)
    for copy in copies[2:5]:
        copy.wait()
    for f in range(fields):
        for g in range(fields):
            scalars[f * fields + g:f * fields + g + 1] = jnp.broadcast_to(mixing[f:f + 1, g:g + 1], (1, lats))
        at = fields * fields + f
        scalars[at:at + 1] = jnp.broadcast_to(diffusion[:, f:f + 1], (1, lats))
    diffusion, mixing = scalars_in(scalars, fields)

    sides = []
    for first, inward, outward in ((strip - 8, 2, 1), (0, 1, 2)):
        tile = [coefficients(courant[0, first:first + 8], courant[1, first:first + 8], diffusion[0, f], mixing[f, f])
                for f in range(fields)]
        sides.append([[c[0], c[inward], c[outward], c[3], c[4]] for c in tile])
    def coefs_at(side, f, k):
        at = places[side][0] + k * places[side][2] - places[side][1]
        return [c[at:at + 1] for c in sides[side][f]]

    def maps_at(side, k):
        at = places[side][0] + k * places[side][2]
        return gain[at:at + 1], target[at:at + 1]

    def moved(side, f, k, here, inner, outer):
        centre, inward, outward, to_north, to_south = coefs_at(side, f, k)
        v = here[f]
        total = centre * v + inward * inner + to_north * north(v) + to_south * south(v) + mixed(mixing, f, here)
        return total if outer is None else total + outward * outer

    def nudged(side, value, k):
        g, v = maps_at(side, k)
        push = g * (v - value)
        return value + push, push

    def first_step(side, out):
        def state_at(f, k):
            at = places[side][0] + k * places[side][2]
            return stack_rows([state[p, f, at:at + 1] for p in range(particles)])

        near = [[state_at(f, k) for f in range(fields)] for k in range(3)]
        third = state_at(0, 3)
        for f in range(fields):
            out[f * particles:(f + 1) * particles] = near[0][f]
        result, pushes = [[], []], []
        for k in range(2):
            for f in range(fields):
                new = moved(side, f, k, near[k], near[k + 1][f], near[k - 1][f] if k else None)
                if f == 0:
                    new, push = nudged(side, new, k)
                    pushes.append(push)
                result[k].append(new)
        inside, _ = nudged(side, moved(side, 0, 2, near[2], third, near[1][0]), 2)
        return result, pushes, inside

    places = ((strip - 1, strip - 8, -1), (0, 0, 1))
    copies[5].wait()
    copies[6].wait()
    started = [first_step(0, send_east), first_step(1, send_west)]
    copies[7].wait()
    copies[8].wait()
    rows0 = jnp.dot(pick0, noise[0].reshape(n * strip, lats), preferred_element_type=F32)
    rows1 = jnp.dot(pick1, noise[1, :, 0].reshape(particles * strip, lats), preferred_element_type=F32)

    def edge(side, out):
        x, _, step = places[side]
        base0, base1 = side * (2 * fields + 1) * particles, side * 2 * particles
        result, pushes, inside = started[side]

        def noisy0(k, f):
            at = base0 + (k * fields + f) * particles
            return rows0[at:at + particles]

        def noisy1(k):
            at = base1 + k * particles
            return rows1[at:at + particles]

        result = [[result[k][f] + noisy0(k, f) for f in range(fields)] for k in range(2)]
        inside = inside + noisy0(2, 0)
        g0, _ = maps_at(side, 0)
        g1, _ = maps_at(side, 1)
        slope = [-(1.0 / noise_var) * g0 * (pushes[0] + noisy0(0, 0))]
        bend = [(0.5 / noise_var) * g0 * g0]
        for k, g in enumerate((g0, g1)):
            new = moved(side, 0, k, result[k], result[1][0] if k == 0 else inside, result[0][0] if k else None)
            new, push = nudged(side, new, k)
            miss = maps_at(side, k)[1] - (new + noisy1(k))
            weight = 4.0 * g
            slope.append(-(1.0 / noise_var) * g * (push + noisy1(k)) - weight * (1.0 - g) * miss)
            bend.append((0.5 / noise_var) * g * g + 0.5 * weight * (1.0 - g) * (1.0 - g))
        outward = coefs_at(side, 0, 0)[2]
        onward = coefs_at(side, 0, 1)[2] * (1.0 - g0) * outward
        for f in range(fields):
            out[n + f * particles:n + (f + 1) * particles] = result[0][f]
        out[2 * n:2 * n + particles] = outward * slope[0] + onward * slope[2]
        out[2 * n + particles:2 * n + 2 * particles] = slope[1]
        inner = x + step
        last = (outward * outward * bend[0] + onward * onward * bend[2], bend[1],
                courant[0, x:x + 1], courant[1, x:x + 1], g0, courant[0, inner:inner + 1], g1,
                jnp.zeros((1, lats), F32))
        out[2 * n + 2 * particles:] = stack_rows(last)

    edge(0, send_east)
    edge(1, send_west)
    copies[9].wait()
    copies[10].wait()


def zero_halo_coefs(sizes, courant, scalars, coefs):
    particles, fields, strip, lats, strips = sizes
    diffusion, mixing = scalars_in(scalars, fields)
    lon = lax.broadcasted_iota(jnp.int32, (strip, lats), 0)
    for f in range(fields):
        centre, east, west, to_north, to_south = coefficients(
            courant[0], courant[1], diffusion[0, f], mixing[f, f])
        coefs[f, 0] = centre
        coefs[f, 1] = jnp.where(lon == strip - 1, 0.0, east)
        coefs[f, 2] = jnp.where(lon == 0, 0.0, west)
        coefs[f, 3] = to_north
        coefs[f, 4] = to_south


def zero_halo_step(sizes, scalars, coefs):
    particles, fields, strip, lats, strips = sizes
    _, mixing = scalars_in(scalars, fields)

    def moved(values, f):
        v = values[f]
        return (coefs[f, 0] * v + coefs[f, 1] * pltpu.roll(v, strip - 1, 0) + coefs[f, 2] * pltpu.roll(v, 1, 0)
                + coefs[f, 3] * north(v) + coefs[f, 4] * south(v) + mixed(mixing, f, values))

    return moved


def observed_bulk(sizes, parity, state, noise, maps, courant, scalars, earlier, middle, out, weight, coefs, partial):
    particles, fields, strip, lats, strips = sizes

    def one(p):
        moved = zero_halo_step(sizes, scalars, coefs)
        values = [state[p, f] for f in range(fields)]
        results = []
        for f in range(fields):
            new = moved(values, f)
            add = noise[0, p, f].astype(F32)
            if f == 0:
                push = maps[0] * (maps[1] - new)
                new = new + push
                total = push * (push + 2.0 * add)
            results.append(new + add)
            middle[p, f] = new + add
        new = moved(results, 0)
        add = noise[1, p, 0].astype(F32)
        push = maps[0] * (maps[1] - new)
        new = new + push + add
        miss = maps[1] - new
        total = (0.5 / noise_var) * (total + push * (push + 2.0 * add)) + (2.0 * maps[0]) * (miss * miss)
        out[p] = new
        partial[pl.ds(p, 1), :] = wide(jnp.sum(total, axis=0, keepdims=True))

    def body(pair, carry):
        one(2 * pair)
        one(2 * pair + 1)
        return carry

    here = lax.axis_index("lon") % 2 == parity

    @pl.when(here)
    def _():
        zero_halo_coefs(sizes, courant, scalars, coefs)
        lax.fori_loop(0, particles // 2, body, 0)
        weight[...] = in_row(partial[...])

    @pl.when(jnp.logical_not(here))
    def _():
        weight[...] = earlier[:1, :128]


def other_bulk(sizes, even_middle, even_observed, even_coefs, odd_middle, odd_observed, odd_coefs,
               noise, scalars, out):
    particles, fields, strip, lats, strips = sizes

    def run(middle, observed, coefs):
        moved = zero_halo_step(sizes, scalars, coefs)

        def body(p, carry):
            values = [middle[p, f] for f in range(fields)]
            out[p, 0] = observed[p]
            for f in range(1, fields):
                out[p, f] = moved(values, f) + noise[1, p, f].astype(F32)
            return carry

        lax.fori_loop(0, particles, body, 0)

    even = lax.axis_index("lon") % 2 == 0

    @pl.when(even)
    def _():
        run(even_middle, even_observed, even_coefs)

    @pl.when(jnp.logical_not(even))
    def _():
        run(odd_middle, odd_observed, odd_coefs)


def correct(sizes, own_east, own_west, from_west, from_east, scalars, bulk_weight, weight, changes):
    particles, fields, strip, lats, strips = sizes
    n = fields * particles
    diffusion, mixing = scalars_in(scalars, fields)

    def field_rows(ref, start, f):
        return ref[start + f * particles:start + (f + 1) * particles]

    packets = (own_east, from_east, own_west, from_west)
    last = 2 * n + 2 * particles
    zonal = stack_rows([ref[last + 2:last + 3] for ref in packets] + [ref[last + 5:last + 6] for ref in packets])
    merid = stack_rows([ref[last + 3:last + 4] for ref in packets] * 2)
    tile = [coefficients(zonal, merid, diffusion[0, f], mixing[f, f]) for f in range(fields)]
    total = jnp.zeros((particles, lats), F32)
    for k, owner in enumerate(packets):
        other_k = k ^ 1
        other = packets[other_k]
        outward_at = (1, 2, 2, 1)[k]
        outward_other = (1, 2, 2, 1)[other_k]
        gain = owner[last + 4:last + 5]
        gain_other = other[last + 4:last + 5]
        first = []
        for f in range(fields):
            step = tile[f][outward_at][k:k + 1] * field_rows(other, 0, f)
            first.append((1.0 - gain) * step if f == 0 else step)
        mine = k in (0, 2)
        for f in range(fields if mine else 1):
            centre, to_north, to_south = [tile[f][c][k:k + 1] for c in (0, 3, 4)]
            outward = tile[f][outward_at][k:k + 1]
            reach = tile[f][outward_other][other_k:other_k + 1]
            if f == 0:
                reach = (1.0 - gain_other) * reach
            outside = field_rows(other, n, f) + reach * field_rows(owner, 0, f)
            step = (centre * first[f] + outward * outside + to_north * north(first[f])
                    + to_south * south(first[f]) + mixed(mixing, f, first))
            if f == 0:
                seen = field_rows(other, 0, 0)
                slope, slope_step = owner[2 * n:2 * n + particles], owner[2 * n + particles:last]
                bend, bend_step = owner[last:last + 1], owner[last + 1:last + 2]
                total = total + seen * (slope + bend * seen) + step * (slope_step + bend_step * step)
            if mine:
                beside = tile[f][outward_at][4 + k:5 + k] * first[f]
                if f == 0:
                    step = (1.0 - gain) * step
                    beside = (1.0 - owner[last + 6:last + 7]) * beside
                edge, inner = (3, 2) if k == 0 else (0, 1)
                changes[edge, f * particles:(f + 1) * particles] = step
                changes[inner, f * particles:(f + 1) * particles] = beside
    weight[...] = in_row(wide(total)) + bulk_weight[...]


def apply_changes(sizes, current, changes, out):
    particles, fields, strip, lats, strips = sizes
    sub = lax.broadcasted_iota(jnp.int32, (8, lats), 0)
    for p in range(particles):
        for f in range(fields):
            row = f * particles + p
            rows = [jnp.broadcast_to(changes[k, row:row + 1], sub.shape) for k in range(4)]
            out[p, f, :8] = current[p, f, :8] + jnp.where(sub == 0, rows[0], jnp.where(sub == 1, rows[1], 0.0))
            out[p, f, 8:strip - 8] = current[p, f, 8:strip - 8]
            out[p, f, strip - 8:] = current[p, f, strip - 8:] + jnp.where(
                sub == 7, rows[3], jnp.where(sub == 6, rows[2], 0.0))


def assemble(sizes, source, current, received, out, sems):
    particles = sizes[0]
    dom = lax.axis_index("dom")

    def copy(j, ref, at):
        return pltpu.make_async_copy(ref.at[at], out.at[j], sems.at[j])

    for j in range(particles):
        wanted = source[dom * particles + j]
        mine = wanted // particles == dom
        at = wanted % particles

        @pl.when(mine)
        def _():
            copy(j, current, at).start()

        @pl.when(jnp.logical_not(mine))
        def _():
            copy(j, received, at).start()

    for j in range(particles):
        copy(j, current, 0).wait()


def local(ensemble_state, proposal_noise, courant, diffusion, mixing, prior_weight, obs_cell, obs_value, source):
    particles, fields, strip, lats = ensemble_state.shape
    strips = lax.axis_size("lon")
    sizes = (particles, fields, strip, lats, strips)
    packet = jax.ShapeDtypeStruct((2 * particles * fields + 2 * particles + 8, lats), F32)
    cell, value = obs_cell[None], obs_value[None]

    def shape(*dims):
        return jax.ShapeDtypeStruct(dims, F32)

    whole = (particles, fields, strip, lats)

    def in_hbm(array):
        return pltpu.with_memory_space_constraint(array, pltpu.HBM)

    arrays = (ensemble_state, proposal_noise, courant, diffusion[None], mixing, cell, value)
    send_east, send_west, state, noise, maps, courant, scalars = pl.pallas_call(
        functools.partial(prepare, sizes),
        out_shape=(packet, packet, shape(*whole), jax.ShapeDtypeStruct((2,) + whole, BF16), shape(2, strip, lats),
                   shape(*courant.shape), shape(fields * (fields + 2), lats)),
        in_specs=[HBM] * 7,
        out_specs=(VMEM,) * 7,
        scratch_shapes=[pltpu.VMEM(array.shape, array.dtype) for array in arrays[3:]]
        + [pltpu.SemaphoreType.DMA((11,))],
        compiler_params=LIMIT,
        cost_estimate=pl.CostEstimate(flops=1000000, bytes_accessed=2000000, transcendentals=0),
    )(*[in_hbm(array) for array in arrays])

    def bulk_of(parity, earlier):
        return pl.pallas_call(
            functools.partial(observed_bulk, sizes, parity),
            out_shape=(shape(*whole), shape(particles, strip, lats), shape(1, 128), shape(fields, 5, strip, lats)),
            in_specs=[VMEM] * 6,
            out_specs=(VMEM,) * 4,
            scratch_shapes=[pltpu.VMEM((particles, 128), F32)],
            compiler_params=LIMIT,
            cost_estimate=pl.CostEstimate(flops=20000000, bytes_accessed=4000000, transcendentals=0),
        )(state, noise, maps, courant, scalars, earlier)

    even_middle, even_observed, bulk_weight, even_coefs = bulk_of(0, scalars)
    send_east, send_west, bulk_weight = lax.optimization_barrier((send_east, send_west, bulk_weight))
    eastward = [(i, (i + 1) % strips) for i in range(strips)]
    westward = [(i, (i - 1) % strips) for i in range(strips)]
    from_west = lax.ppermute(send_east, "lon", eastward)
    from_east = lax.ppermute(send_west, "lon", westward)
    odd_middle, odd_observed, bulk_weight, odd_coefs = bulk_of(1, bulk_weight)
    beside = lax.ppermute(bulk_weight, "lon", [(i, i ^ 1) for i in range(strips)])

    current = pl.pallas_call(
        functools.partial(other_bulk, sizes),
        out_shape=shape(*whole),
        in_specs=[VMEM] * 8,
        out_specs=VMEM,
        compiler_params=LIMIT,
        cost_estimate=FREE,
    )(even_middle, even_observed, even_coefs, odd_middle, odd_observed, odd_coefs, noise, scalars)

    weight, changes = pl.pallas_call(
        functools.partial(correct, sizes),
        out_shape=(shape(1, 128), shape(4, particles * fields, lats)),
        in_specs=[VMEM] * 6,
        out_specs=(VMEM,) * 2,
        compiler_params=LIMIT,
        cost_estimate=FREE,
    )(send_east, send_west, from_west, from_east, scalars, bulk_weight)

    current = pl.pallas_call(
        functools.partial(apply_changes, sizes),
        out_shape=shape(*whole),
        in_specs=[VMEM] * 2,
        out_specs=VMEM,
        compiler_params=LIMIT,
        cost_estimate=FREE,
    )(current, changes)

    current, beside = lax.optimization_barrier((current, beside))
    weight = weight + beside
    received = lax.ppermute(current, "dom", [(0, 1), (1, 0)])
    bit = 2
    while bit < strips:
        steps = (3, 2, 1) if 2 * bit < strips else (1,)
        arrived = []
        for step in steps:
            if step == 1 and bit * (len(steps) + 1) >= strips:
                weight, received = lax.optimization_barrier((weight, received))
            arrived.append(lax.ppermute(weight, "lon", [(i, i ^ (bit * step)) for i in range(strips)]))
        weight = sum(arrived, weight)
        bit *= len(steps) + 1

    new_state = pl.pallas_call(
        functools.partial(assemble, sizes),
        out_shape=shape(*whole),
        in_specs=[SMEM, VMEM, VMEM],
        out_specs=HBM,
        scratch_shapes=[pltpu.SemaphoreType.DMA((particles,))],
        compiler_params=LIMIT,
        cost_estimate=pl.CostEstimate(flops=0, bytes_accessed=2000000, transcendentals=0),
    )(source, current, received)

    log_weight = prior_weight - weight[0, :particles] / (256.0 * obs_cell.shape[0])
    return new_state, log_weight


def solution(mesh):
    placed = (
        P(("groups", "dom"), None, "lon", None),
        P(None, ("groups", "dom"), None, "lon", None),
        P(None, ("groups", "lon"), None),
        P(),
        P(),
        P(("groups", "dom")),
        P(("groups", "lon")),
        P(("groups", "lon")),
        P("groups"),
    )
    return jax.shard_map(
        local,
        mesh=mesh,
        in_specs=placed,
        out_specs=(P(("groups", "dom"), None, "lon", None), P(("groups", "dom"))),
        check_vma=False,
    )
```

```python
import functools

import jax
import jax.numpy as jnp
from jax import lax
from jax.experimental import pallas as pl
from jax.experimental.pallas import tpu as pltpu
from jax.sharding import PartitionSpec as P

noise_var = 0.04
VMEM = pl.BlockSpec(memory_space=pltpu.VMEM)
SMEM = pl.BlockSpec(memory_space=pltpu.SMEM)
HBM = pl.BlockSpec(memory_space=pltpu.HBM)
LIMIT = pltpu.CompilerParams(vmem_limit_bytes=16 * 1024 * 1024)
FREE = pl.CostEstimate(flops=0, bytes_accessed=0, transcendentals=0)
BF16 = jnp.bfloat16
F32 = jnp.float32


def north(v):
    return pltpu.roll(v, v.shape[1] - 1, 1)


def south(v):
    return pltpu.roll(v, 1, 1)


def coefficients(zonal, merid, rate, self_mix):
    lat = lax.broadcasted_iota(jnp.int32, zonal.shape, 1)
    zonal_half, zonal_rate = 0.5 * zonal, 0.5 * zonal * zonal + rate
    merid_half, merid_rate = 0.5 * merid, 0.5 * merid * merid + rate
    east, west = zonal_rate - zonal_half, zonal_rate + zonal_half
    to_north, to_south = merid_rate - merid_half, merid_rate + merid_half
    centre = 1.0 + self_mix - 2.0 * zonal_rate - 2.0 * merid_rate
    last, first = lat == zonal.shape[1] - 1, lat == 0
    centre = centre + jnp.where(last, to_north, 0.0) + jnp.where(first, to_south, 0.0)
    to_north = jnp.where(last, 0.0, to_north)
    to_south = jnp.where(first, 0.0, to_south)
    return centre, east, west, to_north, to_south


def mixed(mixing, field, values):
    total = None
    for other, value in enumerate(values):
        if other != field:
            term = mixing[field, other] * value
            total = term if total is None else total + term
    return total


def pick_rows(kinds, particles, fields, strip):
    shape = (particles, particles * fields * strip)
    place = lax.broadcasted_iota(jnp.int32, shape, 1) - lax.broadcasted_iota(jnp.int32, shape, 0) * (fields * strip)
    blocks = [jnp.where(place == f * strip + x, 1.0, 0.0) for f, x in kinds]
    return jnp.concatenate(blocks, 0).astype(BF16)


def stack_rows(rows):
    sub = lax.broadcasted_iota(jnp.int32, (len(rows), rows[0].shape[1]), 0)
    out = None
    for p, row in enumerate(rows):
        row = jnp.broadcast_to(row, sub.shape)
        out = row if out is None else jnp.where(sub == p, row, out)
    return out


def in_row(column):
    total = jnp.broadcast_to(jnp.sum(column, axis=1, keepdims=True), column.shape)
    diagonal = lax.broadcasted_iota(jnp.int32, total.shape, 0) == lax.broadcasted_iota(jnp.int32, total.shape, 1)
    return jnp.sum(jnp.where(diagonal, total, 0.0), axis=0, keepdims=True)


def wide(v):
    return v[:, :128] + v[:, 128:]


def observation_maps(sizes, cell, value):
    particles, fields, strip, lats, strips = sizes
    x0 = lax.axis_index("lon") * strip
    shift = lats.bit_length() - 1
    local_cell = cell - x0 * lats
    obs_lon = lax.shift_right_arithmetic(local_cell, shift)
    obs_lat = local_cell & (lats - 1)
    count = cell.shape[1]
    here = lax.broadcasted_iota(jnp.int32, (strip, count), 0) == obs_lon
    high = value.astype(BF16)
    rest = value - high.astype(F32)
    mid = rest.astype(BF16)
    low = (rest - mid.astype(F32)).astype(BF16)
    zero = jnp.zeros((strip, count), F32)
    parts = [jnp.where(here, 1.0, zero)]
    parts += [jnp.where(here, p.astype(F32), zero) for p in (high, mid, low)]
    left = jnp.concatenate(parts, 0).astype(BF16)
    right = (lax.broadcasted_iota(jnp.int32, (lats, count), 0) == obs_lat).astype(F32).astype(BF16)
    dense = lax.dot_general(left, right, (((1,), (1,)), ((), ())), preferred_element_type=F32)
    lon = (lax.broadcasted_iota(jnp.int32, (strip, lats), 0) + x0).astype(F32)
    precision = 1.0 + 2.0 * lon / (strip * strips)
    target = dense[strip:2 * strip] + (dense[2 * strip:3 * strip] + dense[3 * strip:])
    return dense[:strip] * (0.25 * precision), target


class Rows:
    def __init__(self, ref, first, columns):
        self.ref, self.first, self.columns = ref, first, columns

    def __getitem__(self, at):
        row = self.first + at[0] * self.columns + at[1]
        return self.ref[row:row + 1]


def scalars_in(ref, fields):
    return Rows(ref, fields * fields, fields), Rows(ref, 0, fields)


def prepare(sizes, state_hbm, noise_hbm, courant_hbm, diffusion_hbm, mixing_hbm, cell_hbm, value_hbm,
            send_east, send_west, state, noise, maps, courant, scalars,
            diffusion, mixing, cell, value, sems):
    particles, fields, strip, lats, strips = sizes
    n = fields * particles
    copies = [pltpu.make_async_copy(source, target, sems.at[k]) for k, (source, target) in enumerate((
        (cell_hbm, cell), (value_hbm, value), (courant_hbm, courant), (diffusion_hbm, diffusion),
        (mixing_hbm, mixing), (state_hbm.at[:, :, :8], state.at[:, :, :8]),
        (state_hbm.at[:, :, strip - 8:], state.at[:, :, strip - 8:]), (noise_hbm.at[0], noise.at[0]),
        (noise_hbm.at[1, :, 0], noise.at[1, :, 0]), (state_hbm.at[:, :, 8:strip - 8], state.at[:, :, 8:strip - 8]),
        (noise_hbm.at[1, :, 1:], noise.at[1, :, 1:])))]
    for copy in copies:
        copy.start()
    copies[0].wait()
    copies[1].wait()
    gain, target = observation_maps(sizes, cell[...], value[...])
    maps[0], maps[1] = gain, target
    kinds = []
    for x, step in ((strip - 1, -1), (0, 1)):
        kinds += [(f, x) for f in range(fields)] + [(f, x + step) for f in range(fields)] + [(0, x + 2 * step)]
    pick0 = pick_rows(kinds, particles, fields, strip)
    pick1 = pick_rows([(0, x) for x in (strip - 1, strip - 2, 0, 1)], particles, 1, strip)
    for copy in copies[2:5]:
        copy.wait()
    for f in range(fields):
        for g in range(fields):
            scalars[f * fields + g:f * fields + g + 1] = jnp.broadcast_to(mixing[f:f + 1, g:g + 1], (1, lats))
        at = fields * fields + f
        scalars[at:at + 1] = jnp.broadcast_to(diffusion[:, f:f + 1], (1, lats))
    diffusion, mixing = scalars_in(scalars, fields)

    sides = []
    for first, inward, outward in ((strip - 8, 2, 1), (0, 1, 2)):
        tile = [coefficients(courant[0, first:first + 8], courant[1, first:first + 8], diffusion[0, f], mixing[f, f])
                for f in range(fields)]
        sides.append([[c[0], c[inward], c[outward], c[3], c[4]] for c in tile])
    def coefs_at(side, f, k):
        at = places[side][0] + k * places[side][2] - places[side][1]
        return [c[at:at + 1] for c in sides[side][f]]

    def maps_at(side, k):
        at = places[side][0] + k * places[side][2]
        return gain[at:at + 1], target[at:at + 1]

    def moved(side, f, k, here, inner, outer):
        centre, inward, outward, to_north, to_south = coefs_at(side, f, k)
        v = here[f]
        total = centre * v + inward * inner + to_north * north(v) + to_south * south(v) + mixed(mixing, f, here)
        return total if outer is None else total + outward * outer

    def nudged(side, value, k):
        g, v = maps_at(side, k)
        push = g * (v - value)
        return value + push, push

    def first_step(side, out):
        def state_at(f, k):
            at = places[side][0] + k * places[side][2]
            return stack_rows([state[p, f, at:at + 1] for p in range(particles)])

        near = [[state_at(f, k) for f in range(fields)] for k in range(3)]
        third = state_at(0, 3)
        for f in range(fields):
            out[f * particles:(f + 1) * particles] = near[0][f]
        result, pushes = [[], []], []
        for k in range(2):
            for f in range(fields):
                new = moved(side, f, k, near[k], near[k + 1][f], near[k - 1][f] if k else None)
                if f == 0:
                    new, push = nudged(side, new, k)
                    pushes.append(push)
                result[k].append(new)
        inside, _ = nudged(side, moved(side, 0, 2, near[2], third, near[1][0]), 2)
        return result, pushes, inside

    places = ((strip - 1, strip - 8, -1), (0, 0, 1))
    copies[5].wait()
    copies[6].wait()
    started = [first_step(0, send_east), first_step(1, send_west)]
    copies[7].wait()
    copies[8].wait()
    rows0 = jnp.dot(pick0, noise[0].reshape(n * strip, lats), preferred_element_type=F32)
    rows1 = jnp.dot(pick1, noise[1, :, 0].reshape(particles * strip, lats), preferred_element_type=F32)

    def edge(side, out):
        x, _, step = places[side]
        base0, base1 = side * (2 * fields + 1) * particles, side * 2 * particles
        result, pushes, inside = started[side]

        def noisy0(k, f):
            at = base0 + (k * fields + f) * particles
            return rows0[at:at + particles]

        def noisy1(k):
            at = base1 + k * particles
            return rows1[at:at + particles]

        result = [[result[k][f] + noisy0(k, f) for f in range(fields)] for k in range(2)]
        inside = inside + noisy0(2, 0)
        g0, _ = maps_at(side, 0)
        g1, _ = maps_at(side, 1)
        slope = [-(1.0 / noise_var) * g0 * (pushes[0] + noisy0(0, 0))]
        bend = [(0.5 / noise_var) * g0 * g0]
        for k, g in enumerate((g0, g1)):
            new = moved(side, 0, k, result[k], result[1][0] if k == 0 else inside, result[0][0] if k else None)
            new, push = nudged(side, new, k)
            miss = maps_at(side, k)[1] - (new + noisy1(k))
            weight = 4.0 * g
            slope.append(-(1.0 / noise_var) * g * (push + noisy1(k)) - weight * (1.0 - g) * miss)
            bend.append((0.5 / noise_var) * g * g + 0.5 * weight * (1.0 - g) * (1.0 - g))
        outward = coefs_at(side, 0, 0)[2]
        onward = coefs_at(side, 0, 1)[2] * (1.0 - g0) * outward
        for f in range(fields):
            out[n + f * particles:n + (f + 1) * particles] = result[0][f]
        out[2 * n:2 * n + particles] = outward * slope[0] + onward * slope[2]
        out[2 * n + particles:2 * n + 2 * particles] = slope[1]
        inner = x + step
        last = (outward * outward * bend[0] + onward * onward * bend[2], bend[1],
                courant[0, x:x + 1], courant[1, x:x + 1], g0, courant[0, inner:inner + 1], g1,
                jnp.zeros((1, lats), F32))
        out[2 * n + 2 * particles:] = stack_rows(last)

    edge(0, send_east)
    edge(1, send_west)
    copies[9].wait()
    copies[10].wait()


def zero_halo_coefs(sizes, courant, scalars, coefs):
    particles, fields, strip, lats, strips = sizes
    diffusion, mixing = scalars_in(scalars, fields)
    lon = lax.broadcasted_iota(jnp.int32, (strip, lats), 0)
    for f in range(fields):
        centre, east, west, to_north, to_south = coefficients(
            courant[0], courant[1], diffusion[0, f], mixing[f, f])
        coefs[f, 0] = centre
        coefs[f, 1] = jnp.where(lon == strip - 1, 0.0, east)
        coefs[f, 2] = jnp.where(lon == 0, 0.0, west)
        coefs[f, 3] = to_north
        coefs[f, 4] = to_south


def zero_halo_step(sizes, scalars, coefs):
    particles, fields, strip, lats, strips = sizes
    _, mixing = scalars_in(scalars, fields)

    def moved(values, f):
        v = values[f]
        return (coefs[f, 0] * v + coefs[f, 1] * pltpu.roll(v, strip - 1, 0) + coefs[f, 2] * pltpu.roll(v, 1, 0)
                + coefs[f, 3] * north(v) + coefs[f, 4] * south(v) + mixed(mixing, f, values))

    return moved


def observed_bulk(sizes, parity, state, noise, maps, courant, scalars, earlier, middle, out, weight, coefs, partial):
    particles, fields, strip, lats, strips = sizes

    def one(p):
        moved = zero_halo_step(sizes, scalars, coefs)
        values = [state[p, f] for f in range(fields)]
        results = []
        for f in range(fields):
            new = moved(values, f)
            add = noise[0, p, f].astype(F32)
            if f == 0:
                push = maps[0] * (maps[1] - new)
                new = new + push
                total = push * (push + 2.0 * add)
            results.append(new + add)
            middle[p, f] = new + add
        new = moved(results, 0)
        add = noise[1, p, 0].astype(F32)
        push = maps[0] * (maps[1] - new)
        new = new + push + add
        miss = maps[1] - new
        total = (0.5 / noise_var) * (total + push * (push + 2.0 * add)) + (2.0 * maps[0]) * (miss * miss)
        out[p] = new
        partial[pl.ds(p, 1), :] = wide(jnp.sum(total, axis=0, keepdims=True))

    def body(pair, carry):
        one(2 * pair)
        one(2 * pair + 1)
        return carry

    here = lax.axis_index("lon") % 2 == parity

    @pl.when(here)
    def _():
        zero_halo_coefs(sizes, courant, scalars, coefs)
        lax.fori_loop(0, particles // 2, body, 0)
        weight[...] = in_row(partial[...])

    @pl.when(jnp.logical_not(here))
    def _():
        weight[...] = earlier[:1, :128]


def other_bulk(sizes, even_middle, even_observed, even_coefs, odd_middle, odd_observed, odd_coefs,
               noise, scalars, out):
    particles, fields, strip, lats, strips = sizes

    def run(middle, observed, coefs):
        moved = zero_halo_step(sizes, scalars, coefs)

        def body(p, carry):
            values = [middle[p, f] for f in range(fields)]
            out[p, 0] = observed[p]
            for f in range(1, fields):
                out[p, f] = moved(values, f) + noise[1, p, f].astype(F32)
            return carry

        lax.fori_loop(0, particles, body, 0)

    even = lax.axis_index("lon") % 2 == 0

    @pl.when(even)
    def _():
        run(even_middle, even_observed, even_coefs)

    @pl.when(jnp.logical_not(even))
    def _():
        run(odd_middle, odd_observed, odd_coefs)


def correct(sizes, own_east, own_west, from_west, from_east, scalars, bulk_weight, weight, changes):
    particles, fields, strip, lats, strips = sizes
    n = fields * particles
    diffusion, mixing = scalars_in(scalars, fields)

    def field_rows(ref, start, f):
        return ref[start + f * particles:start + (f + 1) * particles]

    packets = (own_east, from_east, own_west, from_west)
    last = 2 * n + 2 * particles
    zonal = stack_rows([ref[last + 2:last + 3] for ref in packets] + [ref[last + 5:last + 6] for ref in packets])
    merid = stack_rows([ref[last + 3:last + 4] for ref in packets] * 2)
    tile = [coefficients(zonal, merid, diffusion[0, f], mixing[f, f]) for f in range(fields)]
    total = jnp.zeros((particles, lats), F32)
    for k, owner in enumerate(packets):
        other_k = k ^ 1
        other = packets[other_k]
        outward_at = (1, 2, 2, 1)[k]
        outward_other = (1, 2, 2, 1)[other_k]
        gain = owner[last + 4:last + 5]
        gain_other = other[last + 4:last + 5]
        first = []
        for f in range(fields):
            step = tile[f][outward_at][k:k + 1] * field_rows(other, 0, f)
            first.append((1.0 - gain) * step if f == 0 else step)
        mine = k in (0, 2)
        for f in range(fields if mine else 1):
            centre, to_north, to_south = [tile[f][c][k:k + 1] for c in (0, 3, 4)]
            outward = tile[f][outward_at][k:k + 1]
            reach = tile[f][outward_other][other_k:other_k + 1]
            if f == 0:
                reach = (1.0 - gain_other) * reach
            outside = field_rows(other, n, f) + reach * field_rows(owner, 0, f)
            step = (centre * first[f] + outward * outside + to_north * north(first[f])
                    + to_south * south(first[f]) + mixed(mixing, f, first))
            if f == 0:
                seen = field_rows(other, 0, 0)
                slope, slope_step = owner[2 * n:2 * n + particles], owner[2 * n + particles:last]
                bend, bend_step = owner[last:last + 1], owner[last + 1:last + 2]
                total = total + seen * (slope + bend * seen) + step * (slope_step + bend_step * step)
            if mine:
                beside = tile[f][outward_at][4 + k:5 + k] * first[f]
                if f == 0:
                    step = (1.0 - gain) * step
                    beside = (1.0 - owner[last + 6:last + 7]) * beside
                edge, inner = (3, 2) if k == 0 else (0, 1)
                changes[edge, f * particles:(f + 1) * particles] = step
                changes[inner, f * particles:(f + 1) * particles] = beside
    weight[...] = in_row(wide(total)) + bulk_weight[...]


def apply_changes(sizes, current, changes, out):
    particles, fields, strip, lats, strips = sizes
    sub = lax.broadcasted_iota(jnp.int32, (8, lats), 0)
    for p in range(particles):
        for f in range(fields):
            row = f * particles + p
            rows = [jnp.broadcast_to(changes[k, row:row + 1], sub.shape) for k in range(4)]
            out[p, f, :8] = current[p, f, :8] + jnp.where(sub == 0, rows[0], jnp.where(sub == 1, rows[1], 0.0))
            out[p, f, 8:strip - 8] = current[p, f, 8:strip - 8]
            out[p, f, strip - 8:] = current[p, f, strip - 8:] + jnp.where(
                sub == 7, rows[3], jnp.where(sub == 6, rows[2], 0.0))


def assemble(sizes, source, current, received, out, sems):
    particles = sizes[0]
    dom = lax.axis_index("dom")

    def copy(j, ref, at):
        return pltpu.make_async_copy(ref.at[at], out.at[j], sems.at[j])

    for j in range(particles):
        wanted = source[dom * particles + j]
        mine = wanted // particles == dom
        at = wanted % particles

        @pl.when(mine)
        def _():
            copy(j, current, at).start()

        @pl.when(jnp.logical_not(mine))
        def _():
            copy(j, received, at).start()

    for j in range(particles):
        copy(j, current, 0).wait()


def local(ensemble_state, proposal_noise, courant, diffusion, mixing, prior_weight, obs_cell, obs_value, source):
    particles, fields, strip, lats = ensemble_state.shape
    strips = lax.axis_size("lon")
    sizes = (particles, fields, strip, lats, strips)
    packet = jax.ShapeDtypeStruct((2 * particles * fields + 2 * particles + 8, lats), F32)
    cell, value = obs_cell[None], obs_value[None]

    def shape(*dims):
        return jax.ShapeDtypeStruct(dims, F32)

    whole = (particles, fields, strip, lats)

    def in_hbm(array):
        return pltpu.with_memory_space_constraint(array, pltpu.HBM)

    arrays = (ensemble_state, proposal_noise, courant, diffusion[None], mixing, cell, value)
    send_east, send_west, state, noise, maps, courant, scalars = pl.pallas_call(
        functools.partial(prepare, sizes),
        out_shape=(packet, packet, shape(*whole), jax.ShapeDtypeStruct((2,) + whole, BF16), shape(2, strip, lats),
                   shape(*courant.shape), shape(fields * (fields + 2), lats)),
        in_specs=[HBM] * 7,
        out_specs=(VMEM,) * 7,
        scratch_shapes=[pltpu.VMEM(array.shape, array.dtype) for array in arrays[3:]]
        + [pltpu.SemaphoreType.DMA((11,))],
        compiler_params=LIMIT,
        cost_estimate=pl.CostEstimate(flops=1000000, bytes_accessed=2000000, transcendentals=0),
    )(*[in_hbm(array) for array in arrays])

    def bulk_of(parity, earlier):
        return pl.pallas_call(
            functools.partial(observed_bulk, sizes, parity),
            out_shape=(shape(*whole), shape(particles, strip, lats), shape(1, 128), shape(fields, 5, strip, lats)),
            in_specs=[VMEM] * 6,
            out_specs=(VMEM,) * 4,
            scratch_shapes=[pltpu.VMEM((particles, 128), F32)],
            compiler_params=LIMIT,
            cost_estimate=pl.CostEstimate(flops=20000000, bytes_accessed=4000000, transcendentals=0),
        )(state, noise, maps, courant, scalars, earlier)

    even_middle, even_observed, bulk_weight, even_coefs = bulk_of(0, scalars)
    send_east, send_west, bulk_weight = lax.optimization_barrier((send_east, send_west, bulk_weight))
    eastward = [(i, (i + 1) % strips) for i in range(strips)]
    westward = [(i, (i - 1) % strips) for i in range(strips)]
    from_west = lax.ppermute(send_east, "lon", eastward)
    from_east = lax.ppermute(send_west, "lon", westward)
    odd_middle, odd_observed, bulk_weight, odd_coefs = bulk_of(1, bulk_weight)
    beside = lax.ppermute(bulk_weight, "lon", [(i, i ^ 1) for i in range(strips)])

    current = pl.pallas_call(
        functools.partial(other_bulk, sizes),
        out_shape=shape(*whole),
        in_specs=[VMEM] * 8,
        out_specs=VMEM,
        compiler_params=LIMIT,
        cost_estimate=FREE,
    )(even_middle, even_observed, even_coefs, odd_middle, odd_observed, odd_coefs, noise, scalars)

    weight, changes = pl.pallas_call(
        functools.partial(correct, sizes),
        out_shape=(shape(1, 128), shape(4, particles * fields, lats)),
        in_specs=[VMEM] * 6,
        out_specs=(VMEM,) * 2,
        compiler_params=LIMIT,
        cost_estimate=FREE,
    )(send_east, send_west, from_west, from_east, scalars, bulk_weight)

    current = pl.pallas_call(
        functools.partial(apply_changes, sizes),
        out_shape=shape(*whole),
        in_specs=[VMEM] * 2,
        out_specs=VMEM,
        compiler_params=LIMIT,
        cost_estimate=FREE,
    )(current, changes)

    current, beside = lax.optimization_barrier((current, beside))
    weight = weight + beside
    received = lax.ppermute(current, "dom", [(0, 1), (1, 0)])
    bit = 2
    while bit < strips:
        steps = (3, 2, 1) if 2 * bit < strips else (1,)
        arrived = []
        for step in steps:
            if step == steps[-2:][0] and bit * (len(steps) + 1) >= strips:
                weight, received = lax.optimization_barrier((weight, received))
            arrived.append(lax.ppermute(weight, "lon", [(i, i ^ (bit * step)) for i in range(strips)]))
        weight = sum(arrived, weight)
        bit *= len(steps) + 1

    new_state = pl.pallas_call(
        functools.partial(assemble, sizes),
        out_shape=shape(*whole),
        in_specs=[SMEM, VMEM, VMEM],
        out_specs=HBM,
        scratch_shapes=[pltpu.SemaphoreType.DMA((particles,))],
        compiler_params=LIMIT,
        cost_estimate=pl.CostEstimate(flops=0, bytes_accessed=2000000, transcendentals=0),
    )(source, current, received)

    log_weight = prior_weight - weight[0, :particles] / (256.0 * obs_cell.shape[0])
    return new_state, log_weight


def solution(mesh):
    placed = (
        P(("groups", "dom"), None, "lon", None),
        P(None, ("groups", "dom"), None, "lon", None),
        P(None, ("groups", "lon"), None),
        P(),
        P(),
        P(("groups", "dom")),
        P(("groups", "lon")),
        P(("groups", "lon")),
        P("groups"),
    )
    return jax.shard_map(
        local,
        mesh=mesh,
        in_specs=placed,
        out_specs=(P(("groups", "dom"), None, "lon", None), P(("groups", "dom"))),
        check_vma=False,
    )
```

```python
import functools

import jax
import jax.numpy as jnp
from jax import lax
from jax.experimental import pallas as pl
from jax.experimental.pallas import tpu as pltpu
from jax.sharding import PartitionSpec as P

noise_var = 0.04
VMEM = pl.BlockSpec(memory_space=pltpu.VMEM)
SMEM = pl.BlockSpec(memory_space=pltpu.SMEM)
HBM = pl.BlockSpec(memory_space=pltpu.HBM)
LIMIT = pltpu.CompilerParams(vmem_limit_bytes=16 * 1024 * 1024)
FREE = pl.CostEstimate(flops=0, bytes_accessed=0, transcendentals=0)
BF16 = jnp.bfloat16
F32 = jnp.float32


def north(v):
    return pltpu.roll(v, v.shape[1] - 1, 1)


def south(v):
    return pltpu.roll(v, 1, 1)


def coefficients(zonal, merid, rate, self_mix):
    lat = lax.broadcasted_iota(jnp.int32, zonal.shape, 1)
    zonal_half, zonal_rate = 0.5 * zonal, 0.5 * zonal * zonal + rate
    merid_half, merid_rate = 0.5 * merid, 0.5 * merid * merid + rate
    east, west = zonal_rate - zonal_half, zonal_rate + zonal_half
    to_north, to_south = merid_rate - merid_half, merid_rate + merid_half
    centre = 1.0 + self_mix - 2.0 * zonal_rate - 2.0 * merid_rate
    last, first = lat == zonal.shape[1] - 1, lat == 0
    centre = centre + jnp.where(last, to_north, 0.0) + jnp.where(first, to_south, 0.0)
    to_north = jnp.where(last, 0.0, to_north)
    to_south = jnp.where(first, 0.0, to_south)
    return centre, east, west, to_north, to_south


def mixed(mixing, field, values):
    total = None
    for other, value in enumerate(values):
        if other != field:
            term = mixing[field, other] * value
            total = term if total is None else total + term
    return total


def pick_rows(kinds, particles, fields, strip):
    shape = (particles, particles * fields * strip)
    place = lax.broadcasted_iota(jnp.int32, shape, 1) - lax.broadcasted_iota(jnp.int32, shape, 0) * (fields * strip)
    blocks = [jnp.where(place == f * strip + x, 1.0, 0.0) for f, x in kinds]
    return jnp.concatenate(blocks, 0).astype(BF16)


def stack_rows(rows):
    sub = lax.broadcasted_iota(jnp.int32, (len(rows), rows[0].shape[1]), 0)
    out = None
    for p, row in enumerate(rows):
        row = jnp.broadcast_to(row, sub.shape)
        out = row if out is None else jnp.where(sub == p, row, out)
    return out


def in_row(column):
    total = jnp.broadcast_to(jnp.sum(column, axis=1, keepdims=True), column.shape)
    diagonal = lax.broadcasted_iota(jnp.int32, total.shape, 0) == lax.broadcasted_iota(jnp.int32, total.shape, 1)
    return jnp.sum(jnp.where(diagonal, total, 0.0), axis=0, keepdims=True)


def wide(v):
    return v[:, :128] + v[:, 128:]


def observation_maps(sizes, cell, value):
    particles, fields, strip, lats, strips = sizes
    x0 = lax.axis_index("lon") * strip
    shift = lats.bit_length() - 1
    local_cell = cell - x0 * lats
    obs_lon = lax.shift_right_arithmetic(local_cell, shift)
    obs_lat = local_cell & (lats - 1)
    count = cell.shape[1]
    here = lax.broadcasted_iota(jnp.int32, (strip, count), 0) == obs_lon
    high = value.astype(BF16)
    rest = value - high.astype(F32)
    mid = rest.astype(BF16)
    low = (rest - mid.astype(F32)).astype(BF16)
    zero = jnp.zeros((strip, count), F32)
    parts = [jnp.where(here, 1.0, zero)]
    parts += [jnp.where(here, p.astype(F32), zero) for p in (high, mid, low)]
    left = jnp.concatenate(parts, 0).astype(BF16)
    right = (lax.broadcasted_iota(jnp.int32, (lats, count), 0) == obs_lat).astype(F32).astype(BF16)
    dense = lax.dot_general(left, right, (((1,), (1,)), ((), ())), preferred_element_type=F32)
    lon = (lax.broadcasted_iota(jnp.int32, (strip, lats), 0) + x0).astype(F32)
    precision = 1.0 + 2.0 * lon / (strip * strips)
    target = dense[strip:2 * strip] + (dense[2 * strip:3 * strip] + dense[3 * strip:])
    return dense[:strip] * (0.25 * precision), target


class Rows:
    def __init__(self, ref, first, columns):
        self.ref, self.first, self.columns = ref, first, columns

    def __getitem__(self, at):
        row = self.first + at[0] * self.columns + at[1]
        return self.ref[row:row + 1]


def scalars_in(ref, fields):
    return Rows(ref, fields * fields, fields), Rows(ref, 0, fields)


def prepare(sizes, state_hbm, noise_hbm, courant_hbm, diffusion_hbm, mixing_hbm, cell_hbm, value_hbm,
            send_east, send_west, state, noise, maps, courant, scalars,
            diffusion, mixing, cell, value, sems):
    particles, fields, strip, lats, strips = sizes
    n = fields * particles
    copies = [pltpu.make_async_copy(source, target, sems.at[k]) for k, (source, target) in enumerate((
        (cell_hbm, cell), (value_hbm, value), (courant_hbm, courant), (diffusion_hbm, diffusion),
        (mixing_hbm, mixing), (state_hbm.at[:, :, :8], state.at[:, :, :8]),
        (state_hbm.at[:, :, strip - 8:], state.at[:, :, strip - 8:]), (noise_hbm.at[0], noise.at[0]),
        (noise_hbm.at[1, :, 0], noise.at[1, :, 0]), (state_hbm.at[:, :, 8:strip - 8], state.at[:, :, 8:strip - 8]),
        (noise_hbm.at[1, :, 1:], noise.at[1, :, 1:])))]
    for copy in copies:
        copy.start()
    copies[0].wait()
    copies[1].wait()
    gain, target = observation_maps(sizes, cell[...], value[...])
    maps[0], maps[1] = gain, target
    kinds = []
    for x, step in ((strip - 1, -1), (0, 1)):
        kinds += [(f, x) for f in range(fields)] + [(f, x + step) for f in range(fields)] + [(0, x + 2 * step)]
    pick0 = pick_rows(kinds, particles, fields, strip)
    pick1 = pick_rows([(0, x) for x in (strip - 1, strip - 2, 0, 1)], particles, 1, strip)
    for copy in copies[2:5]:
        copy.wait()
    for f in range(fields):
        for g in range(fields):
            scalars[f * fields + g:f * fields + g + 1] = jnp.broadcast_to(mixing[f:f + 1, g:g + 1], (1, lats))
        at = fields * fields + f
        scalars[at:at + 1] = jnp.broadcast_to(diffusion[:, f:f + 1], (1, lats))
    diffusion, mixing = scalars_in(scalars, fields)

    sides = []
    for first, inward, outward in ((strip - 8, 2, 1), (0, 1, 2)):
        tile = [coefficients(courant[0, first:first + 8], courant[1, first:first + 8], diffusion[0, f], mixing[f, f])
                for f in range(fields)]
        sides.append([[c[0], c[inward], c[outward], c[3], c[4]] for c in tile])
    def coefs_at(side, f, k):
        at = places[side][0] + k * places[side][2] - places[side][1]
        return [c[at:at + 1] for c in sides[side][f]]

    def maps_at(side, k):
        at = places[side][0] + k * places[side][2]
        return gain[at:at + 1], target[at:at + 1]

    def moved(side, f, k, here, inner, outer):
        centre, inward, outward, to_north, to_south = coefs_at(side, f, k)
        v = here[f]
        total = centre * v + inward * inner + to_north * north(v) + to_south * south(v) + mixed(mixing, f, here)
        return total if outer is None else total + outward * outer

    def nudged(side, value, k):
        g, v = maps_at(side, k)
        push = g * (v - value)
        return value + push, push

    def first_step(side, out):
        def state_at(f, k):
            at = places[side][0] + k * places[side][2]
            return stack_rows([state[p, f, at:at + 1] for p in range(particles)])

        near = [[state_at(f, k) for f in range(fields)] for k in range(3)]
        third = state_at(0, 3)
        for f in range(fields):
            out[f * particles:(f + 1) * particles] = near[0][f]
        result, pushes = [[], []], []
        for k in range(2):
            for f in range(fields):
                new = moved(side, f, k, near[k], near[k + 1][f], near[k - 1][f] if k else None)
                if f == 0:
                    new, push = nudged(side, new, k)
                    pushes.append(push)
                result[k].append(new)
        inside, _ = nudged(side, moved(side, 0, 2, near[2], third, near[1][0]), 2)
        return result, pushes, inside

    places = ((strip - 1, strip - 8, -1), (0, 0, 1))
    copies[5].wait()
    copies[6].wait()
    started = [first_step(0, send_east), first_step(1, send_west)]
    copies[7].wait()
    copies[8].wait()
    rows0 = jnp.dot(pick0, noise[0].reshape(n * strip, lats), preferred_element_type=F32)
    rows1 = jnp.dot(pick1, noise[1, :, 0].reshape(particles * strip, lats), preferred_element_type=F32)

    def edge(side, out):
        x, _, step = places[side]
        base0, base1 = side * (2 * fields + 1) * particles, side * 2 * particles
        result, pushes, inside = started[side]

        def noisy0(k, f):
            at = base0 + (k * fields + f) * particles
            return rows0[at:at + particles]

        def noisy1(k):
            at = base1 + k * particles
            return rows1[at:at + particles]

        result = [[result[k][f] + noisy0(k, f) for f in range(fields)] for k in range(2)]
        inside = inside + noisy0(2, 0)
        g0, _ = maps_at(side, 0)
        g1, _ = maps_at(side, 1)
        slope = [-(1.0 / noise_var) * g0 * (pushes[0] + noisy0(0, 0))]
        bend = [(0.5 / noise_var) * g0 * g0]
        for k, g in enumerate((g0, g1)):
            new = moved(side, 0, k, result[k], result[1][0] if k == 0 else inside, result[0][0] if k else None)
            new, push = nudged(side, new, k)
            miss = maps_at(side, k)[1] - (new + noisy1(k))
            weight = 4.0 * g
            slope.append(-(1.0 / noise_var) * g * (push + noisy1(k)) - weight * (1.0 - g) * miss)
            bend.append((0.5 / noise_var) * g * g + 0.5 * weight * (1.0 - g) * (1.0 - g))
        outward = coefs_at(side, 0, 0)[2]
        onward = coefs_at(side, 0, 1)[2] * (1.0 - g0) * outward
        for f in range(fields):
            out[n + f * particles:n + (f + 1) * particles] = result[0][f]
        out[2 * n:2 * n + particles] = outward * slope[0] + onward * slope[2]
        out[2 * n + particles:2 * n + 2 * particles] = slope[1]
        inner = x + step
        last = (outward * outward * bend[0] + onward * onward * bend[2], bend[1],
                courant[0, x:x + 1], courant[1, x:x + 1], g0, courant[0, inner:inner + 1], g1,
                jnp.zeros((1, lats), F32))
        out[2 * n + 2 * particles:] = stack_rows(last)

    edge(0, send_east)
    edge(1, send_west)
    copies[9].wait()
    copies[10].wait()


def zero_halo_coefs(sizes, courant, scalars, coefs):
    particles, fields, strip, lats, strips = sizes
    diffusion, mixing = scalars_in(scalars, fields)
    lon = lax.broadcasted_iota(jnp.int32, (strip, lats), 0)
    for f in range(fields):
        centre, east, west, to_north, to_south = coefficients(
            courant[0], courant[1], diffusion[0, f], mixing[f, f])
        coefs[f, 0] = centre
        coefs[f, 1] = jnp.where(lon == strip - 1, 0.0, east)
        coefs[f, 2] = jnp.where(lon == 0, 0.0, west)
        coefs[f, 3] = to_north
        coefs[f, 4] = to_south


def zero_halo_step(sizes, scalars, coefs):
    particles, fields, strip, lats, strips = sizes
    _, mixing = scalars_in(scalars, fields)

    def moved(values, f):
        v = values[f]
        return (coefs[f, 0] * v + coefs[f, 1] * pltpu.roll(v, strip - 1, 0) + coefs[f, 2] * pltpu.roll(v, 1, 0)
                + coefs[f, 3] * north(v) + coefs[f, 4] * south(v) + mixed(mixing, f, values))

    return moved


def observed_bulk(sizes, parity, state, noise, maps, courant, scalars, earlier, middle, out, weight, coefs, partial):
    particles, fields, strip, lats, strips = sizes

    def one(p):
        moved = zero_halo_step(sizes, scalars, coefs)
        values = [state[p, f] for f in range(fields)]
        results = []
        for f in range(fields):
            new = moved(values, f)
            add = noise[0, p, f].astype(F32)
            if f == 0:
                push = maps[0] * (maps[1] - new)
                new = new + push
                total = push * (push + 2.0 * add)
            results.append(new + add)
            middle[p, f] = new + add
        new = moved(results, 0)
        add = noise[1, p, 0].astype(F32)
        push = maps[0] * (maps[1] - new)
        new = new + push + add
        miss = maps[1] - new
        total = (0.5 / noise_var) * (total + push * (push + 2.0 * add)) + (2.0 * maps[0]) * (miss * miss)
        out[p] = new
        partial[pl.ds(p, 1), :] = wide(jnp.sum(total, axis=0, keepdims=True))

    def body(pair, carry):
        one(2 * pair)
        one(2 * pair + 1)
        return carry

    here = lax.axis_index("lon") % 2 == parity

    @pl.when(here)
    def _():
        zero_halo_coefs(sizes, courant, scalars, coefs)
        lax.fori_loop(0, particles // 2, body, 0)
        weight[...] = in_row(partial[...])

    @pl.when(jnp.logical_not(here))
    def _():
        weight[...] = earlier[:1, :128]


def other_bulk(sizes, even_middle, even_observed, even_coefs, odd_middle, odd_observed, odd_coefs,
               noise, scalars, out):
    particles, fields, strip, lats, strips = sizes

    def run(middle, observed, coefs):
        moved = zero_halo_step(sizes, scalars, coefs)

        def body(p, carry):
            values = [middle[p, f] for f in range(fields)]
            out[p, 0] = observed[p]
            for f in range(1, fields):
                out[p, f] = moved(values, f) + noise[1, p, f].astype(F32)
            return carry

        lax.fori_loop(0, particles, body, 0)

    even = lax.axis_index("lon") % 2 == 0

    @pl.when(even)
    def _():
        run(even_middle, even_observed, even_coefs)

    @pl.when(jnp.logical_not(even))
    def _():
        run(odd_middle, odd_observed, odd_coefs)


def correct(sizes, own_east, own_west, from_west, from_east, scalars, bulk_weight, weight, changes):
    particles, fields, strip, lats, strips = sizes
    n = fields * particles
    diffusion, mixing = scalars_in(scalars, fields)

    def field_rows(ref, start, f):
        return ref[start + f * particles:start + (f + 1) * particles]

    packets = (own_east, from_east, own_west, from_west)
    last = 2 * n + 2 * particles
    zonal = stack_rows([ref[last + 2:last + 3] for ref in packets] + [ref[last + 5:last + 6] for ref in packets])
    merid = stack_rows([ref[last + 3:last + 4] for ref in packets] * 2)
    tile = [coefficients(zonal, merid, diffusion[0, f], mixing[f, f]) for f in range(fields)]
    total = jnp.zeros((particles, lats), F32)
    for k, owner in enumerate(packets):
        other_k = k ^ 1
        other = packets[other_k]
        outward_at = (1, 2, 2, 1)[k]
        outward_other = (1, 2, 2, 1)[other_k]
        gain = owner[last + 4:last + 5]
        gain_other = other[last + 4:last + 5]
        first = []
        for f in range(fields):
            step = tile[f][outward_at][k:k + 1] * field_rows(other, 0, f)
            first.append((1.0 - gain) * step if f == 0 else step)
        mine = k in (0, 2)
        for f in range(fields if mine else 1):
            centre, to_north, to_south = [tile[f][c][k:k + 1] for c in (0, 3, 4)]
            outward = tile[f][outward_at][k:k + 1]
            reach = tile[f][outward_other][other_k:other_k + 1]
            if f == 0:
                reach = (1.0 - gain_other) * reach
            outside = field_rows(other, n, f) + reach * field_rows(owner, 0, f)
            step = (centre * first[f] + outward * outside + to_north * north(first[f])
                    + to_south * south(first[f]) + mixed(mixing, f, first))
            if f == 0:
                seen = field_rows(other, 0, 0)
                slope, slope_step = owner[2 * n:2 * n + particles], owner[2 * n + particles:last]
                bend, bend_step = owner[last:last + 1], owner[last + 1:last + 2]
                total = total + seen * (slope + bend * seen) + step * (slope_step + bend_step * step)
            if mine:
                beside = tile[f][outward_at][4 + k:5 + k] * first[f]
                if f == 0:
                    step = (1.0 - gain) * step
                    beside = (1.0 - owner[last + 6:last + 7]) * beside
                edge, inner = (3, 2) if k == 0 else (0, 1)
                changes[edge, f * particles:(f + 1) * particles] = step
                changes[inner, f * particles:(f + 1) * particles] = beside
    weight[...] = in_row(wide(total)) + bulk_weight[...]


def apply_changes(sizes, current, changes, out):
    particles, fields, strip, lats, strips = sizes
    sub = lax.broadcasted_iota(jnp.int32, (8, lats), 0)
    for p in range(particles):
        for f in range(fields):
            row = f * particles + p
            rows = [jnp.broadcast_to(changes[k, row:row + 1], sub.shape) for k in range(4)]
            out[p, f, :8] = current[p, f, :8] + jnp.where(sub == 0, rows[0], jnp.where(sub == 1, rows[1], 0.0))
            out[p, f, 8:strip - 8] = current[p, f, 8:strip - 8]
            out[p, f, strip - 8:] = current[p, f, strip - 8:] + jnp.where(
                sub == 7, rows[3], jnp.where(sub == 6, rows[2], 0.0))


def assemble(sizes, source, current, received, out, sems):
    particles = sizes[0]
    dom = lax.axis_index("dom")

    def copy(j, ref, at):
        return pltpu.make_async_copy(ref.at[at], out.at[j], sems.at[j])

    for j in range(particles):
        wanted = source[dom * particles + j]
        mine = wanted // particles == dom
        at = wanted % particles

        @pl.when(mine)
        def _():
            copy(j, current, at).start()

        @pl.when(jnp.logical_not(mine))
        def _():
            copy(j, received, at).start()

    for j in range(particles):
        copy(j, current, 0).wait()


def local(ensemble_state, proposal_noise, courant, diffusion, mixing, prior_weight, obs_cell, obs_value, source):
    particles, fields, strip, lats = ensemble_state.shape
    strips = lax.axis_size("lon")
    sizes = (particles, fields, strip, lats, strips)
    packet = jax.ShapeDtypeStruct((2 * particles * fields + 2 * particles + 8, lats), F32)
    cell, value = obs_cell[None], obs_value[None]

    def shape(*dims):
        return jax.ShapeDtypeStruct(dims, F32)

    whole = (particles, fields, strip, lats)

    def in_hbm(array):
        return pltpu.with_memory_space_constraint(array, pltpu.HBM)

    arrays = (ensemble_state, proposal_noise, courant, diffusion[None], mixing, cell, value)
    send_east, send_west, state, noise, maps, courant, scalars = pl.pallas_call(
        functools.partial(prepare, sizes),
        out_shape=(packet, packet, shape(*whole), jax.ShapeDtypeStruct((2,) + whole, BF16), shape(2, strip, lats),
                   shape(*courant.shape), shape(fields * (fields + 2), lats)),
        in_specs=[HBM] * 7,
        out_specs=(VMEM,) * 7,
        scratch_shapes=[pltpu.VMEM(array.shape, array.dtype) for array in arrays[3:]]
        + [pltpu.SemaphoreType.DMA((11,))],
        compiler_params=LIMIT,
        cost_estimate=pl.CostEstimate(flops=1000000, bytes_accessed=2000000, transcendentals=0),
    )(*[in_hbm(array) for array in arrays])

    def bulk_of(parity, earlier):
        return pl.pallas_call(
            functools.partial(observed_bulk, sizes, parity),
            out_shape=(shape(*whole), shape(particles, strip, lats), shape(1, 128), shape(fields, 5, strip, lats)),
            in_specs=[VMEM] * 6,
            out_specs=(VMEM,) * 4,
            scratch_shapes=[pltpu.VMEM((particles, 128), F32)],
            compiler_params=LIMIT,
            cost_estimate=pl.CostEstimate(flops=20000000, bytes_accessed=4000000, transcendentals=0),
        )(state, noise, maps, courant, scalars, earlier)

    even_middle, even_observed, bulk_weight, even_coefs = bulk_of(0, scalars)
    send_east, send_west, bulk_weight = lax.optimization_barrier((send_east, send_west, bulk_weight))
    eastward = [(i, (i + 1) % strips) for i in range(strips)]
    westward = [(i, (i - 1) % strips) for i in range(strips)]
    from_west = lax.ppermute(send_east, "lon", eastward)
    from_east = lax.ppermute(send_west, "lon", westward)
    odd_middle, odd_observed, bulk_weight, odd_coefs = bulk_of(1, bulk_weight)
    beside = lax.ppermute(bulk_weight, "lon", [(i, i ^ 1) for i in range(strips)])

    current = pl.pallas_call(
        functools.partial(other_bulk, sizes),
        out_shape=shape(*whole),
        in_specs=[VMEM] * 8,
        out_specs=VMEM,
        compiler_params=LIMIT,
        cost_estimate=FREE,
    )(even_middle, even_observed, even_coefs, odd_middle, odd_observed, odd_coefs, noise, scalars)

    weight, changes = pl.pallas_call(
        functools.partial(correct, sizes),
        out_shape=(shape(1, 128), shape(4, particles * fields, lats)),
        in_specs=[VMEM] * 6,
        out_specs=(VMEM,) * 2,
        compiler_params=LIMIT,
        cost_estimate=FREE,
    )(send_east, send_west, from_west, from_east, scalars, bulk_weight)

    current = pl.pallas_call(
        functools.partial(apply_changes, sizes),
        out_shape=shape(*whole),
        in_specs=[VMEM] * 2,
        out_specs=VMEM,
        compiler_params=LIMIT,
        cost_estimate=FREE,
    )(current, changes)

    current, beside = lax.optimization_barrier((current, beside))
    weight = weight + beside
    received = lax.ppermute(current, "dom", [(0, 1), (1, 0)])
    bit = 2
    while bit < strips:
        steps = (2, 3, 1) if 2 * bit < strips else (1,)
        arrived = []
        for step in steps:
            if step == 1 and bit * (len(steps) + 1) >= strips:
                weight, received = lax.optimization_barrier((weight, received))
            arrived.append(lax.ppermute(weight, "lon", [(i, i ^ (bit * step)) for i in range(strips)]))
        weight = sum(arrived, weight)
        bit *= len(steps) + 1

    new_state = pl.pallas_call(
        functools.partial(assemble, sizes),
        out_shape=shape(*whole),
        in_specs=[SMEM, VMEM, VMEM],
        out_specs=HBM,
        scratch_shapes=[pltpu.SemaphoreType.DMA((particles,))],
        compiler_params=LIMIT,
        cost_estimate=pl.CostEstimate(flops=0, bytes_accessed=2000000, transcendentals=0),
    )(source, current, received)

    log_weight = prior_weight - weight[0, :particles] / (256.0 * obs_cell.shape[0])
    return new_state, log_weight


def solution(mesh):
    placed = (
        P(("groups", "dom"), None, "lon", None),
        P(None, ("groups", "dom"), None, "lon", None),
        P(None, ("groups", "lon"), None),
        P(),
        P(),
        P(("groups", "dom")),
        P(("groups", "lon")),
        P(("groups", "lon")),
        P("groups"),
    )
    return jax.shard_map(
        local,
        mesh=mesh,
        in_specs=placed,
        out_specs=(P(("groups", "dom"), None, "lon", None), P(("groups", "dom"))),
        check_vma=False,
    )
```

```python
import functools

import jax
import jax.numpy as jnp
from jax import lax
from jax.experimental import pallas as pl
from jax.experimental.pallas import tpu as pltpu
from jax.sharding import PartitionSpec as P

noise_var = 0.04
VMEM = pl.BlockSpec(memory_space=pltpu.VMEM)
SMEM = pl.BlockSpec(memory_space=pltpu.SMEM)
HBM = pl.BlockSpec(memory_space=pltpu.HBM)
LIMIT = pltpu.CompilerParams(vmem_limit_bytes=16 * 1024 * 1024)
FREE = pl.CostEstimate(flops=0, bytes_accessed=0, transcendentals=0)
BF16 = jnp.bfloat16
F32 = jnp.float32


def north(v):
    low, high = (pltpu.roll(v[:, at:at + 128], 127, 1) for at in (0, 128))
    lane = lax.broadcasted_iota(jnp.int32, low.shape, 1)
    return jnp.concatenate([jnp.where(lane == 127, high, low), high], 1)


def south(v):
    low, high = (pltpu.roll(v[:, at:at + 128], 1, 1) for at in (0, 128))
    lane = lax.broadcasted_iota(jnp.int32, low.shape, 1)
    return jnp.concatenate([low, jnp.where(lane == 0, low, high)], 1)


def east_of(v):
    tiles = [pltpu.roll(v[at:at + 8], 7, 0) for at in range(0, v.shape[0], 8)]
    sub = lax.broadcasted_iota(jnp.int32, tiles[0].shape, 0)
    mixed_tiles = [jnp.where(sub == 7, after, tile) for tile, after in zip(tiles[:-1], tiles[1:])]
    return jnp.concatenate(mixed_tiles + tiles[-1:], 0)


def west_of(v):
    tiles = [pltpu.roll(v[at:at + 8], 1, 0) for at in range(0, v.shape[0], 8)]
    sub = lax.broadcasted_iota(jnp.int32, tiles[0].shape, 0)
    mixed_tiles = [jnp.where(sub == 0, before, tile) for before, tile in zip(tiles[:-1], tiles[1:])]
    return jnp.concatenate(tiles[:1] + mixed_tiles, 0)


def coefficients(zonal, merid, rate, self_mix):
    lat = lax.broadcasted_iota(jnp.int32, zonal.shape, 1)
    zonal_half, zonal_rate = 0.5 * zonal, 0.5 * zonal * zonal + rate
    merid_half, merid_rate = 0.5 * merid, 0.5 * merid * merid + rate
    east, west = zonal_rate - zonal_half, zonal_rate + zonal_half
    to_north, to_south = merid_rate - merid_half, merid_rate + merid_half
    centre = 1.0 + self_mix - 2.0 * zonal_rate - 2.0 * merid_rate
    last, first = lat == zonal.shape[1] - 1, lat == 0
    centre = centre + jnp.where(last, to_north, 0.0) + jnp.where(first, to_south, 0.0)
    to_north = jnp.where(last, 0.0, to_north)
    to_south = jnp.where(first, 0.0, to_south)
    return centre, east, west, to_north, to_south


def mixed(mixing, field, values):
    total = None
    for other, value in enumerate(values):
        if other != field:
            term = mixing[field, other] * value
            total = term if total is None else total + term
    return total


def pick_rows(kinds, particles, fields, strip):
    shape = (particles, particles * fields * strip)
    place = lax.broadcasted_iota(jnp.int32, shape, 1) - lax.broadcasted_iota(jnp.int32, shape, 0) * (fields * strip)
    blocks = [jnp.where(place == f * strip + x, 1.0, 0.0) for f, x in kinds]
    return jnp.concatenate(blocks, 0).astype(BF16)


def stack_rows(rows):
    sub = lax.broadcasted_iota(jnp.int32, (len(rows), rows[0].shape[1]), 0)
    out = None
    for p, row in enumerate(rows):
        row = jnp.broadcast_to(row, sub.shape)
        out = row if out is None else jnp.where(sub == p, row, out)
    return out


def in_row(column):
    total = jnp.broadcast_to(jnp.sum(column, axis=1, keepdims=True), column.shape)
    diagonal = lax.broadcasted_iota(jnp.int32, total.shape, 0) == lax.broadcasted_iota(jnp.int32, total.shape, 1)
    return jnp.sum(jnp.where(diagonal, total, 0.0), axis=0, keepdims=True)


def wide(v):
    return v[:, :128] + v[:, 128:]


def observation_maps(sizes, cell, value):
    particles, fields, strip, lats, strips = sizes
    x0 = lax.axis_index("lon") * strip
    shift = lats.bit_length() - 1
    local_cell = cell - x0 * lats
    obs_lon = lax.shift_right_arithmetic(local_cell, shift)
    obs_lat = local_cell & (lats - 1)
    count = cell.shape[1]
    here = lax.broadcasted_iota(jnp.int32, (strip, count), 0) == obs_lon
    high = value.astype(BF16)
    rest = value - high.astype(F32)
    mid = rest.astype(BF16)
    low = (rest - mid.astype(F32)).astype(BF16)
    zero = jnp.zeros((strip, count), F32)
    parts = [jnp.where(here, 1.0, zero)]
    parts += [jnp.where(here, p.astype(F32), zero) for p in (high, mid, low)]
    left = jnp.concatenate(parts, 0).astype(BF16)
    right = (lax.broadcasted_iota(jnp.int32, (lats, count), 0) == obs_lat).astype(F32).astype(BF16)
    dense = lax.dot_general(left, right, (((1,), (1,)), ((), ())), preferred_element_type=F32)
    lon = (lax.broadcasted_iota(jnp.int32, (strip, lats), 0) + x0).astype(F32)
    precision = 1.0 + 2.0 * lon / (strip * strips)
    target = dense[strip:2 * strip] + (dense[2 * strip:3 * strip] + dense[3 * strip:])
    return dense[:strip] * (0.25 * precision), target


class Rows:
    def __init__(self, ref, first, columns):
        self.ref, self.first, self.columns = ref, first, columns

    def __getitem__(self, at):
        row = self.first + at[0] * self.columns + at[1]
        return self.ref[row:row + 1]


def scalars_in(ref, fields):
    return Rows(ref, fields * fields, fields), Rows(ref, 0, fields)


def prepare(sizes, state_hbm, noise_hbm, courant_hbm, diffusion_hbm, mixing_hbm, cell_hbm, value_hbm,
            send_east, send_west, state, noise, maps, courant, scalars,
            diffusion, mixing, cell, value, sems):
    particles, fields, strip, lats, strips = sizes
    n = fields * particles
    copies = [pltpu.make_async_copy(source, target, sems.at[k]) for k, (source, target) in enumerate((
        (cell_hbm, cell), (value_hbm, value), (courant_hbm, courant), (diffusion_hbm, diffusion),
        (mixing_hbm, mixing), (state_hbm.at[:, :, :8], state.at[:, :, :8]),
        (state_hbm.at[:, :, strip - 8:], state.at[:, :, strip - 8:]), (noise_hbm.at[0], noise.at[0]),
        (noise_hbm.at[1, :, 0], noise.at[1, :, 0]), (state_hbm.at[:, :, 8:strip - 8], state.at[:, :, 8:strip - 8]),
        (noise_hbm.at[1, :, 1:], noise.at[1, :, 1:])))]
    for copy in copies:
        copy.start()
    copies[0].wait()
    copies[1].wait()
    gain, target = observation_maps(sizes, cell[...], value[...])
    maps[0], maps[1] = gain, target
    kinds = []
    for x, step in ((strip - 1, -1), (0, 1)):
        kinds += [(f, x) for f in range(fields)] + [(f, x + step) for f in range(fields)] + [(0, x + 2 * step)]
    pick0 = pick_rows(kinds, particles, fields, strip)
    pick1 = pick_rows([(0, x) for x in (strip - 1, strip - 2, 0, 1)], particles, 1, strip)
    for copy in copies[2:5]:
        copy.wait()
    for f in range(fields):
        for g in range(fields):
            scalars[f * fields + g:f * fields + g + 1] = jnp.broadcast_to(mixing[f:f + 1, g:g + 1], (1, lats))
        at = fields * fields + f
        scalars[at:at + 1] = jnp.broadcast_to(diffusion[:, f:f + 1], (1, lats))
    diffusion, mixing = scalars_in(scalars, fields)

    sides = []
    for first, inward, outward in ((strip - 8, 2, 1), (0, 1, 2)):
        tile = [coefficients(courant[0, first:first + 8], courant[1, first:first + 8], diffusion[0, f], mixing[f, f])
                for f in range(fields)]
        sides.append([[c[0], c[inward], c[outward], c[3], c[4]] for c in tile])
    def coefs_at(side, f, k):
        at = places[side][0] + k * places[side][2] - places[side][1]
        return [c[at:at + 1] for c in sides[side][f]]

    def maps_at(side, k):
        at = places[side][0] + k * places[side][2]
        return gain[at:at + 1], target[at:at + 1]

    def moved(side, f, k, here, inner, outer):
        centre, inward, outward, to_north, to_south = coefs_at(side, f, k)
        v = here[f]
        total = centre * v + inward * inner + to_north * north(v) + to_south * south(v) + mixed(mixing, f, here)
        return total if outer is None else total + outward * outer

    def nudged(side, value, k):
        g, v = maps_at(side, k)
        push = g * (v - value)
        return value + push, push

    def first_step(side, out):
        def state_at(f, k):
            at = places[side][0] + k * places[side][2]
            return stack_rows([state[p, f, at:at + 1] for p in range(particles)])

        near = [[state_at(f, k) for f in range(fields)] for k in range(3)]
        third = state_at(0, 3)
        for f in range(fields):
            out[f * particles:(f + 1) * particles] = near[0][f]
        result, pushes = [[], []], []
        for k in range(2):
            for f in range(fields):
                new = moved(side, f, k, near[k], near[k + 1][f], near[k - 1][f] if k else None)
                if f == 0:
                    new, push = nudged(side, new, k)
                    pushes.append(push)
                result[k].append(new)
        inside, _ = nudged(side, moved(side, 0, 2, near[2], third, near[1][0]), 2)
        return result, pushes, inside

    places = ((strip - 1, strip - 8, -1), (0, 0, 1))
    copies[5].wait()
    copies[6].wait()
    started = [first_step(0, send_east), first_step(1, send_west)]
    copies[7].wait()
    copies[8].wait()
    rows0 = jnp.dot(pick0, noise[0].reshape(n * strip, lats), preferred_element_type=F32)
    rows1 = jnp.dot(pick1, noise[1, :, 0].reshape(particles * strip, lats), preferred_element_type=F32)

    def edge(side, out):
        x, _, step = places[side]
        base0, base1 = side * (2 * fields + 1) * particles, side * 2 * particles
        result, pushes, inside = started[side]

        def noisy0(k, f):
            at = base0 + (k * fields + f) * particles
            return rows0[at:at + particles]

        def noisy1(k):
            at = base1 + k * particles
            return rows1[at:at + particles]

        result = [[result[k][f] + noisy0(k, f) for f in range(fields)] for k in range(2)]
        inside = inside + noisy0(2, 0)
        g0, _ = maps_at(side, 0)
        g1, _ = maps_at(side, 1)
        slope = [-(1.0 / noise_var) * g0 * (pushes[0] + noisy0(0, 0))]
        bend = [(0.5 / noise_var) * g0 * g0]
        for k, g in enumerate((g0, g1)):
            new = moved(side, 0, k, result[k], result[1][0] if k == 0 else inside, result[0][0] if k else None)
            new, push = nudged(side, new, k)
            miss = maps_at(side, k)[1] - (new + noisy1(k))
            weight = 4.0 * g
            slope.append(-(1.0 / noise_var) * g * (push + noisy1(k)) - weight * (1.0 - g) * miss)
            bend.append((0.5 / noise_var) * g * g + 0.5 * weight * (1.0 - g) * (1.0 - g))
        outward = coefs_at(side, 0, 0)[2]
        onward = coefs_at(side, 0, 1)[2] * (1.0 - g0) * outward
        for f in range(fields):
            out[n + f * particles:n + (f + 1) * particles] = result[0][f]
        out[2 * n:2 * n + particles] = outward * slope[0] + onward * slope[2]
        out[2 * n + particles:2 * n + 2 * particles] = slope[1]
        inner = x + step
        last = (outward * outward * bend[0] + onward * onward * bend[2], bend[1],
                courant[0, x:x + 1], courant[1, x:x + 1], g0, courant[0, inner:inner + 1], g1,
                jnp.zeros((1, lats), F32))
        out[2 * n + 2 * particles:] = stack_rows(last)

    edge(0, send_east)
    edge(1, send_west)
    copies[9].wait()
    copies[10].wait()


def zero_halo_coefs(sizes, courant, scalars, coefs):
    particles, fields, strip, lats, strips = sizes
    diffusion, mixing = scalars_in(scalars, fields)
    lon = lax.broadcasted_iota(jnp.int32, (strip, lats), 0)
    for f in range(fields):
        centre, east, west, to_north, to_south = coefficients(
            courant[0], courant[1], diffusion[0, f], mixing[f, f])
        coefs[f, 0] = centre
        coefs[f, 1] = jnp.where(lon == strip - 1, 0.0, east)
        coefs[f, 2] = jnp.where(lon == 0, 0.0, west)
        coefs[f, 3] = to_north
        coefs[f, 4] = to_south


def zero_halo_step(sizes, scalars, coefs):
    particles, fields, strip, lats, strips = sizes
    _, mixing = scalars_in(scalars, fields)

    def moved(values, f):
        v = values[f]
        return (coefs[f, 0] * v + coefs[f, 1] * east_of(v) + coefs[f, 2] * west_of(v)
                + coefs[f, 3] * north(v) + coefs[f, 4] * south(v) + mixed(mixing, f, values))

    return moved


def observed_bulk(sizes, parity, state, noise, maps, courant, scalars, earlier, middle, out, weight, coefs, partial):
    particles, fields, strip, lats, strips = sizes

    def one(p):
        moved = zero_halo_step(sizes, scalars, coefs)
        values = [state[p, f] for f in range(fields)]
        results = []
        for f in range(fields):
            new = moved(values, f)
            add = noise[0, p, f].astype(F32)
            if f == 0:
                push = maps[0] * (maps[1] - new)
                new = new + push
                total = push * (push + 2.0 * add)
            results.append(new + add)
            middle[p, f] = new + add
        new = moved(results, 0)
        add = noise[1, p, 0].astype(F32)
        push = maps[0] * (maps[1] - new)
        new = new + push + add
        miss = maps[1] - new
        total = (0.5 / noise_var) * (total + push * (push + 2.0 * add)) + (2.0 * maps[0]) * (miss * miss)
        out[p] = new
        partial[pl.ds(p, 1), :] = wide(jnp.sum(total, axis=0, keepdims=True))

    def body(step, carry):
        for k in range(4):
            one(4 * step + k)
        return carry

    here = lax.axis_index("lon") % 2 == parity

    @pl.when(here)
    def _():
        zero_halo_coefs(sizes, courant, scalars, coefs)
        lax.fori_loop(0, particles // 4, body, 0)
        weight[...] = in_row(partial[...])

    @pl.when(jnp.logical_not(here))
    def _():
        weight[...] = earlier[:1, :128]


def other_bulk(sizes, even_middle, even_observed, even_coefs, odd_middle, odd_observed, odd_coefs,
               noise, scalars, out):
    particles, fields, strip, lats, strips = sizes

    def run(middle, observed, coefs):
        moved = zero_halo_step(sizes, scalars, coefs)

        def body(p, carry):
            values = [middle[p, f] for f in range(fields)]
            out[p, 0] = observed[p]
            for f in range(1, fields):
                out[p, f] = moved(values, f) + noise[1, p, f].astype(F32)
            return carry

        lax.fori_loop(0, particles, body, 0)

    even = lax.axis_index("lon") % 2 == 0

    @pl.when(even)
    def _():
        run(even_middle, even_observed, even_coefs)

    @pl.when(jnp.logical_not(even))
    def _():
        run(odd_middle, odd_observed, odd_coefs)


def correct(sizes, own_east, own_west, from_west, from_east, scalars, bulk_weight, weight, changes):
    particles, fields, strip, lats, strips = sizes
    n = fields * particles
    diffusion, mixing = scalars_in(scalars, fields)

    def field_rows(ref, start, f):
        return ref[start + f * particles:start + (f + 1) * particles]

    packets = (own_east, from_east, own_west, from_west)
    last = 2 * n + 2 * particles
    zonal = stack_rows([ref[last + 2:last + 3] for ref in packets] + [ref[last + 5:last + 6] for ref in packets])
    merid = stack_rows([ref[last + 3:last + 4] for ref in packets] * 2)
    tile = [coefficients(zonal, merid, diffusion[0, f], mixing[f, f]) for f in range(fields)]
    total = jnp.zeros((particles, lats), F32)
    for k, owner in enumerate(packets):
        other_k = k ^ 1
        other = packets[other_k]
        outward_at = (1, 2, 2, 1)[k]
        outward_other = (1, 2, 2, 1)[other_k]
        gain = owner[last + 4:last + 5]
        gain_other = other[last + 4:last + 5]
        first = []
        for f in range(fields):
            step = tile[f][outward_at][k:k + 1] * field_rows(other, 0, f)
            first.append((1.0 - gain) * step if f == 0 else step)
        mine = k in (0, 2)
        for f in range(fields if mine else 1):
            centre, to_north, to_south = [tile[f][c][k:k + 1] for c in (0, 3, 4)]
            outward = tile[f][outward_at][k:k + 1]
            reach = tile[f][outward_other][other_k:other_k + 1]
            if f == 0:
                reach = (1.0 - gain_other) * reach
            outside = field_rows(other, n, f) + reach * field_rows(owner, 0, f)
            step = (centre * first[f] + outward * outside + to_north * north(first[f])
                    + to_south * south(first[f]) + mixed(mixing, f, first))
            if f == 0:
                seen = field_rows(other, 0, 0)
                slope, slope_step = owner[2 * n:2 * n + particles], owner[2 * n + particles:last]
                bend, bend_step = owner[last:last + 1], owner[last + 1:last + 2]
                total = total + seen * (slope + bend * seen) + step * (slope_step + bend_step * step)
            if mine:
                beside = tile[f][outward_at][4 + k:5 + k] * first[f]
                if f == 0:
                    step = (1.0 - gain) * step
                    beside = (1.0 - owner[last + 6:last + 7]) * beside
                edge, inner = (3, 2) if k == 0 else (0, 1)
                changes[edge, f * particles:(f + 1) * particles] = step
                changes[inner, f * particles:(f + 1) * particles] = beside
    weight[...] = in_row(wide(total)) + bulk_weight[...]


def apply_changes(sizes, current, changes, out):
    particles, fields, strip, lats, strips = sizes
    sub = lax.broadcasted_iota(jnp.int32, (8, lats), 0)
    for p in range(particles):
        for f in range(fields):
            row = f * particles + p
            rows = [jnp.broadcast_to(changes[k, row:row + 1], sub.shape) for k in range(4)]
            out[p, f, :8] = current[p, f, :8] + jnp.where(sub == 0, rows[0], jnp.where(sub == 1, rows[1], 0.0))
            out[p, f, 8:strip - 8] = current[p, f, 8:strip - 8]
            out[p, f, strip - 8:] = current[p, f, strip - 8:] + jnp.where(
                sub == 7, rows[3], jnp.where(sub == 6, rows[2], 0.0))


def assemble(sizes, source, current, received, out, sems):
    particles = sizes[0]
    dom = lax.axis_index("dom")

    def copy(j, ref, at):
        return pltpu.make_async_copy(ref.at[at], out.at[j], sems.at[j])

    for j in range(particles):
        wanted = source[dom * particles + j]
        mine = wanted // particles == dom
        at = wanted % particles

        @pl.when(mine)
        def _():
            copy(j, current, at).start()

        @pl.when(jnp.logical_not(mine))
        def _():
            copy(j, received, at).start()

    for j in range(particles):
        copy(j, current, 0).wait()


def local(ensemble_state, proposal_noise, courant, diffusion, mixing, prior_weight, obs_cell, obs_value, source):
    particles, fields, strip, lats = ensemble_state.shape
    strips = lax.axis_size("lon")
    sizes = (particles, fields, strip, lats, strips)
    packet = jax.ShapeDtypeStruct((2 * particles * fields + 2 * particles + 8, lats), F32)
    cell, value = obs_cell[None], obs_value[None]

    def shape(*dims):
        return jax.ShapeDtypeStruct(dims, F32)

    whole = (particles, fields, strip, lats)

    def in_hbm(array):
        return pltpu.with_memory_space_constraint(array, pltpu.HBM)

    arrays = (ensemble_state, proposal_noise, courant, diffusion[None], mixing, cell, value)
    send_east, send_west, state, noise, maps, courant, scalars = pl.pallas_call(
        functools.partial(prepare, sizes),
        out_shape=(packet, packet, shape(*whole), jax.ShapeDtypeStruct((2,) + whole, BF16), shape(2, strip, lats),
                   shape(*courant.shape), shape(fields * (fields + 2), lats)),
        in_specs=[HBM] * 7,
        out_specs=(VMEM,) * 7,
        scratch_shapes=[pltpu.VMEM(array.shape, array.dtype) for array in arrays[3:]]
        + [pltpu.SemaphoreType.DMA((11,))],
        compiler_params=LIMIT,
        cost_estimate=pl.CostEstimate(flops=1000000, bytes_accessed=2000000, transcendentals=0),
    )(*[in_hbm(array) for array in arrays])

    def bulk_of(parity, earlier):
        return pl.pallas_call(
            functools.partial(observed_bulk, sizes, parity),
            out_shape=(shape(*whole), shape(particles, strip, lats), shape(1, 128), shape(fields, 5, strip, lats)),
            in_specs=[VMEM] * 6,
            out_specs=(VMEM,) * 4,
            scratch_shapes=[pltpu.VMEM((particles, 128), F32)],
            compiler_params=LIMIT,
            cost_estimate=pl.CostEstimate(flops=20000000, bytes_accessed=4000000, transcendentals=0),
        )(state, noise, maps, courant, scalars, earlier)

    even_middle, even_observed, bulk_weight, even_coefs = bulk_of(0, scalars)
    send_east, send_west, bulk_weight = lax.optimization_barrier((send_east, send_west, bulk_weight))
    eastward = [(i, (i + 1) % strips) for i in range(strips)]
    westward = [(i, (i - 1) % strips) for i in range(strips)]
    from_west = lax.ppermute(send_east, "lon", eastward)
    from_east = lax.ppermute(send_west, "lon", westward)
    odd_middle, odd_observed, bulk_weight, odd_coefs = bulk_of(1, bulk_weight)
    beside = lax.ppermute(bulk_weight, "lon", [(i, i ^ 1) for i in range(strips)])

    current = pl.pallas_call(
        functools.partial(other_bulk, sizes),
        out_shape=shape(*whole),
        in_specs=[VMEM] * 8,
        out_specs=VMEM,
        compiler_params=LIMIT,
        cost_estimate=FREE,
    )(even_middle, even_observed, even_coefs, odd_middle, odd_observed, odd_coefs, noise, scalars)

    weight, changes = pl.pallas_call(
        functools.partial(correct, sizes),
        out_shape=(shape(1, 128), shape(4, particles * fields, lats)),
        in_specs=[VMEM] * 6,
        out_specs=(VMEM,) * 2,
        compiler_params=LIMIT,
        cost_estimate=FREE,
    )(send_east, send_west, from_west, from_east, scalars, bulk_weight)

    current = pl.pallas_call(
        functools.partial(apply_changes, sizes),
        out_shape=shape(*whole),
        in_specs=[VMEM] * 2,
        out_specs=VMEM,
        compiler_params=LIMIT,
        cost_estimate=FREE,
    )(current, changes)

    current, beside = lax.optimization_barrier((current, beside))
    weight = weight + beside
    received = lax.ppermute(current, "dom", [(0, 1), (1, 0)])
    bit = 2
    while bit < strips:
        steps = (2, 3, 1) if 2 * bit < strips else (1,)
        arrived = []
        for step in steps:
            if step == 1 and bit * (len(steps) + 1) >= strips:
                weight, received = lax.optimization_barrier((weight, received))
            arrived.append(lax.ppermute(weight, "lon", [(i, i ^ (bit * step)) for i in range(strips)]))
        weight = sum(arrived, weight)
        bit *= len(steps) + 1

    new_state = pl.pallas_call(
        functools.partial(assemble, sizes),
        out_shape=shape(*whole),
        in_specs=[SMEM, VMEM, VMEM],
        out_specs=HBM,
        scratch_shapes=[pltpu.SemaphoreType.DMA((particles,))],
        compiler_params=LIMIT,
        cost_estimate=pl.CostEstimate(flops=0, bytes_accessed=2000000, transcendentals=0),
    )(source, current, received)

    log_weight = prior_weight - weight[0, :particles] / (256.0 * obs_cell.shape[0])
    return new_state, log_weight


def solution(mesh):
    placed = (
        P(("groups", "dom"), None, "lon", None),
        P(None, ("groups", "dom"), None, "lon", None),
        P(None, ("groups", "lon"), None),
        P(),
        P(),
        P(("groups", "dom")),
        P(("groups", "lon")),
        P(("groups", "lon")),
        P("groups"),
    )
    return jax.shard_map(
        local,
        mesh=mesh,
        in_specs=placed,
        out_specs=(P(("groups", "dom"), None, "lon", None), P(("groups", "dom"))),
        check_vma=False,
    )
```

```python
import functools

import jax
import jax.numpy as jnp
from jax import lax
from jax.experimental import pallas as pl
from jax.experimental.pallas import tpu as pltpu
from jax.sharding import PartitionSpec as P

noise_var = 0.04
VMEM = pl.BlockSpec(memory_space=pltpu.VMEM)
SMEM = pl.BlockSpec(memory_space=pltpu.SMEM)
HBM = pl.BlockSpec(memory_space=pltpu.HBM)
LIMIT = pltpu.CompilerParams(vmem_limit_bytes=16 * 1024 * 1024)
FREE = pl.CostEstimate(flops=0, bytes_accessed=0, transcendentals=0)
BF16 = jnp.bfloat16
F32 = jnp.float32


def north(v):
    low, high = (pltpu.roll(v[:, at:at + 128], 127, 1) for at in (0, 128))
    lane = lax.broadcasted_iota(jnp.int32, low.shape, 1)
    return jnp.concatenate([jnp.where(lane == 127, high, low), high], 1)


def south(v):
    low, high = (pltpu.roll(v[:, at:at + 128], 1, 1) for at in (0, 128))
    lane = lax.broadcasted_iota(jnp.int32, low.shape, 1)
    return jnp.concatenate([low, jnp.where(lane == 0, low, high)], 1)


def east_of(v):
    tiles = [pltpu.roll(v[at:at + 8], 7, 0) for at in range(0, v.shape[0], 8)]
    sub = lax.broadcasted_iota(jnp.int32, tiles[0].shape, 0)
    mixed_tiles = [jnp.where(sub == 7, after, tile) for tile, after in zip(tiles[:-1], tiles[1:])]
    return jnp.concatenate(mixed_tiles + tiles[-1:], 0)


def west_of(v):
    tiles = [pltpu.roll(v[at:at + 8], 1, 0) for at in range(0, v.shape[0], 8)]
    sub = lax.broadcasted_iota(jnp.int32, tiles[0].shape, 0)
    mixed_tiles = [jnp.where(sub == 0, before, tile) for before, tile in zip(tiles[:-1], tiles[1:])]
    return jnp.concatenate(tiles[:1] + mixed_tiles, 0)


def coefficients(zonal, merid, rate, self_mix):
    lat = lax.broadcasted_iota(jnp.int32, zonal.shape, 1)
    zonal_half, zonal_rate = 0.5 * zonal, 0.5 * zonal * zonal + rate
    merid_half, merid_rate = 0.5 * merid, 0.5 * merid * merid + rate
    east, west = zonal_rate - zonal_half, zonal_rate + zonal_half
    to_north, to_south = merid_rate - merid_half, merid_rate + merid_half
    centre = 1.0 + self_mix - 2.0 * zonal_rate - 2.0 * merid_rate
    last, first = lat == zonal.shape[1] - 1, lat == 0
    centre = centre + jnp.where(last, to_north, 0.0) + jnp.where(first, to_south, 0.0)
    to_north = jnp.where(last, 0.0, to_north)
    to_south = jnp.where(first, 0.0, to_south)
    return centre, east, west, to_north, to_south


def mixed(mixing, field, values):
    total = None
    for other, value in enumerate(values):
        if other != field:
            term = mixing[field, other] * value
            total = term if total is None else total + term
    return total


def pick_rows(kinds, particles, fields, strip):
    shape = (particles, particles * fields * strip)
    place = lax.broadcasted_iota(jnp.int32, shape, 1) - lax.broadcasted_iota(jnp.int32, shape, 0) * (fields * strip)
    blocks = [jnp.where(place == f * strip + x, 1.0, 0.0) for f, x in kinds]
    return jnp.concatenate(blocks, 0).astype(BF16)


def stack_rows(rows):
    sub = lax.broadcasted_iota(jnp.int32, (len(rows), rows[0].shape[1]), 0)
    out = None
    for p, row in enumerate(rows):
        row = jnp.broadcast_to(row, sub.shape)
        out = row if out is None else jnp.where(sub == p, row, out)
    return out


def in_row(column):
    total = jnp.broadcast_to(jnp.sum(column, axis=1, keepdims=True), column.shape)
    diagonal = lax.broadcasted_iota(jnp.int32, total.shape, 0) == lax.broadcasted_iota(jnp.int32, total.shape, 1)
    return jnp.sum(jnp.where(diagonal, total, 0.0), axis=0, keepdims=True)


def wide(v):
    return v[:, :128] + v[:, 128:]


def observation_maps(sizes, cell, value):
    particles, fields, strip, lats, strips = sizes
    x0 = lax.axis_index("lon") * strip
    shift = lats.bit_length() - 1
    local_cell = cell - x0 * lats
    obs_lon = lax.shift_right_arithmetic(local_cell, shift)
    obs_lat = local_cell & (lats - 1)
    count = cell.shape[1]
    here = lax.broadcasted_iota(jnp.int32, (strip, count), 0) == obs_lon
    high = value.astype(BF16)
    rest = value - high.astype(F32)
    mid = rest.astype(BF16)
    low = (rest - mid.astype(F32)).astype(BF16)
    zero = jnp.zeros((strip, count), F32)
    parts = [jnp.where(here, 1.0, zero)]
    parts += [jnp.where(here, p.astype(F32), zero) for p in (high, mid, low)]
    left = jnp.concatenate(parts, 0).astype(BF16)
    right = (lax.broadcasted_iota(jnp.int32, (lats, count), 0) == obs_lat).astype(F32).astype(BF16)
    dense = lax.dot_general(left, right, (((1,), (1,)), ((), ())), preferred_element_type=F32)
    lon = (lax.broadcasted_iota(jnp.int32, (strip, lats), 0) + x0).astype(F32)
    precision = 1.0 + 2.0 * lon / (strip * strips)
    target = dense[strip:2 * strip] + (dense[2 * strip:3 * strip] + dense[3 * strip:])
    return dense[:strip] * (0.25 * precision), target


class Rows:
    def __init__(self, ref, first, columns):
        self.ref, self.first, self.columns = ref, first, columns

    def __getitem__(self, at):
        row = self.first + at[0] * self.columns + at[1]
        return self.ref[row:row + 1]


def scalars_in(ref, fields):
    return Rows(ref, fields * fields, fields), Rows(ref, 0, fields)


def prepare(sizes, state_hbm, noise_hbm, courant_hbm, diffusion_hbm, mixing_hbm, cell_hbm, value_hbm,
            send_east, send_west, state, noise, late_noise, maps, courant, scalars,
            diffusion, mixing, cell, value, sems):
    particles, fields, strip, lats, strips = sizes
    n = fields * particles
    copies = [pltpu.make_async_copy(source, target, sems.at[k]) for k, (source, target) in enumerate((
        (cell_hbm, cell), (value_hbm, value), (courant_hbm, courant), (diffusion_hbm, diffusion),
        (mixing_hbm, mixing), (state_hbm.at[:, :, :8], state.at[:, :, :8]),
        (state_hbm.at[:, :, strip - 8:], state.at[:, :, strip - 8:]), (noise_hbm.at[0], noise),
        (noise_hbm.at[1, :, 0], late_noise), (state_hbm.at[:, :, 8:strip - 8], state.at[:, :, 8:strip - 8])))]
    for copy in copies:
        copy.start()
    copies[0].wait()
    copies[1].wait()
    gain, target = observation_maps(sizes, cell[...], value[...])
    maps[0], maps[1] = gain, target
    kinds = []
    for x, step in ((strip - 1, -1), (0, 1)):
        kinds += [(f, x) for f in range(fields)] + [(f, x + step) for f in range(fields)] + [(0, x + 2 * step)]
    pick0 = pick_rows(kinds, particles, fields, strip)
    pick1 = pick_rows([(0, x) for x in (strip - 1, strip - 2, 0, 1)], particles, 1, strip)
    for copy in copies[2:5]:
        copy.wait()
    for f in range(fields):
        for g in range(fields):
            scalars[f * fields + g:f * fields + g + 1] = jnp.broadcast_to(mixing[f:f + 1, g:g + 1], (1, lats))
        at = fields * fields + f
        scalars[at:at + 1] = jnp.broadcast_to(diffusion[:, f:f + 1], (1, lats))
    diffusion, mixing = scalars_in(scalars, fields)

    sides = []
    for first, inward, outward in ((strip - 8, 2, 1), (0, 1, 2)):
        tile = [coefficients(courant[0, first:first + 8], courant[1, first:first + 8], diffusion[0, f], mixing[f, f])
                for f in range(fields)]
        sides.append([[c[0], c[inward], c[outward], c[3], c[4]] for c in tile])
    def coefs_at(side, f, k):
        at = places[side][0] + k * places[side][2] - places[side][1]
        return [c[at:at + 1] for c in sides[side][f]]

    def maps_at(side, k):
        at = places[side][0] + k * places[side][2]
        return gain[at:at + 1], target[at:at + 1]

    def moved(side, f, k, here, inner, outer):
        centre, inward, outward, to_north, to_south = coefs_at(side, f, k)
        v = here[f]
        total = centre * v + inward * inner + to_north * north(v) + to_south * south(v) + mixed(mixing, f, here)
        return total if outer is None else total + outward * outer

    def nudged(side, value, k):
        g, v = maps_at(side, k)
        push = g * (v - value)
        return value + push, push

    def first_step(side, out):
        def state_at(f, k):
            at = places[side][0] + k * places[side][2]
            return stack_rows([state[p, f, at:at + 1] for p in range(particles)])

        near = [[state_at(f, k) for f in range(fields)] for k in range(3)]
        third = state_at(0, 3)
        for f in range(fields):
            out[f * particles:(f + 1) * particles] = near[0][f]
        result, pushes = [[], []], []
        for k in range(2):
            for f in range(fields):
                new = moved(side, f, k, near[k], near[k + 1][f], near[k - 1][f] if k else None)
                if f == 0:
                    new, push = nudged(side, new, k)
                    pushes.append(push)
                result[k].append(new)
        inside, _ = nudged(side, moved(side, 0, 2, near[2], third, near[1][0]), 2)
        return result, pushes, inside

    places = ((strip - 1, strip - 8, -1), (0, 0, 1))
    copies[5].wait()
    copies[6].wait()
    started = [first_step(0, send_east), first_step(1, send_west)]
    copies[7].wait()
    copies[8].wait()
    rows0 = jnp.dot(pick0, noise[...].reshape(n * strip, lats), preferred_element_type=F32)
    rows1 = jnp.dot(pick1, late_noise[...].reshape(particles * strip, lats), preferred_element_type=F32)

    def edge(side, out):
        x, _, step = places[side]
        base0, base1 = side * (2 * fields + 1) * particles, side * 2 * particles
        result, pushes, inside = started[side]

        def noisy0(k, f):
            at = base0 + (k * fields + f) * particles
            return rows0[at:at + particles]

        def noisy1(k):
            at = base1 + k * particles
            return rows1[at:at + particles]

        result = [[result[k][f] + noisy0(k, f) for f in range(fields)] for k in range(2)]
        inside = inside + noisy0(2, 0)
        g0, _ = maps_at(side, 0)
        g1, _ = maps_at(side, 1)
        slope = [-(1.0 / noise_var) * g0 * (pushes[0] + noisy0(0, 0))]
        bend = [(0.5 / noise_var) * g0 * g0]
        for k, g in enumerate((g0, g1)):
            new = moved(side, 0, k, result[k], result[1][0] if k == 0 else inside, result[0][0] if k else None)
            new, push = nudged(side, new, k)
            miss = maps_at(side, k)[1] - (new + noisy1(k))
            weight = 4.0 * g
            slope.append(-(1.0 / noise_var) * g * (push + noisy1(k)) - weight * (1.0 - g) * miss)
            bend.append((0.5 / noise_var) * g * g + 0.5 * weight * (1.0 - g) * (1.0 - g))
        outward = coefs_at(side, 0, 0)[2]
        onward = coefs_at(side, 0, 1)[2] * (1.0 - g0) * outward
        for f in range(fields):
            out[n + f * particles:n + (f + 1) * particles] = result[0][f]
        out[2 * n:2 * n + particles] = outward * slope[0] + onward * slope[2]
        out[2 * n + particles:2 * n + 2 * particles] = slope[1]
        inner = x + step
        last = (outward * outward * bend[0] + onward * onward * bend[2], bend[1],
                courant[0, x:x + 1], courant[1, x:x + 1], g0, courant[0, inner:inner + 1], g1,
                jnp.zeros((1, lats), F32))
        out[2 * n + 2 * particles:] = stack_rows(last)

    edge(0, send_east)
    edge(1, send_west)
    copies[9].wait()


def zero_halo_coefs(sizes, courant, scalars, coefs):
    particles, fields, strip, lats, strips = sizes
    diffusion, mixing = scalars_in(scalars, fields)
    lon = lax.broadcasted_iota(jnp.int32, (strip, lats), 0)
    for f in range(fields):
        centre, east, west, to_north, to_south = coefficients(
            courant[0], courant[1], diffusion[0, f], mixing[f, f])
        coefs[f, 0] = centre
        coefs[f, 1] = jnp.where(lon == strip - 1, 0.0, east)
        coefs[f, 2] = jnp.where(lon == 0, 0.0, west)
        coefs[f, 3] = to_north
        coefs[f, 4] = to_south


def zero_halo_step(sizes, scalars, coefs):
    particles, fields, strip, lats, strips = sizes
    _, mixing = scalars_in(scalars, fields)

    def moved(values, f):
        v = values[f]
        return (coefs[f, 0] * v + coefs[f, 1] * east_of(v) + coefs[f, 2] * west_of(v)
                + coefs[f, 3] * north(v) + coefs[f, 4] * south(v) + mixed(mixing, f, values))

    return moved


def observed_bulk(sizes, parity, state, noise, late_noise, maps, courant, scalars, earlier, middle, out, weight, coefs, partial):
    particles, fields, strip, lats, strips = sizes

    def one(p):
        moved = zero_halo_step(sizes, scalars, coefs)
        values = [state[p, f] for f in range(fields)]
        results = []
        for f in range(fields):
            new = moved(values, f)
            add = noise[p, f].astype(F32)
            if f == 0:
                push = maps[0] * (maps[1] - new)
                new = new + push
                total = push * (push + 2.0 * add)
            results.append(new + add)
            middle[p, f] = new + add
        new = moved(results, 0)
        add = late_noise[p].astype(F32)
        push = maps[0] * (maps[1] - new)
        new = new + push + add
        miss = maps[1] - new
        total = (0.5 / noise_var) * (total + push * (push + 2.0 * add)) + (2.0 * maps[0]) * (miss * miss)
        out[p] = new
        partial[pl.ds(p, 1), :] = wide(jnp.sum(total, axis=0, keepdims=True))

    def body(step, carry):
        for k in range(4):
            one(4 * step + k)
        return carry

    here = lax.axis_index("lon") % 2 == parity

    @pl.when(here)
    def _():
        zero_halo_coefs(sizes, courant, scalars, coefs)
        lax.fori_loop(0, particles // 4, body, 0)
        weight[...] = in_row(partial[...])

    @pl.when(jnp.logical_not(here))
    def _():
        weight[...] = earlier[:1, :128]


def other_bulk(sizes, even_middle, even_observed, even_coefs, odd_middle, odd_observed, odd_coefs,
               noise_hbm, scalars, out, noise, sem):
    particles, fields, strip, lats, strips = sizes

    fetch = pltpu.make_async_copy(noise_hbm.at[1, :, 1:], noise, sem)
    fetch.start()

    def run(middle, observed, coefs):
        moved = zero_halo_step(sizes, scalars, coefs)
        for p in range(particles):
            out[p, 0] = observed[p]
        fetch.wait()

        def body(p, carry):
            values = [middle[p, f] for f in range(fields)]
            for f in range(1, fields):
                out[p, f] = moved(values, f) + noise[p, f - 1].astype(F32)
            return carry

        lax.fori_loop(0, particles, body, 0)

    even = lax.axis_index("lon") % 2 == 0

    @pl.when(even)
    def _():
        run(even_middle, even_observed, even_coefs)

    @pl.when(jnp.logical_not(even))
    def _():
        run(odd_middle, odd_observed, odd_coefs)


def correct(sizes, own_east, own_west, from_west, from_east, scalars, bulk_weight, weight, changes):
    particles, fields, strip, lats, strips = sizes
    n = fields * particles
    diffusion, mixing = scalars_in(scalars, fields)

    def field_rows(ref, start, f):
        return ref[start + f * particles:start + (f + 1) * particles]

    packets = (own_east, from_east, own_west, from_west)
    last = 2 * n + 2 * particles
    zonal = stack_rows([ref[last + 2:last + 3] for ref in packets] + [ref[last + 5:last + 6] for ref in packets])
    merid = stack_rows([ref[last + 3:last + 4] for ref in packets] * 2)
    tile = [coefficients(zonal, merid, diffusion[0, f], mixing[f, f]) for f in range(fields)]
    total = jnp.zeros((particles, lats), F32)
    for k, owner in enumerate(packets):
        other_k = k ^ 1
        other = packets[other_k]
        outward_at = (1, 2, 2, 1)[k]
        outward_other = (1, 2, 2, 1)[other_k]
        gain = owner[last + 4:last + 5]
        gain_other = other[last + 4:last + 5]
        first = []
        for f in range(fields):
            step = tile[f][outward_at][k:k + 1] * field_rows(other, 0, f)
            first.append((1.0 - gain) * step if f == 0 else step)
        mine = k in (0, 2)
        for f in range(fields if mine else 1):
            centre, to_north, to_south = [tile[f][c][k:k + 1] for c in (0, 3, 4)]
            outward = tile[f][outward_at][k:k + 1]
            reach = tile[f][outward_other][other_k:other_k + 1]
            if f == 0:
                reach = (1.0 - gain_other) * reach
            outside = field_rows(other, n, f) + reach * field_rows(owner, 0, f)
            step = (centre * first[f] + outward * outside + to_north * north(first[f])
                    + to_south * south(first[f]) + mixed(mixing, f, first))
            if f == 0:
                seen = field_rows(other, 0, 0)
                slope, slope_step = owner[2 * n:2 * n + particles], owner[2 * n + particles:last]
                bend, bend_step = owner[last:last + 1], owner[last + 1:last + 2]
                total = total + seen * (slope + bend * seen) + step * (slope_step + bend_step * step)
            if mine:
                beside = tile[f][outward_at][4 + k:5 + k] * first[f]
                if f == 0:
                    step = (1.0 - gain) * step
                    beside = (1.0 - owner[last + 6:last + 7]) * beside
                edge, inner = (3, 2) if k == 0 else (0, 1)
                changes[edge, f * particles:(f + 1) * particles] = step
                changes[inner, f * particles:(f + 1) * particles] = beside
    weight[...] = in_row(wide(total)) + bulk_weight[...]


def apply_changes(sizes, current, changes, out):
    particles, fields, strip, lats, strips = sizes
    sub = lax.broadcasted_iota(jnp.int32, (8, lats), 0)
    for p in range(particles):
        for f in range(fields):
            row = f * particles + p
            rows = [jnp.broadcast_to(changes[k, row:row + 1], sub.shape) for k in range(4)]
            out[p, f, :8] = current[p, f, :8] + jnp.where(sub == 0, rows[0], jnp.where(sub == 1, rows[1], 0.0))
            out[p, f, 8:strip - 8] = current[p, f, 8:strip - 8]
            out[p, f, strip - 8:] = current[p, f, strip - 8:] + jnp.where(
                sub == 7, rows[3], jnp.where(sub == 6, rows[2], 0.0))


def assemble(sizes, source, current, received, out, sems):
    particles = sizes[0]
    dom = lax.axis_index("dom")

    def copy(j, ref, at):
        return pltpu.make_async_copy(ref.at[at], out.at[j], sems.at[j])

    for j in range(particles):
        wanted = source[dom * particles + j]
        mine = wanted // particles == dom
        at = wanted % particles

        @pl.when(mine)
        def _():
            copy(j, current, at).start()

        @pl.when(jnp.logical_not(mine))
        def _():
            copy(j, received, at).start()

    for j in range(particles):
        copy(j, current, 0).wait()


def local(ensemble_state, proposal_noise, courant, diffusion, mixing, prior_weight, obs_cell, obs_value, source):
    particles, fields, strip, lats = ensemble_state.shape
    strips = lax.axis_size("lon")
    sizes = (particles, fields, strip, lats, strips)
    packet = jax.ShapeDtypeStruct((2 * particles * fields + 2 * particles + 8, lats), F32)
    cell, value = obs_cell[None], obs_value[None]

    def shape(*dims):
        return jax.ShapeDtypeStruct(dims, F32)

    whole = (particles, fields, strip, lats)

    def in_hbm(array):
        return pltpu.with_memory_space_constraint(array, pltpu.HBM)

    arrays = (ensemble_state, proposal_noise, courant, diffusion[None], mixing, cell, value)
    send_east, send_west, state, noise, late_noise, maps, courant, scalars = pl.pallas_call(
        functools.partial(prepare, sizes),
        out_shape=(packet, packet, shape(*whole), jax.ShapeDtypeStruct(whole, BF16),
                   jax.ShapeDtypeStruct((particles, strip, lats), BF16), shape(2, strip, lats),
                   shape(*courant.shape), shape(fields * (fields + 2), lats)),
        in_specs=[HBM] * 7,
        out_specs=(VMEM,) * 8,
        scratch_shapes=[pltpu.VMEM(array.shape, array.dtype) for array in arrays[3:]]
        + [pltpu.SemaphoreType.DMA((10,))],
        compiler_params=LIMIT,
        cost_estimate=pl.CostEstimate(flops=1000000, bytes_accessed=2000000, transcendentals=0),
    )(*[in_hbm(array) for array in arrays])

    def bulk_of(parity, earlier):
        return pl.pallas_call(
            functools.partial(observed_bulk, sizes, parity),
            out_shape=(shape(*whole), shape(particles, strip, lats), shape(1, 128), shape(fields, 5, strip, lats)),
            in_specs=[VMEM] * 7,
            out_specs=(VMEM,) * 4,
            scratch_shapes=[pltpu.VMEM((particles, 128), F32)],
            compiler_params=LIMIT,
            cost_estimate=pl.CostEstimate(flops=20000000, bytes_accessed=4000000, transcendentals=0),
        )(state, noise, late_noise, maps, courant, scalars, earlier)

    even_middle, even_observed, bulk_weight, even_coefs = bulk_of(0, scalars)
    send_east, send_west, bulk_weight = lax.optimization_barrier((send_east, send_west, bulk_weight))
    eastward = [(i, (i + 1) % strips) for i in range(strips)]
    westward = [(i, (i - 1) % strips) for i in range(strips)]
    from_west = lax.ppermute(send_east, "lon", eastward)
    from_east = lax.ppermute(send_west, "lon", westward)
    odd_middle, odd_observed, bulk_weight, odd_coefs = bulk_of(1, bulk_weight)
    beside = lax.ppermute(bulk_weight, "lon", [(i, i ^ 1) for i in range(strips)])

    current = pl.pallas_call(
        functools.partial(other_bulk, sizes),
        out_shape=shape(*whole),
        in_specs=[VMEM] * 6 + [HBM, VMEM],
        scratch_shapes=[pltpu.VMEM((particles, fields - 1, strip, lats), BF16), pltpu.SemaphoreType.DMA],
        out_specs=VMEM,
        compiler_params=LIMIT,
        cost_estimate=FREE,
    )(even_middle, even_observed, even_coefs, odd_middle, odd_observed, odd_coefs, in_hbm(proposal_noise), scalars)

    weight, changes = pl.pallas_call(
        functools.partial(correct, sizes),
        out_shape=(shape(1, 128), shape(4, particles * fields, lats)),
        in_specs=[VMEM] * 6,
        out_specs=(VMEM,) * 2,
        compiler_params=LIMIT,
        cost_estimate=FREE,
    )(send_east, send_west, from_west, from_east, scalars, bulk_weight)

    current = pl.pallas_call(
        functools.partial(apply_changes, sizes),
        out_shape=shape(*whole),
        in_specs=[VMEM] * 2,
        out_specs=VMEM,
        compiler_params=LIMIT,
        cost_estimate=FREE,
    )(current, changes)

    current, beside = lax.optimization_barrier((current, beside))
    weight = weight + beside
    received = lax.ppermute(current, "dom", [(0, 1), (1, 0)])
    bit = 2
    while bit < strips:
        steps = (2, 3, 1) if 2 * bit < strips else (1,)
        arrived = []
        for step in steps:
            if step == 1 and bit * (len(steps) + 1) >= strips:
                weight, received = lax.optimization_barrier((weight, received))
            arrived.append(lax.ppermute(weight, "lon", [(i, i ^ (bit * step)) for i in range(strips)]))
        weight = sum(arrived, weight)
        bit *= len(steps) + 1

    new_state = pl.pallas_call(
        functools.partial(assemble, sizes),
        out_shape=shape(*whole),
        in_specs=[SMEM, VMEM, VMEM],
        out_specs=HBM,
        scratch_shapes=[pltpu.SemaphoreType.DMA((particles,))],
        compiler_params=LIMIT,
        cost_estimate=pl.CostEstimate(flops=0, bytes_accessed=2000000, transcendentals=0),
    )(source, current, received)

    log_weight = prior_weight - weight[0, :particles] / (256.0 * obs_cell.shape[0])
    return new_state, log_weight


def solution(mesh):
    placed = (
        P(("groups", "dom"), None, "lon", None),
        P(None, ("groups", "dom"), None, "lon", None),
        P(None, ("groups", "lon"), None),
        P(),
        P(),
        P(("groups", "dom")),
        P(("groups", "lon")),
        P(("groups", "lon")),
        P("groups"),
    )
    return jax.shard_map(
        local,
        mesh=mesh,
        in_specs=placed,
        out_specs=(P(("groups", "dom"), None, "lon", None), P(("groups", "dom"))),
        check_vma=False,
    )
```

```python
import functools

import jax
import jax.numpy as jnp
from jax import lax
from jax.experimental import pallas as pl
from jax.experimental.pallas import tpu as pltpu
from jax.sharding import PartitionSpec as P

noise_var = 0.04
VMEM = pl.BlockSpec(memory_space=pltpu.VMEM)
SMEM = pl.BlockSpec(memory_space=pltpu.SMEM)
HBM = pl.BlockSpec(memory_space=pltpu.HBM)
LIMIT = pltpu.CompilerParams(vmem_limit_bytes=16 * 1024 * 1024)
FREE = pl.CostEstimate(flops=0, bytes_accessed=0, transcendentals=0)
BF16 = jnp.bfloat16
F32 = jnp.float32


def north(v):
    low, high = (pltpu.roll(v[:, at:at + 128], 127, 1) for at in (0, 128))
    lane = lax.broadcasted_iota(jnp.int32, low.shape, 1)
    return jnp.concatenate([jnp.where(lane == 127, high, low), high], 1)


def south(v):
    low, high = (pltpu.roll(v[:, at:at + 128], 1, 1) for at in (0, 128))
    lane = lax.broadcasted_iota(jnp.int32, low.shape, 1)
    return jnp.concatenate([low, jnp.where(lane == 0, low, high)], 1)


def east_of(v):
    tiles = [pltpu.roll(v[at:at + 8], 7, 0) for at in range(0, v.shape[0], 8)]
    sub = lax.broadcasted_iota(jnp.int32, tiles[0].shape, 0)
    mixed_tiles = [jnp.where(sub == 7, after, tile) for tile, after in zip(tiles[:-1], tiles[1:])]
    return jnp.concatenate(mixed_tiles + tiles[-1:], 0)


def west_of(v):
    tiles = [pltpu.roll(v[at:at + 8], 1, 0) for at in range(0, v.shape[0], 8)]
    sub = lax.broadcasted_iota(jnp.int32, tiles[0].shape, 0)
    mixed_tiles = [jnp.where(sub == 0, before, tile) for before, tile in zip(tiles[:-1], tiles[1:])]
    return jnp.concatenate(tiles[:1] + mixed_tiles, 0)


def coefficients(zonal, merid, rate, self_mix):
    lat = lax.broadcasted_iota(jnp.int32, zonal.shape, 1)
    zonal_half, zonal_rate = 0.5 * zonal, 0.5 * zonal * zonal + rate
    merid_half, merid_rate = 0.5 * merid, 0.5 * merid * merid + rate
    east, west = zonal_rate - zonal_half, zonal_rate + zonal_half
    to_north, to_south = merid_rate - merid_half, merid_rate + merid_half
    centre = 1.0 + self_mix - 2.0 * zonal_rate - 2.0 * merid_rate
    last, first = lat == zonal.shape[1] - 1, lat == 0
    centre = centre + jnp.where(last, to_north, 0.0) + jnp.where(first, to_south, 0.0)
    to_north = jnp.where(last, 0.0, to_north)
    to_south = jnp.where(first, 0.0, to_south)
    return centre, east, west, to_north, to_south


def mixed(mixing, field, values):
    total = None
    for other, value in enumerate(values):
        if other != field:
            term = mixing[field, other] * value
            total = term if total is None else total + term
    return total


def pick_rows(kinds, particles, fields, strip):
    shape = (particles, particles * fields * strip)
    place = lax.broadcasted_iota(jnp.int32, shape, 1) - lax.broadcasted_iota(jnp.int32, shape, 0) * (fields * strip)
    blocks = [jnp.where(place == f * strip + x, 1.0, 0.0) for f, x in kinds]
    return jnp.concatenate(blocks, 0).astype(BF16)


def stack_rows(rows):
    sub = lax.broadcasted_iota(jnp.int32, (len(rows), rows[0].shape[1]), 0)
    out = None
    for p, row in enumerate(rows):
        row = jnp.broadcast_to(row, sub.shape)
        out = row if out is None else jnp.where(sub == p, row, out)
    return out


def in_row(column):
    total = jnp.broadcast_to(jnp.sum(column, axis=1, keepdims=True), column.shape)
    diagonal = lax.broadcasted_iota(jnp.int32, total.shape, 0) == lax.broadcasted_iota(jnp.int32, total.shape, 1)
    return jnp.sum(jnp.where(diagonal, total, 0.0), axis=0, keepdims=True)


def wide(v):
    return v[:, :128] + v[:, 128:]


def observation_maps(sizes, cell, value):
    particles, fields, strip, lats, strips = sizes
    x0 = lax.axis_index("lon") * strip
    shift = lats.bit_length() - 1
    local_cell = cell - x0 * lats
    obs_lon = lax.shift_right_arithmetic(local_cell, shift)
    obs_lat = local_cell & (lats - 1)
    count = cell.shape[1]
    here = lax.broadcasted_iota(jnp.int32, (strip, count), 0) == obs_lon
    high = value.astype(BF16)
    rest = value - high.astype(F32)
    mid = rest.astype(BF16)
    low = (rest - mid.astype(F32)).astype(BF16)
    zero = jnp.zeros((strip, count), F32)
    parts = [jnp.where(here, 1.0, zero)]
    parts += [jnp.where(here, p.astype(F32), zero) for p in (high, mid, low)]
    left = jnp.concatenate(parts, 0).astype(BF16)
    right = (lax.broadcasted_iota(jnp.int32, (lats, count), 0) == obs_lat).astype(F32).astype(BF16)
    dense = lax.dot_general(left, right, (((1,), (1,)), ((), ())), preferred_element_type=F32)
    lon = (lax.broadcasted_iota(jnp.int32, (strip, lats), 0) + x0).astype(F32)
    precision = 1.0 + 2.0 * lon / (strip * strips)
    target = dense[strip:2 * strip] + (dense[2 * strip:3 * strip] + dense[3 * strip:])
    return dense[:strip] * (0.25 * precision), target


class Rows:
    def __init__(self, ref, first, columns):
        self.ref, self.first, self.columns = ref, first, columns

    def __getitem__(self, at):
        row = self.first + at[0] * self.columns + at[1]
        return self.ref[row:row + 1]


def scalars_in(ref, fields):
    return Rows(ref, fields * fields, fields), Rows(ref, 0, fields)


def prepare(sizes, state_hbm, noise_hbm, courant_hbm, diffusion_hbm, mixing_hbm, cell_hbm, value_hbm,
            send_east, send_west, state, noise, late_noise, maps, courant, scalars,
            diffusion, mixing, cell, value, sems):
    particles, fields, strip, lats, strips = sizes
    n = fields * particles
    quarter = particles // 4
    noise_parts = [(noise_hbm.at[0, at:at + quarter], noise.at[at:at + quarter])
                   for at in range(0, particles, quarter)]
    copies = [pltpu.make_async_copy(source, target, sems.at[k]) for k, (source, target) in enumerate((
        (cell_hbm, cell), (value_hbm, value), (courant_hbm, courant), (diffusion_hbm, diffusion),
        (mixing_hbm, mixing), (state_hbm.at[:, :, :8], state.at[:, :, :8]),
        (state_hbm.at[:, :, strip - 8:], state.at[:, :, strip - 8:]), *noise_parts,
        (noise_hbm.at[1, :, 0], late_noise), (state_hbm.at[:, :, 8:strip - 8], state.at[:, :, 8:strip - 8])))]
    for copy in copies:
        copy.start()
    copies[0].wait()
    copies[1].wait()
    gain, target = observation_maps(sizes, cell[...], value[...])
    maps[0], maps[1] = gain, target
    kinds = []
    for x, step in ((strip - 1, -1), (0, 1)):
        kinds += [(f, x) for f in range(fields)] + [(f, x + step) for f in range(fields)] + [(0, x + 2 * step)]
    pick0 = pick_rows(kinds, particles, fields, strip)
    pick1 = pick_rows([(0, x) for x in (strip - 1, strip - 2, 0, 1)], particles, 1, strip)
    for copy in copies[2:5]:
        copy.wait()
    for f in range(fields):
        for g in range(fields):
            scalars[f * fields + g:f * fields + g + 1] = jnp.broadcast_to(mixing[f:f + 1, g:g + 1], (1, lats))
        at = fields * fields + f
        scalars[at:at + 1] = jnp.broadcast_to(diffusion[:, f:f + 1], (1, lats))
    diffusion, mixing = scalars_in(scalars, fields)

    sides = []
    for first, inward, outward in ((strip - 8, 2, 1), (0, 1, 2)):
        tile = [coefficients(courant[0, first:first + 8], courant[1, first:first + 8], diffusion[0, f], mixing[f, f])
                for f in range(fields)]
        sides.append([[c[0], c[inward], c[outward], c[3], c[4]] for c in tile])
    def coefs_at(side, f, k):
        at = places[side][0] + k * places[side][2] - places[side][1]
        return [c[at:at + 1] for c in sides[side][f]]

    def maps_at(side, k):
        at = places[side][0] + k * places[side][2]
        return gain[at:at + 1], target[at:at + 1]

    def moved(side, f, k, here, inner, outer):
        centre, inward, outward, to_north, to_south = coefs_at(side, f, k)
        v = here[f]
        total = centre * v + inward * inner + to_north * north(v) + to_south * south(v) + mixed(mixing, f, here)
        return total if outer is None else total + outward * outer

    def nudged(side, value, k):
        g, v = maps_at(side, k)
        push = g * (v - value)
        return value + push, push

    def first_step(side, out):
        def state_at(f, k):
            at = places[side][0] + k * places[side][2]
            return stack_rows([state[p, f, at:at + 1] for p in range(particles)])

        near = [[state_at(f, k) for f in range(fields)] for k in range(3)]
        third = state_at(0, 3)
        for f in range(fields):
            out[f * particles:(f + 1) * particles] = near[0][f]
        result, pushes = [[], []], []
        for k in range(2):
            for f in range(fields):
                new = moved(side, f, k, near[k], near[k + 1][f], near[k - 1][f] if k else None)
                if f == 0:
                    new, push = nudged(side, new, k)
                    pushes.append(push)
                result[k].append(new)
        inside, _ = nudged(side, moved(side, 0, 2, near[2], third, near[1][0]), 2)
        return result, pushes, inside

    places = ((strip - 1, strip - 8, -1), (0, 0, 1))
    copies[5].wait()
    copies[6].wait()
    started = [first_step(0, send_east), first_step(1, send_west)]
    for copy in copies[7:12]:
        copy.wait()
    rows0 = jnp.dot(pick0, noise[...].reshape(n * strip, lats), preferred_element_type=F32)
    rows1 = jnp.dot(pick1, late_noise[...].reshape(particles * strip, lats), preferred_element_type=F32)

    def edge(side, out):
        x, _, step = places[side]
        base0, base1 = side * (2 * fields + 1) * particles, side * 2 * particles
        result, pushes, inside = started[side]

        def noisy0(k, f):
            at = base0 + (k * fields + f) * particles
            return rows0[at:at + particles]

        def noisy1(k):
            at = base1 + k * particles
            return rows1[at:at + particles]

        result = [[result[k][f] + noisy0(k, f) for f in range(fields)] for k in range(2)]
        inside = inside + noisy0(2, 0)
        g0, _ = maps_at(side, 0)
        g1, _ = maps_at(side, 1)
        slope = [-(1.0 / noise_var) * g0 * (pushes[0] + noisy0(0, 0))]
        bend = [(0.5 / noise_var) * g0 * g0]
        for k, g in enumerate((g0, g1)):
            new = moved(side, 0, k, result[k], result[1][0] if k == 0 else inside, result[0][0] if k else None)
            new, push = nudged(side, new, k)
            miss = maps_at(side, k)[1] - (new + noisy1(k))
            weight = 4.0 * g
            slope.append(-(1.0 / noise_var) * g * (push + noisy1(k)) - weight * (1.0 - g) * miss)
            bend.append((0.5 / noise_var) * g * g + 0.5 * weight * (1.0 - g) * (1.0 - g))
        outward = coefs_at(side, 0, 0)[2]
        onward = coefs_at(side, 0, 1)[2] * (1.0 - g0) * outward
        for f in range(fields):
            out[n + f * particles:n + (f + 1) * particles] = result[0][f]
        out[2 * n:2 * n + particles] = outward * slope[0] + onward * slope[2]
        out[2 * n + particles:2 * n + 2 * particles] = slope[1]
        inner = x + step
        last = (outward * outward * bend[0] + onward * onward * bend[2], bend[1],
                courant[0, x:x + 1], courant[1, x:x + 1], g0, courant[0, inner:inner + 1], g1,
                jnp.zeros((1, lats), F32))
        out[2 * n + 2 * particles:] = stack_rows(last)

    edge(0, send_east)
    edge(1, send_west)
    copies[12].wait()


def zero_halo_coefs(sizes, courant, scalars, coefs):
    particles, fields, strip, lats, strips = sizes
    diffusion, mixing = scalars_in(scalars, fields)
    lon = lax.broadcasted_iota(jnp.int32, (strip, lats), 0)
    for f in range(fields):
        centre, east, west, to_north, to_south = coefficients(
            courant[0], courant[1], diffusion[0, f], mixing[f, f])
        coefs[f, 0] = centre
        coefs[f, 1] = jnp.where(lon == strip - 1, 0.0, east)
        coefs[f, 2] = jnp.where(lon == 0, 0.0, west)
        coefs[f, 3] = to_north
        coefs[f, 4] = to_south


def zero_halo_step(sizes, scalars, coefs):
    particles, fields, strip, lats, strips = sizes
    _, mixing = scalars_in(scalars, fields)

    def moved(values, f):
        v = values[f]
        return (coefs[f, 0] * v + coefs[f, 1] * east_of(v) + coefs[f, 2] * west_of(v)
                + coefs[f, 3] * north(v) + coefs[f, 4] * south(v) + mixed(mixing, f, values))

    return moved


def observed_bulk(sizes, parity, state, noise, late_noise, maps, courant, scalars, earlier, middle, out, weight, coefs, partial):
    particles, fields, strip, lats, strips = sizes

    def one(p):
        moved = zero_halo_step(sizes, scalars, coefs)
        values = [state[p, f] for f in range(fields)]
        results = []
        for f in range(fields):
            new = moved(values, f)
            add = noise[p, f].astype(F32)
            if f == 0:
                push = maps[0] * (maps[1] - new)
                new = new + push
                total = push * (push + 2.0 * add)
            results.append(new + add)
            middle[p, f] = new + add
        new = moved(results, 0)
        add = late_noise[p].astype(F32)
        push = maps[0] * (maps[1] - new)
        new = new + push + add
        miss = maps[1] - new
        total = (0.5 / noise_var) * (total + push * (push + 2.0 * add)) + (2.0 * maps[0]) * (miss * miss)
        out[p] = new
        partial[pl.ds(p, 1), :] = wide(jnp.sum(total, axis=0, keepdims=True))

    def body(step, carry):
        for k in range(4):
            one(4 * step + k)
        return carry

    here = lax.axis_index("lon") % 2 == parity

    @pl.when(here)
    def _():
        zero_halo_coefs(sizes, courant, scalars, coefs)
        lax.fori_loop(0, particles // 4, body, 0)
        weight[...] = in_row(partial[...])

    @pl.when(jnp.logical_not(here))
    def _():
        weight[...] = earlier[:1, :128]


def other_bulk(sizes, even_middle, even_observed, even_coefs, odd_middle, odd_observed, odd_coefs,
               noise_hbm, scalars, out, noise, sem):
    particles, fields, strip, lats, strips = sizes

    fetch = pltpu.make_async_copy(noise_hbm.at[1, :, 1:], noise, sem)
    fetch.start()

    def run(middle, observed, coefs):
        moved = zero_halo_step(sizes, scalars, coefs)
        for p in range(particles):
            out[p, 0] = observed[p]
        fetch.wait()

        def body(p, carry):
            values = [middle[p, f] for f in range(fields)]
            for f in range(1, fields):
                out[p, f] = moved(values, f) + noise[p, f - 1].astype(F32)
            return carry

        lax.fori_loop(0, particles, body, 0)

    even = lax.axis_index("lon") % 2 == 0

    @pl.when(even)
    def _():
        run(even_middle, even_observed, even_coefs)

    @pl.when(jnp.logical_not(even))
    def _():
        run(odd_middle, odd_observed, odd_coefs)


def correct(sizes, own_east, own_west, from_west, from_east, scalars, bulk_weight, weight, changes):
    particles, fields, strip, lats, strips = sizes
    n = fields * particles
    diffusion, mixing = scalars_in(scalars, fields)

    def field_rows(ref, start, f):
        return ref[start + f * particles:start + (f + 1) * particles]

    packets = (own_east, from_east, own_west, from_west)
    last = 2 * n + 2 * particles
    zonal = stack_rows([ref[last + 2:last + 3] for ref in packets] + [ref[last + 5:last + 6] for ref in packets])
    merid = stack_rows([ref[last + 3:last + 4] for ref in packets] * 2)
    tile = [coefficients(zonal, merid, diffusion[0, f], mixing[f, f]) for f in range(fields)]
    total = jnp.zeros((particles, lats), F32)
    for k, owner in enumerate(packets):
        other_k = k ^ 1
        other = packets[other_k]
        outward_at = (1, 2, 2, 1)[k]
        outward_other = (1, 2, 2, 1)[other_k]
        gain = owner[last + 4:last + 5]
        gain_other = other[last + 4:last + 5]
        first = []
        for f in range(fields):
            step = tile[f][outward_at][k:k + 1] * field_rows(other, 0, f)
            first.append((1.0 - gain) * step if f == 0 else step)
        mine = k in (0, 2)
        for f in range(fields if mine else 1):
            centre, to_north, to_south = [tile[f][c][k:k + 1] for c in (0, 3, 4)]
            outward = tile[f][outward_at][k:k + 1]
            reach = tile[f][outward_other][other_k:other_k + 1]
            if f == 0:
                reach = (1.0 - gain_other) * reach
            outside = field_rows(other, n, f) + reach * field_rows(owner, 0, f)
            step = (centre * first[f] + outward * outside + to_north * north(first[f])
                    + to_south * south(first[f]) + mixed(mixing, f, first))
            if f == 0:
                seen = field_rows(other, 0, 0)
                slope, slope_step = owner[2 * n:2 * n + particles], owner[2 * n + particles:last]
                bend, bend_step = owner[last:last + 1], owner[last + 1:last + 2]
                total = total + seen * (slope + bend * seen) + step * (slope_step + bend_step * step)
            if mine:
                beside = tile[f][outward_at][4 + k:5 + k] * first[f]
                if f == 0:
                    step = (1.0 - gain) * step
                    beside = (1.0 - owner[last + 6:last + 7]) * beside
                edge, inner = (3, 2) if k == 0 else (0, 1)
                changes[edge, f * particles:(f + 1) * particles] = step
                changes[inner, f * particles:(f + 1) * particles] = beside
    weight[...] = in_row(wide(total)) + bulk_weight[...]


def apply_changes(sizes, current, changes, out):
    particles, fields, strip, lats, strips = sizes
    sub = lax.broadcasted_iota(jnp.int32, (8, lats), 0)
    for p in range(particles):
        for f in range(fields):
            row = f * particles + p
            rows = [jnp.broadcast_to(changes[k, row:row + 1], sub.shape) for k in range(4)]
            out[p, f, :8] = current[p, f, :8] + jnp.where(sub == 0, rows[0], jnp.where(sub == 1, rows[1], 0.0))
            out[p, f, 8:strip - 8] = current[p, f, 8:strip - 8]
            out[p, f, strip - 8:] = current[p, f, strip - 8:] + jnp.where(
                sub == 7, rows[3], jnp.where(sub == 6, rows[2], 0.0))


def assemble(sizes, source, current, received, out, sems):
    particles = sizes[0]
    dom = lax.axis_index("dom")

    def copy(j, ref, at):
        return pltpu.make_async_copy(ref.at[at], out.at[j], sems.at[j])

    for j in range(particles):
        wanted = source[dom * particles + j]
        mine = wanted // particles == dom
        at = wanted % particles

        @pl.when(mine)
        def _():
            copy(j, current, at).start()

        @pl.when(jnp.logical_not(mine))
        def _():
            copy(j, received, at).start()

    for j in range(particles):
        copy(j, current, 0).wait()


def local(ensemble_state, proposal_noise, courant, diffusion, mixing, prior_weight, obs_cell, obs_value, source):
    particles, fields, strip, lats = ensemble_state.shape
    strips = lax.axis_size("lon")
    sizes = (particles, fields, strip, lats, strips)
    packet = jax.ShapeDtypeStruct((2 * particles * fields + 2 * particles + 8, lats), F32)
    cell, value = obs_cell[None], obs_value[None]

    def shape(*dims):
        return jax.ShapeDtypeStruct(dims, F32)

    whole = (particles, fields, strip, lats)

    def in_hbm(array):
        return pltpu.with_memory_space_constraint(array, pltpu.HBM)

    arrays = (ensemble_state, proposal_noise, courant, diffusion[None], mixing, cell, value)
    send_east, send_west, state, noise, late_noise, maps, courant, scalars = pl.pallas_call(
        functools.partial(prepare, sizes),
        out_shape=(packet, packet, shape(*whole), jax.ShapeDtypeStruct(whole, BF16),
                   jax.ShapeDtypeStruct((particles, strip, lats), BF16), shape(2, strip, lats),
                   shape(*courant.shape), shape(fields * (fields + 2), lats)),
        in_specs=[HBM] * 7,
        out_specs=(VMEM,) * 8,
        scratch_shapes=[pltpu.VMEM(array.shape, array.dtype) for array in arrays[3:]]
        + [pltpu.SemaphoreType.DMA((13,))],
        compiler_params=LIMIT,
        cost_estimate=pl.CostEstimate(flops=1000000, bytes_accessed=2000000, transcendentals=0),
    )(*[in_hbm(array) for array in arrays])

    def bulk_of(parity, earlier):
        return pl.pallas_call(
            functools.partial(observed_bulk, sizes, parity),
            out_shape=(shape(*whole), shape(particles, strip, lats), shape(1, 128), shape(fields, 5, strip, lats)),
            in_specs=[VMEM] * 7,
            out_specs=(VMEM,) * 4,
            scratch_shapes=[pltpu.VMEM((particles, 128), F32)],
            compiler_params=LIMIT,
            cost_estimate=pl.CostEstimate(flops=20000000, bytes_accessed=4000000, transcendentals=0),
        )(state, noise, late_noise, maps, courant, scalars, earlier)

    even_middle, even_observed, bulk_weight, even_coefs = bulk_of(0, scalars)
    send_east, send_west, bulk_weight = lax.optimization_barrier((send_east, send_west, bulk_weight))
    eastward = [(i, (i + 1) % strips) for i in range(strips)]
    westward = [(i, (i - 1) % strips) for i in range(strips)]
    from_west = lax.ppermute(send_east, "lon", eastward)
    from_east = lax.ppermute(send_west, "lon", westward)
    odd_middle, odd_observed, bulk_weight, odd_coefs = bulk_of(1, bulk_weight)
    beside = lax.ppermute(bulk_weight, "lon", [(i, i ^ 1) for i in range(strips)])

    current = pl.pallas_call(
        functools.partial(other_bulk, sizes),
        out_shape=shape(*whole),
        in_specs=[VMEM] * 6 + [HBM, VMEM],
        scratch_shapes=[pltpu.VMEM((particles, fields - 1, strip, lats), BF16), pltpu.SemaphoreType.DMA],
        out_specs=VMEM,
        compiler_params=LIMIT,
        cost_estimate=FREE,
    )(even_middle, even_observed, even_coefs, odd_middle, odd_observed, odd_coefs, in_hbm(proposal_noise), scalars)

    weight, changes = pl.pallas_call(
        functools.partial(correct, sizes),
        out_shape=(shape(1, 128), shape(4, particles * fields, lats)),
        in_specs=[VMEM] * 6,
        out_specs=(VMEM,) * 2,
        compiler_params=LIMIT,
        cost_estimate=FREE,
    )(send_east, send_west, from_west, from_east, scalars, bulk_weight)

    current = pl.pallas_call(
        functools.partial(apply_changes, sizes),
        out_shape=shape(*whole),
        in_specs=[VMEM] * 2,
        out_specs=VMEM,
        compiler_params=LIMIT,
        cost_estimate=FREE,
    )(current, changes)

    current, beside = lax.optimization_barrier((current, beside))
    weight = weight + beside
    received = lax.ppermute(current, "dom", [(0, 1), (1, 0)])
    bit = 2
    while bit < strips:
        steps = (2, 3, 1) if 2 * bit < strips else (1,)
        arrived = []
        for step in steps:
            if step == 1 and bit * (len(steps) + 1) >= strips:
                weight, received = lax.optimization_barrier((weight, received))
            arrived.append(lax.ppermute(weight, "lon", [(i, i ^ (bit * step)) for i in range(strips)]))
        weight = sum(arrived, weight)
        bit *= len(steps) + 1

    new_state = pl.pallas_call(
        functools.partial(assemble, sizes),
        out_shape=shape(*whole),
        in_specs=[SMEM, VMEM, VMEM],
        out_specs=HBM,
        scratch_shapes=[pltpu.SemaphoreType.DMA((particles,))],
        compiler_params=LIMIT,
        cost_estimate=pl.CostEstimate(flops=0, bytes_accessed=2000000, transcendentals=0),
    )(source, current, received)

    log_weight = prior_weight - weight[0, :particles] / (256.0 * obs_cell.shape[0])
    return new_state, log_weight


def solution(mesh):
    placed = (
        P(("groups", "dom"), None, "lon", None),
        P(None, ("groups", "dom"), None, "lon", None),
        P(None, ("groups", "lon"), None),
        P(),
        P(),
        P(("groups", "dom")),
        P(("groups", "lon")),
        P(("groups", "lon")),
        P("groups"),
    )
    return jax.shard_map(
        local,
        mesh=mesh,
        in_specs=placed,
        out_specs=(P(("groups", "dom"), None, "lon", None), P(("groups", "dom"))),
        check_vma=False,
    )
```

```python
import functools

import jax
import jax.numpy as jnp
from jax import lax
from jax.experimental import pallas as pl
from jax.experimental.pallas import tpu as pltpu
from jax.sharding import PartitionSpec as P

noise_var = 0.04
VMEM = pl.BlockSpec(memory_space=pltpu.VMEM)
SMEM = pl.BlockSpec(memory_space=pltpu.SMEM)
HBM = pl.BlockSpec(memory_space=pltpu.HBM)
LIMIT = pltpu.CompilerParams(vmem_limit_bytes=16 * 1024 * 1024)
FREE = pl.CostEstimate(flops=0, bytes_accessed=0, transcendentals=0)
BF16 = jnp.bfloat16
F32 = jnp.float32


def north(v):
    low, high = (pltpu.roll(v[:, at:at + 128], 127, 1) for at in (0, 128))
    lane = lax.broadcasted_iota(jnp.int32, low.shape, 1)
    return jnp.concatenate([jnp.where(lane == 127, high, low), high], 1)


def south(v):
    low, high = (pltpu.roll(v[:, at:at + 128], 1, 1) for at in (0, 128))
    lane = lax.broadcasted_iota(jnp.int32, low.shape, 1)
    return jnp.concatenate([low, jnp.where(lane == 0, low, high)], 1)


def east_of(v):
    tiles = [pltpu.roll(v[at:at + 8], 7, 0) for at in range(0, v.shape[0], 8)]
    sub = lax.broadcasted_iota(jnp.int32, tiles[0].shape, 0)
    mixed_tiles = [jnp.where(sub == 7, after, tile) for tile, after in zip(tiles[:-1], tiles[1:])]
    return jnp.concatenate(mixed_tiles + tiles[-1:], 0)


def west_of(v):
    tiles = [pltpu.roll(v[at:at + 8], 1, 0) for at in range(0, v.shape[0], 8)]
    sub = lax.broadcasted_iota(jnp.int32, tiles[0].shape, 0)
    mixed_tiles = [jnp.where(sub == 0, before, tile) for before, tile in zip(tiles[:-1], tiles[1:])]
    return jnp.concatenate(tiles[:1] + mixed_tiles, 0)


def coefficients(zonal, merid, rate, self_mix):
    lat = lax.broadcasted_iota(jnp.int32, zonal.shape, 1)
    zonal_half, zonal_rate = 0.5 * zonal, 0.5 * zonal * zonal + rate
    merid_half, merid_rate = 0.5 * merid, 0.5 * merid * merid + rate
    east, west = zonal_rate - zonal_half, zonal_rate + zonal_half
    to_north, to_south = merid_rate - merid_half, merid_rate + merid_half
    centre = 1.0 + self_mix - 2.0 * zonal_rate - 2.0 * merid_rate
    last, first = lat == zonal.shape[1] - 1, lat == 0
    centre = centre + jnp.where(last, to_north, 0.0) + jnp.where(first, to_south, 0.0)
    to_north = jnp.where(last, 0.0, to_north)
    to_south = jnp.where(first, 0.0, to_south)
    return centre, east, west, to_north, to_south


def mixed(mixing, field, values):
    total = None
    for other, value in enumerate(values):
        if other != field:
            term = mixing[field, other] * value
            total = term if total is None else total + term
    return total


def pick_rows(kinds, particles, fields, strip):
    shape = (particles, particles * fields * strip)
    place = lax.broadcasted_iota(jnp.int32, shape, 1) - lax.broadcasted_iota(jnp.int32, shape, 0) * (fields * strip)
    blocks = [jnp.where(place == f * strip + x, 1.0, 0.0) for f, x in kinds]
    return jnp.concatenate(blocks, 0).astype(BF16)


def stack_rows(rows):
    sub = lax.broadcasted_iota(jnp.int32, (len(rows), rows[0].shape[1]), 0)
    out = None
    for p, row in enumerate(rows):
        row = jnp.broadcast_to(row, sub.shape)
        out = row if out is None else jnp.where(sub == p, row, out)
    return out


def in_row(column):
    total = jnp.broadcast_to(jnp.sum(column, axis=1, keepdims=True), column.shape)
    diagonal = lax.broadcasted_iota(jnp.int32, total.shape, 0) == lax.broadcasted_iota(jnp.int32, total.shape, 1)
    return jnp.sum(jnp.where(diagonal, total, 0.0), axis=0, keepdims=True)


def wide(v):
    return v[:, :128] + v[:, 128:]


def observation_maps(sizes, cell, value):
    particles, fields, strip, lats, strips = sizes
    x0 = lax.axis_index("lon") * strip
    shift = lats.bit_length() - 1
    local_cell = cell - x0 * lats
    obs_lon = lax.shift_right_arithmetic(local_cell, shift)
    obs_lat = local_cell & (lats - 1)
    count = cell.shape[1]
    here = lax.broadcasted_iota(jnp.int32, (strip, count), 0) == obs_lon
    high = value.astype(BF16)
    rest = value - high.astype(F32)
    mid = rest.astype(BF16)
    low = (rest - mid.astype(F32)).astype(BF16)
    zero = jnp.zeros((strip, count), F32)
    parts = [jnp.where(here, 1.0, zero)]
    parts += [jnp.where(here, p.astype(F32), zero) for p in (high, mid, low)]
    left = jnp.concatenate(parts, 0).astype(BF16)
    right = (lax.broadcasted_iota(jnp.int32, (lats, count), 0) == obs_lat).astype(F32).astype(BF16)
    dense = lax.dot_general(left, right, (((1,), (1,)), ((), ())), preferred_element_type=F32)
    lon = (lax.broadcasted_iota(jnp.int32, (strip, lats), 0) + x0).astype(F32)
    precision = 1.0 + 2.0 * lon / (strip * strips)
    target = dense[strip:2 * strip] + (dense[2 * strip:3 * strip] + dense[3 * strip:])
    return dense[:strip] * (0.25 * precision), target


class Rows:
    def __init__(self, ref, first, columns):
        self.ref, self.first, self.columns = ref, first, columns

    def __getitem__(self, at):
        row = self.first + at[0] * self.columns + at[1]
        return self.ref[row:row + 1]


def scalars_in(ref, fields):
    return Rows(ref, fields * fields, fields), Rows(ref, 0, fields)


def prepare(sizes, state_hbm, noise_hbm, courant_hbm, diffusion_hbm, mixing_hbm, cell_hbm, value_hbm,
            send_east, send_west, state, noise, late_noise, maps, courant, scalars,
            diffusion, mixing, cell, value, sems):
    particles, fields, strip, lats, strips = sizes
    n = fields * particles
    copies = [pltpu.make_async_copy(source, target, sems.at[k]) for k, (source, target) in enumerate((
        (cell_hbm, cell), (value_hbm, value), (courant_hbm, courant), (diffusion_hbm, diffusion),
        (mixing_hbm, mixing), (state_hbm.at[:, :, :8], state.at[:, :, :8]),
        (state_hbm.at[:, :, strip - 8:], state.at[:, :, strip - 8:]), (noise_hbm.at[0], noise),
        (noise_hbm.at[1, :, 0], late_noise), (state_hbm.at[:, :, 8:strip - 8], state.at[:, :, 8:strip - 8])))]
    for copy in copies:
        copy.start()
    copies[0].wait()
    copies[1].wait()
    gain, target = observation_maps(sizes, cell[...], value[...])
    maps[0], maps[1] = gain, target
    kinds = []
    for x, step in ((strip - 1, -1), (0, 1)):
        kinds += [(f, x) for f in range(fields)] + [(f, x + step) for f in range(fields)] + [(0, x + 2 * step)]
    pick0 = pick_rows(kinds, particles, fields, strip)
    pick1 = pick_rows([(0, x) for x in (strip - 1, strip - 2, 0, 1)], particles, 1, strip)
    for copy in copies[2:5]:
        copy.wait()
    for f in range(fields):
        for g in range(fields):
            scalars[f * fields + g:f * fields + g + 1] = jnp.broadcast_to(mixing[f:f + 1, g:g + 1], (1, lats))
        at = fields * fields + f
        scalars[at:at + 1] = jnp.broadcast_to(diffusion[:, f:f + 1], (1, lats))
    diffusion, mixing = scalars_in(scalars, fields)

    sides = []
    for first, inward, outward in ((strip - 8, 2, 1), (0, 1, 2)):
        tile = [coefficients(courant[0, first:first + 8], courant[1, first:first + 8], diffusion[0, f], mixing[f, f])
                for f in range(fields)]
        sides.append([[c[0], c[inward], c[outward], c[3], c[4]] for c in tile])
    def coefs_at(side, f, k):
        at = places[side][0] + k * places[side][2] - places[side][1]
        return [c[at:at + 1] for c in sides[side][f]]

    def maps_at(side, k):
        at = places[side][0] + k * places[side][2]
        return gain[at:at + 1], target[at:at + 1]

    def moved(side, f, k, here, inner, outer):
        centre, inward, outward, to_north, to_south = coefs_at(side, f, k)
        v = here[f]
        total = centre * v + inward * inner + to_north * north(v) + to_south * south(v) + mixed(mixing, f, here)
        return total if outer is None else total + outward * outer

    def nudged(side, value, k):
        g, v = maps_at(side, k)
        push = g * (v - value)
        return value + push, push

    def first_step(side, out):
        def state_at(f, k):
            at = places[side][0] + k * places[side][2]
            return stack_rows([state[p, f, at:at + 1] for p in range(particles)])

        near = [[state_at(f, k) for f in range(fields)] for k in range(3)]
        third = state_at(0, 3)
        for f in range(fields):
            out[f * particles:(f + 1) * particles] = near[0][f]
        result, pushes = [[], []], []
        for k in range(2):
            for f in range(fields):
                new = moved(side, f, k, near[k], near[k + 1][f], near[k - 1][f] if k else None)
                if f == 0:
                    new, push = nudged(side, new, k)
                    pushes.append(push)
                result[k].append(new)
        inside, _ = nudged(side, moved(side, 0, 2, near[2], third, near[1][0]), 2)
        return result, pushes, inside

    places = ((strip - 1, strip - 8, -1), (0, 0, 1))
    copies[5].wait()
    copies[6].wait()
    started = [first_step(0, send_east), first_step(1, send_west)]
    copies[7].wait()
    copies[8].wait()
    rows0 = jnp.dot(pick0, noise[...].reshape(n * strip, lats), preferred_element_type=F32)
    rows1 = jnp.dot(pick1, late_noise[...].reshape(particles * strip, lats), preferred_element_type=F32)

    def edge(side, out):
        x, _, step = places[side]
        base0, base1 = side * (2 * fields + 1) * particles, side * 2 * particles
        result, pushes, inside = started[side]

        def noisy0(k, f):
            at = base0 + (k * fields + f) * particles
            return rows0[at:at + particles]

        def noisy1(k):
            at = base1 + k * particles
            return rows1[at:at + particles]

        result = [[result[k][f] + noisy0(k, f) for f in range(fields)] for k in range(2)]
        inside = inside + noisy0(2, 0)
        g0, _ = maps_at(side, 0)
        g1, _ = maps_at(side, 1)
        slope = [-(1.0 / noise_var) * g0 * (pushes[0] + noisy0(0, 0))]
        bend = [(0.5 / noise_var) * g0 * g0]
        for k, g in enumerate((g0, g1)):
            new = moved(side, 0, k, result[k], result[1][0] if k == 0 else inside, result[0][0] if k else None)
            new, push = nudged(side, new, k)
            miss = maps_at(side, k)[1] - (new + noisy1(k))
            weight = 4.0 * g
            slope.append(-(1.0 / noise_var) * g * (push + noisy1(k)) - weight * (1.0 - g) * miss)
            bend.append((0.5 / noise_var) * g * g + 0.5 * weight * (1.0 - g) * (1.0 - g))
        outward = coefs_at(side, 0, 0)[2]
        onward = coefs_at(side, 0, 1)[2] * (1.0 - g0) * outward
        for f in range(fields):
            out[n + f * particles:n + (f + 1) * particles] = result[0][f]
        out[2 * n:2 * n + particles] = outward * slope[0] + onward * slope[2]
        out[2 * n + particles:2 * n + 2 * particles] = slope[1]
        inner = x + step
        last = (outward * outward * bend[0] + onward * onward * bend[2], bend[1],
                courant[0, x:x + 1], courant[1, x:x + 1], g0, courant[0, inner:inner + 1], g1,
                jnp.zeros((1, lats), F32))
        out[2 * n + 2 * particles:] = stack_rows(last)

    edge(0, send_east)
    edge(1, send_west)
    copies[9].wait()


def zero_halo_coefs(sizes, courant, scalars, coefs):
    particles, fields, strip, lats, strips = sizes
    diffusion, mixing = scalars_in(scalars, fields)
    lon = lax.broadcasted_iota(jnp.int32, (strip, lats), 0)
    for f in range(fields):
        centre, east, west, to_north, to_south = coefficients(
            courant[0], courant[1], diffusion[0, f], mixing[f, f])
        coefs[f, 0] = centre
        coefs[f, 1] = jnp.where(lon == strip - 1, 0.0, east)
        coefs[f, 2] = jnp.where(lon == 0, 0.0, west)
        coefs[f, 3] = to_north
        coefs[f, 4] = to_south


def zero_halo_step(sizes, scalars, coefs):
    particles, fields, strip, lats, strips = sizes
    _, mixing = scalars_in(scalars, fields)

    def moved(values, f):
        v = values[f]
        return (coefs[f, 0] * v + coefs[f, 1] * east_of(v) + coefs[f, 2] * west_of(v)
                + coefs[f, 3] * north(v) + coefs[f, 4] * south(v) + mixed(mixing, f, values))

    return moved


def observed_bulk(sizes, parity, state, noise, late_noise, maps, courant, scalars, earlier, middle, out, weight, coefs, partial):
    particles, fields, strip, lats, strips = sizes

    def one(p):
        moved = zero_halo_step(sizes, scalars, coefs)
        values = [state[p, f] for f in range(fields)]
        results = []
        for f in range(fields):
            new = moved(values, f)
            add = noise[p, f].astype(F32)
            if f == 0:
                push = maps[0] * (maps[1] - new)
                new = new + push
                total = push * (push + 2.0 * add)
            results.append(new + add)
            middle[p, f] = new + add
        new = moved(results, 0)
        add = late_noise[p].astype(F32)
        push = maps[0] * (maps[1] - new)
        new = new + push + add
        miss = maps[1] - new
        total = (0.5 / noise_var) * (total + push * (push + 2.0 * add)) + (2.0 * maps[0]) * (miss * miss)
        out[p] = new
        partial[pl.ds(p, 1), :] = wide(jnp.sum(total, axis=0, keepdims=True))

    here = lax.axis_index("lon") % 2 == parity

    @pl.when(here)
    def _():
        zero_halo_coefs(sizes, courant, scalars, coefs)
        for p in range(particles):
            one(p)
        weight[...] = in_row(partial[...])

    @pl.when(jnp.logical_not(here))
    def _():
        weight[...] = earlier[:1, :128]


def other_bulk(sizes, even_middle, even_observed, even_coefs, odd_middle, odd_observed, odd_coefs,
               noise_hbm, scalars, out, noise, sem):
    particles, fields, strip, lats, strips = sizes

    fetch = pltpu.make_async_copy(noise_hbm.at[1, :, 1:], noise, sem)
    fetch.start()

    def run(middle, observed, coefs):
        moved = zero_halo_step(sizes, scalars, coefs)
        for p in range(particles):
            out[p, 0] = observed[p]
        fetch.wait()

        def body(p, carry):
            values = [middle[p, f] for f in range(fields)]
            for f in range(1, fields):
                out[p, f] = moved(values, f) + noise[p, f - 1].astype(F32)
            return carry

        lax.fori_loop(0, particles, body, 0)

    even = lax.axis_index("lon") % 2 == 0

    @pl.when(even)
    def _():
        run(even_middle, even_observed, even_coefs)

    @pl.when(jnp.logical_not(even))
    def _():
        run(odd_middle, odd_observed, odd_coefs)


def correct(sizes, own_east, own_west, from_west, from_east, scalars, bulk_weight, weight, changes):
    particles, fields, strip, lats, strips = sizes
    n = fields * particles
    diffusion, mixing = scalars_in(scalars, fields)

    def field_rows(ref, start, f):
        return ref[start + f * particles:start + (f + 1) * particles]

    packets = (own_east, from_east, own_west, from_west)
    last = 2 * n + 2 * particles
    zonal = stack_rows([ref[last + 2:last + 3] for ref in packets] + [ref[last + 5:last + 6] for ref in packets])
    merid = stack_rows([ref[last + 3:last + 4] for ref in packets] * 2)
    tile = [coefficients(zonal, merid, diffusion[0, f], mixing[f, f]) for f in range(fields)]
    total = jnp.zeros((particles, lats), F32)
    for k, owner in enumerate(packets):
        other_k = k ^ 1
        other = packets[other_k]
        outward_at = (1, 2, 2, 1)[k]
        outward_other = (1, 2, 2, 1)[other_k]
        gain = owner[last + 4:last + 5]
        gain_other = other[last + 4:last + 5]
        first = []
        for f in range(fields):
            step = tile[f][outward_at][k:k + 1] * field_rows(other, 0, f)
            first.append((1.0 - gain) * step if f == 0 else step)
        mine = k in (0, 2)
        for f in range(fields if mine else 1):
            centre, to_north, to_south = [tile[f][c][k:k + 1] for c in (0, 3, 4)]
            outward = tile[f][outward_at][k:k + 1]
            reach = tile[f][outward_other][other_k:other_k + 1]
            if f == 0:
                reach = (1.0 - gain_other) * reach
            outside = field_rows(other, n, f) + reach * field_rows(owner, 0, f)
            step = (centre * first[f] + outward * outside + to_north * north(first[f])
                    + to_south * south(first[f]) + mixed(mixing, f, first))
            if f == 0:
                seen = field_rows(other, 0, 0)
                slope, slope_step = owner[2 * n:2 * n + particles], owner[2 * n + particles:last]
                bend, bend_step = owner[last:last + 1], owner[last + 1:last + 2]
                total = total + seen * (slope + bend * seen) + step * (slope_step + bend_step * step)
            if mine:
                beside = tile[f][outward_at][4 + k:5 + k] * first[f]
                if f == 0:
                    step = (1.0 - gain) * step
                    beside = (1.0 - owner[last + 6:last + 7]) * beside
                edge, inner = (3, 2) if k == 0 else (0, 1)
                changes[edge, f * particles:(f + 1) * particles] = step
                changes[inner, f * particles:(f + 1) * particles] = beside
    weight[...] = in_row(wide(total)) + bulk_weight[...]


def apply_changes(sizes, current, changes, out):
    particles, fields, strip, lats, strips = sizes
    sub = lax.broadcasted_iota(jnp.int32, (8, lats), 0)
    for p in range(particles):
        for f in range(fields):
            row = f * particles + p
            rows = [jnp.broadcast_to(changes[k, row:row + 1], sub.shape) for k in range(4)]
            out[p, f, :8] = current[p, f, :8] + jnp.where(sub == 0, rows[0], jnp.where(sub == 1, rows[1], 0.0))
            out[p, f, 8:strip - 8] = current[p, f, 8:strip - 8]
            out[p, f, strip - 8:] = current[p, f, strip - 8:] + jnp.where(
                sub == 7, rows[3], jnp.where(sub == 6, rows[2], 0.0))


def assemble(sizes, source, current, received, out, sems):
    particles = sizes[0]
    dom = lax.axis_index("dom")

    def copy(j, ref, at):
        return pltpu.make_async_copy(ref.at[at], out.at[j], sems.at[j])

    for j in range(particles):
        wanted = source[dom * particles + j]
        mine = wanted // particles == dom
        at = wanted % particles

        @pl.when(mine)
        def _():
            copy(j, current, at).start()

        @pl.when(jnp.logical_not(mine))
        def _():
            copy(j, received, at).start()

    for j in range(particles):
        copy(j, current, 0).wait()


def local(ensemble_state, proposal_noise, courant, diffusion, mixing, prior_weight, obs_cell, obs_value, source):
    particles, fields, strip, lats = ensemble_state.shape
    strips = lax.axis_size("lon")
    sizes = (particles, fields, strip, lats, strips)
    packet = jax.ShapeDtypeStruct((2 * particles * fields + 2 * particles + 8, lats), F32)
    cell, value = obs_cell[None], obs_value[None]

    def shape(*dims):
        return jax.ShapeDtypeStruct(dims, F32)

    whole = (particles, fields, strip, lats)

    def in_hbm(array):
        return pltpu.with_memory_space_constraint(array, pltpu.HBM)

    arrays = (ensemble_state, proposal_noise, courant, diffusion[None], mixing, cell, value)
    send_east, send_west, state, noise, late_noise, maps, courant, scalars = pl.pallas_call(
        functools.partial(prepare, sizes),
        out_shape=(packet, packet, shape(*whole), jax.ShapeDtypeStruct(whole, BF16),
                   jax.ShapeDtypeStruct((particles, strip, lats), BF16), shape(2, strip, lats),
                   shape(*courant.shape), shape(fields * (fields + 2), lats)),
        in_specs=[HBM] * 7,
        out_specs=(VMEM,) * 8,
        scratch_shapes=[pltpu.VMEM(array.shape, array.dtype) for array in arrays[3:]]
        + [pltpu.SemaphoreType.DMA((10,))],
        compiler_params=LIMIT,
        cost_estimate=pl.CostEstimate(flops=1000000, bytes_accessed=2000000, transcendentals=0),
    )(*[in_hbm(array) for array in arrays])

    def bulk_of(parity, earlier):
        return pl.pallas_call(
            functools.partial(observed_bulk, sizes, parity),
            out_shape=(shape(*whole), shape(particles, strip, lats), shape(1, 128), shape(fields, 5, strip, lats)),
            in_specs=[VMEM] * 7,
            out_specs=(VMEM,) * 4,
            scratch_shapes=[pltpu.VMEM((particles, 128), F32)],
            compiler_params=LIMIT,
            cost_estimate=pl.CostEstimate(flops=20000000, bytes_accessed=4000000, transcendentals=0),
        )(state, noise, late_noise, maps, courant, scalars, earlier)

    even_middle, even_observed, bulk_weight, even_coefs = bulk_of(0, scalars)
    send_east, send_west, bulk_weight = lax.optimization_barrier((send_east, send_west, bulk_weight))
    eastward = [(i, (i + 1) % strips) for i in range(strips)]
    westward = [(i, (i - 1) % strips) for i in range(strips)]
    from_west = lax.ppermute(send_east, "lon", eastward)
    from_east = lax.ppermute(send_west, "lon", westward)
    odd_middle, odd_observed, bulk_weight, odd_coefs = bulk_of(1, bulk_weight)
    beside = lax.ppermute(bulk_weight, "lon", [(i, i ^ 1) for i in range(strips)])

    current = pl.pallas_call(
        functools.partial(other_bulk, sizes),
        out_shape=shape(*whole),
        in_specs=[VMEM] * 6 + [HBM, VMEM],
        scratch_shapes=[pltpu.VMEM((particles, fields - 1, strip, lats), BF16), pltpu.SemaphoreType.DMA],
        out_specs=VMEM,
        compiler_params=LIMIT,
        cost_estimate=FREE,
    )(even_middle, even_observed, even_coefs, odd_middle, odd_observed, odd_coefs, in_hbm(proposal_noise), scalars)

    weight, changes = pl.pallas_call(
        functools.partial(correct, sizes),
        out_shape=(shape(1, 128), shape(4, particles * fields, lats)),
        in_specs=[VMEM] * 6,
        out_specs=(VMEM,) * 2,
        compiler_params=LIMIT,
        cost_estimate=FREE,
    )(send_east, send_west, from_west, from_east, scalars, bulk_weight)

    current = pl.pallas_call(
        functools.partial(apply_changes, sizes),
        out_shape=shape(*whole),
        in_specs=[VMEM] * 2,
        out_specs=VMEM,
        compiler_params=LIMIT,
        cost_estimate=FREE,
    )(current, changes)

    current, beside = lax.optimization_barrier((current, beside))
    weight = weight + beside
    received = lax.ppermute(current, "dom", [(0, 1), (1, 0)])
    bit = 2
    while bit < strips:
        steps = (2, 3, 1) if 2 * bit < strips else (1,)
        arrived = []
        for step in steps:
            if step == 1 and bit * (len(steps) + 1) >= strips:
                weight, received = lax.optimization_barrier((weight, received))
            arrived.append(lax.ppermute(weight, "lon", [(i, i ^ (bit * step)) for i in range(strips)]))
        weight = sum(arrived, weight)
        bit *= len(steps) + 1

    new_state = pl.pallas_call(
        functools.partial(assemble, sizes),
        out_shape=shape(*whole),
        in_specs=[SMEM, VMEM, VMEM],
        out_specs=HBM,
        scratch_shapes=[pltpu.SemaphoreType.DMA((particles,))],
        compiler_params=LIMIT,
        cost_estimate=pl.CostEstimate(flops=0, bytes_accessed=2000000, transcendentals=0),
    )(source, current, received)

    log_weight = prior_weight - weight[0, :particles] / (256.0 * obs_cell.shape[0])
    return new_state, log_weight


def solution(mesh):
    placed = (
        P(("groups", "dom"), None, "lon", None),
        P(None, ("groups", "dom"), None, "lon", None),
        P(None, ("groups", "lon"), None),
        P(),
        P(),
        P(("groups", "dom")),
        P(("groups", "lon")),
        P(("groups", "lon")),
        P("groups"),
    )
    return jax.shard_map(
        local,
        mesh=mesh,
        in_specs=placed,
        out_specs=(P(("groups", "dom"), None, "lon", None), P(("groups", "dom"))),
        check_vma=False,
    )
```

```python
import functools

import jax
import jax.numpy as jnp
from jax import lax
from jax.experimental import pallas as pl
from jax.experimental.pallas import tpu as pltpu
from jax.sharding import PartitionSpec as P

noise_var = 0.04
VMEM = pl.BlockSpec(memory_space=pltpu.VMEM)
SMEM = pl.BlockSpec(memory_space=pltpu.SMEM)
HBM = pl.BlockSpec(memory_space=pltpu.HBM)
LIMIT = pltpu.CompilerParams(vmem_limit_bytes=16 * 1024 * 1024)
FREE = pl.CostEstimate(flops=0, bytes_accessed=0, transcendentals=0)
BF16 = jnp.bfloat16
F32 = jnp.float32


def north(v):
    low, high = (pltpu.roll(v[:, at:at + 128], 127, 1) for at in (0, 128))
    lane = lax.broadcasted_iota(jnp.int32, low.shape, 1)
    return jnp.concatenate([jnp.where(lane == 127, high, low), high], 1)


def south(v):
    low, high = (pltpu.roll(v[:, at:at + 128], 1, 1) for at in (0, 128))
    lane = lax.broadcasted_iota(jnp.int32, low.shape, 1)
    return jnp.concatenate([low, jnp.where(lane == 0, low, high)], 1)


def east_of(v):
    tiles = [pltpu.roll(v[at:at + 8], 7, 0) for at in range(0, v.shape[0], 8)]
    sub = lax.broadcasted_iota(jnp.int32, tiles[0].shape, 0)
    mixed_tiles = [jnp.where(sub == 7, after, tile) for tile, after in zip(tiles[:-1], tiles[1:])]
    return jnp.concatenate(mixed_tiles + tiles[-1:], 0)


def west_of(v):
    tiles = [pltpu.roll(v[at:at + 8], 1, 0) for at in range(0, v.shape[0], 8)]
    sub = lax.broadcasted_iota(jnp.int32, tiles[0].shape, 0)
    mixed_tiles = [jnp.where(sub == 0, before, tile) for before, tile in zip(tiles[:-1], tiles[1:])]
    return jnp.concatenate(tiles[:1] + mixed_tiles, 0)


def coefficients(zonal, merid, rate, self_mix):
    lat = lax.broadcasted_iota(jnp.int32, zonal.shape, 1)
    zonal_half, zonal_rate = 0.5 * zonal, 0.5 * zonal * zonal + rate
    merid_half, merid_rate = 0.5 * merid, 0.5 * merid * merid + rate
    east, west = zonal_rate - zonal_half, zonal_rate + zonal_half
    to_north, to_south = merid_rate - merid_half, merid_rate + merid_half
    centre = 1.0 + self_mix - 2.0 * zonal_rate - 2.0 * merid_rate
    last, first = lat == zonal.shape[1] - 1, lat == 0
    centre = centre + jnp.where(last, to_north, 0.0) + jnp.where(first, to_south, 0.0)
    to_north = jnp.where(last, 0.0, to_north)
    to_south = jnp.where(first, 0.0, to_south)
    return centre, east, west, to_north, to_south


def mixed(mixing, field, values):
    total = None
    for other, value in enumerate(values):
        if other != field:
            term = mixing[field, other] * value
            total = term if total is None else total + term
    return total


def pick_rows(kinds, particles, fields, strip):
    shape = (particles, particles * fields * strip)
    place = lax.broadcasted_iota(jnp.int32, shape, 1) - lax.broadcasted_iota(jnp.int32, shape, 0) * (fields * strip)
    blocks = [jnp.where(place == f * strip + x, 1.0, 0.0) for f, x in kinds]
    return jnp.concatenate(blocks, 0).astype(BF16)


def stack_rows(rows):
    sub = lax.broadcasted_iota(jnp.int32, (len(rows), rows[0].shape[1]), 0)
    out = None
    for p, row in enumerate(rows):
        row = jnp.broadcast_to(row, sub.shape)
        out = row if out is None else jnp.where(sub == p, row, out)
    return out


def in_row(column):
    total = jnp.broadcast_to(jnp.sum(column, axis=1, keepdims=True), column.shape)
    diagonal = lax.broadcasted_iota(jnp.int32, total.shape, 0) == lax.broadcasted_iota(jnp.int32, total.shape, 1)
    return jnp.sum(jnp.where(diagonal, total, 0.0), axis=0, keepdims=True)


def wide(v):
    return v[:, :128] + v[:, 128:]


def observation_maps(sizes, cell, value):
    particles, fields, strip, lats, strips = sizes
    x0 = lax.axis_index("lon") * strip
    shift = lats.bit_length() - 1
    local_cell = cell - x0 * lats
    obs_lon = lax.shift_right_arithmetic(local_cell, shift)
    obs_lat = local_cell & (lats - 1)
    count = cell.shape[1]
    here = lax.broadcasted_iota(jnp.int32, (strip, count), 0) == obs_lon
    high = value.astype(BF16)
    rest = value - high.astype(F32)
    mid = rest.astype(BF16)
    low = (rest - mid.astype(F32)).astype(BF16)
    zero = jnp.zeros((strip, count), F32)
    parts = [jnp.where(here, 1.0, zero)]
    parts += [jnp.where(here, p.astype(F32), zero) for p in (high, mid, low)]
    left = jnp.concatenate(parts, 0).astype(BF16)
    right = (lax.broadcasted_iota(jnp.int32, (lats, count), 0) == obs_lat).astype(F32).astype(BF16)
    dense = lax.dot_general(left, right, (((1,), (1,)), ((), ())), preferred_element_type=F32)
    lon = (lax.broadcasted_iota(jnp.int32, (strip, lats), 0) + x0).astype(F32)
    precision = 1.0 + 2.0 * lon / (strip * strips)
    target = dense[strip:2 * strip] + (dense[2 * strip:3 * strip] + dense[3 * strip:])
    return dense[:strip] * (0.25 * precision), target


class Rows:
    def __init__(self, ref, first, columns):
        self.ref, self.first, self.columns = ref, first, columns

    def __getitem__(self, at):
        row = self.first + at[0] * self.columns + at[1]
        return self.ref[row:row + 1]


def scalars_in(ref, fields):
    return Rows(ref, fields * fields, fields), Rows(ref, 0, fields)


def prepare(sizes, state_hbm, noise_hbm, courant_hbm, diffusion_hbm, mixing_hbm, cell_hbm, value_hbm,
            send_east, send_west, state, noise, late_noise, maps, courant, scalars,
            diffusion, mixing, cell, value, sems):
    particles, fields, strip, lats, strips = sizes
    n = fields * particles
    copies = [pltpu.make_async_copy(source, target, sems.at[k]) for k, (source, target) in enumerate((
        (cell_hbm, cell), (value_hbm, value), (courant_hbm, courant), (diffusion_hbm, diffusion),
        (mixing_hbm, mixing), (state_hbm.at[:, :, :8], state.at[:, :, :8]),
        (state_hbm.at[:, :, strip - 8:], state.at[:, :, strip - 8:]), (noise_hbm.at[0], noise),
        (noise_hbm.at[1, :, 0], late_noise), (state_hbm.at[:, :, 8:strip - 8], state.at[:, :, 8:strip - 8])))]
    for copy in copies[:5] + copies[7:8] + copies[5:7] + copies[8:]:
        copy.start()
    copies[0].wait()
    copies[1].wait()
    gain, target = observation_maps(sizes, cell[...], value[...])
    maps[0], maps[1] = gain, target
    kinds = []
    for x, step in ((strip - 1, -1), (0, 1)):
        kinds += [(f, x) for f in range(fields)] + [(f, x + step) for f in range(fields)] + [(0, x + 2 * step)]
    pick0 = pick_rows(kinds, particles, fields, strip)
    pick1 = pick_rows([(0, x) for x in (strip - 1, strip - 2, 0, 1)], particles, 1, strip)
    for copy in copies[2:5]:
        copy.wait()
    for f in range(fields):
        for g in range(fields):
            scalars[f * fields + g:f * fields + g + 1] = jnp.broadcast_to(mixing[f:f + 1, g:g + 1], (1, lats))
        at = fields * fields + f
        scalars[at:at + 1] = jnp.broadcast_to(diffusion[:, f:f + 1], (1, lats))
    diffusion, mixing = scalars_in(scalars, fields)

    sides = []
    for first, inward, outward in ((strip - 8, 2, 1), (0, 1, 2)):
        tile = [coefficients(courant[0, first:first + 8], courant[1, first:first + 8], diffusion[0, f], mixing[f, f])
                for f in range(fields)]
        sides.append([[c[0], c[inward], c[outward], c[3], c[4]] for c in tile])
    def coefs_at(side, f, k):
        at = places[side][0] + k * places[side][2] - places[side][1]
        return [c[at:at + 1] for c in sides[side][f]]

    def maps_at(side, k):
        at = places[side][0] + k * places[side][2]
        return gain[at:at + 1], target[at:at + 1]

    def moved(side, f, k, here, inner, outer):
        centre, inward, outward, to_north, to_south = coefs_at(side, f, k)
        v = here[f]
        total = centre * v + inward * inner + to_north * north(v) + to_south * south(v) + mixed(mixing, f, here)
        return total if outer is None else total + outward * outer

    def nudged(side, value, k):
        g, v = maps_at(side, k)
        push = g * (v - value)
        return value + push, push

    def first_step(side, out):
        def state_at(f, k):
            at = places[side][0] + k * places[side][2]
            return stack_rows([state[p, f, at:at + 1] for p in range(particles)])

        near = [[state_at(f, k) for f in range(fields)] for k in range(3)]
        third = state_at(0, 3)
        for f in range(fields):
            out[f * particles:(f + 1) * particles] = near[0][f]
        result, pushes = [[], []], []
        for k in range(2):
            for f in range(fields):
                new = moved(side, f, k, near[k], near[k + 1][f], near[k - 1][f] if k else None)
                if f == 0:
                    new, push = nudged(side, new, k)
                    pushes.append(push)
                result[k].append(new)
        inside, _ = nudged(side, moved(side, 0, 2, near[2], third, near[1][0]), 2)
        return result, pushes, inside

    places = ((strip - 1, strip - 8, -1), (0, 0, 1))
    copies[5].wait()
    copies[6].wait()
    started = [first_step(0, send_east), first_step(1, send_west)]
    copies[7].wait()
    copies[8].wait()
    rows0 = jnp.dot(pick0, noise[...].reshape(n * strip, lats), preferred_element_type=F32)
    rows1 = jnp.dot(pick1, late_noise[...].reshape(particles * strip, lats), preferred_element_type=F32)

    def edge(side, out):
        x, _, step = places[side]
        base0, base1 = side * (2 * fields + 1) * particles, side * 2 * particles
        result, pushes, inside = started[side]

        def noisy0(k, f):
            at = base0 + (k * fields + f) * particles
            return rows0[at:at + particles]

        def noisy1(k):
            at = base1 + k * particles
            return rows1[at:at + particles]

        result = [[result[k][f] + noisy0(k, f) for f in range(fields)] for k in range(2)]
        inside = inside + noisy0(2, 0)
        g0, _ = maps_at(side, 0)
        g1, _ = maps_at(side, 1)
        slope = [-(1.0 / noise_var) * g0 * (pushes[0] + noisy0(0, 0))]
        bend = [(0.5 / noise_var) * g0 * g0]
        for k, g in enumerate((g0, g1)):
            new = moved(side, 0, k, result[k], result[1][0] if k == 0 else inside, result[0][0] if k else None)
            new, push = nudged(side, new, k)
            miss = maps_at(side, k)[1] - (new + noisy1(k))
            weight = 4.0 * g
            slope.append(-(1.0 / noise_var) * g * (push + noisy1(k)) - weight * (1.0 - g) * miss)
            bend.append((0.5 / noise_var) * g * g + 0.5 * weight * (1.0 - g) * (1.0 - g))
        outward = coefs_at(side, 0, 0)[2]
        onward = coefs_at(side, 0, 1)[2] * (1.0 - g0) * outward
        for f in range(fields):
            out[n + f * particles:n + (f + 1) * particles] = result[0][f]
        out[2 * n:2 * n + particles] = outward * slope[0] + onward * slope[2]
        out[2 * n + particles:2 * n + 2 * particles] = slope[1]
        inner = x + step
        last = (outward * outward * bend[0] + onward * onward * bend[2], bend[1],
                courant[0, x:x + 1], courant[1, x:x + 1], g0, courant[0, inner:inner + 1], g1,
                jnp.zeros((1, lats), F32))
        out[2 * n + 2 * particles:] = stack_rows(last)

    edge(0, send_east)
    edge(1, send_west)
    copies[9].wait()


def zero_halo_coefs(sizes, courant, scalars, coefs):
    particles, fields, strip, lats, strips = sizes
    diffusion, mixing = scalars_in(scalars, fields)
    lon = lax.broadcasted_iota(jnp.int32, (strip, lats), 0)
    for f in range(fields):
        centre, east, west, to_north, to_south = coefficients(
            courant[0], courant[1], diffusion[0, f], mixing[f, f])
        coefs[f, 0] = centre
        coefs[f, 1] = jnp.where(lon == strip - 1, 0.0, east)
        coefs[f, 2] = jnp.where(lon == 0, 0.0, west)
        coefs[f, 3] = to_north
        coefs[f, 4] = to_south


def zero_halo_step(sizes, scalars, coefs):
    particles, fields, strip, lats, strips = sizes
    _, mixing = scalars_in(scalars, fields)

    def moved(values, f):
        v = values[f]
        return (coefs[f, 0] * v + coefs[f, 1] * east_of(v) + coefs[f, 2] * west_of(v)
                + coefs[f, 3] * north(v) + coefs[f, 4] * south(v) + mixed(mixing, f, values))

    return moved


def observed_bulk(sizes, parity, state, noise, late_noise, maps, courant, scalars, earlier, middle, out, weight, coefs, partial):
    particles, fields, strip, lats, strips = sizes

    def one(p):
        moved = zero_halo_step(sizes, scalars, coefs)
        values = [state[p, f] for f in range(fields)]
        results = []
        for f in range(fields):
            new = moved(values, f)
            add = noise[p, f].astype(F32)
            if f == 0:
                push = maps[0] * (maps[1] - new)
                new = new + push
                total = push * (push + 2.0 * add)
            results.append(new + add)
            middle[p, f] = new + add
        new = moved(results, 0)
        add = late_noise[p].astype(F32)
        push = maps[0] * (maps[1] - new)
        new = new + push + add
        miss = maps[1] - new
        total = (0.5 / noise_var) * (total + push * (push + 2.0 * add)) + (2.0 * maps[0]) * (miss * miss)
        out[p] = new
        partial[pl.ds(p, 1), :] = wide(jnp.sum(total, axis=0, keepdims=True))

    def body(step, carry):
        for k in range(4):
            one(4 * step + k)
        return carry

    here = lax.axis_index("lon") % 2 == parity

    @pl.when(here)
    def _():
        zero_halo_coefs(sizes, courant, scalars, coefs)
        lax.fori_loop(0, particles // 4, body, 0)
        weight[...] = in_row(partial[...])

    @pl.when(jnp.logical_not(here))
    def _():
        weight[...] = earlier[:1, :128]


def other_bulk(sizes, even_middle, even_observed, even_coefs, odd_middle, odd_observed, odd_coefs,
               noise_hbm, scalars, out, noise, sem):
    particles, fields, strip, lats, strips = sizes

    fetch = pltpu.make_async_copy(noise_hbm.at[1, :, 1:], noise, sem)
    fetch.start()

    def run(middle, observed, coefs):
        moved = zero_halo_step(sizes, scalars, coefs)
        for p in range(particles):
            out[p, 0] = observed[p]
        fetch.wait()

        def body(p, carry):
            values = [middle[p, f] for f in range(fields)]
            for f in range(1, fields):
                out[p, f] = moved(values, f) + noise[p, f - 1].astype(F32)
            return carry

        lax.fori_loop(0, particles, body, 0)

    even = lax.axis_index("lon") % 2 == 0

    @pl.when(even)
    def _():
        run(even_middle, even_observed, even_coefs)

    @pl.when(jnp.logical_not(even))
    def _():
        run(odd_middle, odd_observed, odd_coefs)


def correct(sizes, own_east, own_west, from_west, from_east, scalars, bulk_weight, weight, changes):
    particles, fields, strip, lats, strips = sizes
    n = fields * particles
    diffusion, mixing = scalars_in(scalars, fields)

    def field_rows(ref, start, f):
        return ref[start + f * particles:start + (f + 1) * particles]

    packets = (own_east, from_east, own_west, from_west)
    last = 2 * n + 2 * particles
    zonal = stack_rows([ref[last + 2:last + 3] for ref in packets] + [ref[last + 5:last + 6] for ref in packets])
    merid = stack_rows([ref[last + 3:last + 4] for ref in packets] * 2)
    tile = [coefficients(zonal, merid, diffusion[0, f], mixing[f, f]) for f in range(fields)]
    total = jnp.zeros((particles, lats), F32)
    for k, owner in enumerate(packets):
        other_k = k ^ 1
        other = packets[other_k]
        outward_at = (1, 2, 2, 1)[k]
        outward_other = (1, 2, 2, 1)[other_k]
        gain = owner[last + 4:last + 5]
        gain_other = other[last + 4:last + 5]
        first = []
        for f in range(fields):
            step = tile[f][outward_at][k:k + 1] * field_rows(other, 0, f)
            first.append((1.0 - gain) * step if f == 0 else step)
        mine = k in (0, 2)
        for f in range(fields if mine else 1):
            centre, to_north, to_south = [tile[f][c][k:k + 1] for c in (0, 3, 4)]
            outward = tile[f][outward_at][k:k + 1]
            reach = tile[f][outward_other][other_k:other_k + 1]
            if f == 0:
                reach = (1.0 - gain_other) * reach
            outside = field_rows(other, n, f) + reach * field_rows(owner, 0, f)
            step = (centre * first[f] + outward * outside + to_north * north(first[f])
                    + to_south * south(first[f]) + mixed(mixing, f, first))
            if f == 0:
                seen = field_rows(other, 0, 0)
                slope, slope_step = owner[2 * n:2 * n + particles], owner[2 * n + particles:last]
                bend, bend_step = owner[last:last + 1], owner[last + 1:last + 2]
                total = total + seen * (slope + bend * seen) + step * (slope_step + bend_step * step)
            if mine:
                beside = tile[f][outward_at][4 + k:5 + k] * first[f]
                if f == 0:
                    step = (1.0 - gain) * step
                    beside = (1.0 - owner[last + 6:last + 7]) * beside
                edge, inner = (3, 2) if k == 0 else (0, 1)
                changes[edge, f * particles:(f + 1) * particles] = step
                changes[inner, f * particles:(f + 1) * particles] = beside
    weight[...] = in_row(wide(total)) + bulk_weight[...]


def apply_changes(sizes, current, changes, out):
    particles, fields, strip, lats, strips = sizes
    sub = lax.broadcasted_iota(jnp.int32, (8, lats), 0)
    for p in range(particles):
        for f in range(fields):
            row = f * particles + p
            rows = [jnp.broadcast_to(changes[k, row:row + 1], sub.shape) for k in range(4)]
            out[p, f, :8] = current[p, f, :8] + jnp.where(sub == 0, rows[0], jnp.where(sub == 1, rows[1], 0.0))
            out[p, f, 8:strip - 8] = current[p, f, 8:strip - 8]
            out[p, f, strip - 8:] = current[p, f, strip - 8:] + jnp.where(
                sub == 7, rows[3], jnp.where(sub == 6, rows[2], 0.0))


def assemble(sizes, source, current, received, out, sems):
    particles = sizes[0]
    dom = lax.axis_index("dom")

    def copy(j, ref, at):
        return pltpu.make_async_copy(ref.at[at], out.at[j], sems.at[j])

    for j in range(particles):
        wanted = source[dom * particles + j]
        mine = wanted // particles == dom
        at = wanted % particles

        @pl.when(mine)
        def _():
            copy(j, current, at).start()

        @pl.when(jnp.logical_not(mine))
        def _():
            copy(j, received, at).start()

    for j in range(particles):
        copy(j, current, 0).wait()


def local(ensemble_state, proposal_noise, courant, diffusion, mixing, prior_weight, obs_cell, obs_value, source):
    particles, fields, strip, lats = ensemble_state.shape
    strips = lax.axis_size("lon")
    sizes = (particles, fields, strip, lats, strips)
    packet = jax.ShapeDtypeStruct((2 * particles * fields + 2 * particles + 8, lats), F32)
    cell, value = obs_cell[None], obs_value[None]

    def shape(*dims):
        return jax.ShapeDtypeStruct(dims, F32)

    whole = (particles, fields, strip, lats)

    def in_hbm(array):
        return pltpu.with_memory_space_constraint(array, pltpu.HBM)

    arrays = (ensemble_state, proposal_noise, courant, diffusion[None], mixing, cell, value)
    send_east, send_west, state, noise, late_noise, maps, courant, scalars = pl.pallas_call(
        functools.partial(prepare, sizes),
        out_shape=(packet, packet, shape(*whole), jax.ShapeDtypeStruct(whole, BF16),
                   jax.ShapeDtypeStruct((particles, strip, lats), BF16), shape(2, strip, lats),
                   shape(*courant.shape), shape(fields * (fields + 2), lats)),
        in_specs=[HBM] * 7,
        out_specs=(VMEM,) * 8,
        scratch_shapes=[pltpu.VMEM(array.shape, array.dtype) for array in arrays[3:]]
        + [pltpu.SemaphoreType.DMA((10,))],
        compiler_params=LIMIT,
        cost_estimate=pl.CostEstimate(flops=1000000, bytes_accessed=2000000, transcendentals=0),
    )(*[in_hbm(array) for array in arrays])

    def bulk_of(parity, earlier):
        return pl.pallas_call(
            functools.partial(observed_bulk, sizes, parity),
            out_shape=(shape(*whole), shape(particles, strip, lats), shape(1, 128), shape(fields, 5, strip, lats)),
            in_specs=[VMEM] * 7,
            out_specs=(VMEM,) * 4,
            scratch_shapes=[pltpu.VMEM((particles, 128), F32)],
            compiler_params=LIMIT,
            cost_estimate=pl.CostEstimate(flops=20000000, bytes_accessed=4000000, transcendentals=0),
        )(state, noise, late_noise, maps, courant, scalars, earlier)

    even_middle, even_observed, bulk_weight, even_coefs = bulk_of(0, scalars)
    send_east, send_west, bulk_weight = lax.optimization_barrier((send_east, send_west, bulk_weight))
    eastward = [(i, (i + 1) % strips) for i in range(strips)]
    westward = [(i, (i - 1) % strips) for i in range(strips)]
    from_west = lax.ppermute(send_east, "lon", eastward)
    from_east = lax.ppermute(send_west, "lon", westward)
    odd_middle, odd_observed, bulk_weight, odd_coefs = bulk_of(1, bulk_weight)
    beside = lax.ppermute(bulk_weight, "lon", [(i, i ^ 1) for i in range(strips)])

    current = pl.pallas_call(
        functools.partial(other_bulk, sizes),
        out_shape=shape(*whole),
        in_specs=[VMEM] * 6 + [HBM, VMEM],
        scratch_shapes=[pltpu.VMEM((particles, fields - 1, strip, lats), BF16), pltpu.SemaphoreType.DMA],
        out_specs=VMEM,
        compiler_params=LIMIT,
        cost_estimate=FREE,
    )(even_middle, even_observed, even_coefs, odd_middle, odd_observed, odd_coefs, in_hbm(proposal_noise), scalars)

    weight, changes = pl.pallas_call(
        functools.partial(correct, sizes),
        out_shape=(shape(1, 128), shape(4, particles * fields, lats)),
        in_specs=[VMEM] * 6,
        out_specs=(VMEM,) * 2,
        compiler_params=LIMIT,
        cost_estimate=FREE,
    )(send_east, send_west, from_west, from_east, scalars, bulk_weight)

    current = pl.pallas_call(
        functools.partial(apply_changes, sizes),
        out_shape=shape(*whole),
        in_specs=[VMEM] * 2,
        out_specs=VMEM,
        compiler_params=LIMIT,
        cost_estimate=FREE,
    )(current, changes)

    current, beside = lax.optimization_barrier((current, beside))
    weight = weight + beside
    received = lax.ppermute(current, "dom", [(0, 1), (1, 0)])
    bit = 2
    while bit < strips:
        steps = (2, 3, 1) if 2 * bit < strips else (1,)
        arrived = []
        for step in steps:
            if step == 1 and bit * (len(steps) + 1) >= strips:
                weight, received = lax.optimization_barrier((weight, received))
            arrived.append(lax.ppermute(weight, "lon", [(i, i ^ (bit * step)) for i in range(strips)]))
        weight = sum(arrived, weight)
        bit *= len(steps) + 1

    new_state = pl.pallas_call(
        functools.partial(assemble, sizes),
        out_shape=shape(*whole),
        in_specs=[SMEM, VMEM, VMEM],
        out_specs=HBM,
        scratch_shapes=[pltpu.SemaphoreType.DMA((particles,))],
        compiler_params=LIMIT,
        cost_estimate=pl.CostEstimate(flops=0, bytes_accessed=2000000, transcendentals=0),
    )(source, current, received)

    log_weight = prior_weight - weight[0, :particles] / (256.0 * obs_cell.shape[0])
    return new_state, log_weight


def solution(mesh):
    placed = (
        P(("groups", "dom"), None, "lon", None),
        P(None, ("groups", "dom"), None, "lon", None),
        P(None, ("groups", "lon"), None),
        P(),
        P(),
        P(("groups", "dom")),
        P(("groups", "lon")),
        P(("groups", "lon")),
        P("groups"),
    )
    return jax.shard_map(
        local,
        mesh=mesh,
        in_specs=placed,
        out_specs=(P(("groups", "dom"), None, "lon", None), P(("groups", "dom"))),
        check_vma=False,
    )
```
